32 devices in a mesh: enc: 4 (over z), seq: 2 (over x), req: 4 (over y, core).
Axes of the slice: x: 2, y: 2, z: 4, core: 2. Of those that a mesh axis runs over, the one named last changes fastest.
Arguments:
- encoder_hidden: bfloat16 [2, 128, 4096], P('seq', None, ('enc', 'req'))
- prompt_token_ids: int32 [2, 128], replicated, may hold values from 0 to 32127, as said below
- context_weight: bfloat16 [4096, 3072], P(('enc', 'req'))
- context_bias: bfloat16 [3072], P(('enc', 'req')), may hold values from -16 to 16
- modulation_shift: bfloat16 [2, 3072], P('seq', ('enc', 'req')), may hold values from -6 to 6
- modulation_scale: bfloat16 [2, 3072], P('seq', ('enc', 'req')), may hold values from -3 to 3
- key_value_weight: bfloat16 [3072, 6144], P(('enc', 'req')), may hold values from -0.109375 to 0.109375
- key_value_bias: bfloat16 [6144], replicated, may hold values from -6 to 6
- request_prompt: int32 [4, 4], P('enc', 'req'), may hold values from 0 to 1
- adapter_of_request: int32 [4, 4], P('enc', 'req'), may hold values from 0 to 3
- adapter_down_maps: bfloat16 [4, 3072, 64], P('req'), may hold values from -0.109375 to 0.109375
- adapter_up_maps: bfloat16 [4, 64, 3072], P('req'), may hold values from -0.75 to 0.75
- image_stream_input: bfloat16 [4, 4, 128, 3072], P('enc', 'req', 'seq'), may hold values from -6 to 6
- image_query_key: bfloat16 [4, 4, 128, 6144], P('enc', 'req', 'seq'), may hold values from -4.5 to 4.5
- image_value_rows: bfloat16 [4, 4, 128, 3072], P('enc', 'req', 'seq'), may hold values from -6 to 6
Outputs:
- attended: bfloat16 [4, 4, 128, 3072], P('enc', 'req', 'seq')
The draws below stay inside these ranges and needn't reach their ends.
Inputs may be any that keep to these rules, and one draw needn't show every extreme that they name: `prompt_token_ids`: id 0 marks padding; in each prompt the live tokens come first, end with id 1 and number at least 32; some prompt has no padding. `request_prompt`: a prompt index below 2. `adapter_of_request`: an adapter index below 4.
All inputs are finite; a program needn't handle non-finite values.
Results may differ from the reference program's by a relative error of at most 0.0039.
Values may be sent and summed in bfloat16 or wider, within the bound.
No kernel may reach another device: no remote copies, remote signals or barrier semaphores. Data moves between devices by JAX's collectives and lax.ppermute only.
A program may use at most 64 MiB of HBM per device.

```python
import math
import jax
import jax.numpy as jnp
import numpy as np
from jax import lax

MODEL_WIDTH = 3072
T5D = 4096
HDIM = 128
ADAPTER_RANK = 64
VOCAB = 32128
TXT = 128
HEAD_COLUMNS = 3072
IMG = 128
PROMPTS = 2
ADAPTER_COUNT = 4
N_ENC = 4
N_REQ = 4


def draw_encoder_hidden(key, part):
    key = jax.random.fold_in(key, 11)
    first_key, second_key = jax.random.split(key, 2)
    values = jnp.clip(jax.random.normal(first_key, (PROMPTS, TXT, T5D), jnp.float32), -4.0, 4.0)
    scales = jnp.exp(jax.random.uniform(second_key, (PROMPTS, TXT, 1), jnp.float32) * math.log(10.0))
    return (values * scales).astype(jnp.bfloat16)


def draw_context_weight(key, part):
    key = jax.random.fold_in(key, 12)
    first_key, second_key = jax.random.split(key, 2)
    position = jnp.arange(MODEL_WIDTH, dtype=jnp.float32)[None, :] / MODEL_WIDTH
    values = jnp.clip(jax.random.normal(first_key, (T5D, MODEL_WIDTH), jnp.float32), -4.0, 4.0) / math.sqrt(T5D)
    columns = jnp.exp(jax.random.uniform(second_key, (1, MODEL_WIDTH), jnp.float32) * math.log(10.0)) * jnp.exp(0.5 * math.log(3.0) * position)
    return (values * columns).astype(jnp.bfloat16)


def draw_image_query_key(key, part):
    key = jax.random.fold_in(key, 13)
    first_key = jax.random.fold_in(key, 0)
    shape_full = (N_ENC, N_REQ, IMG, 2 * HEAD_COLUMNS)
    values = jnp.clip(jax.random.normal(first_key, shape_full, jnp.float32), -4.5, 4.5)
    return values.astype(jnp.bfloat16)


def draw_prompt_token_ids(key, part):
    key = jax.random.fold_in(key, 14)
    first_key, second_key, third_key = jax.random.split(key, 3)
    lengths = jax.random.randint(first_key, (PROMPTS, 1), TXT // 4, TXT + 1)
    full_row = jax.random.randint(second_key, (), 0, PROMPTS)
    short_row = (full_row + 1) % PROMPTS
    rows = jnp.arange(PROMPTS)[:, None]
    lengths = jnp.where(rows == short_row, TXT // 4, lengths)
    lengths = jnp.where(rows == full_row, TXT, lengths)
    tokens = jax.random.randint(third_key, (PROMPTS, TXT), 2, VOCAB)
    position = jnp.arange(TXT)[None, :]
    tokens = jnp.where((rows == full_row) & (position == 0), VOCAB - 1, tokens)
    tokens = jnp.where(position == lengths - 1, 1, tokens)
    return jnp.where(position < lengths, tokens, 0).astype(jnp.int32)


def plant(values, rng, low, top_value):
    extent = values.shape
    spot = [jax.random.randint(jax.random.fold_in(rng, axis), (), 0, extent[axis]) for axis in range(len(extent))]
    values = values.at[tuple(spot)].set(low)
    longest = extent.index(max(extent))
    spot[longest] = (spot[longest] + 1) % extent[longest]
    return values.at[tuple(spot)].set(top_value)


def shard_levels(stream_key, dims, cuts, low, high):
    level = 1.0
    for dim, parts in cuts:
        heights = jax.random.uniform(jax.random.fold_in(jax.random.fold_in(stream_key, 6), dim), (parts,), jnp.float32, low / len(cuts), high / len(cuts))
        level = level * jnp.repeat(jnp.exp(heights), dims[dim] // parts).reshape((-1,) + (1,) * (len(dims) - 1 - dim))
    return level


def rank_bounds(number_of, slope):
    weights = [(1 << 20) // math.isqrt(rank ** slope) + 1 for rank in range(1, number_of + 1)]
    deviation = 1 + sum(weights) // (1 << 30)
    return np.cumsum(np.array([max(1, weight // deviation) for weight in weights]))


def skewed_ids(key, dims, amount, skew):
    grid = rank_bounds(amount, skew)
    lot = jax.random.randint(jax.random.fold_in(key, 1), dims, 0, int(grid[amount - 1]))
    grade = jnp.searchsorted(jnp.asarray(grid, jnp.int32), lot, side="right")
    return jax.random.permutation(jax.random.fold_in(key, 2), amount)[grade].astype(jnp.int32)


def normal_values(rng, extent, scale, most, cuts=(), kind=jnp.bfloat16):
    loudness = shard_levels(rng, extent, cuts, -0.22, 0.18) if cuts else 1.0
    result = jax.random.normal(rng, extent, jnp.float32) * scale * loudness
    return jnp.minimum(jnp.maximum(result, -most), most).astype(kind)


def setup_inputs(seed: int = 0) -> dict:
    key_of = jax.random.split(jax.random.key(seed), 16)
    return {
        "encoder_hidden": draw_encoder_hidden(jax.random.fold_in(key_of[15], 71), 0),
        "prompt_token_ids": draw_prompt_token_ids(jax.random.fold_in(key_of[15], 71), 0),
        "context_weight": draw_context_weight(jax.random.fold_in(key_of[15], 71), 0),
        "context_bias": normal_values(key_of[3], (MODEL_WIDTH,), 3.0, 16.0, ((0, 16),)),
        "modulation_shift": normal_values(key_of[4], (PROMPTS, MODEL_WIDTH), 1.0, 6.0, ((0, 2), (1, 16))),
        "modulation_scale": normal_values(key_of[5], (PROMPTS, MODEL_WIDTH), 0.5, 3.0, ((0, 2), (1, 16))),
        "key_value_weight": normal_values(key_of[6], (MODEL_WIDTH, 2 * HEAD_COLUMNS), MODEL_WIDTH ** -0.5, 0.109375, ((0, 16),)),
        "key_value_bias": normal_values(key_of[7], (2 * HEAD_COLUMNS,), 1.0, 6.0),
        "request_prompt": plant(skewed_ids(key_of[8], (N_ENC, N_REQ), PROMPTS, 2), jax.random.fold_in(key_of[8], 3), 0, PROMPTS - 1).astype(jnp.int32),
        "adapter_of_request": plant(jax.random.randint(key_of[9], (N_ENC, N_REQ), 0, ADAPTER_COUNT), jax.random.fold_in(key_of[9], 1), 0, ADAPTER_COUNT - 1).astype(jnp.int32),
        "adapter_down_maps": normal_values(key_of[10], (ADAPTER_COUNT, MODEL_WIDTH, ADAPTER_RANK), MODEL_WIDTH ** -0.5, 0.109375, ((0, 4),)),
        "adapter_up_maps": normal_values(key_of[11], (ADAPTER_COUNT, ADAPTER_RANK, HEAD_COLUMNS), ADAPTER_RANK ** -0.5, 0.75, ((0, 4),)),
        "image_stream_input": normal_values(key_of[12], (N_ENC, N_REQ, IMG, MODEL_WIDTH), 1.0, 6.0, ((0, 4), (1, 4), (2, 2))),
        "image_query_key": draw_image_query_key(jax.random.fold_in(key_of[15], 71), 0),
        "image_value_rows": normal_values(key_of[14], (N_ENC, N_REQ, IMG, HEAD_COLUMNS), 1.0, 6.0, ((0, 4), (1, 4), (2, 2))),
    }


epsilon_norm = 1e-06

def finish_rows(projected):
    row_count = projected.shape[0]
    inner_width = projected.shape[1] // 2
    key_part = projected[:, :inner_width].reshape(row_count, inner_width // HDIM, HDIM)
    key_part = key_part * lax.rsqrt(lax.optimization_barrier(jnp.mean(key_part * key_part, axis=2, keepdims=True)) + epsilon_norm)
    return jnp.concatenate([key_part.reshape(row_count, inner_width), projected[:, inner_width:]], axis=1).astype(jnp.bfloat16)

def text_stream(hidden, context_weight, context_bias, shift_row, scale_row, key_value_weight, key_value_bias):
    embedded = jnp.dot(hidden, context_weight, preferred_element_type=jnp.float32) + context_bias.astype(jnp.float32)
    average = lax.optimization_barrier(jnp.sum(embedded, axis=1)) / MODEL_WIDTH
    spread = lax.optimization_barrier(jnp.sum(embedded * embedded, axis=1)) / MODEL_WIDTH - average * average
    normed = (embedded - average[:, None]) * lax.rsqrt(spread + epsilon_norm)[:, None]
    modulated = ((1.0 + scale_row.astype(jnp.float32)) * normed + shift_row.astype(jnp.float32)).astype(jnp.bfloat16)
    projected = jnp.dot(modulated, key_value_weight, preferred_element_type=jnp.float32) + key_value_bias.astype(jnp.float32)
    return finish_rows(projected)

def attend(queries, key_rows, value_rows, live_keys):
    scores = jnp.einsum('qhd,khd->hqk', queries.astype(jnp.float32), key_rows.astype(jnp.float32)) * HDIM ** (-0.5)
    scores = jnp.where(live_keys[None, None, :], scores, -jnp.inf)
    largest = lax.optimization_barrier(jnp.max(scores, axis=2, keepdims=True))
    weights = jnp.exp(scores - largest)
    totals = lax.optimization_barrier(jnp.sum(weights, axis=2, keepdims=True))
    rounded = weights.astype(jnp.bfloat16)
    mixed = jnp.einsum('hqk,khd->hqd', rounded.astype(jnp.float32), value_rows.astype(jnp.float32)) / totals
    return jnp.swapaxes(mixed, 0, 1).astype(jnp.bfloat16)

def reference(encoder_hidden, prompt_token_ids, context_weight, context_bias, modulation_shift, modulation_scale, key_value_weight, key_value_bias, request_prompt, adapter_of_request, adapter_down_maps, adapter_up_maps, image_stream_input, image_query_key, image_value_rows):

    def one_prompt(pieces):
        return text_stream(pieces[0], context_weight, context_bias, pieces[1], pieces[2], key_value_weight, key_value_bias)
    text_rows = lax.map(one_prompt, (encoder_hidden, modulation_shift, modulation_scale))

    def one_request(pieces):
        chosen, request_adapter, image_inputs, qk_rows, base_value = pieces
        adapter_delta = jnp.dot(image_inputs, adapter_down_maps[request_adapter], preferred_element_type=jnp.float32).astype(jnp.bfloat16)
        image_value_base = (base_value.astype(jnp.float32) + jnp.dot(adapter_delta, adapter_up_maps[request_adapter], preferred_element_type=jnp.float32)).astype(jnp.bfloat16)
        inner_width = base_value.shape[1]
        head_count = inner_width // HDIM
        text_kv = text_rows[chosen]
        live_keys = jnp.concatenate([prompt_token_ids[chosen] != 0, jnp.ones((IMG,), dtype=jnp.bool_)])
        queries = qk_rows[:, :inner_width].reshape(IMG, head_count, HDIM)
        key_rows = jnp.concatenate([text_kv[:, :inner_width], qk_rows[:, inner_width:]], axis=0).reshape(TXT + IMG, head_count, HDIM)
        value_rows = jnp.concatenate([text_kv[:, inner_width:], image_value_base], axis=0).reshape(TXT + IMG, head_count, HDIM)
        return attend(queries, key_rows, value_rows, live_keys).reshape(IMG, inner_width)
    results = lax.map(one_request, (request_prompt.reshape(-1), adapter_of_request.reshape(-1), image_stream_input.reshape(-1, IMG, MODEL_WIDTH), image_query_key.reshape(-1, IMG, 2 * HEAD_COLUMNS), image_value_rows.reshape(-1, IMG, HEAD_COLUMNS)))
    return results.reshape(image_value_rows.shape)
```

```python
import functools

import jax
import jax.numpy as jnp
from jax import lax
from jax.experimental import pallas as pl
from jax.experimental.pallas import tpu as pltpu
from jax.sharding import PartitionSpec as P

HDIM = 128
ROWS = 16

epsilon_norm = 1e-06


def swap(block, axis, size, step):
    return lax.ppermute(block, axis, [(i, i ^ step) for i in range(size)])


def pick(array, index, dim):
    return lax.dynamic_index_in_dim(array, index, dim, keepdims=False)


def split_two(value):
    high = lax.reduce_precision(value, 8, 7)
    return high.astype(jnp.bfloat16), (value - high).astype(jnp.bfloat16)


def bits_of(size):
    return [1 << b for b in range(size.bit_length() - 1)]


def with_stat_rows(data, stat):
    high, low = split_two(stat)
    rows = jnp.concatenate(
        [high[None], low[None], jnp.zeros((ROWS - 2, stat.shape[0]), jnp.bfloat16)], axis=0
    )
    rows = jnp.broadcast_to(rows, data.shape[:-2] + rows.shape)
    return jnp.concatenate([data.astype(jnp.bfloat16), rows], axis=-2)


def attention_kernel(heads, inner, scale, mask_ref, q_ref, kt_ref, vt_ref, ki_ref, vi_ref, o_ref):
    live = mask_ref[...] != 0
    for h in range(heads):
        cols = slice(h * HDIM, (h + 1) * HDIM)
        q = q_ref[:, cols]
        dims = (((1,), (1,)), ((), ()))
        st = lax.dot_general(q, kt_ref[:, cols], dims, preferred_element_type=jnp.float32) * scale
        si = lax.dot_general(q, ki_ref[:, cols], dims, preferred_element_type=jnp.float32) * scale
        st = jnp.where(live, st, -jnp.inf)
        top = jnp.maximum(
            jnp.max(st, axis=1, keepdims=True), jnp.max(si, axis=1, keepdims=True)
        )
        wt = jnp.exp(st - top)
        wi = jnp.exp(si - top)
        total = jnp.sum(wt, axis=1, keepdims=True) + jnp.sum(wi, axis=1, keepdims=True)
        mixed = jnp.dot(
            wt.astype(jnp.bfloat16), vt_ref[:, cols], preferred_element_type=jnp.float32
        ) + jnp.dot(wi.astype(jnp.bfloat16), vi_ref[:, cols], preferred_element_type=jnp.float32)
        o_ref[:, cols] = (mixed / total).astype(o_ref.dtype)


def attention(queries, text_keys, text_values, image_keys, image_values, live):
    width = queries.shape[1]
    heads = width // HDIM
    rows = queries.shape[0]
    mask = jnp.broadcast_to(live.astype(jnp.int32)[None, :], (8, live.shape[0]))[:1]
    return pl.pallas_call(
        functools.partial(attention_kernel, heads, width, HDIM ** (-0.5)),
        out_shape=jax.ShapeDtypeStruct((rows, width), jnp.bfloat16),
        compiler_params=pltpu.CompilerParams(vmem_limit_bytes=48 * 1024 * 1024),
        name="attention",
    )(mask, queries, text_keys, text_values, image_keys, image_values)


def per_device(
    n_enc,
    n_req,
    n_seq,
    encoder_hidden,
    prompt_token_ids,
    context_weight,
    context_bias,
    modulation_shift,
    modulation_scale,
    key_value_weight,
    key_value_bias,
    request_prompt,
    adapter_of_request,
    adapter_down_maps,
    adapter_up_maps,
    image_stream_input,
    image_query_key,
    image_value_rows,
):
    f32, bf16 = jnp.float32, jnp.bfloat16
    e, r, s = lax.axis_index("enc"), lax.axis_index("req"), lax.axis_index("seq")
    req_bits = bits_of(n_req)
    model_width = context_weight.shape[1]
    features = context_bias.shape[0]
    tokens = encoder_hidden.shape[1]
    inner = key_value_weight.shape[1] // 2
    part = inner // n_seq

    def heads_of(array, share):
        return lax.dynamic_slice_in_dim(array, share * part, part, 1)

    qk = image_query_key[0, 0]
    sources = [qk[:, :inner], qk[:, inner:], image_value_rows[0, 0], image_stream_input[0, 0]]
    image_parts = [
        jnp.stack([heads_of(a, s ^ k) for a in sources]) for k in range(n_seq)
    ]
    image_parts = [image_parts[0]] + [
        swap(image_parts[k], "seq", n_seq, k) for k in range(1, n_seq)
    ]
    image_all = jnp.concatenate(image_parts, axis=1)
    queries, image_keys, base_values, stream = [image_all[i] for i in range(4)]

    partial_value = lax.dot_general(
        context_weight, encoder_hidden[0], (((0,), (1,)), ((), ())), preferred_element_type=f32
    )
    stat = jnp.sum(partial_value, axis=0) + jnp.sum(context_bias.astype(f32))
    acc = partial_value.reshape((n_enc,) + (2,) * len(req_bits) + (features, tokens))
    for i, bit in enumerate(req_bits):
        mine = (r // bit) % 2
        dim = len(req_bits) - i
        got = swap(with_stat_rows(pick(acc, 1 - mine, dim), stat), "req", n_req, bit).astype(f32)
        acc = pick(acc, mine, dim) + got[..., :features, :]
        got_stat = got.reshape((-1,) + got.shape[-2:])[0, features:]
        stat = stat + got_stat[0] + got_stat[1]
    arrived = [
        swap(with_stat_rows(pick(acc, e ^ k, 0), stat), "enc", n_enc, k).astype(f32)
        for k in range(1, n_enc)
    ]
    embedded = pick(acc, e, 0)
    for got in arrived:
        embedded = embedded + got[:features]
        stat = stat + got[features] + got[features + 1]
    embedded = embedded + context_bias.astype(f32)[:, None]
    centred = embedded - (stat / model_width)[None, :]
    squares = jnp.sum(centred * centred, axis=0)
    scaled = (1.0 + modulation_scale[0].astype(f32))[:, None] * centred

    own = with_stat_rows(scaled, squares)
    blocks = [own] + [swap(own, "seq", n_seq, k) for k in range(1, n_seq)]
    scaled_all = jnp.concatenate([b[:features] for b in blocks], axis=1)
    squares_all = jnp.concatenate(
        [b[features].astype(f32) + b[features + 1].astype(f32) for b in blocks]
    )
    weight_own = jnp.concatenate(
        [heads_of(key_value_weight[:, :inner], s), heads_of(key_value_weight[:, inner:], s)], axis=1
    )
    width = 2 * part
    projected = lax.dot_general(
        scaled_all, weight_own, (((0,), (0,)), ((), ())), preferred_element_type=f32
    )

    shift_part = jnp.dot(modulation_shift, key_value_weight, preferred_element_type=f32)
    for bit in req_bits:
        shift_part = shift_part + swap(shift_part, "req", n_req, bit)
    for bit in bits_of(n_enc):
        shift_part = shift_part + swap(shift_part, "enc", n_enc, bit)
    shift_part = shift_part + key_value_bias.astype(f32)[None]

    def columns_of(row, share):
        return jnp.concatenate(
            [heads_of(row[:, :inner], share), heads_of(row[:, inner:], share)], axis=1
        )

    shift_rows = jnp.concatenate(
        [columns_of(shift_part, s)]
        + [swap(columns_of(shift_part, s ^ k), "seq", n_seq, k) for k in range(1, n_seq)],
        axis=0,
    )

    halves = tokens // n_req // ROWS
    split = (n_seq,) + (2,) * len(req_bits) + (halves, ROWS)
    acc = projected.reshape(split + (width,))
    acc_stat = squares_all.reshape(split)

    def with_stat_columns(data, stat):
        high, low = split_two(stat)
        lane = lax.broadcasted_iota(jnp.int32, stat.shape + (HDIM,), stat.ndim)
        columns = jnp.where(
            lane == 0, high[..., None], jnp.where(lane == 1, low[..., None], jnp.zeros((), bf16))
        )
        return jnp.concatenate([data.astype(bf16), columns], axis=-1)

    for i, bit in enumerate(req_bits):
        mine = (r // bit) % 2
        dim = len(req_bits) - i
        got = swap(
            with_stat_columns(pick(acc, 1 - mine, dim), pick(acc_stat, 1 - mine, dim)),
            "req", n_req, bit,
        ).astype(f32)
        acc = pick(acc, mine, dim) + got[..., :width]
        acc_stat = pick(acc_stat, mine, dim) + got[..., width] + got[..., width + 1]
    acc = acc.reshape(n_enc, ROWS, width)
    acc_stat = acc_stat.reshape(n_enc, ROWS)
    arrived = [
        swap(with_stat_columns(pick(acc, e ^ k, 0), pick(acc_stat, e ^ k, 0)), "enc", n_enc, k)
        .astype(f32)
        for k in range(1, n_enc)
    ]
    rows = pick(acc, e, 0)
    row_squares = pick(acc_stat, e, 0)
    for got in arrived:
        rows = rows + got[:, :width]
        row_squares = row_squares + got[:, width] + got[:, width + 1]
    rows = rows * lax.rsqrt(row_squares / model_width + epsilon_norm)[:, None]
    rows = rows + pick(shift_rows, e // halves, 0)[None]
    keys = rows[:, :part].reshape(ROWS, part // HDIM, HDIM)
    keys = keys * lax.rsqrt(jnp.mean(keys * keys, axis=2, keepdims=True) + epsilon_norm)
    text = jnp.concatenate([keys.reshape(ROWS, part), rows[:, part:]], axis=1).astype(bf16)

    chosen = request_prompt[0, 0]
    relative = s ^ chosen
    by_enc = [text] + [swap(text, "enc", n_enc, k) for k in range(1, n_enc)]
    by_enc = jnp.stack(by_enc)
    by_enc = jnp.stack([pick(by_enc, k ^ e, 0) for k in range(n_enc)])
    held = by_enc.reshape(1, n_seq, halves, ROWS, width)
    first = req_bits[0]
    held = jnp.concatenate([held, swap(held, "req", n_req, first)], axis=0)
    groups = [pick(held, relative, 1)]
    for step in range(2, n_req, 2):
        wanted = swap(relative, "req", n_req, step)
        groups.append(swap(pick(held, wanted, 1), "req", n_req, step))
    text_rows = jnp.concatenate(groups, axis=0).reshape(-1, width)
    live = pick(prompt_token_ids, chosen, 0) != 0
    live = live.reshape(n_req, halves * ROWS)
    live = jnp.concatenate([pick(live, r ^ k, 0) for k in range(n_req)])

    down = lax.dynamic_slice_in_dim(adapter_down_maps[0], s * part, part, 0).T
    up = heads_of(adapter_up_maps[0], s)
    maps = jnp.concatenate([down, up], axis=0)[None]
    for bit in reversed(req_bits):
        maps = jnp.concatenate([maps, swap(maps, "req", n_req, bit)], axis=0)
    other = adapter_of_request[0, 0] ^ r
    index = 0
    for bit in req_bits:
        index = index * 2 + (other // bit) % 2
    chosen_maps = pick(maps, index, 0)
    rank = up.shape[0]
    lowrank = lax.dot_general(
        stream, chosen_maps[:rank], (((1,), (1,)), ((), ())), preferred_element_type=f32
    ).reshape(n_seq, -1, rank)
    for bit in bits_of(n_seq):
        got = swap(lowrank, "seq", n_seq, bit)
        lowrank = lowrank + jnp.stack([got[k ^ bit] for k in range(n_seq)])
    lowrank = lowrank.reshape(-1, rank).astype(bf16)
    image_values = (
        base_values.astype(f32) + jnp.dot(lowrank, chosen_maps[rank:], preferred_element_type=f32)
    ).astype(bf16)

    mixed = attention(
        queries, text_rows[:, :part], text_rows[:, part:], image_keys, image_values, live
    ).reshape(n_seq, -1, part)
    pieces = jnp.stack([mixed[0]] + [swap(mixed[k], "seq", n_seq, k) for k in range(1, n_seq)])
    result = jnp.concatenate([pick(pieces, s ^ k, 0) for k in range(n_seq)], axis=1)
    return result[None, None]


def solution(mesh):
    sizes = mesh.shape
    return jax.shard_map(
        functools.partial(per_device, sizes["enc"], sizes["req"], sizes["seq"]),
        mesh=mesh,
        in_specs=(
            P("seq", None, ("enc", "req")),
            P(),
            P(("enc", "req"), None),
            P(("enc", "req")),
            P("seq", ("enc", "req")),
            P("seq", ("enc", "req")),
            P(("enc", "req"), None),
            P(),
            P("enc", "req"),
            P("enc", "req"),
            P("req", None, None),
            P("req", None, None),
            P("enc", "req", "seq", None),
            P("enc", "req", "seq", None),
            P("enc", "req", "seq", None),
        ),
        out_specs=P("enc", "req", "seq", None),
        check_vma=False,
    )
```

```python
import functools

import jax
import jax.numpy as jnp
from jax import lax
from jax.experimental import pallas as pl
from jax.experimental.pallas import tpu as pltpu
from jax.sharding import PartitionSpec as P

HDIM = 128
ROWS = 16

epsilon_norm = 1e-06


def swap(block, axis, size, step):
    return lax.ppermute(block, axis, [(i, i ^ step) for i in range(size)])


def pick(array, index, dim):
    return lax.dynamic_index_in_dim(array, index, dim, keepdims=False)


def split_two(value):
    high = lax.reduce_precision(value, 8, 7)
    return high.astype(jnp.bfloat16), (value - high).astype(jnp.bfloat16)


def bits_of(size):
    return [1 << b for b in range(size.bit_length() - 1)]


def with_stat_rows(data, stat):
    high, low = split_two(stat)
    rows = jnp.concatenate(
        [high[None], low[None], jnp.zeros((ROWS - 2, stat.shape[0]), jnp.bfloat16)], axis=0
    )
    rows = jnp.broadcast_to(rows, data.shape[:-2] + rows.shape)
    return jnp.concatenate([data.astype(jnp.bfloat16), rows], axis=-2)


def attention_kernel(heads, inner, scale, mask_ref, q_ref, kt_ref, vt_ref, ki_ref, vi_ref, o_ref):
    live = mask_ref[...] != 0
    for h in range(heads):
        cols = slice(h * HDIM, (h + 1) * HDIM)
        q = q_ref[:, cols]
        dims = (((1,), (1,)), ((), ()))
        st = lax.dot_general(q, kt_ref[:, cols], dims, preferred_element_type=jnp.float32) * scale
        si = lax.dot_general(q, ki_ref[:, cols], dims, preferred_element_type=jnp.float32) * scale
        st = jnp.where(live, st, -jnp.inf)
        top = jnp.maximum(
            jnp.max(st, axis=1, keepdims=True), jnp.max(si, axis=1, keepdims=True)
        )
        wt = jnp.exp(st - top)
        wi = jnp.exp(si - top)
        total = jnp.sum(wt, axis=1, keepdims=True) + jnp.sum(wi, axis=1, keepdims=True)
        mixed = jnp.dot(
            wt.astype(jnp.bfloat16), vt_ref[:, cols], preferred_element_type=jnp.float32
        ) + jnp.dot(wi.astype(jnp.bfloat16), vi_ref[:, cols], preferred_element_type=jnp.float32)
        o_ref[:, cols] = (mixed / total).astype(o_ref.dtype)


def attention(queries, text_keys, text_values, image_keys, image_values, live):
    width = queries.shape[1]
    heads = width // HDIM
    rows = queries.shape[0]
    mask = jnp.broadcast_to(live.astype(jnp.int32)[None, :], (8, live.shape[0]))[:1]
    return pl.pallas_call(
        functools.partial(attention_kernel, heads, width, HDIM ** (-0.5)),
        out_shape=jax.ShapeDtypeStruct((rows, width), jnp.bfloat16),
        compiler_params=pltpu.CompilerParams(vmem_limit_bytes=48 * 1024 * 1024),
        name="attention",
    )(mask, queries, text_keys, text_values, image_keys, image_values)


def per_device(
    n_enc,
    n_req,
    n_seq,
    encoder_hidden,
    prompt_token_ids,
    context_weight,
    context_bias,
    modulation_shift,
    modulation_scale,
    key_value_weight,
    key_value_bias,
    request_prompt,
    adapter_of_request,
    adapter_down_maps,
    adapter_up_maps,
    image_stream_input,
    image_query_key,
    image_value_rows,
):
    f32, bf16 = jnp.float32, jnp.bfloat16
    e, r, s = lax.axis_index("enc"), lax.axis_index("req"), lax.axis_index("seq")
    req_bits = bits_of(n_req)
    model_width = context_weight.shape[1]
    features = context_bias.shape[0]
    tokens = encoder_hidden.shape[1]
    inner = key_value_weight.shape[1] // 2
    part = inner // n_seq

    def heads_of(array, share):
        return lax.dynamic_slice_in_dim(array, share * part, part, 1)

    qk = image_query_key[0, 0]
    sources = [qk[:, :inner], qk[:, inner:], image_value_rows[0, 0], image_stream_input[0, 0]]
    image_parts = [
        jnp.stack([heads_of(a, s ^ k) for a in sources]) for k in range(n_seq)
    ]
    image_parts = [image_parts[0]] + [
        swap(image_parts[k], "seq", n_seq, k) for k in range(1, n_seq)
    ]
    image_all = jnp.concatenate(image_parts, axis=1)
    queries, image_keys, base_values, stream = [image_all[i] for i in range(4)]

    partial_value = lax.dot_general(
        context_weight, encoder_hidden[0], (((0,), (1,)), ((), ())), preferred_element_type=f32
    )
    stat = jnp.sum(partial_value, axis=0) + jnp.sum(context_bias.astype(f32))
    acc = partial_value.reshape((n_enc,) + (2,) * len(req_bits) + (features, tokens))
    for i, bit in enumerate(req_bits):
        mine = (r // bit) % 2
        dim = len(req_bits) - i
        got = swap(with_stat_rows(pick(acc, 1 - mine, dim), stat), "req", n_req, bit).astype(f32)
        acc = pick(acc, mine, dim) + got[..., :features, :]
        got_stat = got.reshape((-1,) + got.shape[-2:])[0, features:]
        stat = stat + got_stat[0] + got_stat[1]
    arrived = [
        swap(with_stat_rows(pick(acc, e ^ k, 0), stat), "enc", n_enc, k).astype(f32)
        for k in range(1, n_enc)
    ]
    embedded = pick(acc, e, 0)
    for got in arrived:
        embedded = embedded + got[:features]
        stat = stat + got[features] + got[features + 1]
    embedded = embedded + context_bias.astype(f32)[:, None]
    centred = embedded - (stat / model_width)[None, :]
    squares = jnp.sum(centred * centred, axis=0)
    scaled = (1.0 + modulation_scale[0].astype(f32))[:, None] * centred

    own = with_stat_rows(scaled, squares)
    blocks = [own] + [swap(own, "seq", n_seq, k) for k in range(1, n_seq)]
    scaled_all = jnp.concatenate([b[:features] for b in blocks], axis=1)
    squares_all = jnp.concatenate(
        [b[features].astype(f32) + b[features + 1].astype(f32) for b in blocks]
    )
    weight_own = jnp.concatenate(
        [heads_of(key_value_weight[:, :inner], s), heads_of(key_value_weight[:, inner:], s)], axis=1
    )
    width = 2 * part
    projected = lax.dot_general(
        scaled_all, weight_own, (((0,), (0,)), ((), ())), preferred_element_type=f32
    )

    shift_part = jnp.dot(modulation_shift, key_value_weight, preferred_element_type=f32)
    for bit in req_bits:
        shift_part = shift_part + swap(shift_part, "req", n_req, bit)
    for bit in bits_of(n_enc):
        shift_part = shift_part + swap(shift_part, "enc", n_enc, bit)
    shift_part = shift_part + key_value_bias.astype(f32)[None]

    def columns_of(row, share):
        return jnp.concatenate(
            [heads_of(row[:, :inner], share), heads_of(row[:, inner:], share)], axis=1
        )

    shift_rows = jnp.concatenate(
        [columns_of(shift_part, s)]
        + [swap(columns_of(shift_part, s ^ k), "seq", n_seq, k) for k in range(1, n_seq)],
        axis=0,
    )

    halves = tokens // n_req // ROWS
    split = (n_seq,) + (2,) * len(req_bits) + (halves, ROWS)
    acc = projected.reshape(split + (width,))
    acc_stat = squares_all.reshape(split)

    def with_stat_columns(data, stat):
        high, low = split_two(stat)
        lane = lax.broadcasted_iota(jnp.int32, stat.shape + (HDIM,), stat.ndim)
        columns = jnp.where(
            lane == 0, high[..., None], jnp.where(lane == 1, low[..., None], jnp.zeros((), bf16))
        )
        return jnp.concatenate([data.astype(bf16), columns], axis=-1)

    for i, bit in enumerate(req_bits):
        mine = (r // bit) % 2
        dim = len(req_bits) - i
        got = swap(
            with_stat_columns(pick(acc, 1 - mine, dim), pick(acc_stat, 1 - mine, dim)),
            "req", n_req, bit,
        ).astype(f32)
        acc = pick(acc, mine, dim) + got[..., :width]
        acc_stat = pick(acc_stat, mine, dim) + got[..., width] + got[..., width + 1]
    acc = acc.reshape(n_enc, ROWS, width)
    acc_stat = acc_stat.reshape(n_enc, ROWS)
    arrived = [
        swap(with_stat_columns(pick(acc, e ^ k, 0), pick(acc_stat, e ^ k, 0)), "enc", n_enc, k)
        .astype(f32)
        for k in range(1, n_enc)
    ]
    rows = pick(acc, e, 0)
    row_squares = pick(acc_stat, e, 0)
    for got in arrived:
        rows = rows + got[:, :width]
        row_squares = row_squares + got[:, width] + got[:, width + 1]
    rows = rows * lax.rsqrt(row_squares / model_width + epsilon_norm)[:, None]
    rows = rows + pick(shift_rows, e // halves, 0)[None]
    keys = rows[:, :part].reshape(ROWS, part // HDIM, HDIM)
    keys = keys * lax.rsqrt(jnp.mean(keys * keys, axis=2, keepdims=True) + epsilon_norm)
    text = jnp.concatenate([keys.reshape(ROWS, part), rows[:, part:]], axis=1).astype(bf16)

    chosen = request_prompt[0, 0]
    relative = s ^ chosen
    by_enc = [text] + [swap(text, "enc", n_enc, k) for k in range(1, n_enc)]
    by_enc = jnp.stack(by_enc)
    by_enc = jnp.stack([pick(by_enc, k ^ e, 0) for k in range(n_enc)])
    held = by_enc.reshape(1, n_seq, halves, ROWS, width)
    first = req_bits[0]
    held = jnp.concatenate([held, swap(held, "req", n_req, first)], axis=0)
    groups = [pick(held, relative, 1)]
    for step in range(2, n_req, 2):
        wanted = swap(relative, "req", n_req, step)
        groups.append(swap(pick(held, wanted, 1), "req", n_req, step))
    text_rows = jnp.concatenate(groups, axis=0).reshape(-1, width)
    live = pick(prompt_token_ids, chosen, 0) != 0
    live = live.reshape(n_req, halves * ROWS)
    live = jnp.concatenate([pick(live, r ^ k, 0) for k in range(n_req)])

    down = lax.dynamic_slice_in_dim(adapter_down_maps[0], s * part, part, 0).T
    up = heads_of(adapter_up_maps[0], s)
    maps = jnp.concatenate([down, up], axis=0)[None]
    for bit in reversed(req_bits):
        maps = jnp.concatenate([maps, swap(maps, "req", n_req, bit)], axis=0)
    other = adapter_of_request[0, 0] ^ r
    index = 0
    for bit in req_bits:
        index = index * 2 + (other // bit) % 2
    chosen_maps = pick(maps, index, 0)
    rank = up.shape[0]
    lowrank = lax.dot_general(
        stream, chosen_maps[:rank], (((1,), (1,)), ((), ())), preferred_element_type=f32
    ).reshape(n_seq, -1, rank)
    for bit in bits_of(n_seq):
        got = swap(lowrank, "seq", n_seq, bit)
        lowrank = lowrank + jnp.stack([got[k ^ bit] for k in range(n_seq)])
    lowrank = lowrank.reshape(-1, rank).astype(bf16)
    image_values = (
        base_values.astype(f32) + jnp.dot(lowrank, chosen_maps[rank:], preferred_element_type=f32)
    ).astype(bf16)

    mixed = attention(
        queries, text_rows[:, :part], text_rows[:, part:], image_keys, image_values, live
    ).reshape(n_seq, -1, part)
    pieces = jnp.stack([mixed[0]] + [swap(mixed[k], "seq", n_seq, k) for k in range(1, n_seq)])
    result = jnp.concatenate([pick(pieces, s ^ k, 0) for k in range(n_seq)], axis=1)
    return result[None, None]


F32, BF16 = jnp.float32, jnp.bfloat16
ANY = pl.BlockSpec(memory_space=pl.ANY)
VMEM = pl.BlockSpec(memory_space=pltpu.VMEM)
SMEM = pl.BlockSpec(memory_space=pltpu.SMEM)
NT = (((1,), (1,)), ((), ()))
TN = (((0,), (0,)), ((), ()))


def call(kernel, outs, ins, specs=None, scratch=(), name=None):
    return pl.pallas_call(
        kernel,
        out_shape=outs,
        in_specs=specs if specs is not None else [VMEM] * len(ins),
        out_specs=jax.tree.map(lambda _: VMEM, outs),
        scratch_shapes=list(scratch),
        compiler_params=pltpu.CompilerParams(vmem_limit_bytes=40 * 1024 * 1024),
        name=name,
    )(*ins)


def struct(shape, dtype=BF16):
    return jax.ShapeDtypeStruct(shape, dtype)


def at(index, size):
    return pl.ds(pl.multiple_of(index * size, size), size)


def stat_rows(stat):
    high = stat.astype(BF16).astype(F32)
    row = lax.broadcasted_iota(jnp.int32, (ROWS, stat.shape[1]), 0)
    return jnp.where(row == 0, high, jnp.where(row == 1, stat - high, 0.0)).astype(BF16)


def stat_of(rows):
    rows = rows.astype(F32)
    return rows[0:1] + rows[1:2]


def context_kernel(h_ref, w_ref, b_ref, send_ref, keep_ref, stat_ref):
    mine = lax.rem(lax.axis_index("req"), 2)
    features = b_ref.shape[1]
    pairs = w_ref.shape[1] // (2 * features)
    total = jnp.zeros((1, h_ref.shape[0]), F32)
    for p in range(pairs):
        product = jnp.dot(
            h_ref[...], w_ref[:, p * 2 * features : (p + 1) * 2 * features],
            preferred_element_type=F32,
        ).T
        total = total + jnp.sum(product, axis=0, keepdims=True)
        low, high = product[:features], product[features:]
        rows = slice(p * features, (p + 1) * features)
        keep_ref[rows] = jnp.where(mine == 0, low, high)
        send_ref[rows] = jnp.where(mine == 0, high, low).astype(BF16)
    stat = total + jnp.sum(b_ref[...].astype(F32))
    send_ref[pairs * features :] = stat_rows(stat)
    stat_ref[...] = jnp.broadcast_to(stat, stat_ref.shape)


def halve_kernel(features, got_ref, keep_ref, stat_ref, send_ref, kept_ref, out_stat_ref):
    mine = lax.rem(lax.axis_index("req") // 2, 2)
    count = keep_ref.shape[0] // (2 * features)
    for i in range(count):
        rows = slice(i * features, (i + 1) * features)
        own, other = at(2 * i + mine, features), at(2 * i + 1 - mine, features)
        kept_ref[rows] = keep_ref[own] + got_ref[own].astype(F32)
        send_ref[rows] = (keep_ref[other] + got_ref[other].astype(F32)).astype(BF16)
    stat = stat_ref[0:1] + stat_of(got_ref[2 * count * features :])
    send_ref[count * features :] = stat_rows(stat)
    out_stat_ref[...] = jnp.broadcast_to(stat, out_stat_ref.shape)


def scatter_kernel(features, got_ref, keep_ref, stat_ref, kept_ref, out_stat_ref, *send_refs):
    e = lax.axis_index("enc")
    count = keep_ref.shape[0] // features
    stat = stat_ref[0:1] + stat_of(got_ref[count * features :])
    own = at(e, features)
    for k, send_ref in enumerate(send_refs):
        other = at(e ^ (k + 1), features)
        send_ref[:features] = (keep_ref[other] + got_ref[other].astype(F32)).astype(BF16)
        send_ref[features:] = stat_rows(stat)
    kept_ref[...] = keep_ref[own] + got_ref[own].astype(F32)
    out_stat_ref[...] = jnp.broadcast_to(stat, out_stat_ref.shape)


def centre_kernel(width, keep_ref, stat_ref, bias_ref, scale_ref, *refs):
    got_refs, out_ref = refs[:-1], refs[-1]
    features = keep_ref.shape[0]
    total = keep_ref[...] + bias_ref[...]
    stat = stat_ref[0:1]
    for got_ref in got_refs:
        total = total + got_ref[:features].astype(F32)
        stat = stat + stat_of(got_ref[features:])
    centred = total - stat * (1.0 / width)
    out_ref[:features] = (scale_ref[...] * centred).astype(BF16)
    out_ref[features:] = stat_rows(jnp.sum(centred * centred, axis=0, keepdims=True))


def project_kernel(n_seq, n_req, n_enc, *refs):
    payload_refs = refs[: n_seq * n_req]
    weight_refs = refs[n_seq * n_req : n_seq * n_req + n_req]
    keep_ref = refs[n_seq * n_req + n_req]
    send_refs = refs[n_seq * n_req + n_req + 1 : -1]
    rows_ref = refs[-1]
    features, width = weight_refs[0].shape
    tokens = payload_refs[0].shape[1]
    lane = lax.broadcasted_iota(jnp.int32, (tokens, HDIM), 1)
    for p in range(n_seq):
        total, squares = None, None
        for k in range(n_req):
            payload = payload_refs[p * n_req + k]
            term = lax.dot_general(
                payload[:features], weight_refs[k][...], TN, preferred_element_type=F32
            )
            part = stat_of(payload[features:])
            total = term if total is None else total + term
            squares = part if squares is None else squares + part
        rows = slice(p * tokens, (p + 1) * tokens)
        rows_ref[rows, :width] = total
        column = jnp.broadcast_to(squares, (HDIM, tokens)).T
        high = column.astype(BF16).astype(F32)
        rows_ref[rows, width:] = jnp.where(
            lane == 0, high, jnp.where(lane == 1, column - high, 0.0)
        )
    e = lax.axis_index("enc")
    size = n_seq * tokens // n_enc
    keep_ref[...] = rows_ref[at(e, size)]
    for k, send_ref in enumerate(send_refs):
        send_ref[...] = rows_ref[at(e ^ (k + 1), size)].astype(BF16)


def finish_kernel(n_seq, n_enc, n_req, model_width, keep_ref, shift_ref, bias_ref, *refs):
    got_refs, out_ref = refs[:-1], refs[-1]
    e, r, s = lax.axis_index("enc"), lax.axis_index("req"), lax.axis_index("seq")
    width = out_ref.shape[1]
    half = width // 2
    inner = shift_ref.shape[1] // 2
    total = keep_ref[...]
    for got_ref in got_refs:
        total = total + got_ref[...].astype(F32)
    squares = total[:, width : width + 1] + total[:, width + 1 : width + 2]
    factor = lax.rsqrt(squares * (1.0 / model_width) + epsilon_norm)
    prompt = s ^ (e // (n_enc // n_seq))
    for part in range(2):
        columns = pl.ds(
            pl.multiple_of(part * inner + (s * n_req + r) * half, HDIM), half
        )
        shift = shift_ref[pl.ds(prompt, 1), columns] + bias_ref[:, columns].astype(F32)
        rows = total[:, part * half : (part + 1) * half] * factor + shift
        for h in range(half // HDIM):
            head = rows[:, h * HDIM : (h + 1) * HDIM]
            if part == 0:
                head = head * lax.rsqrt(
                    jnp.mean(head * head, axis=1, keepdims=True) + epsilon_norm
                )
            place = part * half + h * HDIM
            out_ref[:, place : place + HDIM] = head.astype(BF16)


def choose_kernel(n_seq, n_enc, chosen_ref, *refs):
    part_refs, out_refs = refs[:n_enc], refs[n_enc:]
    e, r, s = lax.axis_index("enc"), lax.axis_index("req"), lax.axis_index("seq")
    halves = n_enc // n_seq
    size = part_refs[0].shape[0]
    for k, out_ref in enumerate(out_refs):
        prompt = s ^ chosen_ref[r ^ k]
        for h in range(halves):
            place = e ^ (prompt * halves + h)
            for j in range(n_enc):
                @pl.when(place == j)
                def _():
                    out_ref[h * size : (h + 1) * size] = part_refs[j][...]


def weight_kernel(n_req, part, inner, *refs):
    w_ref, out_refs, sems = refs[0], refs[2:-1], refs[-1]
    r, s = lax.axis_index("req"), lax.axis_index("seq")
    half = part // n_req
    copies = []
    for k, out_ref in enumerate(out_refs):
        for side in range(2):
            columns = pl.ds(
                pl.multiple_of(side * inner + (s * n_req + (r ^ k)) * half, HDIM), half
            )
            copies.append(
                pltpu.make_async_copy(
                    w_ref.at[:, columns],
                    out_ref.at[:, pl.ds(side * half, half)],
                    sems.at[2 * k + side],
                )
            )
    for copy in copies:
        copy.start()
    for copy in copies:
        copy.wait()


def image_kernel(part, inner, step, qk_ref, v_ref, x_ref, dep_ref, out_ref, sems):
    start = (lax.axis_index("seq") ^ step) * part
    copies = []
    for i, (ref, base) in enumerate(((qk_ref, 0), (qk_ref, inner), (v_ref, 0), (x_ref, 0))):
        columns = pl.ds(pl.multiple_of(base + start, HDIM), part)
        copies.append(pltpu.make_async_copy(ref.at[:, columns], out_ref.at[i], sems.at[i]))
    for copy in copies:
        copy.start()
    for copy in copies:
        copy.wait()


def maps_kernel(part, down_ref, up_ref, dep_ref, out_ref, sems):
    rank = down_ref.shape[0]
    columns = pl.ds(pl.multiple_of(lax.axis_index("seq") * part, HDIM), part)
    copies = [
        pltpu.make_async_copy(down_ref.at[:, columns], out_ref.at[pl.ds(0, rank)], sems.at[0]),
        pltpu.make_async_copy(up_ref.at[:, columns], out_ref.at[pl.ds(rank, rank)], sems.at[1]),
    ]
    for copy in copies:
        copy.start()
    for copy in copies:
        copy.wait()


def lowrank_kernel(n_req, part, adapter_ref, x_ref, *refs):
    out_ref, chosen_ref = refs[-2:]
    map_refs = refs[:n_req]
    got_refs = refs[n_req:-2]
    place = adapter_ref[0, 0] ^ lax.axis_index("req")
    for k in range(n_req):
        @pl.when(place == k)
        def _():
            chosen_ref[...] = map_refs[k][...]
    rank = out_ref.shape[-1]
    down = chosen_ref[:rank]
    own = x_ref[:, pl.ds(pl.multiple_of(lax.axis_index("seq") * part, HDIM), part)]
    out_ref[0] = lax.dot_general(own, down, NT, preferred_element_type=F32)
    for k, got_ref in enumerate(got_refs):
        out_ref[k + 1] = lax.dot_general(got_ref[3], down, NT, preferred_element_type=F32)


def arrange_kernel(n_req, part, inner, low_ref, maps_ref, qk_ref, v_ref, *refs):
    got_refs, (q_out, k_out, v_out) = refs[:-3], refs[-3:]
    r, s = lax.axis_index("req"), lax.axis_index("seq")
    rank = maps_ref.shape[0] // 2
    half = part // n_req
    tokens = qk_ref.shape[0]
    low = low_ref[...].astype(BF16)
    for k in range(n_req):
        place = (r ^ k) * half
        up = maps_ref[rank:, pl.ds(pl.multiple_of(place, HDIM), half)]
        for i in range(len(got_refs) + 1):
            rows = slice(i * tokens, (i + 1) * tokens)
            if i == 0:
                own = s * part + place
                q = qk_ref[:, pl.ds(pl.multiple_of(own, HDIM), half)]
                key = qk_ref[:, pl.ds(pl.multiple_of(inner + own, HDIM), half)]
                base = v_ref[:, pl.ds(pl.multiple_of(own, HDIM), half)]
            else:
                columns = pl.ds(pl.multiple_of(place, HDIM), half)
                q = got_refs[i - 1][0, :, columns]
                key = got_refs[i - 1][1, :, columns]
                base = got_refs[i - 1][2, :, columns]
            q_out[k, rows] = q
            k_out[k, rows] = key
            v_out[k, rows] = (
                base.astype(F32) + jnp.dot(low[i], up, preferred_element_type=F32)
            ).astype(BF16)


def heads_kernel(scale, live_ref, text_ref, q_ref, k_ref, v_ref, *out_refs):
    live = live_ref[...] != 0
    half = q_ref.shape[2]
    size = out_refs[0].shape[0]
    for h in range(half // HDIM):
        cols = slice(h * HDIM, (h + 1) * HDIM)
        vals = slice(half + h * HDIM, half + (h + 1) * HDIM)
        q = q_ref[0, :, cols]
        st = lax.dot_general(q, text_ref[:, cols], NT, preferred_element_type=F32) * scale
        si = lax.dot_general(q, k_ref[0, :, cols], NT, preferred_element_type=F32) * scale
        st = jnp.where(live, st, -jnp.inf)
        top = jnp.maximum(
            jnp.max(st, axis=1, keepdims=True), jnp.max(si, axis=1, keepdims=True)
        )
        wt = jnp.exp(st - top)
        wi = jnp.exp(si - top)
        total = jnp.sum(wt, axis=1, keepdims=True) + jnp.sum(wi, axis=1, keepdims=True)
        mixed = jnp.dot(
            wt.astype(BF16), text_ref[:, vals], preferred_element_type=F32
        ) + jnp.dot(wi.astype(BF16), v_ref[0, :, cols], preferred_element_type=F32)
        mixed = (mixed / total).astype(BF16)
        for i, out_ref in enumerate(out_refs):
            out_ref[:, cols] = mixed[i * size : (i + 1) * size]


def assemble_kernel(n_req, n_seq, *refs):
    out_ref = refs[-1]
    r, s = lax.axis_index("req"), lax.axis_index("seq")
    half = refs[0].shape[1]
    for k in range(n_req):
        for i in range(n_seq):
            start = ((s ^ i) * n_req + (r ^ k)) * half
            out_ref[:, pl.ds(pl.multiple_of(start, HDIM), half)] = refs[k * n_seq + i][...]


def per_device_heads(
    n_enc,
    n_req,
    n_seq,
    encoder_hidden,
    prompt_token_ids,
    context_weight,
    context_bias,
    modulation_shift,
    modulation_scale,
    key_value_weight,
    key_value_bias,
    request_prompt,
    adapter_of_request,
    adapter_down_maps,
    adapter_up_maps,
    image_stream_input,
    image_query_key,
    image_value_rows,
):
    e, r, s = lax.axis_index("enc"), lax.axis_index("req"), lax.axis_index("seq")
    model_width = context_weight.shape[1]
    features = context_bias.shape[0]
    tokens = encoder_hidden.shape[1]
    inner = key_value_weight.shape[1] // 2
    part = inner // n_seq
    half = part // n_req
    image_rows = image_query_key.shape[2]
    rank = adapter_up_maps.shape[1]
    qk, base, stream = image_query_key[0, 0], image_value_rows[0, 0], image_stream_input[0, 0]
    dma = pltpu.SemaphoreType.DMA
    stat = struct((8, tokens), F32)

    send, keep, sums = call(
        context_kernel,
        (
            struct((model_width // 2 + ROWS, tokens)),
            struct((model_width // 2, tokens), F32),
            stat,
        ),
        (encoder_hidden[0], context_weight, context_bias[None]),
        name="context",
    )
    got = swap(send, "req", n_req, 1)

    packed = [
        call(
            functools.partial(image_kernel, part, inner, k),
            struct((4, image_rows, part)),
            (qk, base, stream, keep),
            [ANY] * 4,
            [dma((4,))],
            name="image_pack",
        )
        for k in range(1, n_seq)
    ]
    image_got = [swap(packed[k - 1], "seq", n_seq, k) for k in range(1, n_seq)]
    weights = call(
        functools.partial(weight_kernel, n_req, part, inner),
        tuple(struct((features, 2 * half)) for _ in range(n_req)),
        (key_value_weight, keep),
        [ANY] * 2,
        [dma((2 * n_req,))],
        name="weight_pack",
    )

    send, keep, sums = call(
        functools.partial(halve_kernel, features),
        (
            struct((n_enc * features + ROWS, tokens)),
            struct((n_enc * features, tokens), F32),
            stat,
        ),
        (got, keep, sums),
        name="halve",
    )
    got = swap(send, "req", n_req, 2)
    keep, sums, *sends = call(
        functools.partial(scatter_kernel, features),
        (struct((features, tokens), F32), stat)
        + tuple(struct((features + ROWS, tokens)) for _ in range(1, n_enc)),
        (got, keep, sums),
        name="scatter",
    )
    arrived = [swap(sends[k - 1], "enc", n_enc, k) for k in range(1, n_enc)]
    weights = lax.optimization_barrier((weights, keep))[0]
    weights = [weights[0]] + [swap(weights[k], "req", n_req, k) for k in range(1, n_req)]

    bias_columns = jnp.broadcast_to(context_bias.astype(F32)[:, None], (features, tokens))
    scale_columns = jnp.broadcast_to(
        1.0 + modulation_scale[0].astype(F32)[:, None], (features, tokens)
    )
    own = call(
        functools.partial(centre_kernel, model_width),
        struct((features + ROWS, tokens)),
        (keep, sums, bias_columns, scale_columns, *arrived),
        name="centre",
    )
    payloads = []
    for i in range(n_seq):
        for k in range(n_req):
            block = own
            if i or k:
                block = lax.ppermute(
                    own,
                    ("seq", "req"),
                    [
                        (a * n_req + b, (a ^ i) * n_req + (b ^ k))
                        for a in range(n_seq)
                        for b in range(n_req)
                    ],
                )
            payloads.append(block)

    shift_part = jnp.dot(modulation_shift, key_value_weight, preferred_element_type=F32)
    wide = 2 * inner
    index = jnp.arange(n_seq + 1)[:, None]
    lane = jnp.arange(wide)[None, :]
    asked = jnp.where(
        (lane == e * n_req + r) & (s == 0), request_prompt[0, 0].astype(F32), 0.0
    )
    table = jnp.where(
        index == s, shift_part, jnp.where(index == n_seq, asked, jnp.zeros((), F32))
    )
    table = lax.psum(table, ("enc", "seq", "req"))
    prompts = lax.dynamic_slice_in_dim(table[n_seq], e * n_req, n_req, 0).astype(jnp.int32)

    size = n_seq * tokens // n_enc
    wide_rows = 2 * half + HDIM
    keep, *sends = call(
        functools.partial(project_kernel, n_seq, n_req, n_enc),
        (struct((size, wide_rows), F32),)
        + tuple(struct((size, wide_rows)) for _ in range(1, n_enc)),
        (*payloads, *weights),
        scratch=[pltpu.VMEM((n_seq * tokens, wide_rows), F32)],
        name="project",
    )
    arrived = [swap(sends[k - 1], "enc", n_enc, k) for k in range(1, n_enc)]

    maps = call(
        functools.partial(maps_kernel, part),
        struct((2 * rank, part)),
        (adapter_down_maps[0].T, adapter_up_maps[0], keep),
        [ANY] * 3,
        [dma((2,))],
        name="maps_pack",
    )
    maps = [maps]
    step = n_req // 2
    while step:
        maps = maps + [swap(m, "req", n_req, step) for m in maps]
        step //= 2
    ordered = [None] * n_req
    place = [0]
    step = n_req // 2
    while step:
        place = place + [p ^ step for p in place]
        step //= 2
    for p, m in zip(place, maps):
        ordered[p] = m
    low, chosen_maps = call(
        functools.partial(lowrank_kernel, n_req, part),
        (struct((n_seq, image_rows, rank), F32), struct((2 * rank, part))),
        (adapter_of_request, stream, *ordered, *image_got),
        [SMEM] + [VMEM] * (1 + n_req + len(image_got)),
        name="lowrank",
    )
    for bit in bits_of(n_seq):
        other = swap(low, "seq", n_seq, bit)
        low = low + jnp.stack([other[k ^ bit] for k in range(n_seq)])
    arranged = struct((n_req, n_seq * image_rows, half))
    queries, image_keys, image_values = call(
        functools.partial(arrange_kernel, n_req, part, inner),
        (arranged, arranged, arranged),
        (low, chosen_maps, qk, base, *image_got),
        name="arrange",
    )

    text = call(
        functools.partial(finish_kernel, n_seq, n_enc, n_req, model_width),
        struct((size, 2 * half)),
        (keep, table, key_value_bias[None], *arrived),
        name="finish",
    )
    parts = [text] + [swap(text, "enc", n_enc, k) for k in range(1, n_enc)]
    rows = call(
        functools.partial(choose_kernel, n_seq, n_enc),
        tuple(struct((tokens, 2 * half)) for _ in range(n_req)),
        (prompts, *parts),
        [SMEM] + [VMEM] * n_enc,
        name="choose",
    )
    rows = [rows[0]] + [swap(rows[k], "req", n_req, k) for k in range(1, n_req)]
    live = lax.dynamic_slice_in_dim(prompt_token_ids, request_prompt[0, 0], 1, 0)
    pieces = [None] * n_req
    for k in range(n_req):
        block = pl.BlockSpec((1, n_seq * image_rows, half), lambda i, k=k: (k, 0, 0))
        whole = lambda shape: pl.BlockSpec(shape, lambda i: (0, 0))
        mixed = pl.pallas_call(
            functools.partial(heads_kernel, HDIM ** (-0.5)),
            grid=(1,),
            out_shape=[struct((image_rows, half)) for _ in range(n_seq)],
            in_specs=[whole((1, tokens)), whole((tokens, 2 * half)), block, block, block],
            out_specs=[whole((image_rows, half)) for _ in range(n_seq)],
            compiler_params=pltpu.CompilerParams(vmem_limit_bytes=40 * 1024 * 1024),
            name="heads",
        )(live, rows[k], queries, image_keys, image_values)
        pieces[k] = [mixed[0]] + [swap(mixed[i], "seq", n_seq, i) for i in range(1, n_seq)]
    result = call(
        functools.partial(assemble_kernel, n_req, n_seq),
        struct((image_rows, inner)),
        tuple(p for group in pieces for p in group),
        name="assemble",
    )
    return result[None, None]


def solution(mesh):
    sizes = mesh.shape
    n_enc, n_req, n_seq = sizes["enc"], sizes["req"], sizes["seq"]

    def run(*arrays):
        heads = arrays[6].shape[1] // (2 * HDIM)
        pick_body = per_device_heads if heads % (n_seq * n_req) == 0 else per_device
        return pick_body(n_enc, n_req, n_seq, *arrays)

    return jax.shard_map(
        run,
        mesh=mesh,
        in_specs=(
            P("seq", None, ("enc", "req")),
            P(),
            P(("enc", "req"), None),
            P(("enc", "req")),
            P("seq", ("enc", "req")),
            P("seq", ("enc", "req")),
            P(("enc", "req"), None),
            P(),
            P("enc", "req"),
            P("enc", "req"),
            P("req", None, None),
            P("req", None, None),
            P("enc", "req", "seq", None),
            P("enc", "req", "seq", None),
            P("enc", "req", "seq", None),
        ),
        out_specs=P("enc", "req", "seq", None),
        check_vma=False,
    )
```

```python
import functools

import jax
import jax.numpy as jnp
from jax import lax
from jax.experimental import pallas as pl
from jax.experimental.pallas import tpu as pltpu
from jax.sharding import PartitionSpec as P

HDIM = 128
ROWS = 16

epsilon_norm = 1e-06


def swap(block, axis, size, step):
    return lax.ppermute(block, axis, [(i, i ^ step) for i in range(size)])


def pick(array, index, dim):
    return lax.dynamic_index_in_dim(array, index, dim, keepdims=False)


def split_two(value):
    high = lax.reduce_precision(value, 8, 7)
    return high.astype(jnp.bfloat16), (value - high).astype(jnp.bfloat16)


def bits_of(size):
    return [1 << b for b in range(size.bit_length() - 1)]


def with_stat_rows(data, stat):
    high, low = split_two(stat)
    rows = jnp.concatenate(
        [high[None], low[None], jnp.zeros((ROWS - 2, stat.shape[0]), jnp.bfloat16)], axis=0
    )
    rows = jnp.broadcast_to(rows, data.shape[:-2] + rows.shape)
    return jnp.concatenate([data.astype(jnp.bfloat16), rows], axis=-2)


def attention_kernel(heads, inner, scale, mask_ref, q_ref, kt_ref, vt_ref, ki_ref, vi_ref, o_ref):
    live = mask_ref[...] != 0
    for h in range(heads):
        cols = slice(h * HDIM, (h + 1) * HDIM)
        q = q_ref[:, cols]
        dims = (((1,), (1,)), ((), ()))
        st = lax.dot_general(q, kt_ref[:, cols], dims, preferred_element_type=jnp.float32) * scale
        si = lax.dot_general(q, ki_ref[:, cols], dims, preferred_element_type=jnp.float32) * scale
        st = jnp.where(live, st, -jnp.inf)
        top = jnp.maximum(
            jnp.max(st, axis=1, keepdims=True), jnp.max(si, axis=1, keepdims=True)
        )
        wt = jnp.exp(st - top)
        wi = jnp.exp(si - top)
        total = jnp.sum(wt, axis=1, keepdims=True) + jnp.sum(wi, axis=1, keepdims=True)
        mixed = jnp.dot(
            wt.astype(jnp.bfloat16), vt_ref[:, cols], preferred_element_type=jnp.float32
        ) + jnp.dot(wi.astype(jnp.bfloat16), vi_ref[:, cols], preferred_element_type=jnp.float32)
        o_ref[:, cols] = (mixed / total).astype(o_ref.dtype)


def attention(queries, text_keys, text_values, image_keys, image_values, live):
    width = queries.shape[1]
    heads = width // HDIM
    rows = queries.shape[0]
    mask = jnp.broadcast_to(live.astype(jnp.int32)[None, :], (8, live.shape[0]))[:1]
    return pl.pallas_call(
        functools.partial(attention_kernel, heads, width, HDIM ** (-0.5)),
        out_shape=jax.ShapeDtypeStruct((rows, width), jnp.bfloat16),
        compiler_params=pltpu.CompilerParams(vmem_limit_bytes=48 * 1024 * 1024),
        name="attention",
    )(mask, queries, text_keys, text_values, image_keys, image_values)


def per_device(
    n_enc,
    n_req,
    n_seq,
    encoder_hidden,
    prompt_token_ids,
    context_weight,
    context_bias,
    modulation_shift,
    modulation_scale,
    key_value_weight,
    key_value_bias,
    request_prompt,
    adapter_of_request,
    adapter_down_maps,
    adapter_up_maps,
    image_stream_input,
    image_query_key,
    image_value_rows,
):
    f32, bf16 = jnp.float32, jnp.bfloat16
    e, r, s = lax.axis_index("enc"), lax.axis_index("req"), lax.axis_index("seq")
    req_bits = bits_of(n_req)
    model_width = context_weight.shape[1]
    features = context_bias.shape[0]
    tokens = encoder_hidden.shape[1]
    inner = key_value_weight.shape[1] // 2
    part = inner // n_seq

    def heads_of(array, share):
        return lax.dynamic_slice_in_dim(array, share * part, part, 1)

    qk = image_query_key[0, 0]
    sources = [qk[:, :inner], qk[:, inner:], image_value_rows[0, 0], image_stream_input[0, 0]]
    image_parts = [
        jnp.stack([heads_of(a, s ^ k) for a in sources]) for k in range(n_seq)
    ]
    image_parts = [image_parts[0]] + [
        swap(image_parts[k], "seq", n_seq, k) for k in range(1, n_seq)
    ]
    image_all = jnp.concatenate(image_parts, axis=1)
    queries, image_keys, base_values, stream = [image_all[i] for i in range(4)]

    partial_value = lax.dot_general(
        context_weight, encoder_hidden[0], (((0,), (1,)), ((), ())), preferred_element_type=f32
    )
    stat = jnp.sum(partial_value, axis=0) + jnp.sum(context_bias.astype(f32))
    acc = partial_value.reshape((n_enc,) + (2,) * len(req_bits) + (features, tokens))
    for i, bit in enumerate(req_bits):
        mine = (r // bit) % 2
        dim = len(req_bits) - i
        got = swap(with_stat_rows(pick(acc, 1 - mine, dim), stat), "req", n_req, bit).astype(f32)
        acc = pick(acc, mine, dim) + got[..., :features, :]
        got_stat = got.reshape((-1,) + got.shape[-2:])[0, features:]
        stat = stat + got_stat[0] + got_stat[1]
    arrived = [
        swap(with_stat_rows(pick(acc, e ^ k, 0), stat), "enc", n_enc, k).astype(f32)
        for k in range(1, n_enc)
    ]
    embedded = pick(acc, e, 0)
    for got in arrived:
        embedded = embedded + got[:features]
        stat = stat + got[features] + got[features + 1]
    embedded = embedded + context_bias.astype(f32)[:, None]
    centred = embedded - (stat / model_width)[None, :]
    squares = jnp.sum(centred * centred, axis=0)
    scaled = (1.0 + modulation_scale[0].astype(f32))[:, None] * centred

    own = with_stat_rows(scaled, squares)
    blocks = [own] + [swap(own, "seq", n_seq, k) for k in range(1, n_seq)]
    scaled_all = jnp.concatenate([b[:features] for b in blocks], axis=1)
    squares_all = jnp.concatenate(
        [b[features].astype(f32) + b[features + 1].astype(f32) for b in blocks]
    )
    weight_own = jnp.concatenate(
        [heads_of(key_value_weight[:, :inner], s), heads_of(key_value_weight[:, inner:], s)], axis=1
    )
    width = 2 * part
    projected = lax.dot_general(
        scaled_all, weight_own, (((0,), (0,)), ((), ())), preferred_element_type=f32
    )

    shift_part = jnp.dot(modulation_shift, key_value_weight, preferred_element_type=f32)
    for bit in req_bits:
        shift_part = shift_part + swap(shift_part, "req", n_req, bit)
    for bit in bits_of(n_enc):
        shift_part = shift_part + swap(shift_part, "enc", n_enc, bit)
    shift_part = shift_part + key_value_bias.astype(f32)[None]

    def columns_of(row, share):
        return jnp.concatenate(
            [heads_of(row[:, :inner], share), heads_of(row[:, inner:], share)], axis=1
        )

    shift_rows = jnp.concatenate(
        [columns_of(shift_part, s)]
        + [swap(columns_of(shift_part, s ^ k), "seq", n_seq, k) for k in range(1, n_seq)],
        axis=0,
    )

    halves = tokens // n_req // ROWS
    split = (n_seq,) + (2,) * len(req_bits) + (halves, ROWS)
    acc = projected.reshape(split + (width,))
    acc_stat = squares_all.reshape(split)

    def with_stat_columns(data, stat):
        high, low = split_two(stat)
        lane = lax.broadcasted_iota(jnp.int32, stat.shape + (HDIM,), stat.ndim)
        columns = jnp.where(
            lane == 0, high[..., None], jnp.where(lane == 1, low[..., None], jnp.zeros((), bf16))
        )
        return jnp.concatenate([data.astype(bf16), columns], axis=-1)

    for i, bit in enumerate(req_bits):
        mine = (r // bit) % 2
        dim = len(req_bits) - i
        got = swap(
            with_stat_columns(pick(acc, 1 - mine, dim), pick(acc_stat, 1 - mine, dim)),
            "req", n_req, bit,
        ).astype(f32)
        acc = pick(acc, mine, dim) + got[..., :width]
        acc_stat = pick(acc_stat, mine, dim) + got[..., width] + got[..., width + 1]
    acc = acc.reshape(n_enc, ROWS, width)
    acc_stat = acc_stat.reshape(n_enc, ROWS)
    arrived = [
        swap(with_stat_columns(pick(acc, e ^ k, 0), pick(acc_stat, e ^ k, 0)), "enc", n_enc, k)
        .astype(f32)
        for k in range(1, n_enc)
    ]
    rows = pick(acc, e, 0)
    row_squares = pick(acc_stat, e, 0)
    for got in arrived:
        rows = rows + got[:, :width]
        row_squares = row_squares + got[:, width] + got[:, width + 1]
    rows = rows * lax.rsqrt(row_squares / model_width + epsilon_norm)[:, None]
    rows = rows + pick(shift_rows, e // halves, 0)[None]
    keys = rows[:, :part].reshape(ROWS, part // HDIM, HDIM)
    keys = keys * lax.rsqrt(jnp.mean(keys * keys, axis=2, keepdims=True) + epsilon_norm)
    text = jnp.concatenate([keys.reshape(ROWS, part), rows[:, part:]], axis=1).astype(bf16)

    chosen = request_prompt[0, 0]
    relative = s ^ chosen
    by_enc = [text] + [swap(text, "enc", n_enc, k) for k in range(1, n_enc)]
    by_enc = jnp.stack(by_enc)
    by_enc = jnp.stack([pick(by_enc, k ^ e, 0) for k in range(n_enc)])
    held = by_enc.reshape(1, n_seq, halves, ROWS, width)
    first = req_bits[0]
    held = jnp.concatenate([held, swap(held, "req", n_req, first)], axis=0)
    groups = [pick(held, relative, 1)]
    for step in range(2, n_req, 2):
        wanted = swap(relative, "req", n_req, step)
        groups.append(swap(pick(held, wanted, 1), "req", n_req, step))
    text_rows = jnp.concatenate(groups, axis=0).reshape(-1, width)
    live = pick(prompt_token_ids, chosen, 0) != 0
    live = live.reshape(n_req, halves * ROWS)
    live = jnp.concatenate([pick(live, r ^ k, 0) for k in range(n_req)])

    down = lax.dynamic_slice_in_dim(adapter_down_maps[0], s * part, part, 0).T
    up = heads_of(adapter_up_maps[0], s)
    maps = jnp.concatenate([down, up], axis=0)[None]
    for bit in reversed(req_bits):
        maps = jnp.concatenate([maps, swap(maps, "req", n_req, bit)], axis=0)
    other = adapter_of_request[0, 0] ^ r
    index = 0
    for bit in req_bits:
        index = index * 2 + (other // bit) % 2
    chosen_maps = pick(maps, index, 0)
    rank = up.shape[0]
    lowrank = lax.dot_general(
        stream, chosen_maps[:rank], (((1,), (1,)), ((), ())), preferred_element_type=f32
    ).reshape(n_seq, -1, rank)
    for bit in bits_of(n_seq):
        got = swap(lowrank, "seq", n_seq, bit)
        lowrank = lowrank + jnp.stack([got[k ^ bit] for k in range(n_seq)])
    lowrank = lowrank.reshape(-1, rank).astype(bf16)
    image_values = (
        base_values.astype(f32) + jnp.dot(lowrank, chosen_maps[rank:], preferred_element_type=f32)
    ).astype(bf16)

    mixed = attention(
        queries, text_rows[:, :part], text_rows[:, part:], image_keys, image_values, live
    ).reshape(n_seq, -1, part)
    pieces = jnp.stack([mixed[0]] + [swap(mixed[k], "seq", n_seq, k) for k in range(1, n_seq)])
    result = jnp.concatenate([pick(pieces, s ^ k, 0) for k in range(n_seq)], axis=1)
    return result[None, None]


F32, BF16 = jnp.float32, jnp.bfloat16
ANY = pl.BlockSpec(memory_space=pl.ANY)
VMEM = pl.BlockSpec(memory_space=pltpu.VMEM)
SMEM = pl.BlockSpec(memory_space=pltpu.SMEM)
NT = (((1,), (1,)), ((), ()))
TN = (((0,), (0,)), ((), ()))


def call(kernel, outs, ins, specs=None, scratch=(), name=None, out_specs=None):
    return pl.pallas_call(
        kernel,
        out_shape=outs,
        in_specs=specs if specs is not None else [VMEM] * len(ins),
        out_specs=out_specs if out_specs is not None else jax.tree.map(lambda _: VMEM, outs),
        scratch_shapes=list(scratch),
        compiler_params=pltpu.CompilerParams(vmem_limit_bytes=16 * 1024 * 1024),
        name=name,
    )(*ins)


def struct(shape, dtype=BF16):
    return jax.ShapeDtypeStruct(shape, dtype)


def at(index, size):
    return pl.ds(pl.multiple_of(index * size, size), size)


def stat_rows(stat):
    high = stat.astype(BF16).astype(F32)
    row = lax.broadcasted_iota(jnp.int32, (ROWS, stat.shape[1]), 0)
    return jnp.where(row == 0, high, jnp.where(row == 1, stat - high, 0.0)).astype(BF16)


def stat_of(rows):
    rows = rows.astype(F32)
    return rows[0:1] + rows[1:2]


def context_kernel(h_ref, w_ref, b_ref, send_ref, keep_ref, stat_ref):
    mine = lax.rem(lax.axis_index("req"), 2)
    features = b_ref.shape[1]
    pairs = w_ref.shape[1] // (2 * features)
    total = jnp.zeros((1, h_ref.shape[0]), F32)
    for p in range(pairs):
        product = jnp.dot(
            h_ref[...], w_ref[:, p * 2 * features : (p + 1) * 2 * features],
            preferred_element_type=F32,
        ).T
        total = total + jnp.sum(product, axis=0, keepdims=True)
        low, high = product[:features], product[features:]
        rows = slice(p * features, (p + 1) * features)
        keep_ref[rows] = jnp.where(mine == 0, low, high)
        send_ref[rows] = jnp.where(mine == 0, high, low).astype(BF16)
    stat = total + jnp.sum(b_ref[...].astype(F32))
    send_ref[pairs * features :] = stat_rows(stat)
    stat_ref[...] = jnp.broadcast_to(stat, stat_ref.shape)


def halve_kernel(features, got_ref, keep_ref, stat_ref, send_ref, kept_ref, out_stat_ref):
    mine = lax.rem(lax.axis_index("req") // 2, 2)
    count = keep_ref.shape[0] // (2 * features)
    for i in range(count):
        rows = slice(i * features, (i + 1) * features)
        own, other = at(2 * i + mine, features), at(2 * i + 1 - mine, features)
        kept_ref[rows] = keep_ref[own] + got_ref[own].astype(F32)
        send_ref[rows] = (keep_ref[other] + got_ref[other].astype(F32)).astype(BF16)
    stat = stat_ref[0:1] + stat_of(got_ref[2 * count * features :])
    send_ref[count * features :] = stat_rows(stat)
    out_stat_ref[...] = jnp.broadcast_to(stat, out_stat_ref.shape)


def scatter_kernel(features, deps, got_ref, keep_ref, stat_ref, *refs):
    kept_ref, out_stat_ref, *send_refs = refs[deps:]
    e = lax.axis_index("enc")
    count = keep_ref.shape[0] // features
    stat = stat_ref[0:1] + stat_of(got_ref[count * features :])
    own = at(e, features)
    for k, send_ref in enumerate(send_refs):
        other = at(e ^ (k + 1), features)
        send_ref[:features] = (keep_ref[other] + got_ref[other].astype(F32)).astype(BF16)
        send_ref[features:] = stat_rows(stat)
    kept_ref[...] = keep_ref[own] + got_ref[own].astype(F32)
    out_stat_ref[...] = jnp.broadcast_to(stat, out_stat_ref.shape)


def centre_kernel(width, prompt_ref, keep_ref, stat_ref, bias_ref, scale_ref, shift_ref, *refs):
    got_refs, out_ref = refs[:-1], refs[-1]
    features, tokens = keep_ref.shape
    total = keep_ref[...] + bias_ref[...]
    stat = stat_ref[0:1]
    for got_ref in got_refs:
        total = total + got_ref[:features].astype(F32)
        stat = stat + stat_of(got_ref[features:])
    centred = total - stat * (1.0 / width)
    out_ref[:features] = (scale_ref[...] * centred).astype(BF16)
    squares = jnp.sum(centred * centred, axis=0, keepdims=True)
    high = squares.astype(BF16).astype(F32)
    row = lax.broadcasted_iota(jnp.int32, (ROWS, tokens), 0)
    extra = jnp.where(row == 0, high, jnp.where(row == 1, squares - high, 0.0))
    for j in range(pl.cdiv(features, tokens)):
        piece = shift_ref[:, j * tokens : min((j + 1) * tokens, features)].astype(F32)
        gap = tokens - piece.shape[1]
        if gap:
            piece = jnp.concatenate([piece, jnp.zeros((1, gap), F32)], axis=1)
        extra = jnp.where(row == 2 + j, piece, extra)
    extra = jnp.where(row == ROWS - 1, prompt_ref[0, 0].astype(F32), extra)
    out_ref[features:] = extra.astype(BF16)


def join_kernel(own_ref, got_ref, out_ref):
    size = own_ref.shape[0]
    out_ref[:size] = own_ref[...]
    out_ref[size:] = got_ref[...]


def project_kernel(n_seq, n_req, n_enc, *refs):
    payload_refs = refs[:n_req]
    weight_refs = refs[n_req : 2 * n_req]
    prompts_ref, keep_ref = refs[2 * n_req : 2 * n_req + 2]
    send_refs = refs[2 * n_req + 2 : -1]
    rows_ref = refs[-1]
    features, width = weight_refs[0].shape
    tokens = payload_refs[0].shape[1]
    stride = features + ROWS
    total = None
    squares = [jnp.zeros((1, tokens), F32) for _ in range(n_seq)]
    for k in range(n_req):
        left = []
        shifts = []
        for p in range(n_seq):
            payload = payload_refs[k]
            left.append(payload[p * stride : p * stride + features].T)
            extra = payload[p * stride + features : (p + 1) * stride].astype(F32)
            squares[p] = squares[p] + extra[0:1] + extra[1:2]
            pieces = [extra[2 + j : 3 + j] for j in range(pl.cdiv(features, tokens))]
            shifts.append(jnp.concatenate(pieces, axis=1)[:, :features])
            if p == 0:
                prompts_ref[k] = jnp.max(extra[ROWS - 1 : ROWS]).astype(jnp.int32)
        shifts.append(jnp.zeros((ROWS - n_seq, features), F32))
        left.append(jnp.concatenate(shifts, axis=0).astype(BF16))
        term = jnp.dot(
            jnp.concatenate(left, axis=0), weight_refs[k][...], preferred_element_type=F32
        )
        total = term if total is None else total + term
    size = n_seq * tokens // n_enc
    heads = width // HDIM
    step = heads * size + ROWS
    row = lax.broadcasted_iota(jnp.int32, (ROWS, HDIM), 0)
    for z in range(n_enc):
        p, first = divmod(z * size, tokens)
        shift = total[n_seq * tokens + p : n_seq * tokens + p + 1]
        square = squares[p][:, first : first + size]
        square = jnp.concatenate([square, jnp.zeros((1, HDIM - size), F32)], axis=1)
        high = square.astype(BF16).astype(F32)
        extra = jnp.where(
            row == 2 * heads, high, jnp.where(row == 2 * heads + 1, square - high, 0.0)
        )
        for h in range(heads):
            cols = slice(h * HDIM, (h + 1) * HDIM)
            rows_ref[z * step + h * size : z * step + (h + 1) * size] = total[
                z * size : (z + 1) * size, cols
            ]
            high = shift[:, cols].astype(BF16).astype(F32)
            extra = jnp.where(
                row == h, high, jnp.where(row == heads + h, shift[:, cols] - high, extra)
            )
        rows_ref[z * step + heads * size : (z + 1) * step] = extra
    e = lax.axis_index("enc")
    keep_ref[...] = rows_ref[at(e, step)]
    for k, send_ref in enumerate(send_refs):
        send_ref[...] = rows_ref[at(e ^ (k + 1), step)].astype(BF16)


def finish_kernel(n_req, model_width, keep_ref, bias_ref, *refs):
    got_refs, out_ref = refs[:-1], refs[-1]
    r, s = lax.axis_index("req"), lax.axis_index("seq")
    size, width = out_ref.shape
    heads = width // HDIM
    half = width // 2
    inner = bias_ref.shape[1] // 2
    total = keep_ref[...]
    for got_ref in got_refs:
        total = total + got_ref[...].astype(F32)
    extra = total[heads * size :]
    squares = extra[2 * heads : 2 * heads + 1] + extra[2 * heads + 1 : 2 * heads + 2]
    squares = jnp.broadcast_to(squares, (HDIM, HDIM)).T[:size]
    factor = lax.rsqrt(squares * (1.0 / model_width) + epsilon_norm)
    for h in range(heads):
        start = (h * HDIM // half) * inner + (s * n_req + r) * half + h * HDIM % half
        bias = bias_ref[:, pl.ds(pl.multiple_of(start, HDIM), HDIM)].astype(F32)
        shift = extra[h : h + 1] + extra[heads + h : heads + h + 1] + bias
        head = total[h * size : (h + 1) * size] * factor + shift
        if h * HDIM < half:
            head = head * lax.rsqrt(jnp.mean(head * head, axis=1, keepdims=True) + epsilon_norm)
        out_ref[:, h * HDIM : (h + 1) * HDIM] = head.astype(BF16)


def choose_kernel(n_seq, n_enc, chosen_ref, *refs):
    part_refs, out_refs = refs[:n_enc], refs[n_enc:]
    e, r, s = lax.axis_index("enc"), lax.axis_index("req"), lax.axis_index("seq")
    halves = n_enc // n_seq
    size = part_refs[0].shape[0]
    for k, out_ref in enumerate(out_refs):
        prompt = s ^ chosen_ref[k]
        for h in range(halves):
            place = e ^ (prompt * halves + h)
            for j in range(n_enc):
                @pl.when(place == j)
                def _():
                    out_ref[h * size : (h + 1) * size] = part_refs[j][...]


def weight_kernel(n_req, part, inner, w_ref, dep_ref, own_ref, core_ref, pair_ref, sems):
    r, s = lax.axis_index("req"), lax.axis_index("seq")
    half = part // n_req
    copies = []
    for k, out_ref in enumerate((own_ref, core_ref, pair_ref.at[0], pair_ref.at[1])):
        for side in range(2):
            columns = pl.ds(
                pl.multiple_of(side * inner + (s * n_req + (r ^ k)) * half, HDIM), half
            )
            copies.append(
                pltpu.make_async_copy(
                    w_ref.at[:, columns],
                    out_ref.at[:, pl.ds(side * half, half)],
                    sems.at[2 * k + side],
                )
            )
    for copy in copies:
        copy.start()
    for copy in copies:
        copy.wait()


def image_kernel(part, inner, step, qk_ref, v_ref, x_ref, dep_ref, out_ref, sems):
    start = (lax.axis_index("seq") ^ step) * part
    copies = []
    for i, (ref, base) in enumerate(((qk_ref, 0), (qk_ref, inner), (v_ref, 0), (x_ref, 0))):
        columns = pl.ds(pl.multiple_of(base + start, HDIM), part)
        copies.append(pltpu.make_async_copy(ref.at[:, columns], out_ref.at[i], sems.at[i]))
    for copy in copies:
        copy.start()
    for copy in copies:
        copy.wait()


def maps_kernel(part, down_ref, up_ref, dep_ref, out_ref, sems):
    rank = down_ref.shape[0]
    columns = pl.ds(pl.multiple_of(lax.axis_index("seq") * part, HDIM), part)
    copies = [
        pltpu.make_async_copy(down_ref.at[:, columns], out_ref.at[pl.ds(0, rank)], sems.at[0]),
        pltpu.make_async_copy(up_ref.at[:, columns], out_ref.at[pl.ds(rank, rank)], sems.at[1]),
    ]
    for copy in copies:
        copy.start()
    for copy in copies:
        copy.wait()


def lowrank_kernel(n_req, part, adapter_ref, x_ref, *refs):
    out_ref, chosen_ref = refs[-2:]
    map_refs = refs[:n_req]
    got_refs = refs[n_req:-2]
    place = adapter_ref[0, 0] ^ lax.axis_index("req")
    for k in range(n_req):
        @pl.when(place == k)
        def _():
            chosen_ref[...] = map_refs[k][...]
    rank = out_ref.shape[-1]
    down = chosen_ref[:rank]
    own = x_ref[:, pl.ds(pl.multiple_of(lax.axis_index("seq") * part, HDIM), part)]
    out_ref[0] = lax.dot_general(own, down, NT, preferred_element_type=F32)
    for k, got_ref in enumerate(got_refs):
        out_ref[k + 1] = lax.dot_general(got_ref[3], down, NT, preferred_element_type=F32)


def arrange_kernel(n_req, part, inner, low_ref, maps_ref, qk_ref, v_ref, *refs):
    got_refs, (q_out, k_out, v_out) = refs[:-3], refs[-3:]
    r, s = lax.axis_index("req"), lax.axis_index("seq")
    rank = maps_ref.shape[0] // 2
    half = part // n_req
    tokens = qk_ref.shape[0]
    low = low_ref[...].astype(BF16)
    for k in range(n_req):
        place = (r ^ k) * half
        up = maps_ref[rank:, pl.ds(pl.multiple_of(place, HDIM), half)]
        for i in range(len(got_refs) + 1):
            rows = slice(i * tokens, (i + 1) * tokens)
            if i == 0:
                own = s * part + place
                q = qk_ref[:, pl.ds(pl.multiple_of(own, HDIM), half)]
                key = qk_ref[:, pl.ds(pl.multiple_of(inner + own, HDIM), half)]
                base = v_ref[:, pl.ds(pl.multiple_of(own, HDIM), half)]
            else:
                columns = pl.ds(pl.multiple_of(place, HDIM), half)
                q = got_refs[i - 1][0, :, columns]
                key = got_refs[i - 1][1, :, columns]
                base = got_refs[i - 1][2, :, columns]
            q_out[k, rows] = q
            k_out[k, rows] = key
            v_out[k, rows] = (
                base.astype(F32) + jnp.dot(low[i], up, preferred_element_type=F32)
            ).astype(BF16)


def heads_kernel(scale, live_ref, text_ref, q_ref, k_ref, v_ref, dep_ref, *out_refs):
    live = live_ref[...] != 0
    half = q_ref.shape[2]
    size = out_refs[0].shape[0]
    for h in range(half // HDIM):
        cols = slice(h * HDIM, (h + 1) * HDIM)
        vals = slice(half + h * HDIM, half + (h + 1) * HDIM)
        q = q_ref[0, :, cols]
        st = lax.dot_general(q, text_ref[:, cols], NT, preferred_element_type=F32) * scale
        si = lax.dot_general(q, k_ref[0, :, cols], NT, preferred_element_type=F32) * scale
        st = jnp.where(live, st, -jnp.inf)
        top = jnp.maximum(
            jnp.max(st, axis=1, keepdims=True), jnp.max(si, axis=1, keepdims=True)
        )
        wt = jnp.exp(st - top)
        wi = jnp.exp(si - top)
        total = jnp.sum(wt, axis=1, keepdims=True) + jnp.sum(wi, axis=1, keepdims=True)
        mixed = jnp.dot(
            wt.astype(BF16), text_ref[:, vals], preferred_element_type=F32
        ) + jnp.dot(wi.astype(BF16), v_ref[0, :, cols], preferred_element_type=F32)
        mixed = (mixed / total).astype(BF16)
        for i, out_ref in enumerate(out_refs):
            out_ref[:, cols] = mixed[i * size : (i + 1) * size]


def assemble_kernel(n_req, n_seq, *refs):
    out_ref = refs[-1]
    r, s = lax.axis_index("req"), lax.axis_index("seq")
    half = refs[0].shape[1]
    for k in range(n_req):
        for i in range(n_seq):
            start = ((s ^ i) * n_req + (r ^ k)) * half
            out_ref[:, pl.ds(pl.multiple_of(start, HDIM), half)] = refs[k * n_seq + i][...]


def per_device_heads(
    n_enc,
    n_req,
    n_seq,
    encoder_hidden,
    prompt_token_ids,
    context_weight,
    context_bias,
    modulation_shift,
    modulation_scale,
    key_value_weight,
    key_value_bias,
    request_prompt,
    adapter_of_request,
    adapter_down_maps,
    adapter_up_maps,
    image_stream_input,
    image_query_key,
    image_value_rows,
):
    e, r, s = lax.axis_index("enc"), lax.axis_index("req"), lax.axis_index("seq")
    model_width = context_weight.shape[1]
    features = context_bias.shape[0]
    tokens = encoder_hidden.shape[1]
    inner = key_value_weight.shape[1] // 2
    part = inner // n_seq
    half = part // n_req
    image_rows = image_query_key.shape[2]
    rank = adapter_up_maps.shape[1]
    qk, base, stream = image_query_key[0, 0], image_value_rows[0, 0], image_stream_input[0, 0]
    dma = pltpu.SemaphoreType.DMA
    stat = struct((8, tokens), F32)

    send, keep, sums = call(
        context_kernel,
        (
            struct((model_width // 2 + ROWS, tokens)),
            struct((model_width // 2, tokens), F32),
            stat,
        ),
        (encoder_hidden[0], context_weight, context_bias[None]),
        name="context",
    )
    got = swap(send, "req", n_req, 1)

    packed = [
        call(
            functools.partial(image_kernel, part, inner, k),
            struct((4, image_rows, part)),
            (qk, base, stream, keep),
            [ANY] * 4,
            [dma((4,))],
            name="image_pack",
        )
        for k in range(1, n_seq)
    ]
    image_got = [swap(packed[k - 1], "seq", n_seq, k) for k in range(1, n_seq)]
    weight = struct((features, 2 * half))
    weight_own, weight_core, weight_pair = call(
        functools.partial(weight_kernel, n_req, part, inner),
        (weight, weight, struct((2, features, 2 * half))),
        (key_value_weight, keep),
        [ANY] * 2,
        [dma((2 * n_req,))],
        name="weight_pack",
    )
    weight_core_got = swap(weight_core, "req", n_req, 1)

    send, keep, sums = call(
        functools.partial(halve_kernel, features),
        (
            struct((n_enc * features + ROWS, tokens)),
            struct((n_enc * features, tokens), F32),
            stat,
        ),
        (got, keep, sums),
        name="halve",
    )
    got = swap(send, "req", n_req, 2)
    keep, sums, *sends = call(
        functools.partial(scatter_kernel, features, 2),
        (struct((features, tokens), F32), stat)
        + tuple(struct((features + ROWS, tokens)) for _ in range(1, n_enc)),
        (got, keep, sums, weight_pair, packed[0]),
        [VMEM] * 3 + [ANY] * 2,
        name="scatter",
    )
    arrived = [swap(sends[k - 1], "enc", n_enc, k) for k in range(1, n_enc)]
    weight_pair = lax.optimization_barrier((weight_pair, keep))[0]
    weight_pair_got = swap(weight_pair, "req", n_req, 2)
    weights = (
        weight_own,
        weight_core_got,
        weight_pair_got[0],
        swap(weight_pair_got[1], "req", n_req, 1),
    )

    bias_columns = jnp.broadcast_to(context_bias.astype(F32)[:, None], (features, tokens))
    scale_columns = jnp.broadcast_to(
        1.0 + modulation_scale[0].astype(F32)[:, None], (features, tokens)
    )
    own = call(
        functools.partial(centre_kernel, model_width),
        struct((features + ROWS, tokens)),
        (request_prompt, keep, sums, bias_columns, scale_columns, modulation_shift, *arrived),
        [SMEM] + [VMEM] * (5 + len(arrived)),
        name="centre",
    )
    joined = call(
        join_kernel,
        struct((n_seq * (features + ROWS), tokens)),
        (own, swap(own, "seq", n_seq, 1)),
        name="join",
    )
    payloads = [joined] + [swap(joined, "req", n_req, k) for k in range(1, n_req)]

    size = n_seq * tokens // n_enc
    step = 2 * half // HDIM * size + ROWS
    prompts, keep, *sends = call(
        functools.partial(project_kernel, n_seq, n_req, n_enc),
        (struct((n_req,), jnp.int32), struct((step, HDIM), F32))
        + tuple(struct((step, HDIM)) for _ in range(1, n_enc)),
        (*payloads, *weights),
        scratch=[pltpu.VMEM((n_enc * step, HDIM), F32)],
        out_specs=(SMEM,) + (VMEM,) * n_enc,
        name="project",
    )
    arrived = [swap(sends[k - 1], "enc", n_enc, k) for k in range(1, n_enc)]

    maps = call(
        functools.partial(maps_kernel, part),
        struct((2 * rank, part)),
        (adapter_down_maps[0].T, adapter_up_maps[0], arrived[0]),
        [ANY] * 3,
        [dma((2,))],
        name="maps_pack",
    )
    maps = [maps]
    step = n_req // 2
    while step:
        maps = maps + [swap(m, "req", n_req, step) for m in maps]
        step //= 2
    ordered = [None] * n_req
    place = [0]
    step = n_req // 2
    while step:
        place = place + [p ^ step for p in place]
        step //= 2
    for p, m in zip(place, maps):
        ordered[p] = m
    low, chosen_maps = call(
        functools.partial(lowrank_kernel, n_req, part),
        (struct((n_seq, image_rows, rank), F32), struct((2 * rank, part))),
        (adapter_of_request, stream, *ordered, *image_got),
        [SMEM] + [VMEM] * (1 + n_req + len(image_got)),
        name="lowrank",
    )
    for bit in bits_of(n_seq):
        other = swap(low, "seq", n_seq, bit)
        low = low + jnp.stack([other[k ^ bit] for k in range(n_seq)])
    arranged = struct((n_req, n_seq * image_rows, half))
    queries, image_keys, image_values = call(
        functools.partial(arrange_kernel, n_req, part, inner),
        (arranged, arranged, arranged),
        (low, chosen_maps, qk, base, *image_got),
        name="arrange",
    )

    text = call(
        functools.partial(finish_kernel, n_req, model_width),
        struct((size, 2 * half)),
        (keep, key_value_bias[None], *arrived),
        name="finish",
    )
    parts = [text] + [swap(text, "enc", n_enc, k) for k in range(1, n_enc)]
    rows = call(
        functools.partial(choose_kernel, n_seq, n_enc),
        tuple(struct((tokens, 2 * half)) for _ in range(n_req)),
        (prompts, *parts),
        [SMEM] + [VMEM] * n_enc,
        name="choose",
    )
    rows = [rows[0]] + [swap(rows[k], "req", n_req, k) for k in range(1, n_req)]
    live = lax.dynamic_slice_in_dim(prompt_token_ids, request_prompt[0, 0], 1, 0)
    pieces = [None] * n_req
    last = live
    for k in range(n_req):
        block = pl.BlockSpec((1, n_seq * image_rows, half), lambda i, k=k: (k, 0, 0))
        whole = lambda shape: pl.BlockSpec(shape, lambda i: (0, 0))
        mixed = pl.pallas_call(
            functools.partial(heads_kernel, HDIM ** (-0.5)),
            grid=(1,),
            out_shape=[struct((image_rows, half)) for _ in range(n_seq)],
            in_specs=[whole((1, tokens)), whole((tokens, 2 * half)), block, block, block, ANY],
            out_specs=[whole((image_rows, half)) for _ in range(n_seq)],
            compiler_params=pltpu.CompilerParams(vmem_limit_bytes=16 * 1024 * 1024),
            name="heads",
        )(live, rows[k], queries, image_keys, image_values, last)
        last = mixed[0]
        pieces[k] = [mixed[0]] + [swap(mixed[i], "seq", n_seq, i) for i in range(1, n_seq)]
    result = call(
        functools.partial(assemble_kernel, n_req, n_seq),
        struct((image_rows, inner)),
        tuple(p for group in pieces for p in group),
        name="assemble",
    )
    return result[None, None]


def solution(mesh):
    sizes = mesh.shape
    n_enc, n_req, n_seq = sizes["enc"], sizes["req"], sizes["seq"]

    def run(*arrays):
        heads = arrays[6].shape[1] // (2 * HDIM)
        fits = n_seq == 2 and n_req == 4 and heads % (n_seq * n_req) == 0
        return (per_device_heads if fits else per_device)(n_enc, n_req, n_seq, *arrays)

    return jax.shard_map(
        run,
        mesh=mesh,
        in_specs=(
            P("seq", None, ("enc", "req")),
            P(),
            P(("enc", "req"), None),
            P(("enc", "req")),
            P("seq", ("enc", "req")),
            P("seq", ("enc", "req")),
            P(("enc", "req"), None),
            P(),
            P("enc", "req"),
            P("enc", "req"),
            P("req", None, None),
            P("req", None, None),
            P("enc", "req", "seq", None),
            P("enc", "req", "seq", None),
            P("enc", "req", "seq", None),
        ),
        out_specs=P("enc", "req", "seq", None),
        check_vma=False,
    )
```

```python
import functools

import jax
import jax.numpy as jnp
from jax import lax
from jax.experimental import pallas as pl
from jax.experimental.pallas import tpu as pltpu
from jax.sharding import PartitionSpec as P

HDIM = 128
ROWS = 16

epsilon_norm = 1e-06


def swap(block, axis, size, step):
    return lax.ppermute(block, axis, [(i, i ^ step) for i in range(size)])


def pick(array, index, dim):
    return lax.dynamic_index_in_dim(array, index, dim, keepdims=False)


def split_two(value):
    high = lax.reduce_precision(value, 8, 7)
    return high.astype(jnp.bfloat16), (value - high).astype(jnp.bfloat16)


def bits_of(size):
    return [1 << b for b in range(size.bit_length() - 1)]


def with_stat_rows(data, stat):
    high, low = split_two(stat)
    rows = jnp.concatenate(
        [high[None], low[None], jnp.zeros((ROWS - 2, stat.shape[0]), jnp.bfloat16)], axis=0
    )
    rows = jnp.broadcast_to(rows, data.shape[:-2] + rows.shape)
    return jnp.concatenate([data.astype(jnp.bfloat16), rows], axis=-2)


def attention_kernel(heads, inner, scale, mask_ref, q_ref, kt_ref, vt_ref, ki_ref, vi_ref, o_ref):
    live = mask_ref[...] != 0
    for h in range(heads):
        cols = slice(h * HDIM, (h + 1) * HDIM)
        q = q_ref[:, cols]
        dims = (((1,), (1,)), ((), ()))
        st = lax.dot_general(q, kt_ref[:, cols], dims, preferred_element_type=jnp.float32) * scale
        si = lax.dot_general(q, ki_ref[:, cols], dims, preferred_element_type=jnp.float32) * scale
        st = jnp.where(live, st, -jnp.inf)
        top = jnp.maximum(
            jnp.max(st, axis=1, keepdims=True), jnp.max(si, axis=1, keepdims=True)
        )
        wt = jnp.exp(st - top)
        wi = jnp.exp(si - top)
        total = jnp.sum(wt, axis=1, keepdims=True) + jnp.sum(wi, axis=1, keepdims=True)
        mixed = jnp.dot(
            wt.astype(jnp.bfloat16), vt_ref[:, cols], preferred_element_type=jnp.float32
        ) + jnp.dot(wi.astype(jnp.bfloat16), vi_ref[:, cols], preferred_element_type=jnp.float32)
        o_ref[:, cols] = (mixed / total).astype(o_ref.dtype)


def attention(queries, text_keys, text_values, image_keys, image_values, live):
    width = queries.shape[1]
    heads = width // HDIM
    rows = queries.shape[0]
    mask = jnp.broadcast_to(live.astype(jnp.int32)[None, :], (8, live.shape[0]))[:1]
    return pl.pallas_call(
        functools.partial(attention_kernel, heads, width, HDIM ** (-0.5)),
        out_shape=jax.ShapeDtypeStruct((rows, width), jnp.bfloat16),
        compiler_params=pltpu.CompilerParams(vmem_limit_bytes=48 * 1024 * 1024),
        name="attention",
    )(mask, queries, text_keys, text_values, image_keys, image_values)


def per_device(
    n_enc,
    n_req,
    n_seq,
    encoder_hidden,
    prompt_token_ids,
    context_weight,
    context_bias,
    modulation_shift,
    modulation_scale,
    key_value_weight,
    key_value_bias,
    request_prompt,
    adapter_of_request,
    adapter_down_maps,
    adapter_up_maps,
    image_stream_input,
    image_query_key,
    image_value_rows,
):
    f32, bf16 = jnp.float32, jnp.bfloat16
    e, r, s = lax.axis_index("enc"), lax.axis_index("req"), lax.axis_index("seq")
    req_bits = bits_of(n_req)
    model_width = context_weight.shape[1]
    features = context_bias.shape[0]
    tokens = encoder_hidden.shape[1]
    inner = key_value_weight.shape[1] // 2
    part = inner // n_seq

    def heads_of(array, share):
        return lax.dynamic_slice_in_dim(array, share * part, part, 1)

    qk = image_query_key[0, 0]
    sources = [qk[:, :inner], qk[:, inner:], image_value_rows[0, 0], image_stream_input[0, 0]]
    image_parts = [
        jnp.stack([heads_of(a, s ^ k) for a in sources]) for k in range(n_seq)
    ]
    image_parts = [image_parts[0]] + [
        swap(image_parts[k], "seq", n_seq, k) for k in range(1, n_seq)
    ]
    image_all = jnp.concatenate(image_parts, axis=1)
    queries, image_keys, base_values, stream = [image_all[i] for i in range(4)]

    partial_value = lax.dot_general(
        context_weight, encoder_hidden[0], (((0,), (1,)), ((), ())), preferred_element_type=f32
    )
    stat = jnp.sum(partial_value, axis=0) + jnp.sum(context_bias.astype(f32))
    acc = partial_value.reshape((n_enc,) + (2,) * len(req_bits) + (features, tokens))
    for i, bit in enumerate(req_bits):
        mine = (r // bit) % 2
        dim = len(req_bits) - i
        got = swap(with_stat_rows(pick(acc, 1 - mine, dim), stat), "req", n_req, bit).astype(f32)
        acc = pick(acc, mine, dim) + got[..., :features, :]
        got_stat = got.reshape((-1,) + got.shape[-2:])[0, features:]
        stat = stat + got_stat[0] + got_stat[1]
    arrived = [
        swap(with_stat_rows(pick(acc, e ^ k, 0), stat), "enc", n_enc, k).astype(f32)
        for k in range(1, n_enc)
    ]
    embedded = pick(acc, e, 0)
    for got in arrived:
        embedded = embedded + got[:features]
        stat = stat + got[features] + got[features + 1]
    embedded = embedded + context_bias.astype(f32)[:, None]
    centred = embedded - (stat / model_width)[None, :]
    squares = jnp.sum(centred * centred, axis=0)
    scaled = (1.0 + modulation_scale[0].astype(f32))[:, None] * centred

    own = with_stat_rows(scaled, squares)
    blocks = [own] + [swap(own, "seq", n_seq, k) for k in range(1, n_seq)]
    scaled_all = jnp.concatenate([b[:features] for b in blocks], axis=1)
    squares_all = jnp.concatenate(
        [b[features].astype(f32) + b[features + 1].astype(f32) for b in blocks]
    )
    weight_own = jnp.concatenate(
        [heads_of(key_value_weight[:, :inner], s), heads_of(key_value_weight[:, inner:], s)], axis=1
    )
    width = 2 * part
    projected = lax.dot_general(
        scaled_all, weight_own, (((0,), (0,)), ((), ())), preferred_element_type=f32
    )

    shift_part = jnp.dot(modulation_shift, key_value_weight, preferred_element_type=f32)
    for bit in req_bits:
        shift_part = shift_part + swap(shift_part, "req", n_req, bit)
    for bit in bits_of(n_enc):
        shift_part = shift_part + swap(shift_part, "enc", n_enc, bit)
    shift_part = shift_part + key_value_bias.astype(f32)[None]

    def columns_of(row, share):
        return jnp.concatenate(
            [heads_of(row[:, :inner], share), heads_of(row[:, inner:], share)], axis=1
        )

    shift_rows = jnp.concatenate(
        [columns_of(shift_part, s)]
        + [swap(columns_of(shift_part, s ^ k), "seq", n_seq, k) for k in range(1, n_seq)],
        axis=0,
    )

    halves = tokens // n_req // ROWS
    split = (n_seq,) + (2,) * len(req_bits) + (halves, ROWS)
    acc = projected.reshape(split + (width,))
    acc_stat = squares_all.reshape(split)

    def with_stat_columns(data, stat):
        high, low = split_two(stat)
        lane = lax.broadcasted_iota(jnp.int32, stat.shape + (HDIM,), stat.ndim)
        columns = jnp.where(
            lane == 0, high[..., None], jnp.where(lane == 1, low[..., None], jnp.zeros((), bf16))
        )
        return jnp.concatenate([data.astype(bf16), columns], axis=-1)

    for i, bit in enumerate(req_bits):
        mine = (r // bit) % 2
        dim = len(req_bits) - i
        got = swap(
            with_stat_columns(pick(acc, 1 - mine, dim), pick(acc_stat, 1 - mine, dim)),
            "req", n_req, bit,
        ).astype(f32)
        acc = pick(acc, mine, dim) + got[..., :width]
        acc_stat = pick(acc_stat, mine, dim) + got[..., width] + got[..., width + 1]
    acc = acc.reshape(n_enc, ROWS, width)
    acc_stat = acc_stat.reshape(n_enc, ROWS)
    arrived = [
        swap(with_stat_columns(pick(acc, e ^ k, 0), pick(acc_stat, e ^ k, 0)), "enc", n_enc, k)
        .astype(f32)
        for k in range(1, n_enc)
    ]
    rows = pick(acc, e, 0)
    row_squares = pick(acc_stat, e, 0)
    for got in arrived:
        rows = rows + got[:, :width]
        row_squares = row_squares + got[:, width] + got[:, width + 1]
    rows = rows * lax.rsqrt(row_squares / model_width + epsilon_norm)[:, None]
    rows = rows + pick(shift_rows, e // halves, 0)[None]
    keys = rows[:, :part].reshape(ROWS, part // HDIM, HDIM)
    keys = keys * lax.rsqrt(jnp.mean(keys * keys, axis=2, keepdims=True) + epsilon_norm)
    text = jnp.concatenate([keys.reshape(ROWS, part), rows[:, part:]], axis=1).astype(bf16)

    chosen = request_prompt[0, 0]
    relative = s ^ chosen
    by_enc = [text] + [swap(text, "enc", n_enc, k) for k in range(1, n_enc)]
    by_enc = jnp.stack(by_enc)
    by_enc = jnp.stack([pick(by_enc, k ^ e, 0) for k in range(n_enc)])
    held = by_enc.reshape(1, n_seq, halves, ROWS, width)
    first = req_bits[0]
    held = jnp.concatenate([held, swap(held, "req", n_req, first)], axis=0)
    groups = [pick(held, relative, 1)]
    for step in range(2, n_req, 2):
        wanted = swap(relative, "req", n_req, step)
        groups.append(swap(pick(held, wanted, 1), "req", n_req, step))
    text_rows = jnp.concatenate(groups, axis=0).reshape(-1, width)
    live = pick(prompt_token_ids, chosen, 0) != 0
    live = live.reshape(n_req, halves * ROWS)
    live = jnp.concatenate([pick(live, r ^ k, 0) for k in range(n_req)])

    down = lax.dynamic_slice_in_dim(adapter_down_maps[0], s * part, part, 0).T
    up = heads_of(adapter_up_maps[0], s)
    maps = jnp.concatenate([down, up], axis=0)[None]
    for bit in reversed(req_bits):
        maps = jnp.concatenate([maps, swap(maps, "req", n_req, bit)], axis=0)
    other = adapter_of_request[0, 0] ^ r
    index = 0
    for bit in req_bits:
        index = index * 2 + (other // bit) % 2
    chosen_maps = pick(maps, index, 0)
    rank = up.shape[0]
    lowrank = lax.dot_general(
        stream, chosen_maps[:rank], (((1,), (1,)), ((), ())), preferred_element_type=f32
    ).reshape(n_seq, -1, rank)
    for bit in bits_of(n_seq):
        got = swap(lowrank, "seq", n_seq, bit)
        lowrank = lowrank + jnp.stack([got[k ^ bit] for k in range(n_seq)])
    lowrank = lowrank.reshape(-1, rank).astype(bf16)
    image_values = (
        base_values.astype(f32) + jnp.dot(lowrank, chosen_maps[rank:], preferred_element_type=f32)
    ).astype(bf16)

    mixed = attention(
        queries, text_rows[:, :part], text_rows[:, part:], image_keys, image_values, live
    ).reshape(n_seq, -1, part)
    pieces = jnp.stack([mixed[0]] + [swap(mixed[k], "seq", n_seq, k) for k in range(1, n_seq)])
    result = jnp.concatenate([pick(pieces, s ^ k, 0) for k in range(n_seq)], axis=1)
    return result[None, None]


F32, BF16 = jnp.float32, jnp.bfloat16
ANY = pl.BlockSpec(memory_space=pl.ANY)
VMEM = pl.BlockSpec(memory_space=pltpu.VMEM)
SMEM = pl.BlockSpec(memory_space=pltpu.SMEM)
HBM = pl.BlockSpec(memory_space=pltpu.HBM)
NT = (((1,), (1,)), ((), ()))
TN = (((0,), (0,)), ((), ()))


def call(kernel, outs, ins, specs=None, scratch=(), name=None, out_specs=None):
    return pl.pallas_call(
        kernel,
        out_shape=outs,
        in_specs=specs if specs is not None else [VMEM] * len(ins),
        out_specs=out_specs if out_specs is not None else jax.tree.map(lambda _: VMEM, outs),
        scratch_shapes=list(scratch),
        compiler_params=pltpu.CompilerParams(vmem_limit_bytes=16 * 1024 * 1024),
        name=name,
    )(*ins)


def struct(shape, dtype=BF16):
    return jax.ShapeDtypeStruct(shape, dtype)


def at(index, size):
    return pl.ds(pl.multiple_of(index * size, size), size)


def stat_rows(stat):
    high = stat.astype(BF16).astype(F32)
    row = lax.broadcasted_iota(jnp.int32, (ROWS, stat.shape[1]), 0)
    return jnp.where(row == 0, high, jnp.where(row == 1, stat - high, 0.0)).astype(BF16)


def stat_of(rows):
    rows = rows.astype(F32)
    return rows[0:1] + rows[1:2]


def context_kernel(
    h_hbm, w_hbm, b_hbm, send_ref, keep_ref, stat_ref, h_ref, w_ref, b_ref, sems
):
    mine = lax.rem(lax.axis_index("req"), 2)
    features = b_ref.shape[0]
    pairs = w_ref.shape[1] // (2 * features)
    count = sems.shape[0] - 2
    chunk = w_ref.shape[1] // count
    copies = [pltpu.make_async_copy(h_hbm, h_ref, sems.at[0])]
    for i in range(count):
        columns = pl.ds(i * chunk, chunk)
        copies.append(
            pltpu.make_async_copy(w_hbm.at[:, columns], w_ref.at[:, columns], sems.at[i + 1])
        )
    copies.append(pltpu.make_async_copy(b_hbm, b_ref, sems.at[count + 1]))
    for copy in copies:
        copy.start()
    copies[0].wait()
    arrived = 0
    total = jnp.zeros((1, h_ref.shape[0]), F32)
    for p in range(pairs):
        while arrived * chunk < (p + 1) * 2 * features:
            arrived += 1
            copies[arrived].wait()
        product = jnp.dot(
            h_ref[...], w_ref[:, p * 2 * features : (p + 1) * 2 * features],
            preferred_element_type=F32,
        ).T
        total = total + jnp.sum(product, axis=0, keepdims=True)
        low, high = product[:features], product[features:]
        rows = slice(p * features, (p + 1) * features)
        keep_ref[rows] = jnp.where(mine == 0, low, high)
        send_ref[rows] = jnp.where(mine == 0, high, low).astype(BF16)
    copies[-1].wait()
    stat = total + jnp.sum(b_ref[...].astype(F32))
    send_ref[pairs * features :] = stat_rows(stat)
    stat_ref[...] = jnp.broadcast_to(stat, stat_ref.shape)


def halve_kernel(features, got_ref, keep_ref, stat_ref, send_ref, kept_ref, out_stat_ref):
    mine = lax.rem(lax.axis_index("req") // 2, 2)
    count = keep_ref.shape[0] // (2 * features)
    for i in range(count):
        rows = slice(i * features, (i + 1) * features)
        own, other = at(2 * i + mine, features), at(2 * i + 1 - mine, features)
        kept_ref[rows] = keep_ref[own] + got_ref[own].astype(F32)
        send_ref[rows] = (keep_ref[other] + got_ref[other].astype(F32)).astype(BF16)
    stat = stat_ref[0:1] + stat_of(got_ref[2 * count * features :])
    send_ref[count * features :] = stat_rows(stat)
    out_stat_ref[...] = jnp.broadcast_to(stat, out_stat_ref.shape)


def scatter_kernel(features, deps, got_ref, keep_ref, stat_ref, *refs):
    kept_ref, out_stat_ref, *send_refs = refs[deps:]
    e = lax.axis_index("enc")
    count = keep_ref.shape[0] // features
    stat = stat_ref[0:1] + stat_of(got_ref[count * features :])
    own = at(e, features)
    for k, send_ref in enumerate(send_refs):
        other = at(e ^ (k + 1), features)
        send_ref[:features] = (keep_ref[other] + got_ref[other].astype(F32)).astype(BF16)
        send_ref[features:] = stat_rows(stat)
    kept_ref[...] = keep_ref[own] + got_ref[own].astype(F32)
    out_stat_ref[...] = jnp.broadcast_to(stat, out_stat_ref.shape)


def centre_kernel(width, prompt_ref, adapter_ref, keep_ref, stat_ref, bias_ref, scale_ref, shift_ref, *refs):
    got_refs, out_ref = refs[:-1], refs[-1]
    features, tokens = keep_ref.shape
    total = keep_ref[...] + bias_ref[...]
    stat = stat_ref[0:1]
    for got_ref in got_refs:
        total = total + got_ref[:features].astype(F32)
        stat = stat + stat_of(got_ref[features:])
    centred = total - stat * (1.0 / width)
    out_ref[:features] = (scale_ref[...] * centred).astype(BF16)
    squares = jnp.sum(centred * centred, axis=0, keepdims=True)
    high = squares.astype(BF16).astype(F32)
    row = lax.broadcasted_iota(jnp.int32, (ROWS, tokens), 0)
    extra = jnp.where(row == 0, high, jnp.where(row == 1, squares - high, 0.0))
    for j in range(pl.cdiv(features, tokens)):
        piece = shift_ref[:, j * tokens : min((j + 1) * tokens, features)].astype(F32)
        gap = tokens - piece.shape[1]
        if gap:
            piece = jnp.concatenate([piece, jnp.zeros((1, gap), F32)], axis=1)
        extra = jnp.where(row == 2 + j, piece, extra)
    extra = jnp.where(row == ROWS - 1, prompt_ref[0, 0].astype(F32), extra)
    extra = jnp.where(row == ROWS - 2, adapter_ref[0, 0].astype(F32), extra)
    out_ref[features:] = extra.astype(BF16)


def pass_on_kernel(got_ref, dep_ref, own_ref, next_ref):
    own_ref[...] = got_ref[0]
    next_ref[...] = got_ref[1]


def join_kernel(own_ref, got_ref, out_ref):
    size = own_ref.shape[0]
    out_ref[:size] = own_ref[...]
    out_ref[size:] = got_ref[...]


def project_kernel(n_seq, n_req, n_enc, dep_ref, *refs):
    payload_refs = refs[:n_req]
    weight_refs = refs[n_req : 2 * n_req]
    prompts_ref, keep_ref = refs[2 * n_req : 2 * n_req + 2]
    send_refs = refs[2 * n_req + 2 : -1]
    rows_ref = refs[-1]
    features, width = weight_refs[0].shape
    tokens = payload_refs[0].shape[1]
    stride = features + ROWS
    total = None
    squares = [jnp.zeros((1, tokens), F32) for _ in range(n_seq)]
    for k in range(n_req):
        left = []
        shifts = []
        for p in range(n_seq):
            payload = payload_refs[k]
            left.append(payload[p * stride : p * stride + features].T)
            extra = payload[p * stride + features : (p + 1) * stride].astype(F32)
            squares[p] = squares[p] + extra[0:1] + extra[1:2]
            pieces = [extra[2 + j : 3 + j] for j in range(pl.cdiv(features, tokens))]
            shifts.append(jnp.concatenate(pieces, axis=1)[:, :features])
            if p == 0:
                prompts_ref[k] = jnp.max(extra[ROWS - 1 : ROWS]).astype(jnp.int32)
                prompts_ref[n_req + k] = jnp.max(extra[ROWS - 2 : ROWS - 1]).astype(jnp.int32)
        shifts.append(jnp.zeros((ROWS - n_seq, features), F32))
        left.append(jnp.concatenate(shifts, axis=0).astype(BF16))
        term = jnp.dot(
            jnp.concatenate(left, axis=0), weight_refs[k][...], preferred_element_type=F32
        )
        total = term if total is None else total + term
    size = n_seq * tokens // n_enc
    heads = width // HDIM
    step = heads * size + ROWS
    row = lax.broadcasted_iota(jnp.int32, (ROWS, HDIM), 0)
    for z in range(n_enc):
        p, first = divmod(z * size, tokens)
        shift = total[n_seq * tokens + p : n_seq * tokens + p + 1]
        square = squares[p][:, first : first + size]
        square = jnp.concatenate([square, jnp.zeros((1, HDIM - size), F32)], axis=1)
        high = square.astype(BF16).astype(F32)
        extra = jnp.where(
            row == 2 * heads, high, jnp.where(row == 2 * heads + 1, square - high, 0.0)
        )
        for h in range(heads):
            cols = slice(h * HDIM, (h + 1) * HDIM)
            rows_ref[z * step + h * size : z * step + (h + 1) * size] = total[
                z * size : (z + 1) * size, cols
            ]
            high = shift[:, cols].astype(BF16).astype(F32)
            extra = jnp.where(
                row == h, high, jnp.where(row == heads + h, shift[:, cols] - high, extra)
            )
        rows_ref[z * step + heads * size : (z + 1) * step] = extra
    e = lax.axis_index("enc")
    keep_ref[...] = rows_ref[at(e, step)]
    for k, send_ref in enumerate(send_refs):
        send_ref[...] = rows_ref[at(e ^ (k + 1), step)].astype(BF16)


def finish_kernel(n_req, model_width, dep_ref, keep_ref, bias_ref, *refs):
    got_refs, out_ref = refs[:-1], refs[-1]
    r, s = lax.axis_index("req"), lax.axis_index("seq")
    size, width = out_ref.shape
    heads = width // HDIM
    half = width // 2
    inner = bias_ref.shape[1] // 2
    total = keep_ref[...]
    for got_ref in got_refs:
        total = total + got_ref[...].astype(F32)
    extra = total[heads * size :]
    squares = extra[2 * heads : 2 * heads + 1] + extra[2 * heads + 1 : 2 * heads + 2]
    squares = jnp.broadcast_to(squares, (HDIM, HDIM)).T[:size]
    factor = lax.rsqrt(squares * (1.0 / model_width) + epsilon_norm)
    for h in range(heads):
        start = (h * HDIM // half) * inner + (s * n_req + r) * half + h * HDIM % half
        bias = bias_ref[:, pl.ds(pl.multiple_of(start, HDIM), HDIM)].astype(F32)
        shift = extra[h : h + 1] + extra[heads + h : heads + h + 1] + bias
        head = total[h * size : (h + 1) * size] * factor + shift
        if h * HDIM < half:
            head = head * lax.rsqrt(jnp.mean(head * head, axis=1, keepdims=True) + epsilon_norm)
        out_ref[:, h * HDIM : (h + 1) * HDIM] = head.astype(BF16)


def choose_kernel(n_seq, n_enc, chosen_ref, dep_ref, *refs):
    part_refs, out_refs = refs[:n_enc], refs[n_enc:]
    e, r, s = lax.axis_index("enc"), lax.axis_index("req"), lax.axis_index("seq")
    halves = n_enc // n_seq
    size = part_refs[0].shape[0]
    for k, out_ref in enumerate(out_refs):
        prompt = s ^ chosen_ref[k]
        for h in range(halves):
            place = e ^ (prompt * halves + h)
            for j in range(n_enc):
                @pl.when(place == j)
                def _():
                    out_ref[h * size : (h + 1) * size] = part_refs[j][...]


def weight_kernel(n_req, part, inner, w_ref, dep_ref, own_ref, core_ref, pair_ref, sems):
    r, s = lax.axis_index("req"), lax.axis_index("seq")
    half = part // n_req
    copies = []
    for k, out_ref in enumerate((own_ref, core_ref, pair_ref.at[0], pair_ref.at[1])):
        for side in range(2):
            columns = pl.ds(
                pl.multiple_of(side * inner + (s * n_req + (r ^ k)) * half, HDIM), half
            )
            copies.append(
                pltpu.make_async_copy(
                    w_ref.at[:, columns],
                    out_ref.at[:, pl.ds(side * half, half)],
                    sems.at[2 * k + side],
                )
            )
    for copy in copies:
        copy.start()
    for copy in copies:
        copy.wait()


def image_kernel(part, inner, step, qk_ref, v_ref, x_ref, dep_ref, out_ref, sems):
    start = (lax.axis_index("seq") ^ step) * part
    copies = []
    for i, (ref, base) in enumerate(((qk_ref, 0), (qk_ref, inner), (v_ref, 0), (x_ref, 0))):
        columns = pl.ds(pl.multiple_of(base + start, HDIM), part)
        copies.append(pltpu.make_async_copy(ref.at[:, columns], out_ref.at[i], sems.at[i]))
    for copy in copies:
        copy.start()
    for copy in copies:
        copy.wait()


def maps_kernel(part, down_ref, up_ref, dep_ref, out_ref, sems):
    rank = down_ref.shape[0]
    columns = pl.ds(pl.multiple_of(lax.axis_index("seq") * part, HDIM), part)
    copies = [
        pltpu.make_async_copy(down_ref.at[:, columns], out_ref.at[pl.ds(0, rank)], sems.at[0]),
        pltpu.make_async_copy(up_ref.at[:, columns], out_ref.at[pl.ds(rank, rank)], sems.at[1]),
    ]
    for copy in copies:
        copy.start()
    for copy in copies:
        copy.wait()


def select_kernel(ids_ref, own_ref, pair_ref, dep_ref, mine_ref, core_ref):
    r = lax.axis_index("req")
    for out_ref, adapter in ((mine_ref, ids_ref[4]), (core_ref, ids_ref[5])):
        other = lax.rem((adapter ^ r) // 2, 2)

        @pl.when(other == 0)
        def _():
            out_ref[...] = own_ref[...]

        @pl.when(other == 1)
        def _():
            out_ref[...] = pair_ref[...]


def lowrank_kernel(part, adapter_ref, x_ref, mine_ref, core_ref, got_ref, out_ref, chosen_ref):
    other = lax.rem(adapter_ref[0, 0] ^ lax.axis_index("req"), 2)
    rank = out_ref.shape[-1]
    for k, ref in enumerate((mine_ref, core_ref)):
        @pl.when(other == k)
        def _():
            chosen_ref[...] = ref[rank:]
            own = x_ref[:, pl.ds(pl.multiple_of(lax.axis_index("seq") * part, HDIM), part)]
            for i, rows in enumerate((own, got_ref[3])):
                out_ref[i] = lax.dot_general(
                    rows, ref[:rank], NT, preferred_element_type=F32
                )


def arrange_kernel(n_req, part, inner, low_ref, other_ref, maps_ref, qk_ref, v_ref, *refs):
    got_refs, (q_out, k_out, v_out) = refs[:-3], refs[-3:]
    r, s = lax.axis_index("req"), lax.axis_index("seq")
    half = part // n_req
    tokens = qk_ref.shape[0]
    low = [(low_ref[i] + other_ref[i ^ 1]).astype(BF16) for i in range(2)]
    for k in range(n_req):
        place = (r ^ k) * half
        up = maps_ref[:, pl.ds(pl.multiple_of(place, HDIM), half)]
        for i in range(len(got_refs) + 1):
            rows = slice(i * tokens, (i + 1) * tokens)
            if i == 0:
                own = s * part + place
                q = qk_ref[:, pl.ds(pl.multiple_of(own, HDIM), half)]
                key = qk_ref[:, pl.ds(pl.multiple_of(inner + own, HDIM), half)]
                base = v_ref[:, pl.ds(pl.multiple_of(own, HDIM), half)]
            else:
                columns = pl.ds(pl.multiple_of(place, HDIM), half)
                q = got_refs[i - 1][0, :, columns]
                key = got_refs[i - 1][1, :, columns]
                base = got_refs[i - 1][2, :, columns]
            q_out[k, rows] = q
            k_out[k, rows] = key
            v_out[k, rows] = (
                base.astype(F32) + jnp.dot(low[i], up, preferred_element_type=F32)
            ).astype(BF16)


def heads_kernel(scale, live_ref, text_ref, q_ref, k_ref, v_ref, *refs):
    out_refs = refs[2:]
    live = live_ref[...] != 0
    half = q_ref.shape[2]
    size = out_refs[0].shape[0]
    for h in range(half // HDIM):
        cols = slice(h * HDIM, (h + 1) * HDIM)
        vals = slice(half + h * HDIM, half + (h + 1) * HDIM)
        q = q_ref[0, :, cols]
        st = lax.dot_general(q, text_ref[:, cols], NT, preferred_element_type=F32) * scale
        si = lax.dot_general(q, k_ref[0, :, cols], NT, preferred_element_type=F32) * scale
        st = jnp.where(live, st, -jnp.inf)
        top = jnp.maximum(
            jnp.max(st, axis=1, keepdims=True), jnp.max(si, axis=1, keepdims=True)
        )
        wt = jnp.exp(st - top)
        wi = jnp.exp(si - top)
        total = jnp.sum(wt, axis=1, keepdims=True) + jnp.sum(wi, axis=1, keepdims=True)
        mixed = jnp.dot(
            wt.astype(BF16), text_ref[:, vals], preferred_element_type=F32
        ) + jnp.dot(wi.astype(BF16), v_ref[0, :, cols], preferred_element_type=F32)
        mixed = (mixed / total).astype(BF16)
        for i, out_ref in enumerate(out_refs):
            out_ref[:, cols] = mixed[i * size : (i + 1) * size]


def assemble_kernel(n_req, n_seq, *refs):
    out_ref = refs[-1]
    r, s = lax.axis_index("req"), lax.axis_index("seq")
    half = refs[0].shape[1]
    for k in range(n_req):
        for i in range(n_seq):
            start = ((s ^ i) * n_req + (r ^ k)) * half
            out_ref[:, pl.ds(pl.multiple_of(start, HDIM), half)] = refs[k * n_seq + i][...]


def per_device_heads(
    n_enc,
    n_req,
    n_seq,
    encoder_hidden,
    prompt_token_ids,
    context_weight,
    context_bias,
    modulation_shift,
    modulation_scale,
    key_value_weight,
    key_value_bias,
    request_prompt,
    adapter_of_request,
    adapter_down_maps,
    adapter_up_maps,
    image_stream_input,
    image_query_key,
    image_value_rows,
):
    e, r, s = lax.axis_index("enc"), lax.axis_index("req"), lax.axis_index("seq")
    model_width = context_weight.shape[1]
    features = context_bias.shape[0]
    tokens = encoder_hidden.shape[1]
    inner = key_value_weight.shape[1] // 2
    part = inner // n_seq
    half = part // n_req
    image_rows = image_query_key.shape[2]
    rank = adapter_up_maps.shape[1]
    qk, base, stream = image_query_key[0, 0], image_value_rows[0, 0], image_stream_input[0, 0]
    dma = pltpu.SemaphoreType.DMA
    stat = struct((8, tokens), F32)

    send, keep, sums = call(
        context_kernel,
        (
            struct((model_width // 2 + ROWS, tokens)),
            struct((model_width // 2, tokens), F32),
            stat,
        ),
        (encoder_hidden[0], context_weight, context_bias),
        [HBM] * 3,
        [
            pltpu.VMEM(encoder_hidden.shape[1:], BF16),
            pltpu.VMEM(context_weight.shape, BF16),
            pltpu.VMEM(context_bias.shape, BF16),
            dma((2 + n_enc,)),
        ],
        name="context",
    )
    got = swap(send, "req", n_req, 1)

    packed = [
        call(
            functools.partial(image_kernel, part, inner, k),
            struct((4, image_rows, part)),
            (qk, base, stream, keep),
            [ANY] * 4,
            [dma((4,))],
            name="image_pack",
        )
        for k in range(1, n_seq)
    ]
    image_got = [swap(packed[k - 1], "seq", n_seq, k) for k in range(1, n_seq)]
    weight = struct((features, 2 * half))
    weight_own, weight_core, weight_pair = call(
        functools.partial(weight_kernel, n_req, part, inner),
        (weight, weight, struct((2, features, 2 * half))),
        (key_value_weight, keep),
        [ANY] * 2,
        [dma((2 * n_req,))],
        name="weight_pack",
    )
    weight_core_got = swap(weight_core, "req", n_req, 1)

    send, keep, sums = call(
        functools.partial(halve_kernel, features),
        (
            struct((n_enc * features + ROWS, tokens)),
            struct((n_enc * features, tokens), F32),
            stat,
        ),
        (got, keep, sums),
        name="halve",
    )
    got = swap(send, "req", n_req, 2)
    keep, sums, *sends = call(
        functools.partial(scatter_kernel, features, 3),
        (struct((features, tokens), F32), stat)
        + tuple(struct((features + ROWS, tokens)) for _ in range(1, n_enc)),
        (got, keep, sums, weight_pair, packed[0], weight_core_got),
        [VMEM] * 3 + [ANY] * 3,
        name="scatter",
    )
    arrived = [swap(sends[k - 1], "enc", n_enc, k) for k in range(1, n_enc)]
    weight_pair = lax.optimization_barrier((weight_pair, keep))[0]
    weight_pair_got = swap(weight_pair, "req", n_req, 2)

    bias_columns = jnp.broadcast_to(context_bias.astype(F32)[:, None], (features, tokens))
    scale_columns = jnp.broadcast_to(
        1.0 + modulation_scale[0].astype(F32)[:, None], (features, tokens)
    )
    own = call(
        functools.partial(centre_kernel, model_width),
        struct((features + ROWS, tokens)),
        (
            request_prompt,
            adapter_of_request,
            keep,
            sums,
            bias_columns,
            scale_columns,
            modulation_shift,
            *arrived,
        ),
        [SMEM] * 2 + [VMEM] * (5 + len(arrived)),
        name="centre",
    )
    joined = call(
        join_kernel,
        struct((n_seq * (features + ROWS), tokens)),
        (own, swap(own, "seq", n_seq, 1)),
        name="join",
    )
    payloads = [joined] + [swap(joined, "req", n_req, k) for k in range(1, n_req)]
    weight_own_pair, weight_next = call(
        pass_on_kernel,
        (weight, weight),
        (weight_pair_got, joined),
        [VMEM, ANY],
        name="pass_on",
    )
    weights = (weight_own, weight_core_got, weight_own_pair, swap(weight_next, "req", n_req, 1))

    size = n_seq * tokens // n_enc
    step = 2 * half // HDIM * size + ROWS
    ids, keep, *sends = call(
        functools.partial(project_kernel, n_seq, n_req, n_enc),
        (struct((2 * n_req,), jnp.int32), struct((step, HDIM), F32))
        + tuple(struct((step, HDIM)) for _ in range(1, n_enc)),
        (image_got[0], *payloads, *weights),
        [ANY] + [VMEM] * (2 * n_req),
        scratch=[pltpu.VMEM((n_enc * step, HDIM), F32)],
        out_specs=(SMEM,) + (VMEM,) * n_enc,
        name="project",
    )
    arrived = [swap(sends[k - 1], "enc", n_enc, k) for k in range(1, n_enc)]

    maps = call(
        functools.partial(maps_kernel, part),
        struct((2 * rank, part)),
        (adapter_down_maps[0].T, adapter_up_maps[0], keep),
        [ANY] * 3,
        [dma((2,))],
        name="maps_pack",
    )
    maps_pair = swap(maps, "req", n_req, 2)

    text = call(
        functools.partial(finish_kernel, n_req, model_width),
        struct((size, 2 * half)),
        (maps_pair, keep, key_value_bias[None], *arrived),
        [ANY] + [VMEM] * (2 + len(arrived)),
        name="finish",
    )
    maps_mine, maps_core = call(
        select_kernel,
        (struct((2 * rank, part)), struct((2 * rank, part))),
        (ids, maps, maps_pair, text),
        [SMEM, VMEM, VMEM, ANY],
        name="select",
    )
    low, chosen_maps = call(
        functools.partial(lowrank_kernel, part),
        (struct((n_seq, image_rows, rank), F32), struct((rank, part))),
        (adapter_of_request, stream, maps_mine, swap(maps_core, "req", n_req, 1), image_got[0]),
        [SMEM] + [VMEM] * 4,
        name="lowrank",
    )
    arranged = struct((n_req, n_seq * image_rows, half))
    queries, image_keys, image_values = call(
        functools.partial(arrange_kernel, n_req, part, inner),
        (arranged, arranged, arranged),
        (low, swap(low, "seq", n_seq, 1), chosen_maps, qk, base, *image_got),
        name="arrange",
    )
    parts = [text] + [swap(text, "enc", n_enc, k) for k in range(1, n_enc)]
    rows = call(
        functools.partial(choose_kernel, n_seq, n_enc),
        tuple(struct((tokens, 2 * half)) for _ in range(n_req)),
        (ids, image_values, *parts),
        [SMEM, ANY] + [VMEM] * n_enc,
        name="choose",
    )
    rows = [rows[0]] + [swap(rows[k], "req", n_req, k) for k in range(1, n_req)]
    live = lax.dynamic_slice_in_dim(prompt_token_ids, request_prompt[0, 0], 1, 0)
    pieces = [None] * n_req
    last = (live, live)
    for k in range(n_req):
        block = pl.BlockSpec((1, n_seq * image_rows, half), lambda i, k=k: (k, 0, 0))
        whole = lambda shape: pl.BlockSpec(shape, lambda i: (0, 0))
        mixed = pl.pallas_call(
            functools.partial(heads_kernel, HDIM ** (-0.5)),
            grid=(1,),
            out_shape=[struct((image_rows, half)) for _ in range(n_seq)],
            in_specs=[whole((1, tokens)), whole((tokens, 2 * half)), block, block, block, ANY, ANY],
            out_specs=[whole((image_rows, half)) for _ in range(n_seq)],
            compiler_params=pltpu.CompilerParams(vmem_limit_bytes=16 * 1024 * 1024),
            name="heads",
        )(live, rows[k], queries, image_keys, image_values, *last)
        pieces[k] = [mixed[0], swap(mixed[1], "seq", n_seq, 1)]
        last = (mixed[0], pieces[k - 1][1] if k else live)
    result = call(
        functools.partial(assemble_kernel, n_req, n_seq),
        struct((image_rows, inner)),
        tuple(p for group in pieces for p in group),
        name="assemble",
    )
    return result[None, None]


def solution(mesh):
    sizes = mesh.shape
    n_enc, n_req, n_seq = sizes["enc"], sizes["req"], sizes["seq"]

    def run(*arrays):
        heads = arrays[6].shape[1] // (2 * HDIM)
        fits = n_seq == 2 and n_req == 4 and heads % (n_seq * n_req) == 0
        return (per_device_heads if fits else per_device)(n_enc, n_req, n_seq, *arrays)

    return jax.shard_map(
        run,
        mesh=mesh,
        in_specs=(
            P("seq", None, ("enc", "req")),
            P(),
            P(("enc", "req"), None),
            P(("enc", "req")),
            P("seq", ("enc", "req")),
            P("seq", ("enc", "req")),
            P(("enc", "req"), None),
            P(),
            P("enc", "req"),
            P("enc", "req"),
            P("req", None, None),
            P("req", None, None),
            P("enc", "req", "seq", None),
            P("enc", "req", "seq", None),
            P("enc", "req", "seq", None),
        ),
        out_specs=P("enc", "req", "seq", None),
        check_vma=False,
    )
```

```python
import functools

import jax
import jax.numpy as jnp
from jax import lax
from jax.experimental import pallas as pl
from jax.experimental.pallas import tpu as pltpu
from jax.sharding import PartitionSpec as P

HDIM = 128
ROWS = 16

epsilon_norm = 1e-06


def swap(block, axis, size, step):
    return lax.ppermute(block, axis, [(i, i ^ step) for i in range(size)])


def pick(array, index, dim):
    return lax.dynamic_index_in_dim(array, index, dim, keepdims=False)


def split_two(value):
    high = lax.reduce_precision(value, 8, 7)
    return high.astype(jnp.bfloat16), (value - high).astype(jnp.bfloat16)


def bits_of(size):
    return [1 << b for b in range(size.bit_length() - 1)]


def with_stat_rows(data, stat):
    high, low = split_two(stat)
    rows = jnp.concatenate(
        [high[None], low[None], jnp.zeros((ROWS - 2, stat.shape[0]), jnp.bfloat16)], axis=0
    )
    rows = jnp.broadcast_to(rows, data.shape[:-2] + rows.shape)
    return jnp.concatenate([data.astype(jnp.bfloat16), rows], axis=-2)


def attention_kernel(heads, inner, scale, mask_ref, q_ref, kt_ref, vt_ref, ki_ref, vi_ref, o_ref):
    live = mask_ref[...] != 0
    for h in range(heads):
        cols = slice(h * HDIM, (h + 1) * HDIM)
        q = q_ref[:, cols]
        dims = (((1,), (1,)), ((), ()))
        st = lax.dot_general(q, kt_ref[:, cols], dims, preferred_element_type=jnp.float32) * scale
        si = lax.dot_general(q, ki_ref[:, cols], dims, preferred_element_type=jnp.float32) * scale
        st = jnp.where(live, st, -jnp.inf)
        top = jnp.maximum(
            jnp.max(st, axis=1, keepdims=True), jnp.max(si, axis=1, keepdims=True)
        )
        wt = jnp.exp(st - top)
        wi = jnp.exp(si - top)
        total = jnp.sum(wt, axis=1, keepdims=True) + jnp.sum(wi, axis=1, keepdims=True)
        mixed = jnp.dot(
            wt.astype(jnp.bfloat16), vt_ref[:, cols], preferred_element_type=jnp.float32
        ) + jnp.dot(wi.astype(jnp.bfloat16), vi_ref[:, cols], preferred_element_type=jnp.float32)
        o_ref[:, cols] = (mixed / total).astype(o_ref.dtype)


def attention(queries, text_keys, text_values, image_keys, image_values, live):
    width = queries.shape[1]
    heads = width // HDIM
    rows = queries.shape[0]
    mask = jnp.broadcast_to(live.astype(jnp.int32)[None, :], (8, live.shape[0]))[:1]
    return pl.pallas_call(
        functools.partial(attention_kernel, heads, width, HDIM ** (-0.5)),
        out_shape=jax.ShapeDtypeStruct((rows, width), jnp.bfloat16),
        compiler_params=pltpu.CompilerParams(vmem_limit_bytes=48 * 1024 * 1024),
        name="attention",
    )(mask, queries, text_keys, text_values, image_keys, image_values)


def per_device(
    n_enc,
    n_req,
    n_seq,
    encoder_hidden,
    prompt_token_ids,
    context_weight,
    context_bias,
    modulation_shift,
    modulation_scale,
    key_value_weight,
    key_value_bias,
    request_prompt,
    adapter_of_request,
    adapter_down_maps,
    adapter_up_maps,
    image_stream_input,
    image_query_key,
    image_value_rows,
):
    f32, bf16 = jnp.float32, jnp.bfloat16
    e, r, s = lax.axis_index("enc"), lax.axis_index("req"), lax.axis_index("seq")
    req_bits = bits_of(n_req)
    model_width = context_weight.shape[1]
    features = context_bias.shape[0]
    tokens = encoder_hidden.shape[1]
    inner = key_value_weight.shape[1] // 2
    part = inner // n_seq

    def heads_of(array, share):
        return lax.dynamic_slice_in_dim(array, share * part, part, 1)

    qk = image_query_key[0, 0]
    sources = [qk[:, :inner], qk[:, inner:], image_value_rows[0, 0], image_stream_input[0, 0]]
    image_parts = [
        jnp.stack([heads_of(a, s ^ k) for a in sources]) for k in range(n_seq)
    ]
    image_parts = [image_parts[0]] + [
        swap(image_parts[k], "seq", n_seq, k) for k in range(1, n_seq)
    ]
    image_all = jnp.concatenate(image_parts, axis=1)
    queries, image_keys, base_values, stream = [image_all[i] for i in range(4)]

    partial_value = lax.dot_general(
        context_weight, encoder_hidden[0], (((0,), (1,)), ((), ())), preferred_element_type=f32
    )
    stat = jnp.sum(partial_value, axis=0) + jnp.sum(context_bias.astype(f32))
    acc = partial_value.reshape((n_enc,) + (2,) * len(req_bits) + (features, tokens))
    for i, bit in enumerate(req_bits):
        mine = (r // bit) % 2
        dim = len(req_bits) - i
        got = swap(with_stat_rows(pick(acc, 1 - mine, dim), stat), "req", n_req, bit).astype(f32)
        acc = pick(acc, mine, dim) + got[..., :features, :]
        got_stat = got.reshape((-1,) + got.shape[-2:])[0, features:]
        stat = stat + got_stat[0] + got_stat[1]
    arrived = [
        swap(with_stat_rows(pick(acc, e ^ k, 0), stat), "enc", n_enc, k).astype(f32)
        for k in range(1, n_enc)
    ]
    embedded = pick(acc, e, 0)
    for got in arrived:
        embedded = embedded + got[:features]
        stat = stat + got[features] + got[features + 1]
    embedded = embedded + context_bias.astype(f32)[:, None]
    centred = embedded - (stat / model_width)[None, :]
    squares = jnp.sum(centred * centred, axis=0)
    scaled = (1.0 + modulation_scale[0].astype(f32))[:, None] * centred

    own = with_stat_rows(scaled, squares)
    blocks = [own] + [swap(own, "seq", n_seq, k) for k in range(1, n_seq)]
    scaled_all = jnp.concatenate([b[:features] for b in blocks], axis=1)
    squares_all = jnp.concatenate(
        [b[features].astype(f32) + b[features + 1].astype(f32) for b in blocks]
    )
    weight_own = jnp.concatenate(
        [heads_of(key_value_weight[:, :inner], s), heads_of(key_value_weight[:, inner:], s)], axis=1
    )
    width = 2 * part
    projected = lax.dot_general(
        scaled_all, weight_own, (((0,), (0,)), ((), ())), preferred_element_type=f32
    )

    shift_part = jnp.dot(modulation_shift, key_value_weight, preferred_element_type=f32)
    for bit in req_bits:
        shift_part = shift_part + swap(shift_part, "req", n_req, bit)
    for bit in bits_of(n_enc):
        shift_part = shift_part + swap(shift_part, "enc", n_enc, bit)
    shift_part = shift_part + key_value_bias.astype(f32)[None]

    def columns_of(row, share):
        return jnp.concatenate(
            [heads_of(row[:, :inner], share), heads_of(row[:, inner:], share)], axis=1
        )

    shift_rows = jnp.concatenate(
        [columns_of(shift_part, s)]
        + [swap(columns_of(shift_part, s ^ k), "seq", n_seq, k) for k in range(1, n_seq)],
        axis=0,
    )

    halves = tokens // n_req // ROWS
    split = (n_seq,) + (2,) * len(req_bits) + (halves, ROWS)
    acc = projected.reshape(split + (width,))
    acc_stat = squares_all.reshape(split)

    def with_stat_columns(data, stat):
        high, low = split_two(stat)
        lane = lax.broadcasted_iota(jnp.int32, stat.shape + (HDIM,), stat.ndim)
        columns = jnp.where(
            lane == 0, high[..., None], jnp.where(lane == 1, low[..., None], jnp.zeros((), bf16))
        )
        return jnp.concatenate([data.astype(bf16), columns], axis=-1)

    for i, bit in enumerate(req_bits):
        mine = (r // bit) % 2
        dim = len(req_bits) - i
        got = swap(
            with_stat_columns(pick(acc, 1 - mine, dim), pick(acc_stat, 1 - mine, dim)),
            "req", n_req, bit,
        ).astype(f32)
        acc = pick(acc, mine, dim) + got[..., :width]
        acc_stat = pick(acc_stat, mine, dim) + got[..., width] + got[..., width + 1]
    acc = acc.reshape(n_enc, ROWS, width)
    acc_stat = acc_stat.reshape(n_enc, ROWS)
    arrived = [
        swap(with_stat_columns(pick(acc, e ^ k, 0), pick(acc_stat, e ^ k, 0)), "enc", n_enc, k)
        .astype(f32)
        for k in range(1, n_enc)
    ]
    rows = pick(acc, e, 0)
    row_squares = pick(acc_stat, e, 0)
    for got in arrived:
        rows = rows + got[:, :width]
        row_squares = row_squares + got[:, width] + got[:, width + 1]
    rows = rows * lax.rsqrt(row_squares / model_width + epsilon_norm)[:, None]
    rows = rows + pick(shift_rows, e // halves, 0)[None]
    keys = rows[:, :part].reshape(ROWS, part // HDIM, HDIM)
    keys = keys * lax.rsqrt(jnp.mean(keys * keys, axis=2, keepdims=True) + epsilon_norm)
    text = jnp.concatenate([keys.reshape(ROWS, part), rows[:, part:]], axis=1).astype(bf16)

    chosen = request_prompt[0, 0]
    relative = s ^ chosen
    by_enc = [text] + [swap(text, "enc", n_enc, k) for k in range(1, n_enc)]
    by_enc = jnp.stack(by_enc)
    by_enc = jnp.stack([pick(by_enc, k ^ e, 0) for k in range(n_enc)])
    held = by_enc.reshape(1, n_seq, halves, ROWS, width)
    first = req_bits[0]
    held = jnp.concatenate([held, swap(held, "req", n_req, first)], axis=0)
    groups = [pick(held, relative, 1)]
    for step in range(2, n_req, 2):
        wanted = swap(relative, "req", n_req, step)
        groups.append(swap(pick(held, wanted, 1), "req", n_req, step))
    text_rows = jnp.concatenate(groups, axis=0).reshape(-1, width)
    live = pick(prompt_token_ids, chosen, 0) != 0
    live = live.reshape(n_req, halves * ROWS)
    live = jnp.concatenate([pick(live, r ^ k, 0) for k in range(n_req)])

    down = lax.dynamic_slice_in_dim(adapter_down_maps[0], s * part, part, 0).T
    up = heads_of(adapter_up_maps[0], s)
    maps = jnp.concatenate([down, up], axis=0)[None]
    for bit in reversed(req_bits):
        maps = jnp.concatenate([maps, swap(maps, "req", n_req, bit)], axis=0)
    other = adapter_of_request[0, 0] ^ r
    index = 0
    for bit in req_bits:
        index = index * 2 + (other // bit) % 2
    chosen_maps = pick(maps, index, 0)
    rank = up.shape[0]
    lowrank = lax.dot_general(
        stream, chosen_maps[:rank], (((1,), (1,)), ((), ())), preferred_element_type=f32
    ).reshape(n_seq, -1, rank)
    for bit in bits_of(n_seq):
        got = swap(lowrank, "seq", n_seq, bit)
        lowrank = lowrank + jnp.stack([got[k ^ bit] for k in range(n_seq)])
    lowrank = lowrank.reshape(-1, rank).astype(bf16)
    image_values = (
        base_values.astype(f32) + jnp.dot(lowrank, chosen_maps[rank:], preferred_element_type=f32)
    ).astype(bf16)

    mixed = attention(
        queries, text_rows[:, :part], text_rows[:, part:], image_keys, image_values, live
    ).reshape(n_seq, -1, part)
    pieces = jnp.stack([mixed[0]] + [swap(mixed[k], "seq", n_seq, k) for k in range(1, n_seq)])
    result = jnp.concatenate([pick(pieces, s ^ k, 0) for k in range(n_seq)], axis=1)
    return result[None, None]


F32, BF16 = jnp.float32, jnp.bfloat16
ANY = pl.BlockSpec(memory_space=pl.ANY)
VMEM = pl.BlockSpec(memory_space=pltpu.VMEM)
SMEM = pl.BlockSpec(memory_space=pltpu.SMEM)
HBM = pl.BlockSpec(memory_space=pltpu.HBM)
NT = (((1,), (1,)), ((), ()))
TN = (((0,), (0,)), ((), ()))


def call(kernel, outs, ins, specs=None, scratch=(), name=None, out_specs=None, vmem=16):
    return pl.pallas_call(
        kernel,
        out_shape=outs,
        in_specs=specs if specs is not None else [VMEM] * len(ins),
        out_specs=out_specs if out_specs is not None else jax.tree.map(lambda _: VMEM, outs),
        scratch_shapes=list(scratch),
        compiler_params=pltpu.CompilerParams(vmem_limit_bytes=int(vmem * 1024 * 1024)),
        name=name,
    )(*ins)


def struct(shape, dtype=BF16):
    return jax.ShapeDtypeStruct(shape, dtype)


def at(index, size):
    return pl.ds(pl.multiple_of(index * size, size), size)


def stat_rows(stat):
    high = stat.astype(BF16).astype(F32)
    row = lax.broadcasted_iota(jnp.int32, (ROWS, stat.shape[1]), 0)
    return jnp.where(row == 0, high, jnp.where(row == 1, stat - high, 0.0)).astype(BF16)


def stat_of(rows):
    rows = rows.astype(F32)
    return rows[0:1] + rows[1:2]


def context_kernel(
    h_hbm, w_hbm, b_hbm, send_ref, keep_ref, stat_ref, h_ref, w_ref, b_ref, sems
):
    mine = lax.rem(lax.axis_index("req"), 2)
    features = b_ref.shape[0]
    pairs = w_ref.shape[1] // (2 * features)
    count = sems.shape[0] - 2
    chunk = w_ref.shape[1] // count
    copies = [pltpu.make_async_copy(h_hbm, h_ref, sems.at[0])]
    for i in range(count):
        columns = pl.ds(i * chunk, chunk)
        copies.append(
            pltpu.make_async_copy(w_hbm.at[:, columns], w_ref.at[:, columns], sems.at[i + 1])
        )
    copies.append(pltpu.make_async_copy(b_hbm, b_ref, sems.at[count + 1]))
    for copy in copies:
        copy.start()
    copies[0].wait()
    arrived = 0
    total = jnp.zeros((1, h_ref.shape[0]), F32)
    for p in range(pairs):
        while arrived * chunk < (p + 1) * 2 * features:
            arrived += 1
            copies[arrived].wait()
        product = jnp.dot(
            h_ref[...], w_ref[:, p * 2 * features : (p + 1) * 2 * features],
            preferred_element_type=F32,
        ).T
        total = total + jnp.sum(product, axis=0, keepdims=True)
        low, high = product[:features], product[features:]
        rows = slice(p * features, (p + 1) * features)
        keep_ref[rows] = jnp.where(mine == 0, low, high)
        send_ref[rows] = jnp.where(mine == 0, high, low).astype(BF16)
    copies[-1].wait()
    stat = total + jnp.sum(b_ref[...].astype(F32))
    send_ref[pairs * features :] = stat_rows(stat)
    stat_ref[...] = jnp.broadcast_to(stat, stat_ref.shape)


def halve_kernel(features, got_ref, keep_ref, stat_ref, send_ref, kept_ref, out_stat_ref):
    mine = lax.rem(lax.axis_index("req") // 2, 2)
    count = keep_ref.shape[0] // (2 * features)
    for i in range(count):
        rows = slice(i * features, (i + 1) * features)
        own, other = at(2 * i + mine, features), at(2 * i + 1 - mine, features)
        kept_ref[rows] = keep_ref[own] + got_ref[own].astype(F32)
        send_ref[rows] = (keep_ref[other] + got_ref[other].astype(F32)).astype(BF16)
    stat = stat_ref[0:1] + stat_of(got_ref[2 * count * features :])
    send_ref[count * features :] = stat_rows(stat)
    out_stat_ref[...] = jnp.broadcast_to(stat, out_stat_ref.shape)


def scatter_kernel(features, deps, got_ref, keep_ref, stat_ref, *refs):
    kept_ref, out_stat_ref, send_ref = refs[deps:]
    e = lax.axis_index("enc")
    count = keep_ref.shape[0] // features
    stat = stat_ref[0:1] + stat_of(got_ref[count * features :])
    for i in range(count):
        rows = slice(i * features, (i + 1) * features)
        total = keep_ref[rows] + got_ref[rows].astype(F32)
        send_ref[i, :features] = total.astype(BF16)
        send_ref[i, features:] = stat_rows(stat)
    own = at(e, features)
    kept_ref[...] = keep_ref[own] + got_ref[own].astype(F32)
    out_stat_ref[...] = jnp.broadcast_to(stat, out_stat_ref.shape)


def add_others(total, got_ref):
    e = lax.axis_index("enc")
    for i in range(got_ref.shape[0]):
        total = total + jnp.where(e == i, 0.0, got_ref[i].astype(F32))
    return total


def centre_kernel(width, prompt_ref, adapter_ref, keep_ref, stat_ref, bias_ref, scale_ref, shift_ref, *refs):
    got_ref, out_ref = refs
    features, tokens = keep_ref.shape
    others = add_others(0.0, got_ref)
    total = keep_ref[...] + bias_ref[...] + others[:features]
    stat = stat_ref[0:1] + stat_of(others[features:])
    centred = total - stat * (1.0 / width)
    out_ref[:features] = (scale_ref[...] * centred).astype(BF16)
    squares = jnp.sum(centred * centred, axis=0, keepdims=True)
    high = squares.astype(BF16).astype(F32)
    row = lax.broadcasted_iota(jnp.int32, (ROWS, tokens), 0)
    extra = jnp.where(row == 0, high, jnp.where(row == 1, squares - high, 0.0))
    for j in range(pl.cdiv(features, tokens)):
        piece = shift_ref[:, j * tokens : min((j + 1) * tokens, features)].astype(F32)
        gap = tokens - piece.shape[1]
        if gap:
            piece = jnp.concatenate([piece, jnp.zeros((1, gap), F32)], axis=1)
        extra = jnp.where(row == 2 + j, piece, extra)
    extra = jnp.where(row == ROWS - 1, prompt_ref[0, 0].astype(F32), extra)
    extra = jnp.where(row == ROWS - 2, adapter_ref[0, 0].astype(F32), extra)
    out_ref[features:] = extra.astype(BF16)


def pass_on_kernel(got_ref, dep_ref, own_ref, next_ref):
    own_ref[...] = got_ref[0]
    next_ref[...] = got_ref[1]


def join_kernel(own_ref, got_ref, out_ref):
    size = own_ref.shape[0]
    out_ref[:size] = own_ref[...]
    out_ref[size:] = got_ref[...]


def project_kernel(n_seq, n_req, n_enc, *refs):
    payload_refs = refs[:n_req]
    weight_refs = refs[n_req : 2 * n_req]
    prompts_ref, keep_ref = refs[2 * n_req : 2 * n_req + 2]
    send_ref, rows_ref = refs[-2:]
    features, width = weight_refs[0].shape
    tokens = payload_refs[0].shape[1]
    stride = features + ROWS
    total = None
    squares = [jnp.zeros((1, tokens), F32) for _ in range(n_seq)]
    for k in range(n_req):
        left = []
        shifts = []
        for p in range(n_seq):
            payload = payload_refs[k]
            left.append(payload[p * stride : p * stride + features].T)
            extra = payload[p * stride + features : (p + 1) * stride].astype(F32)
            squares[p] = squares[p] + extra[0:1] + extra[1:2]
            pieces = [extra[2 + j : 3 + j] for j in range(pl.cdiv(features, tokens))]
            shifts.append(jnp.concatenate(pieces, axis=1)[:, :features])
            if p == 0:
                prompts_ref[k] = jnp.max(extra[ROWS - 1 : ROWS]).astype(jnp.int32)
                prompts_ref[n_req + k] = jnp.max(extra[ROWS - 2 : ROWS - 1]).astype(jnp.int32)
        shifts.append(jnp.zeros((ROWS - n_seq, features), F32))
        left.append(jnp.concatenate(shifts, axis=0).astype(BF16))
        term = jnp.dot(
            jnp.concatenate(left, axis=0), weight_refs[k][...], preferred_element_type=F32
        )
        total = term if total is None else total + term
    size = n_seq * tokens // n_enc
    heads = width // HDIM
    step = heads * size + ROWS
    row = lax.broadcasted_iota(jnp.int32, (ROWS, HDIM), 0)
    for z in range(n_enc):
        p, first = divmod(z * size, tokens)
        shift = total[n_seq * tokens + p : n_seq * tokens + p + 1]
        square = squares[p][:, first : first + size]
        square = jnp.concatenate([square, jnp.zeros((1, HDIM - size), F32)], axis=1)
        high = square.astype(BF16).astype(F32)
        extra = jnp.where(
            row == 2 * heads, high, jnp.where(row == 2 * heads + 1, square - high, 0.0)
        )
        for h in range(heads):
            cols = slice(h * HDIM, (h + 1) * HDIM)
            rows_ref[z * step + h * size : z * step + (h + 1) * size] = total[
                z * size : (z + 1) * size, cols
            ]
            high = shift[:, cols].astype(BF16).astype(F32)
            extra = jnp.where(
                row == h, high, jnp.where(row == heads + h, shift[:, cols] - high, extra)
            )
        rows_ref[z * step + heads * size : (z + 1) * step] = extra
    e = lax.axis_index("enc")
    keep_ref[...] = rows_ref[at(e, step)]
    for z in range(n_enc):
        send_ref[z] = rows_ref[z * step : (z + 1) * step].astype(BF16)


def finish_kernel(n_req, model_width, dep_ref, keep_ref, bias_ref, *refs):
    got_ref, out_ref = refs
    r, s = lax.axis_index("req"), lax.axis_index("seq")
    size, width = out_ref.shape
    heads = width // HDIM
    half = width // 2
    inner = bias_ref.shape[1] // 2
    total = add_others(keep_ref[...], got_ref)
    extra = total[heads * size :]
    squares = extra[2 * heads : 2 * heads + 1] + extra[2 * heads + 1 : 2 * heads + 2]
    squares = jnp.broadcast_to(squares, (HDIM, HDIM)).T[:size]
    factor = lax.rsqrt(squares * (1.0 / model_width) + epsilon_norm)
    for h in range(heads):
        start = (h * HDIM // half) * inner + (s * n_req + r) * half + h * HDIM % half
        bias = bias_ref[:, pl.ds(pl.multiple_of(start, HDIM), HDIM)].astype(F32)
        shift = extra[h : h + 1] + extra[heads + h : heads + h + 1] + bias
        head = total[h * size : (h + 1) * size] * factor + shift
        if h * HDIM < half:
            head = head * lax.rsqrt(jnp.mean(head * head, axis=1, keepdims=True) + epsilon_norm)
        out_ref[:, h * HDIM : (h + 1) * HDIM] = head.astype(BF16)


def choose_kernel(n_seq, chosen_ref, dep_ref, part_ref, *out_refs):
    s = lax.axis_index("seq")
    halves = part_ref.shape[0] // n_seq
    size = part_ref.shape[1]
    for k, out_ref in enumerate(out_refs):
        prompt = s ^ chosen_ref[k]
        for h in range(halves):
            out_ref[h * size : (h + 1) * size] = part_ref[prompt * halves + h]


def weight_kernel(n_req, part, inner, w_ref, dep_ref, own_ref, core_ref, pair_ref, sems):
    r, s = lax.axis_index("req"), lax.axis_index("seq")
    half = part // n_req
    copies = []
    for k, out_ref in enumerate((own_ref, core_ref, pair_ref.at[0], pair_ref.at[1])):
        for side in range(2):
            columns = pl.ds(
                pl.multiple_of(side * inner + (s * n_req + (r ^ k)) * half, HDIM), half
            )
            copies.append(
                pltpu.make_async_copy(
                    w_ref.at[:, columns],
                    out_ref.at[:, pl.ds(side * half, half)],
                    sems.at[2 * k + side],
                )
            )
    for copy in copies:
        copy.start()
    for copy in copies:
        copy.wait()


def image_kernel(part, inner, step, qk_ref, v_ref, x_ref, dep_ref, out_ref, sems):
    start = (lax.axis_index("seq") ^ step) * part
    copies = []
    for i, (ref, base) in enumerate(((qk_ref, 0), (qk_ref, inner), (v_ref, 0), (x_ref, 0))):
        columns = pl.ds(pl.multiple_of(base + start, HDIM), part)
        copies.append(pltpu.make_async_copy(ref.at[:, columns], out_ref.at[i], sems.at[i]))
    for copy in copies:
        copy.start()
    for copy in copies:
        copy.wait()


def maps_kernel(part, down_ref, up_ref, dep_ref, out_ref, sems):
    rank = down_ref.shape[0]
    columns = pl.ds(pl.multiple_of(lax.axis_index("seq") * part, HDIM), part)
    copies = [
        pltpu.make_async_copy(down_ref.at[:, columns], out_ref.at[pl.ds(0, rank)], sems.at[0]),
        pltpu.make_async_copy(up_ref.at[:, columns], out_ref.at[pl.ds(rank, rank)], sems.at[1]),
    ]
    for copy in copies:
        copy.start()
    for copy in copies:
        copy.wait()


def select_kernel(ids_ref, own_ref, pair_ref, dep_ref, mine_ref, core_ref):
    r = lax.axis_index("req")
    for out_ref, adapter in ((mine_ref, ids_ref[4]), (core_ref, ids_ref[5])):
        other = lax.rem((adapter ^ r) // 2, 2)

        @pl.when(other == 0)
        def _():
            out_ref[...] = own_ref[...]

        @pl.when(other == 1)
        def _():
            out_ref[...] = pair_ref[...]


def lowrank_kernel(part, adapter_ref, x_ref, mine_ref, core_ref, got_ref, out_ref, chosen_ref):
    other = lax.rem(adapter_ref[0, 0] ^ lax.axis_index("req"), 2)
    rank = out_ref.shape[-1]
    for k, ref in enumerate((mine_ref, core_ref)):
        @pl.when(other == k)
        def _():
            chosen_ref[...] = ref[rank:]
            own = x_ref[:, pl.ds(pl.multiple_of(lax.axis_index("seq") * part, HDIM), part)]
            for i, rows in enumerate((own, got_ref[3])):
                out_ref[i] = lax.dot_general(
                    rows, ref[:rank], NT, preferred_element_type=F32
                )


def arrange_kernel(n_req, part, inner, low_ref, other_ref, maps_ref, qk_ref, v_ref, *refs):
    got_refs, (q_out, k_out, v_out) = refs[:-3], refs[-3:]
    r, s = lax.axis_index("req"), lax.axis_index("seq")
    half = part // n_req
    tokens = qk_ref.shape[0]
    low = [(low_ref[i] + other_ref[i ^ 1]).astype(BF16) for i in range(2)]
    for k in range(n_req):
        place = (r ^ k) * half
        up = maps_ref[:, pl.ds(pl.multiple_of(place, HDIM), half)]
        for i in range(len(got_refs) + 1):
            rows = slice(i * tokens, (i + 1) * tokens)
            if i == 0:
                own = s * part + place
                q = qk_ref[:, pl.ds(pl.multiple_of(own, HDIM), half)]
                key = qk_ref[:, pl.ds(pl.multiple_of(inner + own, HDIM), half)]
                base = v_ref[:, pl.ds(pl.multiple_of(own, HDIM), half)]
            else:
                columns = pl.ds(pl.multiple_of(place, HDIM), half)
                q = got_refs[i - 1][0, :, columns]
                key = got_refs[i - 1][1, :, columns]
                base = got_refs[i - 1][2, :, columns]
            q_out[k, rows] = q
            k_out[k, rows] = key
            v_out[k, rows] = (
                base.astype(F32) + jnp.dot(low[i], up, preferred_element_type=F32)
            ).astype(BF16)


def heads_kernel(scale, live_ref, text_ref, q_ref, k_ref, v_ref, *refs):
    out_refs = refs[2:]
    live = live_ref[...] != 0
    half = q_ref.shape[2]
    size = out_refs[0].shape[0]
    for h in range(half // HDIM):
        cols = slice(h * HDIM, (h + 1) * HDIM)
        vals = slice(half + h * HDIM, half + (h + 1) * HDIM)
        q = q_ref[0, :, cols]
        st = lax.dot_general(q, text_ref[:, cols], NT, preferred_element_type=F32) * scale
        si = lax.dot_general(q, k_ref[0, :, cols], NT, preferred_element_type=F32) * scale
        st = jnp.where(live, st, -jnp.inf)
        top = jnp.maximum(
            jnp.max(st, axis=1, keepdims=True), jnp.max(si, axis=1, keepdims=True)
        )
        wt = jnp.exp(st - top)
        wi = jnp.exp(si - top)
        total = jnp.sum(wt, axis=1, keepdims=True) + jnp.sum(wi, axis=1, keepdims=True)
        mixed = jnp.dot(
            wt.astype(BF16), text_ref[:, vals], preferred_element_type=F32
        ) + jnp.dot(wi.astype(BF16), v_ref[0, :, cols], preferred_element_type=F32)
        mixed = (mixed / total).astype(BF16)
        for i, out_ref in enumerate(out_refs):
            out_ref[:, cols] = mixed[i * size : (i + 1) * size]


def assemble_kernel(n_req, n_seq, *refs):
    out_ref = refs[-1]
    r, s = lax.axis_index("req"), lax.axis_index("seq")
    half = refs[0].shape[1]
    for k in range(n_req):
        for i in range(n_seq):
            start = ((s ^ i) * n_req + (r ^ k)) * half
            out_ref[:, pl.ds(pl.multiple_of(start, HDIM), half)] = refs[k * n_seq + i][...]


def per_device_heads(
    n_enc,
    n_req,
    n_seq,
    encoder_hidden,
    prompt_token_ids,
    context_weight,
    context_bias,
    modulation_shift,
    modulation_scale,
    key_value_weight,
    key_value_bias,
    request_prompt,
    adapter_of_request,
    adapter_down_maps,
    adapter_up_maps,
    image_stream_input,
    image_query_key,
    image_value_rows,
):
    e, r, s = lax.axis_index("enc"), lax.axis_index("req"), lax.axis_index("seq")
    model_width = context_weight.shape[1]
    features = context_bias.shape[0]
    tokens = encoder_hidden.shape[1]
    inner = key_value_weight.shape[1] // 2
    part = inner // n_seq
    half = part // n_req
    image_rows = image_query_key.shape[2]
    rank = adapter_up_maps.shape[1]
    qk, base, stream = image_query_key[0, 0], image_value_rows[0, 0], image_stream_input[0, 0]
    dma = pltpu.SemaphoreType.DMA
    stat = struct((8, tokens), F32)

    send, keep, sums = call(
        context_kernel,
        (
            struct((model_width // 2 + ROWS, tokens)),
            struct((model_width // 2, tokens), F32),
            stat,
        ),
        (encoder_hidden[0], context_weight, context_bias),
        [HBM] * 3,
        [
            pltpu.VMEM(encoder_hidden.shape[1:], BF16),
            pltpu.VMEM(context_weight.shape, BF16),
            pltpu.VMEM(context_bias.shape, BF16),
            dma((2 + n_enc,)),
        ],
        name="context",
        vmem=52.25,
    )
    got = swap(send, "req", n_req, 1)

    send, keep, sums = call(
        functools.partial(halve_kernel, features),
        (
            struct((n_enc * features + ROWS, tokens)),
            struct((n_enc * features, tokens), F32),
            stat,
        ),
        (got, keep, sums),
        name="halve",
    )
    got = swap(send, "req", n_req, 2)
    weight = struct((features, 2 * half))
    weight_own, weight_core, weight_pair = call(
        functools.partial(weight_kernel, n_req, part, inner),
        (weight, weight, struct((2, features, 2 * half))),
        (key_value_weight, keep),
        [ANY] * 2,
        [dma((2 * n_req,))],
        name="weight_pack",
    )
    weight_core_got = swap(weight_core, "req", n_req, 1)
    keep, sums, send = call(
        functools.partial(scatter_kernel, features, 2),
        (
            struct((features, tokens), F32),
            stat,
            struct((n_enc, features + ROWS, tokens)),
        ),
        (got, keep, sums, weight_pair, weight_core_got),
        [VMEM] * 3 + [ANY] * 2,
        name="scatter",
    )
    arrived = lax.all_to_all(send, "enc", 0, 0, tiled=True)
    weight_pair = lax.optimization_barrier((weight_pair, keep))[0]
    weight_pair_got = swap(weight_pair, "req", n_req, 2)

    bias_columns = jnp.broadcast_to(context_bias.astype(F32)[:, None], (features, tokens))
    scale_columns = jnp.broadcast_to(
        1.0 + modulation_scale[0].astype(F32)[:, None], (features, tokens)
    )
    own = call(
        functools.partial(centre_kernel, model_width),
        struct((features + ROWS, tokens)),
        (
            request_prompt,
            adapter_of_request,
            keep,
            sums,
            bias_columns,
            scale_columns,
            modulation_shift,
            arrived,
        ),
        [SMEM] * 2 + [VMEM] * 6,
        name="centre",
    )
    joined = call(
        join_kernel,
        struct((n_seq * (features + ROWS), tokens)),
        (own, swap(own, "seq", n_seq, 1)),
        name="join",
    )
    payloads = [joined] + [swap(joined, "req", n_req, k) for k in range(1, n_req)]
    packed = [
        call(
            functools.partial(image_kernel, part, inner, k),
            struct((4, image_rows, part)),
            (qk, base, stream, joined),
            [ANY] * 4,
            [dma((4,))],
            name="image_pack",
        )
        for k in range(1, n_seq)
    ]
    image_got = [swap(packed[k - 1], "seq", n_seq, k) for k in range(1, n_seq)]
    weight_own_pair, weight_next = call(
        pass_on_kernel,
        (weight, weight),
        (weight_pair_got, joined),
        [VMEM, ANY],
        name="pass_on",
    )
    weights = (weight_own, weight_core_got, weight_own_pair, swap(weight_next, "req", n_req, 1))

    size = n_seq * tokens // n_enc
    step = 2 * half // HDIM * size + ROWS
    ids, keep, send = call(
        functools.partial(project_kernel, n_seq, n_req, n_enc),
        (
            struct((2 * n_req,), jnp.int32),
            struct((step, HDIM), F32),
            struct((n_enc, step, HDIM)),
        ),
        (*payloads, *weights),
        scratch=[pltpu.VMEM((n_enc * step, HDIM), F32)],
        out_specs=(SMEM, VMEM, VMEM),
        name="project",
    )
    arrived = lax.all_to_all(send, "enc", 0, 0, tiled=True)

    maps = call(
        functools.partial(maps_kernel, part),
        struct((2 * rank, part)),
        (adapter_down_maps[0].T, adapter_up_maps[0], keep),
        [ANY] * 3,
        [dma((2,))],
        name="maps_pack",
    )
    maps_pair = swap(maps, "req", n_req, 2)

    text = call(
        functools.partial(finish_kernel, n_req, model_width),
        struct((size, 2 * half)),
        (maps_pair, keep, key_value_bias[None], arrived),
        [ANY] + [VMEM] * 3,
        name="finish",
    )
    maps_mine, maps_core = call(
        select_kernel,
        (struct((2 * rank, part)), struct((2 * rank, part))),
        (ids, maps, maps_pair, text),
        [SMEM, VMEM, VMEM, ANY],
        name="select",
    )
    low, chosen_maps = call(
        functools.partial(lowrank_kernel, part),
        (struct((n_seq, image_rows, rank), F32), struct((rank, part))),
        (adapter_of_request, stream, maps_mine, swap(maps_core, "req", n_req, 1), image_got[0]),
        [SMEM] + [VMEM] * 4,
        name="lowrank",
    )
    arranged = struct((n_req, n_seq * image_rows, half))
    queries, image_keys, image_values = call(
        functools.partial(arrange_kernel, n_req, part, inner),
        (arranged, arranged, arranged),
        (low, swap(low, "seq", n_seq, 1), chosen_maps, qk, base, *image_got),
        name="arrange",
    )
    parts = lax.all_gather(text, "enc", axis=0, tiled=False)
    rows = call(
        functools.partial(choose_kernel, n_seq),
        tuple(struct((tokens, 2 * half)) for _ in range(n_req)),
        (ids, image_values, parts),
        [SMEM, ANY, VMEM],
        name="choose",
    )
    rows = [rows[0]] + [swap(rows[k], "req", n_req, k) for k in range(1, n_req)]
    live = lax.dynamic_slice_in_dim(prompt_token_ids, request_prompt[0, 0], 1, 0)
    pieces = [None] * n_req
    last = (live, live)
    for k in range(n_req):
        block = pl.BlockSpec((1, n_seq * image_rows, half), lambda i, k=k: (k, 0, 0))
        whole = lambda shape: pl.BlockSpec(shape, lambda i: (0, 0))
        mixed = pl.pallas_call(
            functools.partial(heads_kernel, HDIM ** (-0.5)),
            grid=(1,),
            out_shape=[struct((image_rows, half)) for _ in range(n_seq)],
            in_specs=[whole((1, tokens)), whole((tokens, 2 * half)), block, block, block, ANY, ANY],
            out_specs=[whole((image_rows, half)) for _ in range(n_seq)],
            compiler_params=pltpu.CompilerParams(vmem_limit_bytes=16 * 1024 * 1024),
            name="heads",
        )(live, rows[k], queries, image_keys, image_values, *last)
        pieces[k] = [mixed[0], swap(mixed[1], "seq", n_seq, 1)]
        last = (mixed[0], pieces[k - 1][1] if k else live)
    result = call(
        functools.partial(assemble_kernel, n_req, n_seq),
        struct((image_rows, inner)),
        tuple(p for group in pieces for p in group),
        name="assemble",
    )
    return result[None, None]


def solution(mesh):
    sizes = mesh.shape
    n_enc, n_req, n_seq = sizes["enc"], sizes["req"], sizes["seq"]

    def run(*arrays):
        heads = arrays[6].shape[1] // (2 * HDIM)
        fits = n_seq == 2 and n_req == 4 and heads % (n_seq * n_req) == 0
        return (per_device_heads if fits else per_device)(n_enc, n_req, n_seq, *arrays)

    return jax.shard_map(
        run,
        mesh=mesh,
        in_specs=(
            P("seq", None, ("enc", "req")),
            P(),
            P(("enc", "req"), None),
            P(("enc", "req")),
            P("seq", ("enc", "req")),
            P("seq", ("enc", "req")),
            P(("enc", "req"), None),
            P(),
            P("enc", "req"),
            P("enc", "req"),
            P("req", None, None),
            P("req", None, None),
            P("enc", "req", "seq", None),
            P("enc", "req", "seq", None),
            P("enc", "req", "seq", None),
        ),
        out_specs=P("enc", "req", "seq", None),
        check_vma=False,
    )
```

```python
import functools

import jax
import jax.numpy as jnp
from jax import lax
from jax.experimental import pallas as pl
from jax.experimental.pallas import tpu as pltpu
from jax.sharding import PartitionSpec as P

HDIM = 128
ROWS = 16

epsilon_norm = 1e-06


def swap(block, axis, size, step):
    return lax.ppermute(block, axis, [(i, i ^ step) for i in range(size)])


def pick(array, index, dim):
    return lax.dynamic_index_in_dim(array, index, dim, keepdims=False)


def split_two(value):
    high = lax.reduce_precision(value, 8, 7)
    return high.astype(jnp.bfloat16), (value - high).astype(jnp.bfloat16)


def bits_of(size):
    return [1 << b for b in range(size.bit_length() - 1)]


def with_stat_rows(data, stat):
    high, low = split_two(stat)
    rows = jnp.concatenate(
        [high[None], low[None], jnp.zeros((ROWS - 2, stat.shape[0]), jnp.bfloat16)], axis=0
    )
    rows = jnp.broadcast_to(rows, data.shape[:-2] + rows.shape)
    return jnp.concatenate([data.astype(jnp.bfloat16), rows], axis=-2)


def attention_kernel(heads, inner, scale, mask_ref, q_ref, kt_ref, vt_ref, ki_ref, vi_ref, o_ref):
    live = mask_ref[...] != 0
    for h in range(heads):
        cols = slice(h * HDIM, (h + 1) * HDIM)
        q = q_ref[:, cols]
        dims = (((1,), (1,)), ((), ()))
        st = lax.dot_general(q, kt_ref[:, cols], dims, preferred_element_type=jnp.float32) * scale
        si = lax.dot_general(q, ki_ref[:, cols], dims, preferred_element_type=jnp.float32) * scale
        st = jnp.where(live, st, -jnp.inf)
        top = jnp.maximum(
            jnp.max(st, axis=1, keepdims=True), jnp.max(si, axis=1, keepdims=True)
        )
        wt = jnp.exp(st - top)
        wi = jnp.exp(si - top)
        total = jnp.sum(wt, axis=1, keepdims=True) + jnp.sum(wi, axis=1, keepdims=True)
        mixed = jnp.dot(
            wt.astype(jnp.bfloat16), vt_ref[:, cols], preferred_element_type=jnp.float32
        ) + jnp.dot(wi.astype(jnp.bfloat16), vi_ref[:, cols], preferred_element_type=jnp.float32)
        o_ref[:, cols] = (mixed / total).astype(o_ref.dtype)


def attention(queries, text_keys, text_values, image_keys, image_values, live):
    width = queries.shape[1]
    heads = width // HDIM
    rows = queries.shape[0]
    mask = jnp.broadcast_to(live.astype(jnp.int32)[None, :], (8, live.shape[0]))[:1]
    return pl.pallas_call(
        functools.partial(attention_kernel, heads, width, HDIM ** (-0.5)),
        out_shape=jax.ShapeDtypeStruct((rows, width), jnp.bfloat16),
        compiler_params=pltpu.CompilerParams(vmem_limit_bytes=48 * 1024 * 1024),
        name="attention",
    )(mask, queries, text_keys, text_values, image_keys, image_values)


def per_device(
    n_enc,
    n_req,
    n_seq,
    encoder_hidden,
    prompt_token_ids,
    context_weight,
    context_bias,
    modulation_shift,
    modulation_scale,
    key_value_weight,
    key_value_bias,
    request_prompt,
    adapter_of_request,
    adapter_down_maps,
    adapter_up_maps,
    image_stream_input,
    image_query_key,
    image_value_rows,
):
    f32, bf16 = jnp.float32, jnp.bfloat16
    e, r, s = lax.axis_index("enc"), lax.axis_index("req"), lax.axis_index("seq")
    req_bits = bits_of(n_req)
    model_width = context_weight.shape[1]
    features = context_bias.shape[0]
    tokens = encoder_hidden.shape[1]
    inner = key_value_weight.shape[1] // 2
    part = inner // n_seq

    def heads_of(array, share):
        return lax.dynamic_slice_in_dim(array, share * part, part, 1)

    qk = image_query_key[0, 0]
    sources = [qk[:, :inner], qk[:, inner:], image_value_rows[0, 0], image_stream_input[0, 0]]
    image_parts = [
        jnp.stack([heads_of(a, s ^ k) for a in sources]) for k in range(n_seq)
    ]
    image_parts = [image_parts[0]] + [
        swap(image_parts[k], "seq", n_seq, k) for k in range(1, n_seq)
    ]
    image_all = jnp.concatenate(image_parts, axis=1)
    queries, image_keys, base_values, stream = [image_all[i] for i in range(4)]

    partial_value = lax.dot_general(
        context_weight, encoder_hidden[0], (((0,), (1,)), ((), ())), preferred_element_type=f32
    )
    stat = jnp.sum(partial_value, axis=0) + jnp.sum(context_bias.astype(f32))
    acc = partial_value.reshape((n_enc,) + (2,) * len(req_bits) + (features, tokens))
    for i, bit in enumerate(req_bits):
        mine = (r // bit) % 2
        dim = len(req_bits) - i
        got = swap(with_stat_rows(pick(acc, 1 - mine, dim), stat), "req", n_req, bit).astype(f32)
        acc = pick(acc, mine, dim) + got[..., :features, :]
        got_stat = got.reshape((-1,) + got.shape[-2:])[0, features:]
        stat = stat + got_stat[0] + got_stat[1]
    arrived = [
        swap(with_stat_rows(pick(acc, e ^ k, 0), stat), "enc", n_enc, k).astype(f32)
        for k in range(1, n_enc)
    ]
    embedded = pick(acc, e, 0)
    for got in arrived:
        embedded = embedded + got[:features]
        stat = stat + got[features] + got[features + 1]
    embedded = embedded + context_bias.astype(f32)[:, None]
    centred = embedded - (stat / model_width)[None, :]
    squares = jnp.sum(centred * centred, axis=0)
    scaled = (1.0 + modulation_scale[0].astype(f32))[:, None] * centred

    own = with_stat_rows(scaled, squares)
    blocks = [own] + [swap(own, "seq", n_seq, k) for k in range(1, n_seq)]
    scaled_all = jnp.concatenate([b[:features] for b in blocks], axis=1)
    squares_all = jnp.concatenate(
        [b[features].astype(f32) + b[features + 1].astype(f32) for b in blocks]
    )
    weight_own = jnp.concatenate(
        [heads_of(key_value_weight[:, :inner], s), heads_of(key_value_weight[:, inner:], s)], axis=1
    )
    width = 2 * part
    projected = lax.dot_general(
        scaled_all, weight_own, (((0,), (0,)), ((), ())), preferred_element_type=f32
    )

    shift_part = jnp.dot(modulation_shift, key_value_weight, preferred_element_type=f32)
    for bit in req_bits:
        shift_part = shift_part + swap(shift_part, "req", n_req, bit)
    for bit in bits_of(n_enc):
        shift_part = shift_part + swap(shift_part, "enc", n_enc, bit)
    shift_part = shift_part + key_value_bias.astype(f32)[None]

    def columns_of(row, share):
        return jnp.concatenate(
            [heads_of(row[:, :inner], share), heads_of(row[:, inner:], share)], axis=1
        )

    shift_rows = jnp.concatenate(
        [columns_of(shift_part, s)]
        + [swap(columns_of(shift_part, s ^ k), "seq", n_seq, k) for k in range(1, n_seq)],
        axis=0,
    )

    halves = tokens // n_req // ROWS
    split = (n_seq,) + (2,) * len(req_bits) + (halves, ROWS)
    acc = projected.reshape(split + (width,))
    acc_stat = squares_all.reshape(split)

    def with_stat_columns(data, stat):
        high, low = split_two(stat)
        lane = lax.broadcasted_iota(jnp.int32, stat.shape + (HDIM,), stat.ndim)
        columns = jnp.where(
            lane == 0, high[..., None], jnp.where(lane == 1, low[..., None], jnp.zeros((), bf16))
        )
        return jnp.concatenate([data.astype(bf16), columns], axis=-1)

    for i, bit in enumerate(req_bits):
        mine = (r // bit) % 2
        dim = len(req_bits) - i
        got = swap(
            with_stat_columns(pick(acc, 1 - mine, dim), pick(acc_stat, 1 - mine, dim)),
            "req", n_req, bit,
        ).astype(f32)
        acc = pick(acc, mine, dim) + got[..., :width]
        acc_stat = pick(acc_stat, mine, dim) + got[..., width] + got[..., width + 1]
    acc = acc.reshape(n_enc, ROWS, width)
    acc_stat = acc_stat.reshape(n_enc, ROWS)
    arrived = [
        swap(with_stat_columns(pick(acc, e ^ k, 0), pick(acc_stat, e ^ k, 0)), "enc", n_enc, k)
        .astype(f32)
        for k in range(1, n_enc)
    ]
    rows = pick(acc, e, 0)
    row_squares = pick(acc_stat, e, 0)
    for got in arrived:
        rows = rows + got[:, :width]
        row_squares = row_squares + got[:, width] + got[:, width + 1]
    rows = rows * lax.rsqrt(row_squares / model_width + epsilon_norm)[:, None]
    rows = rows + pick(shift_rows, e // halves, 0)[None]
    keys = rows[:, :part].reshape(ROWS, part // HDIM, HDIM)
    keys = keys * lax.rsqrt(jnp.mean(keys * keys, axis=2, keepdims=True) + epsilon_norm)
    text = jnp.concatenate([keys.reshape(ROWS, part), rows[:, part:]], axis=1).astype(bf16)

    chosen = request_prompt[0, 0]
    relative = s ^ chosen
    by_enc = [text] + [swap(text, "enc", n_enc, k) for k in range(1, n_enc)]
    by_enc = jnp.stack(by_enc)
    by_enc = jnp.stack([pick(by_enc, k ^ e, 0) for k in range(n_enc)])
    held = by_enc.reshape(1, n_seq, halves, ROWS, width)
    first = req_bits[0]
    held = jnp.concatenate([held, swap(held, "req", n_req, first)], axis=0)
    groups = [pick(held, relative, 1)]
    for step in range(2, n_req, 2):
        wanted = swap(relative, "req", n_req, step)
        groups.append(swap(pick(held, wanted, 1), "req", n_req, step))
    text_rows = jnp.concatenate(groups, axis=0).reshape(-1, width)
    live = pick(prompt_token_ids, chosen, 0) != 0
    live = live.reshape(n_req, halves * ROWS)
    live = jnp.concatenate([pick(live, r ^ k, 0) for k in range(n_req)])

    down = lax.dynamic_slice_in_dim(adapter_down_maps[0], s * part, part, 0).T
    up = heads_of(adapter_up_maps[0], s)
    maps = jnp.concatenate([down, up], axis=0)[None]
    for bit in reversed(req_bits):
        maps = jnp.concatenate([maps, swap(maps, "req", n_req, bit)], axis=0)
    other = adapter_of_request[0, 0] ^ r
    index = 0
    for bit in req_bits:
        index = index * 2 + (other // bit) % 2
    chosen_maps = pick(maps, index, 0)
    rank = up.shape[0]
    lowrank = lax.dot_general(
        stream, chosen_maps[:rank], (((1,), (1,)), ((), ())), preferred_element_type=f32
    ).reshape(n_seq, -1, rank)
    for bit in bits_of(n_seq):
        got = swap(lowrank, "seq", n_seq, bit)
        lowrank = lowrank + jnp.stack([got[k ^ bit] for k in range(n_seq)])
    lowrank = lowrank.reshape(-1, rank).astype(bf16)
    image_values = (
        base_values.astype(f32) + jnp.dot(lowrank, chosen_maps[rank:], preferred_element_type=f32)
    ).astype(bf16)

    mixed = attention(
        queries, text_rows[:, :part], text_rows[:, part:], image_keys, image_values, live
    ).reshape(n_seq, -1, part)
    pieces = jnp.stack([mixed[0]] + [swap(mixed[k], "seq", n_seq, k) for k in range(1, n_seq)])
    result = jnp.concatenate([pick(pieces, s ^ k, 0) for k in range(n_seq)], axis=1)
    return result[None, None]


F32, BF16 = jnp.float32, jnp.bfloat16
ANY = pl.BlockSpec(memory_space=pl.ANY)
VMEM = pl.BlockSpec(memory_space=pltpu.VMEM)
SMEM = pl.BlockSpec(memory_space=pltpu.SMEM)
HBM = pl.BlockSpec(memory_space=pltpu.HBM)
NT = (((1,), (1,)), ((), ()))
TN = (((0,), (0,)), ((), ()))


def partners(send, axis, size):
    return {k: swap(send(k), axis, size, k) for k in far_first(size)}


def far_first(size):
    return [k for k in range(2, size)] + [1]


def call(kernel, outs, ins, specs=None, scratch=(), name=None, out_specs=None, vmem=16):
    return pl.pallas_call(
        kernel,
        out_shape=outs,
        in_specs=specs if specs is not None else [VMEM] * len(ins),
        out_specs=out_specs if out_specs is not None else jax.tree.map(lambda _: VMEM, outs),
        scratch_shapes=list(scratch),
        compiler_params=pltpu.CompilerParams(vmem_limit_bytes=int(vmem * 1024 * 1024)),
        name=name,
    )(*ins)


def struct(shape, dtype=BF16):
    return jax.ShapeDtypeStruct(shape, dtype)


def at(index, size):
    return pl.ds(pl.multiple_of(index * size, size), size)


def stat_rows(stat):
    high = stat.astype(BF16).astype(F32)
    row = lax.broadcasted_iota(jnp.int32, (ROWS, stat.shape[1]), 0)
    return jnp.where(row == 0, high, jnp.where(row == 1, stat - high, 0.0)).astype(BF16)


def stat_of(rows):
    rows = rows.astype(F32)
    return rows[0:1] + rows[1:2]


def context_kernel(
    h_hbm, w_hbm, b_hbm, send_ref, keep_ref, stat_ref, h_ref, w_ref, b_ref, sems
):
    mine = lax.rem(lax.axis_index("req"), 2)
    features = b_ref.shape[0]
    pairs = w_ref.shape[1] // (2 * features)
    count = sems.shape[0] - 2
    chunk = w_ref.shape[1] // count
    copies = [pltpu.make_async_copy(h_hbm, h_ref, sems.at[0])]
    for i in range(count):
        columns = pl.ds(i * chunk, chunk)
        copies.append(
            pltpu.make_async_copy(w_hbm.at[:, columns], w_ref.at[:, columns], sems.at[i + 1])
        )
    copies.append(pltpu.make_async_copy(b_hbm, b_ref, sems.at[count + 1]))
    for copy in copies:
        copy.start()
    copies[0].wait()
    arrived = 0
    total = jnp.zeros((1, h_ref.shape[0]), F32)
    for p in range(pairs):
        while arrived * chunk < (p + 1) * 2 * features:
            arrived += 1
            copies[arrived].wait()
        product = jnp.dot(
            h_ref[...], w_ref[:, p * 2 * features : (p + 1) * 2 * features],
            preferred_element_type=F32,
        ).T
        total = total + jnp.sum(product, axis=0, keepdims=True)
        low, high = product[:features], product[features:]
        rows = slice(p * features, (p + 1) * features)
        keep_ref[rows] = jnp.where(mine == 0, low, high)
        send_ref[rows] = jnp.where(mine == 0, high, low).astype(BF16)
    copies[-1].wait()
    stat = total + jnp.sum(b_ref[...].astype(F32))
    send_ref[pairs * features :] = stat_rows(stat)
    stat_ref[...] = jnp.broadcast_to(stat, stat_ref.shape)


def halve_kernel(features, got_ref, keep_ref, stat_ref, send_ref, kept_ref, out_stat_ref):
    mine = lax.rem(lax.axis_index("req") // 2, 2)
    count = keep_ref.shape[0] // (2 * features)
    for i in range(count):
        rows = slice(i * features, (i + 1) * features)
        own, other = at(2 * i + mine, features), at(2 * i + 1 - mine, features)
        kept_ref[rows] = keep_ref[own] + got_ref[own].astype(F32)
        send_ref[rows] = (keep_ref[other] + got_ref[other].astype(F32)).astype(BF16)
    stat = stat_ref[0:1] + stat_of(got_ref[2 * count * features :])
    send_ref[count * features :] = stat_rows(stat)
    out_stat_ref[...] = jnp.broadcast_to(stat, out_stat_ref.shape)


def scatter_kernel(features, deps, got_ref, keep_ref, stat_ref, *refs):
    kept_ref, out_stat_ref, *send_refs = refs[deps:]
    e = lax.axis_index("enc")
    count = keep_ref.shape[0] // features
    stat = stat_ref[0:1] + stat_of(got_ref[count * features :])
    own = at(e, features)
    for k, send_ref in enumerate(send_refs):
        other = at(e ^ (k + 1), features)
        send_ref[:features] = (keep_ref[other] + got_ref[other].astype(F32)).astype(BF16)
        send_ref[features:] = stat_rows(stat)
    kept_ref[...] = keep_ref[own] + got_ref[own].astype(F32)
    out_stat_ref[...] = jnp.broadcast_to(stat, out_stat_ref.shape)


def centre_kernel(width, prompt_ref, adapter_ref, keep_ref, stat_ref, bias_ref, scale_ref, shift_ref, *refs):
    got_refs, out_ref = refs[:-1], refs[-1]
    features, tokens = keep_ref.shape
    total = keep_ref[...] + bias_ref[...]
    stat = stat_ref[0:1]
    for got_ref in got_refs:
        total = total + got_ref[:features].astype(F32)
        stat = stat + stat_of(got_ref[features:])
    centred = total - stat * (1.0 / width)
    out_ref[:features] = (scale_ref[...] * centred).astype(BF16)
    squares = jnp.sum(centred * centred, axis=0, keepdims=True)
    high = squares.astype(BF16).astype(F32)
    row = lax.broadcasted_iota(jnp.int32, (ROWS, tokens), 0)
    extra = jnp.where(row == 0, high, jnp.where(row == 1, squares - high, 0.0))
    for j in range(pl.cdiv(features, tokens)):
        piece = shift_ref[:, j * tokens : min((j + 1) * tokens, features)].astype(F32)
        gap = tokens - piece.shape[1]
        if gap:
            piece = jnp.concatenate([piece, jnp.zeros((1, gap), F32)], axis=1)
        extra = jnp.where(row == 2 + j, piece, extra)
    extra = jnp.where(row == ROWS - 1, prompt_ref[0, 0].astype(F32), extra)
    extra = jnp.where(row == ROWS - 2, adapter_ref[0, 0].astype(F32), extra)
    out_ref[features:] = extra.astype(BF16)


def pass_on_kernel(core_ref, got_ref, dep_ref, own_ref, next_ref):
    own_ref[...] = got_ref[0]
    next_ref[0] = core_ref[...]
    next_ref[1] = got_ref[1]


def join_kernel(own_ref, got_ref, dep_ref, out_ref):
    size = own_ref.shape[0]
    out_ref[:size] = own_ref[...]
    out_ref[size:] = got_ref[...]


def project_kernel(n_seq, n_req, n_enc, own_ref, pair_ref, next_ref, *refs):
    payload_refs = dict(zip([0] + far_first(n_req), refs))
    weight_refs = (own_ref, next_ref.at[0], pair_ref, next_ref.at[1])
    prompts_ref, keep_ref = refs[n_req : n_req + 2]
    send_refs = refs[n_req + 2 : -1]
    rows_ref = refs[-1]
    features, width = weight_refs[0].shape
    tokens = payload_refs[0].shape[1]
    stride = features + ROWS
    total = None
    squares = [jnp.zeros((1, tokens), F32) for _ in range(n_seq)]
    for k in range(n_req):
        left = []
        shifts = []
        for p in range(n_seq):
            payload = payload_refs[k]
            left.append(payload[p * stride : p * stride + features].T)
            extra = payload[p * stride + features : (p + 1) * stride].astype(F32)
            squares[p] = squares[p] + extra[0:1] + extra[1:2]
            pieces = [extra[2 + j : 3 + j] for j in range(pl.cdiv(features, tokens))]
            shifts.append(jnp.concatenate(pieces, axis=1)[:, :features])
            if p == 0:
                prompts_ref[k] = jnp.max(extra[ROWS - 1 : ROWS]).astype(jnp.int32)
                prompts_ref[n_req + k] = jnp.max(extra[ROWS - 2 : ROWS - 1]).astype(jnp.int32)
        shifts.append(jnp.zeros((ROWS - n_seq, features), F32))
        left.append(jnp.concatenate(shifts, axis=0).astype(BF16))
        term = jnp.dot(
            jnp.concatenate(left, axis=0), weight_refs[k][...], preferred_element_type=F32
        )
        total = term if total is None else total + term
    size = n_seq * tokens // n_enc
    heads = width // HDIM
    step = heads * size + ROWS
    row = lax.broadcasted_iota(jnp.int32, (ROWS, HDIM), 0)
    for z in range(n_enc):
        p, first = divmod(z * size, tokens)
        shift = total[n_seq * tokens + p : n_seq * tokens + p + 1]
        square = squares[p][:, first : first + size]
        square = jnp.concatenate([square, jnp.zeros((1, HDIM - size), F32)], axis=1)
        high = square.astype(BF16).astype(F32)
        extra = jnp.where(
            row == 2 * heads, high, jnp.where(row == 2 * heads + 1, square - high, 0.0)
        )
        for h in range(heads):
            cols = slice(h * HDIM, (h + 1) * HDIM)
            rows_ref[z * step + h * size : z * step + (h + 1) * size] = total[
                z * size : (z + 1) * size, cols
            ]
            high = shift[:, cols].astype(BF16).astype(F32)
            extra = jnp.where(
                row == h, high, jnp.where(row == heads + h, shift[:, cols] - high, extra)
            )
        rows_ref[z * step + heads * size : (z + 1) * step] = extra
    e = lax.axis_index("enc")
    keep_ref[...] = rows_ref[at(e, step)]
    for k, send_ref in enumerate(send_refs):
        send_ref[...] = rows_ref[at(e ^ (k + 1), step)].astype(BF16)


def finish_kernel(n_req, model_width, dep_ref, image_ref, keep_ref, bias_ref, *refs):
    got_refs, out_ref = refs[:-1], refs[-1]
    r, s = lax.axis_index("req"), lax.axis_index("seq")
    size, width = out_ref.shape
    heads = width // HDIM
    half = width // 2
    inner = bias_ref.shape[1] // 2
    total = keep_ref[...]
    for got_ref in got_refs:
        total = total + got_ref[...].astype(F32)
    extra = total[heads * size :]
    squares = extra[2 * heads : 2 * heads + 1] + extra[2 * heads + 1 : 2 * heads + 2]
    squares = jnp.broadcast_to(squares, (HDIM, HDIM)).T[:size]
    factor = lax.rsqrt(squares * (1.0 / model_width) + epsilon_norm)
    for h in range(heads):
        start = (h * HDIM // half) * inner + (s * n_req + r) * half + h * HDIM % half
        bias = bias_ref[:, pl.ds(pl.multiple_of(start, HDIM), HDIM)].astype(F32)
        shift = extra[h : h + 1] + extra[heads + h : heads + h + 1] + bias
        head = total[h * size : (h + 1) * size] * factor + shift
        if h * HDIM < half:
            head = head * lax.rsqrt(jnp.mean(head * head, axis=1, keepdims=True) + epsilon_norm)
        out_ref[:, h * HDIM : (h + 1) * HDIM] = head.astype(BF16)


def choose_kernel(n_seq, n_enc, chosen_ref, dep_ref, *refs):
    part_refs, out_refs = dict(zip([0] + far_first(n_enc), refs)), refs[n_enc:]
    e, r, s = lax.axis_index("enc"), lax.axis_index("req"), lax.axis_index("seq")
    halves = n_enc // n_seq
    size = part_refs[0].shape[0]
    for k, out_ref in enumerate(out_refs):
        prompt = s ^ chosen_ref[k]
        for h in range(halves):
            place = e ^ (prompt * halves + h)
            for j in range(n_enc):
                @pl.when(place == j)
                def _():
                    out_ref[h * size : (h + 1) * size] = part_refs[j][...]


def weight_kernel(n_req, part, inner, w_ref, dep_ref, own_ref, core_ref, pair_ref, sems):
    r, s = lax.axis_index("req"), lax.axis_index("seq")
    half = part // n_req
    copies = []
    for k, out_ref in enumerate((own_ref, core_ref, pair_ref.at[0], pair_ref.at[1])):
        for side in range(2):
            columns = pl.ds(
                pl.multiple_of(side * inner + (s * n_req + (r ^ k)) * half, HDIM), half
            )
            copies.append(
                pltpu.make_async_copy(
                    w_ref.at[:, columns],
                    out_ref.at[:, pl.ds(side * half, half)],
                    sems.at[2 * k + side],
                )
            )
    for copy in copies:
        copy.start()
    for copy in copies:
        copy.wait()


def image_kernel(part, inner, step, qk_ref, v_ref, x_ref, dep_ref, out_ref, sems):
    start = (lax.axis_index("seq") ^ step) * part
    copies = []
    for i, (ref, base) in enumerate(((qk_ref, 0), (qk_ref, inner), (v_ref, 0), (x_ref, 0))):
        columns = pl.ds(pl.multiple_of(base + start, HDIM), part)
        copies.append(pltpu.make_async_copy(ref.at[:, columns], out_ref.at[i], sems.at[i]))
    for copy in copies:
        copy.start()
    for copy in copies:
        copy.wait()


def maps_kernel(part, down_ref, up_ref, dep_ref, out_ref, sems):
    rank = down_ref.shape[0]
    columns = pl.ds(pl.multiple_of(lax.axis_index("seq") * part, HDIM), part)
    copies = [
        pltpu.make_async_copy(down_ref.at[:, columns], out_ref.at[pl.ds(0, rank)], sems.at[0]),
        pltpu.make_async_copy(up_ref.at[:, columns], out_ref.at[pl.ds(rank, rank)], sems.at[1]),
    ]
    for copy in copies:
        copy.start()
    for copy in copies:
        copy.wait()


def select_kernel(ids_ref, own_ref, pair_ref, dep_ref, core_ref):
    other = lax.rem((ids_ref[5] ^ lax.axis_index("req")) // 2, 2)
    for k, ref in enumerate((own_ref, pair_ref)):
        @pl.when(other == k)
        def _():
            core_ref[...] = ref[...]


def lowrank_kernel(part, adapter_ref, x_ref, got_ref, *refs):
    map_refs, (out_ref, chosen_ref) = refs[:3], refs[3:]
    other = adapter_ref[0, 0] ^ lax.axis_index("req")
    place = jnp.where(lax.rem(other, 2) == 1, 2, other // 2)
    rank = out_ref.shape[-1]
    for k, ref in enumerate(map_refs):
        @pl.when(place == k)
        def _():
            chosen_ref[...] = ref[rank:]
            own = x_ref[:, pl.ds(pl.multiple_of(lax.axis_index("seq") * part, HDIM), part)]
            for i, rows in enumerate((own, got_ref[3])):
                out_ref[i] = lax.dot_general(
                    rows, ref[:rank], NT, preferred_element_type=F32
                )


def arrange_kernel(n_req, part, inner, low_ref, other_ref, maps_ref, qk_ref, v_ref, *refs):
    got_refs, (q_out, k_out, v_out) = refs[:-3], refs[-3:]
    r, s = lax.axis_index("req"), lax.axis_index("seq")
    half = part // n_req
    tokens = qk_ref.shape[0]
    low = [(low_ref[i] + other_ref[i ^ 1]).astype(BF16) for i in range(2)]
    for k in range(n_req):
        place = (r ^ k) * half
        up = maps_ref[:, pl.ds(pl.multiple_of(place, HDIM), half)]
        for i in range(len(got_refs) + 1):
            rows = slice(i * tokens, (i + 1) * tokens)
            if i == 0:
                own = s * part + place
                q = qk_ref[:, pl.ds(pl.multiple_of(own, HDIM), half)]
                key = qk_ref[:, pl.ds(pl.multiple_of(inner + own, HDIM), half)]
                base = v_ref[:, pl.ds(pl.multiple_of(own, HDIM), half)]
            else:
                columns = pl.ds(pl.multiple_of(place, HDIM), half)
                q = got_refs[i - 1][0, :, columns]
                key = got_refs[i - 1][1, :, columns]
                base = got_refs[i - 1][2, :, columns]
            q_out[k, rows] = q
            k_out[k, rows] = key
            v_out[k, rows] = (
                base.astype(F32) + jnp.dot(low[i], up, preferred_element_type=F32)
            ).astype(BF16)


def heads_kernel(scale, live_ref, text_ref, q_ref, k_ref, v_ref, *refs):
    out_refs = refs[2:]
    live = live_ref[...] != 0
    half = q_ref.shape[2]
    size = out_refs[0].shape[0]
    for h in range(half // HDIM):
        cols = slice(h * HDIM, (h + 1) * HDIM)
        vals = slice(half + h * HDIM, half + (h + 1) * HDIM)
        q = q_ref[0, :, cols]
        st = lax.dot_general(q, text_ref[:, cols], NT, preferred_element_type=F32) * scale
        si = lax.dot_general(q, k_ref[0, :, cols], NT, preferred_element_type=F32) * scale
        st = jnp.where(live, st, -jnp.inf)
        top = jnp.maximum(
            jnp.max(st, axis=1, keepdims=True), jnp.max(si, axis=1, keepdims=True)
        )
        wt = jnp.exp(st - top)
        wi = jnp.exp(si - top)
        total = jnp.sum(wt, axis=1, keepdims=True) + jnp.sum(wi, axis=1, keepdims=True)
        mixed = jnp.dot(
            wt.astype(BF16), text_ref[:, vals], preferred_element_type=F32
        ) + jnp.dot(wi.astype(BF16), v_ref[0, :, cols], preferred_element_type=F32)
        mixed = (mixed / total).astype(BF16)
        for i, out_ref in enumerate(out_refs):
            out_ref[:, cols] = mixed[i * size : (i + 1) * size]


def assemble_kernel(n_req, n_seq, *refs):
    out_ref = refs[-1]
    r, s = lax.axis_index("req"), lax.axis_index("seq")
    half = refs[0].shape[1]
    for k in range(n_req):
        for i in range(n_seq):
            start = ((s ^ i) * n_req + (r ^ k)) * half
            out_ref[:, pl.ds(pl.multiple_of(start, HDIM), half)] = refs[k * n_seq + i][...]


def per_device_heads(
    n_enc,
    n_req,
    n_seq,
    encoder_hidden,
    prompt_token_ids,
    context_weight,
    context_bias,
    modulation_shift,
    modulation_scale,
    key_value_weight,
    key_value_bias,
    request_prompt,
    adapter_of_request,
    adapter_down_maps,
    adapter_up_maps,
    image_stream_input,
    image_query_key,
    image_value_rows,
):
    e, r, s = lax.axis_index("enc"), lax.axis_index("req"), lax.axis_index("seq")
    model_width = context_weight.shape[1]
    features = context_bias.shape[0]
    tokens = encoder_hidden.shape[1]
    inner = key_value_weight.shape[1] // 2
    part = inner // n_seq
    half = part // n_req
    image_rows = image_query_key.shape[2]
    rank = adapter_up_maps.shape[1]
    qk, base, stream = image_query_key[0, 0], image_value_rows[0, 0], image_stream_input[0, 0]
    dma = pltpu.SemaphoreType.DMA
    stat = struct((8, tokens), F32)

    send, keep, sums = call(
        context_kernel,
        (
            struct((model_width // 2 + ROWS, tokens)),
            struct((model_width // 2, tokens), F32),
            stat,
        ),
        (encoder_hidden[0], context_weight, context_bias),
        [HBM] * 3,
        [
            pltpu.VMEM(encoder_hidden.shape[1:], BF16),
            pltpu.VMEM(context_weight.shape, BF16),
            pltpu.VMEM(context_bias.shape, BF16),
            dma((2 + 2 * n_enc,)),
        ],
        name="context",
        vmem=52.65,
    )
    got = swap(send, "req", n_req, 1)

    weight = struct((features, 2 * half))
    weight_own, weight_core, weight_pair = call(
        functools.partial(weight_kernel, n_req, part, inner),
        (weight, weight, struct((2, features, 2 * half))),
        (key_value_weight, send),
        [ANY] * 2,
        [dma((2 * n_req,))],
        name="weight_pack",
    )

    send, keep, sums = call(
        functools.partial(halve_kernel, features),
        (
            struct((n_enc * features + ROWS, tokens)),
            struct((n_enc * features, tokens), F32),
            stat,
        ),
        (got, keep, sums),
        name="halve",
    )
    got = swap(send, "req", n_req, 2)
    packed = [
        call(
            functools.partial(image_kernel, part, inner, k),
            struct((4, image_rows, part)),
            (qk, base, stream, keep),
            [ANY] * 4,
            [dma((4,))],
            name="image_pack",
        )
        for k in range(1, n_seq)
    ]
    image_got = [swap(packed[k - 1], "seq", n_seq, k) for k in range(1, n_seq)]
    keep, sums, *sends = call(
        functools.partial(scatter_kernel, features, 1),
        (struct((features, tokens), F32), stat)
        + tuple(struct((features + ROWS, tokens)) for _ in range(1, n_enc)),
        (got, keep, sums, weight_pair),
        [VMEM] * 3 + [ANY],
        name="scatter",
    )
    arrived = partners(lambda k: sends[k - 1], "enc", n_enc).values()
    weight_pair = lax.optimization_barrier((weight_pair, keep))[0]
    weight_pair_got = swap(weight_pair, "req", n_req, 2)

    bias_columns = jnp.broadcast_to(context_bias.astype(F32)[:, None], (features, tokens))
    scale_columns = jnp.broadcast_to(
        1.0 + modulation_scale[0].astype(F32)[:, None], (features, tokens)
    )
    own = call(
        functools.partial(centre_kernel, model_width),
        struct((features + ROWS, tokens)),
        (
            request_prompt,
            adapter_of_request,
            keep,
            sums,
            bias_columns,
            scale_columns,
            modulation_shift,
            *arrived,
        ),
        [SMEM] * 2 + [VMEM] * (5 + len(arrived)),
        name="centre",
    )
    joined = call(
        join_kernel,
        struct((n_seq * (features + ROWS), tokens)),
        (own, swap(own, "seq", n_seq, 1), image_got[0]),
        [VMEM, VMEM, ANY],
        name="join",
    )
    payloads = partners(lambda k: joined, "req", n_req)
    weight_own_pair, weight_next = call(
        pass_on_kernel,
        (weight, struct((2, features, 2 * half))),
        (weight_core, weight_pair_got, joined),
        [VMEM, VMEM, ANY],
        name="pass_on",
    )
    weight_next = swap(weight_next, "req", n_req, 1)

    size = n_seq * tokens // n_enc
    step = 2 * half // HDIM * size + ROWS
    ids, keep, *sends = call(
        functools.partial(project_kernel, n_seq, n_req, n_enc),
        (struct((2 * n_req,), jnp.int32), struct((step, HDIM), F32))
        + tuple(struct((step, HDIM)) for _ in range(1, n_enc)),
        (weight_own, weight_own_pair, weight_next, joined, *payloads.values()),
        scratch=[pltpu.VMEM((n_enc * step, HDIM), F32)],
        out_specs=(SMEM,) + (VMEM,) * n_enc,
        name="project",
    )
    arrived = partners(lambda k: sends[k - 1], "enc", n_enc).values()

    maps = call(
        functools.partial(maps_kernel, part),
        struct((2 * rank, part)),
        (adapter_down_maps[0].T, adapter_up_maps[0], keep),
        [ANY] * 3,
        [dma((2,))],
        name="maps_pack",
    )
    maps_pair = swap(maps, "req", n_req, 2)

    text = call(
        functools.partial(finish_kernel, n_req, model_width),
        struct((size, 2 * half)),
        (maps_pair, image_got[0], keep, key_value_bias[None], *arrived),
        [ANY] * 2 + [VMEM] * (2 + len(arrived)),
        name="finish",
    )
    maps_core = call(
        select_kernel,
        struct((2 * rank, part)),
        (ids, maps, maps_pair, text),
        [SMEM, VMEM, VMEM, ANY],
        name="select",
    )
    low, chosen_maps = call(
        functools.partial(lowrank_kernel, part),
        (struct((n_seq, image_rows, rank), F32), struct((rank, part))),
        (
            adapter_of_request,
            stream,
            image_got[0],
            maps,
            maps_pair,
            swap(maps_core, "req", n_req, 1),
        ),
        [SMEM] + [VMEM] * 5,
        name="lowrank",
    )
    arranged = struct((n_req, n_seq * image_rows, half))
    queries, image_keys, image_values = call(
        functools.partial(arrange_kernel, n_req, part, inner),
        (arranged, arranged, arranged),
        (low, swap(low, "seq", n_seq, 1), chosen_maps, qk, base, *image_got),
        name="arrange",
    )
    parts = partners(lambda k: text, "enc", n_enc)
    rows = call(
        functools.partial(choose_kernel, n_seq, n_enc),
        tuple(struct((tokens, 2 * half)) for _ in range(n_req)),
        (ids, image_values, text, *parts.values()),
        [SMEM, ANY] + [VMEM] * n_enc,
        name="choose",
    )
    rows = {0: rows[0], **partners(lambda k: rows[k], "req", n_req)}
    live = lax.dynamic_slice_in_dim(prompt_token_ids, request_prompt[0, 0], 1, 0)
    pieces = [None] * n_req
    last = (live, live)
    for k in range(n_req):
        block = pl.BlockSpec((1, n_seq * image_rows, half), lambda i, k=k: (k, 0, 0))
        whole = lambda shape: pl.BlockSpec(shape, lambda i: (0, 0))
        mixed = pl.pallas_call(
            functools.partial(heads_kernel, HDIM ** (-0.5)),
            grid=(1,),
            out_shape=[struct((image_rows, half)) for _ in range(n_seq)],
            in_specs=[whole((1, tokens)), whole((tokens, 2 * half)), block, block, block, ANY, ANY],
            out_specs=[whole((image_rows, half)) for _ in range(n_seq)],
            compiler_params=pltpu.CompilerParams(vmem_limit_bytes=16 * 1024 * 1024),
            name="heads",
        )(live, rows[k], queries, image_keys, image_values, *last)
        pieces[k] = [mixed[0], swap(mixed[1], "seq", n_seq, 1)]
        last = (mixed[0], pieces[k - 1][1] if k else live)
    result = call(
        functools.partial(assemble_kernel, n_req, n_seq),
        struct((image_rows, inner)),
        tuple(p for group in pieces for p in group),
        name="assemble",
    )
    return result[None, None]


def solution(mesh):
    sizes = mesh.shape
    n_enc, n_req, n_seq = sizes["enc"], sizes["req"], sizes["seq"]

    def run(*arrays):
        heads = arrays[6].shape[1] // (2 * HDIM)
        fits = n_seq == 2 and n_req == 4 and heads % (n_seq * n_req) == 0
        return (per_device_heads if fits else per_device)(n_enc, n_req, n_seq, *arrays)

    return jax.shard_map(
        run,
        mesh=mesh,
        in_specs=(
            P("seq", None, ("enc", "req")),
            P(),
            P(("enc", "req"), None),
            P(("enc", "req")),
            P("seq", ("enc", "req")),
            P("seq", ("enc", "req")),
            P(("enc", "req"), None),
            P(),
            P("enc", "req"),
            P("enc", "req"),
            P("req", None, None),
            P("req", None, None),
            P("enc", "req", "seq", None),
            P("enc", "req", "seq", None),
            P("enc", "req", "seq", None),
        ),
        out_specs=P("enc", "req", "seq", None),
        check_vma=False,
    )
```

```python
import functools

import jax
import jax.numpy as jnp
from jax import lax
from jax.experimental import pallas as pl
from jax.experimental.pallas import tpu as pltpu
from jax.sharding import PartitionSpec as P

HDIM = 128
ROWS = 16

epsilon_norm = 1e-06


def swap(block, axis, size, step):
    return lax.ppermute(block, axis, [(i, i ^ step) for i in range(size)])


def pick(array, index, dim):
    return lax.dynamic_index_in_dim(array, index, dim, keepdims=False)


def split_two(value):
    high = lax.reduce_precision(value, 8, 7)
    return high.astype(jnp.bfloat16), (value - high).astype(jnp.bfloat16)


def bits_of(size):
    return [1 << b for b in range(size.bit_length() - 1)]


def with_stat_rows(data, stat):
    high, low = split_two(stat)
    rows = jnp.concatenate(
        [high[None], low[None], jnp.zeros((ROWS - 2, stat.shape[0]), jnp.bfloat16)], axis=0
    )
    rows = jnp.broadcast_to(rows, data.shape[:-2] + rows.shape)
    return jnp.concatenate([data.astype(jnp.bfloat16), rows], axis=-2)


def attention_kernel(heads, inner, scale, mask_ref, q_ref, kt_ref, vt_ref, ki_ref, vi_ref, o_ref):
    live = mask_ref[...] != 0
    for h in range(heads):
        cols = slice(h * HDIM, (h + 1) * HDIM)
        q = q_ref[:, cols]
        dims = (((1,), (1,)), ((), ()))
        st = lax.dot_general(q, kt_ref[:, cols], dims, preferred_element_type=jnp.float32) * scale
        si = lax.dot_general(q, ki_ref[:, cols], dims, preferred_element_type=jnp.float32) * scale
        st = jnp.where(live, st, -jnp.inf)
        top = jnp.maximum(
            jnp.max(st, axis=1, keepdims=True), jnp.max(si, axis=1, keepdims=True)
        )
        wt = jnp.exp(st - top)
        wi = jnp.exp(si - top)
        total = jnp.sum(wt, axis=1, keepdims=True) + jnp.sum(wi, axis=1, keepdims=True)
        mixed = jnp.dot(
            wt.astype(jnp.bfloat16), vt_ref[:, cols], preferred_element_type=jnp.float32
        ) + jnp.dot(wi.astype(jnp.bfloat16), vi_ref[:, cols], preferred_element_type=jnp.float32)
        o_ref[:, cols] = (mixed / total).astype(o_ref.dtype)


def attention(queries, text_keys, text_values, image_keys, image_values, live):
    width = queries.shape[1]
    heads = width // HDIM
    rows = queries.shape[0]
    mask = jnp.broadcast_to(live.astype(jnp.int32)[None, :], (8, live.shape[0]))[:1]
    return pl.pallas_call(
        functools.partial(attention_kernel, heads, width, HDIM ** (-0.5)),
        out_shape=jax.ShapeDtypeStruct((rows, width), jnp.bfloat16),
        compiler_params=pltpu.CompilerParams(vmem_limit_bytes=48 * 1024 * 1024),
        name="attention",
    )(mask, queries, text_keys, text_values, image_keys, image_values)


def per_device(
    n_enc,
    n_req,
    n_seq,
    encoder_hidden,
    prompt_token_ids,
    context_weight,
    context_bias,
    modulation_shift,
    modulation_scale,
    key_value_weight,
    key_value_bias,
    request_prompt,
    adapter_of_request,
    adapter_down_maps,
    adapter_up_maps,
    image_stream_input,
    image_query_key,
    image_value_rows,
):
    f32, bf16 = jnp.float32, jnp.bfloat16
    e, r, s = lax.axis_index("enc"), lax.axis_index("req"), lax.axis_index("seq")
    req_bits = bits_of(n_req)
    model_width = context_weight.shape[1]
    features = context_bias.shape[0]
    tokens = encoder_hidden.shape[1]
    inner = key_value_weight.shape[1] // 2
    part = inner // n_seq

    def heads_of(array, share):
        return lax.dynamic_slice_in_dim(array, share * part, part, 1)

    qk = image_query_key[0, 0]
    sources = [qk[:, :inner], qk[:, inner:], image_value_rows[0, 0], image_stream_input[0, 0]]
    image_parts = [
        jnp.stack([heads_of(a, s ^ k) for a in sources]) for k in range(n_seq)
    ]
    image_parts = [image_parts[0]] + [
        swap(image_parts[k], "seq", n_seq, k) for k in range(1, n_seq)
    ]
    image_all = jnp.concatenate(image_parts, axis=1)
    queries, image_keys, base_values, stream = [image_all[i] for i in range(4)]

    partial_value = lax.dot_general(
        context_weight, encoder_hidden[0], (((0,), (1,)), ((), ())), preferred_element_type=f32
    )
    stat = jnp.sum(partial_value, axis=0) + jnp.sum(context_bias.astype(f32))
    acc = partial_value.reshape((n_enc,) + (2,) * len(req_bits) + (features, tokens))
    for i, bit in enumerate(req_bits):
        mine = (r // bit) % 2
        dim = len(req_bits) - i
        got = swap(with_stat_rows(pick(acc, 1 - mine, dim), stat), "req", n_req, bit).astype(f32)
        acc = pick(acc, mine, dim) + got[..., :features, :]
        got_stat = got.reshape((-1,) + got.shape[-2:])[0, features:]
        stat = stat + got_stat[0] + got_stat[1]
    arrived = [
        swap(with_stat_rows(pick(acc, e ^ k, 0), stat), "enc", n_enc, k).astype(f32)
        for k in range(1, n_enc)
    ]
    embedded = pick(acc, e, 0)
    for got in arrived:
        embedded = embedded + got[:features]
        stat = stat + got[features] + got[features + 1]
    embedded = embedded + context_bias.astype(f32)[:, None]
    centred = embedded - (stat / model_width)[None, :]
    squares = jnp.sum(centred * centred, axis=0)
    scaled = (1.0 + modulation_scale[0].astype(f32))[:, None] * centred

    own = with_stat_rows(scaled, squares)
    blocks = [own] + [swap(own, "seq", n_seq, k) for k in range(1, n_seq)]
    scaled_all = jnp.concatenate([b[:features] for b in blocks], axis=1)
    squares_all = jnp.concatenate(
        [b[features].astype(f32) + b[features + 1].astype(f32) for b in blocks]
    )
    weight_own = jnp.concatenate(
        [heads_of(key_value_weight[:, :inner], s), heads_of(key_value_weight[:, inner:], s)], axis=1
    )
    width = 2 * part
    projected = lax.dot_general(
        scaled_all, weight_own, (((0,), (0,)), ((), ())), preferred_element_type=f32
    )

    shift_part = jnp.dot(modulation_shift, key_value_weight, preferred_element_type=f32)
    for bit in req_bits:
        shift_part = shift_part + swap(shift_part, "req", n_req, bit)
    for bit in bits_of(n_enc):
        shift_part = shift_part + swap(shift_part, "enc", n_enc, bit)
    shift_part = shift_part + key_value_bias.astype(f32)[None]

    def columns_of(row, share):
        return jnp.concatenate(
            [heads_of(row[:, :inner], share), heads_of(row[:, inner:], share)], axis=1
        )

    shift_rows = jnp.concatenate(
        [columns_of(shift_part, s)]
        + [swap(columns_of(shift_part, s ^ k), "seq", n_seq, k) for k in range(1, n_seq)],
        axis=0,
    )

    halves = tokens // n_req // ROWS
    split = (n_seq,) + (2,) * len(req_bits) + (halves, ROWS)
    acc = projected.reshape(split + (width,))
    acc_stat = squares_all.reshape(split)

    def with_stat_columns(data, stat):
        high, low = split_two(stat)
        lane = lax.broadcasted_iota(jnp.int32, stat.shape + (HDIM,), stat.ndim)
        columns = jnp.where(
            lane == 0, high[..., None], jnp.where(lane == 1, low[..., None], jnp.zeros((), bf16))
        )
        return jnp.concatenate([data.astype(bf16), columns], axis=-1)

    for i, bit in enumerate(req_bits):
        mine = (r // bit) % 2
        dim = len(req_bits) - i
        got = swap(
            with_stat_columns(pick(acc, 1 - mine, dim), pick(acc_stat, 1 - mine, dim)),
            "req", n_req, bit,
        ).astype(f32)
        acc = pick(acc, mine, dim) + got[..., :width]
        acc_stat = pick(acc_stat, mine, dim) + got[..., width] + got[..., width + 1]
    acc = acc.reshape(n_enc, ROWS, width)
    acc_stat = acc_stat.reshape(n_enc, ROWS)
    arrived = [
        swap(with_stat_columns(pick(acc, e ^ k, 0), pick(acc_stat, e ^ k, 0)), "enc", n_enc, k)
        .astype(f32)
        for k in range(1, n_enc)
    ]
    rows = pick(acc, e, 0)
    row_squares = pick(acc_stat, e, 0)
    for got in arrived:
        rows = rows + got[:, :width]
        row_squares = row_squares + got[:, width] + got[:, width + 1]
    rows = rows * lax.rsqrt(row_squares / model_width + epsilon_norm)[:, None]
    rows = rows + pick(shift_rows, e // halves, 0)[None]
    keys = rows[:, :part].reshape(ROWS, part // HDIM, HDIM)
    keys = keys * lax.rsqrt(jnp.mean(keys * keys, axis=2, keepdims=True) + epsilon_norm)
    text = jnp.concatenate([keys.reshape(ROWS, part), rows[:, part:]], axis=1).astype(bf16)

    chosen = request_prompt[0, 0]
    relative = s ^ chosen
    by_enc = [text] + [swap(text, "enc", n_enc, k) for k in range(1, n_enc)]
    by_enc = jnp.stack(by_enc)
    by_enc = jnp.stack([pick(by_enc, k ^ e, 0) for k in range(n_enc)])
    held = by_enc.reshape(1, n_seq, halves, ROWS, width)
    first = req_bits[0]
    held = jnp.concatenate([held, swap(held, "req", n_req, first)], axis=0)
    groups = [pick(held, relative, 1)]
    for step in range(2, n_req, 2):
        wanted = swap(relative, "req", n_req, step)
        groups.append(swap(pick(held, wanted, 1), "req", n_req, step))
    text_rows = jnp.concatenate(groups, axis=0).reshape(-1, width)
    live = pick(prompt_token_ids, chosen, 0) != 0
    live = live.reshape(n_req, halves * ROWS)
    live = jnp.concatenate([pick(live, r ^ k, 0) for k in range(n_req)])

    down = lax.dynamic_slice_in_dim(adapter_down_maps[0], s * part, part, 0).T
    up = heads_of(adapter_up_maps[0], s)
    maps = jnp.concatenate([down, up], axis=0)[None]
    for bit in reversed(req_bits):
        maps = jnp.concatenate([maps, swap(maps, "req", n_req, bit)], axis=0)
    other = adapter_of_request[0, 0] ^ r
    index = 0
    for bit in req_bits:
        index = index * 2 + (other // bit) % 2
    chosen_maps = pick(maps, index, 0)
    rank = up.shape[0]
    lowrank = lax.dot_general(
        stream, chosen_maps[:rank], (((1,), (1,)), ((), ())), preferred_element_type=f32
    ).reshape(n_seq, -1, rank)
    for bit in bits_of(n_seq):
        got = swap(lowrank, "seq", n_seq, bit)
        lowrank = lowrank + jnp.stack([got[k ^ bit] for k in range(n_seq)])
    lowrank = lowrank.reshape(-1, rank).astype(bf16)
    image_values = (
        base_values.astype(f32) + jnp.dot(lowrank, chosen_maps[rank:], preferred_element_type=f32)
    ).astype(bf16)

    mixed = attention(
        queries, text_rows[:, :part], text_rows[:, part:], image_keys, image_values, live
    ).reshape(n_seq, -1, part)
    pieces = jnp.stack([mixed[0]] + [swap(mixed[k], "seq", n_seq, k) for k in range(1, n_seq)])
    result = jnp.concatenate([pick(pieces, s ^ k, 0) for k in range(n_seq)], axis=1)
    return result[None, None]


F32, BF16 = jnp.float32, jnp.bfloat16
ANY = pl.BlockSpec(memory_space=pl.ANY)
VMEM = pl.BlockSpec(memory_space=pltpu.VMEM)
SMEM = pl.BlockSpec(memory_space=pltpu.SMEM)
NT = (((1,), (1,)), ((), ()))
TN = (((0,), (0,)), ((), ()))


def partners(send, axis, size):
    return {k: swap(send(k), axis, size, k) for k in far_first(size)}


def far_first(size):
    return [k for k in range(2, size)] + [1]


def call(kernel, outs, ins, specs=None, scratch=(), name=None, out_specs=None, vmem=16):
    return pl.pallas_call(
        kernel,
        out_shape=outs,
        in_specs=specs if specs is not None else [VMEM] * len(ins),
        out_specs=out_specs if out_specs is not None else jax.tree.map(lambda _: VMEM, outs),
        scratch_shapes=list(scratch),
        compiler_params=pltpu.CompilerParams(vmem_limit_bytes=int(vmem * 1024 * 1024)),
        name=name,
    )(*ins)


def struct(shape, dtype=BF16):
    return jax.ShapeDtypeStruct(shape, dtype)


def at(index, size):
    return pl.ds(pl.multiple_of(index * size, size), size)


def stat_rows(stat):
    high = stat.astype(BF16).astype(F32)
    row = lax.broadcasted_iota(jnp.int32, (ROWS, stat.shape[1]), 0)
    return jnp.where(row == 0, high, jnp.where(row == 1, stat - high, 0.0)).astype(BF16)


def stat_of(rows):
    rows = rows.astype(F32)
    return rows[0:1] + rows[1:2]


def context_kernel(h_ref, w_ref, b_ref, send_ref, keep_ref, stat_ref):
    mine = lax.rem(lax.axis_index("req"), 2)
    features = b_ref.shape[0]
    pairs = w_ref.shape[1] // (2 * features)
    total = jnp.zeros((1, h_ref.shape[0]), F32)
    for p in range(pairs):
        product = jnp.dot(
            h_ref[...], w_ref[:, p * 2 * features : (p + 1) * 2 * features],
            preferred_element_type=F32,
        ).T
        total = total + jnp.sum(product, axis=0, keepdims=True)
        low, high = product[:features], product[features:]
        rows = slice(p * features, (p + 1) * features)
        keep_ref[rows] = jnp.where(mine == 0, low, high)
        send_ref[rows] = jnp.where(mine == 0, high, low).astype(BF16)
    stat = total + jnp.sum(b_ref[...].astype(F32))
    send_ref[pairs * features :] = stat_rows(stat)
    stat_ref[...] = jnp.broadcast_to(stat, stat_ref.shape)


def halve_kernel(features, got_ref, keep_ref, stat_ref, send_ref, kept_ref, out_stat_ref):
    mine = lax.rem(lax.axis_index("req") // 2, 2)
    count = keep_ref.shape[0] // (2 * features)
    for i in range(count):
        rows = slice(i * features, (i + 1) * features)
        own, other = at(2 * i + mine, features), at(2 * i + 1 - mine, features)
        kept_ref[rows] = keep_ref[own] + got_ref[own].astype(F32)
        send_ref[rows] = (keep_ref[other] + got_ref[other].astype(F32)).astype(BF16)
    stat = stat_ref[0:1] + stat_of(got_ref[2 * count * features :])
    send_ref[count * features :] = stat_rows(stat)
    out_stat_ref[...] = jnp.broadcast_to(stat, out_stat_ref.shape)


def scatter_kernel(features, deps, got_ref, keep_ref, stat_ref, *refs):
    kept_ref, out_stat_ref, *send_refs = refs[deps:]
    e = lax.axis_index("enc")
    count = keep_ref.shape[0] // features
    stat = stat_ref[0:1] + stat_of(got_ref[count * features :])
    own = at(e, features)
    for k, send_ref in enumerate(send_refs):
        other = at(e ^ (k + 1), features)
        send_ref[:features] = (keep_ref[other] + got_ref[other].astype(F32)).astype(BF16)
        send_ref[features:] = stat_rows(stat)
    kept_ref[...] = keep_ref[own] + got_ref[own].astype(F32)
    out_stat_ref[...] = jnp.broadcast_to(stat, out_stat_ref.shape)


def centre_kernel(width, prompt_ref, dep_ref, keep_ref, stat_ref, bias_ref, scale_ref, shift_ref, *refs):
    got_refs, out_ref = refs[:-1], refs[-1]
    features, tokens = keep_ref.shape
    total = keep_ref[...] + bias_ref[...]
    stat = stat_ref[0:1]
    for got_ref in got_refs:
        total = total + got_ref[:features].astype(F32)
        stat = stat + stat_of(got_ref[features:])
    centred = total - stat * (1.0 / width)
    out_ref[:features] = (scale_ref[...] * centred).astype(BF16)
    squares = jnp.sum(centred * centred, axis=0, keepdims=True)
    high = squares.astype(BF16).astype(F32)
    row = lax.broadcasted_iota(jnp.int32, (ROWS, tokens), 0)
    extra = jnp.where(row == 0, high, jnp.where(row == 1, squares - high, 0.0))
    for j in range(pl.cdiv(features, tokens)):
        piece = shift_ref[:, j * tokens : min((j + 1) * tokens, features)].astype(F32)
        gap = tokens - piece.shape[1]
        if gap:
            piece = jnp.concatenate([piece, jnp.zeros((1, gap), F32)], axis=1)
        extra = jnp.where(row == 2 + j, piece, extra)
    extra = jnp.where(row == ROWS - 1, prompt_ref[0, 0].astype(F32), extra)
    out_ref[features:] = extra.astype(BF16)


def pass_on_kernel(core_ref, got_ref, dep_ref, own_ref, next_ref):
    own_ref[...] = got_ref[0]
    next_ref[0] = core_ref[...]
    next_ref[1] = got_ref[1]


def join_kernel(own_ref, got_ref, dep_ref, out_ref):
    size = own_ref.shape[0]
    out_ref[:size] = own_ref[...]
    out_ref[size:] = got_ref[...]


def project_kernel(n_seq, n_req, n_enc, own_ref, pair_ref, next_ref, *refs):
    payload_refs = dict(zip([0] + far_first(n_req), refs))
    weight_refs = (own_ref, next_ref.at[0], pair_ref, next_ref.at[1])
    prompts_ref, keep_ref = refs[n_req : n_req + 2]
    send_refs = refs[n_req + 2 : -1]
    rows_ref = refs[-1]
    features, width = weight_refs[0].shape
    tokens = payload_refs[0].shape[1]
    stride = features + ROWS
    total = None
    squares = [jnp.zeros((1, tokens), F32) for _ in range(n_seq)]
    for k in range(n_req):
        left = []
        shifts = []
        for p in range(n_seq):
            payload = payload_refs[k]
            left.append(payload[p * stride : p * stride + features].T)
            extra = payload[p * stride + features : (p + 1) * stride].astype(F32)
            squares[p] = squares[p] + extra[0:1] + extra[1:2]
            pieces = [extra[2 + j : 3 + j] for j in range(pl.cdiv(features, tokens))]
            shifts.append(jnp.concatenate(pieces, axis=1)[:, :features])
            if p == 0:
                prompts_ref[k] = jnp.max(extra[ROWS - 1 : ROWS]).astype(jnp.int32)
        shifts.append(jnp.zeros((ROWS - n_seq, features), F32))
        left.append(jnp.concatenate(shifts, axis=0).astype(BF16))
        term = jnp.dot(
            jnp.concatenate(left, axis=0), weight_refs[k][...], preferred_element_type=F32
        )
        total = term if total is None else total + term
    size = n_seq * tokens // n_enc
    heads = width // HDIM
    step = heads * size + ROWS
    row = lax.broadcasted_iota(jnp.int32, (ROWS, HDIM), 0)
    for z in range(n_enc):
        p, first = divmod(z * size, tokens)
        shift = total[n_seq * tokens + p : n_seq * tokens + p + 1]
        square = squares[p][:, first : first + size]
        square = jnp.concatenate([square, jnp.zeros((1, HDIM - size), F32)], axis=1)
        high = square.astype(BF16).astype(F32)
        extra = jnp.where(
            row == 2 * heads, high, jnp.where(row == 2 * heads + 1, square - high, 0.0)
        )
        for h in range(heads):
            cols = slice(h * HDIM, (h + 1) * HDIM)
            rows_ref[z * step + h * size : z * step + (h + 1) * size] = total[
                z * size : (z + 1) * size, cols
            ]
            high = shift[:, cols].astype(BF16).astype(F32)
            extra = jnp.where(
                row == h, high, jnp.where(row == heads + h, shift[:, cols] - high, extra)
            )
        rows_ref[z * step + heads * size : (z + 1) * step] = extra
    e = lax.axis_index("enc")
    keep_ref[...] = rows_ref[at(e, step)]
    for k, send_ref in enumerate(send_refs):
        send_ref[...] = rows_ref[at(e ^ (k + 1), step)].astype(BF16)


def finish_kernel(n_req, model_width, keep_ref, bias_ref, *refs):
    got_refs, out_ref = refs[:-1], refs[-1]
    r, s = lax.axis_index("req"), lax.axis_index("seq")
    size, width = out_ref.shape
    heads = width // HDIM
    half = width // 2
    inner = bias_ref.shape[1] // 2
    total = keep_ref[...]
    for got_ref in got_refs:
        total = total + got_ref[...].astype(F32)
    extra = total[heads * size :]
    squares = extra[2 * heads : 2 * heads + 1] + extra[2 * heads + 1 : 2 * heads + 2]
    squares = jnp.broadcast_to(squares, (HDIM, HDIM)).T[:size]
    factor = lax.rsqrt(squares * (1.0 / model_width) + epsilon_norm)
    for h in range(heads):
        start = (h * HDIM // half) * inner + (s * n_req + r) * half + h * HDIM % half
        bias = bias_ref[:, pl.ds(pl.multiple_of(start, HDIM), HDIM)].astype(F32)
        shift = extra[h : h + 1] + extra[heads + h : heads + h + 1] + bias
        head = total[h * size : (h + 1) * size] * factor + shift
        if h * HDIM < half:
            head = head * lax.rsqrt(jnp.mean(head * head, axis=1, keepdims=True) + epsilon_norm)
        out_ref[:, h * HDIM : (h + 1) * HDIM] = head.astype(BF16)


def choose_kernel(n_seq, n_enc, chosen_ref, dep_ref, *refs):
    part_refs, out_refs = dict(zip([0] + far_first(n_enc), refs)), refs[n_enc:]
    e, r, s = lax.axis_index("enc"), lax.axis_index("req"), lax.axis_index("seq")
    halves = n_enc // n_seq
    size = part_refs[0].shape[0]
    for k, out_ref in enumerate(out_refs):
        prompt = s ^ chosen_ref[k]
        for h in range(halves):
            place = e ^ (prompt * halves + h)
            for j in range(n_enc):
                @pl.when(place == j)
                def _():
                    out_ref[h * size : (h + 1) * size] = part_refs[j][...]


def weight_kernel(n_req, part, inner, w_ref, dep_ref, own_ref, core_ref, pair_ref, sems):
    r, s = lax.axis_index("req"), lax.axis_index("seq")
    half = part // n_req
    copies = []
    for k, out_ref in enumerate((own_ref, core_ref, pair_ref.at[0], pair_ref.at[1])):
        for side in range(2):
            columns = pl.ds(
                pl.multiple_of(side * inner + (s * n_req + (r ^ k)) * half, HDIM), half
            )
            copies.append(
                pltpu.make_async_copy(
                    w_ref.at[:, columns],
                    out_ref.at[:, pl.ds(side * half, half)],
                    sems.at[2 * k + side],
                )
            )
    for copy in copies:
        copy.start()
    for copy in copies:
        copy.wait()


def image_kernel(part, inner, step, qk_ref, v_ref, x_ref, dep_ref, out_ref, sems):
    start = (lax.axis_index("seq") ^ step) * part
    copies = []
    for i, (ref, base) in enumerate(((qk_ref, 0), (qk_ref, inner), (v_ref, 0), (x_ref, 0))):
        columns = pl.ds(pl.multiple_of(base + start, HDIM), part)
        copies.append(pltpu.make_async_copy(ref.at[:, columns], out_ref.at[i], sems.at[i]))
    for copy in copies:
        copy.start()
    for copy in copies:
        copy.wait()


def maps_kernel(part, down_ref, up_ref, dep_ref, out_ref, sems):
    rank = down_ref.shape[0]
    columns = pl.ds(pl.multiple_of(lax.axis_index("seq") * part, HDIM), part)
    copies = [
        pltpu.make_async_copy(down_ref.at[:, columns], out_ref.at[pl.ds(0, rank)], sems.at[0]),
        pltpu.make_async_copy(up_ref.at[:, columns], out_ref.at[pl.ds(rank, rank)], sems.at[1]),
    ]
    for copy in copies:
        copy.start()
    for copy in copies:
        copy.wait()


def join_maps_kernel(own_ref, core_ref, dep_ref, out_ref):
    out_ref[0] = own_ref[...]
    out_ref[1] = core_ref[...]


def lowrank_kernel(part, adapter_ref, x_ref, got_ref, *refs):
    own_ref, pair_ref, out_ref, chosen_ref = refs
    map_refs = (own_ref.at[0], own_ref.at[1], pair_ref.at[0], pair_ref.at[1])
    place = adapter_ref[0, 0] ^ lax.axis_index("req")
    rank = out_ref.shape[-1]
    for k, ref in enumerate(map_refs):
        @pl.when(place == k)
        def _():
            chosen_ref[...] = ref[rank:]
            own = x_ref[:, pl.ds(pl.multiple_of(lax.axis_index("seq") * part, HDIM), part)]
            for i, rows in enumerate((own, got_ref[3])):
                out_ref[i] = lax.dot_general(
                    rows, ref[:rank], NT, preferred_element_type=F32
                )


def arrange_kernel(n_req, part, inner, low_ref, other_ref, maps_ref, qk_ref, v_ref, *refs):
    got_refs, (q_out, k_out, v_out) = refs[:-3], refs[-3:]
    r, s = lax.axis_index("req"), lax.axis_index("seq")
    half = part // n_req
    tokens = qk_ref.shape[0]
    low = [(low_ref[i] + other_ref[i ^ 1]).astype(BF16) for i in range(2)]
    for k in range(n_req):
        place = (r ^ k) * half
        up = maps_ref[:, pl.ds(pl.multiple_of(place, HDIM), half)]
        for i in range(len(got_refs) + 1):
            rows = slice(i * tokens, (i + 1) * tokens)
            if i == 0:
                own = s * part + place
                q = qk_ref[:, pl.ds(pl.multiple_of(own, HDIM), half)]
                key = qk_ref[:, pl.ds(pl.multiple_of(inner + own, HDIM), half)]
                base = v_ref[:, pl.ds(pl.multiple_of(own, HDIM), half)]
            else:
                columns = pl.ds(pl.multiple_of(place, HDIM), half)
                q = got_refs[i - 1][0, :, columns]
                key = got_refs[i - 1][1, :, columns]
                base = got_refs[i - 1][2, :, columns]
            q_out[k, rows] = q
            k_out[k, rows] = key
            v_out[k, rows] = (
                base.astype(F32) + jnp.dot(low[i], up, preferred_element_type=F32)
            ).astype(BF16)


def heads_kernel(place, scale, live_ref, text_ref, q_ref, k_ref, v_ref, *refs):
    out_refs = refs[2:]
    live = live_ref[...] != 0
    half = q_ref.shape[2]
    size = out_refs[0].shape[0]
    for h in range(half // HDIM):
        cols = slice(h * HDIM, (h + 1) * HDIM)
        vals = slice(half + h * HDIM, half + (h + 1) * HDIM)
        q = q_ref[place, :, cols]
        st = lax.dot_general(q, text_ref[:, cols], NT, preferred_element_type=F32) * scale
        si = lax.dot_general(q, k_ref[place, :, cols], NT, preferred_element_type=F32) * scale
        st = jnp.where(live, st, -jnp.inf)
        top = jnp.maximum(
            jnp.max(st, axis=1, keepdims=True), jnp.max(si, axis=1, keepdims=True)
        )
        wt = jnp.exp(st - top)
        wi = jnp.exp(si - top)
        total = jnp.sum(wt, axis=1, keepdims=True) + jnp.sum(wi, axis=1, keepdims=True)
        mixed = jnp.dot(
            wt.astype(BF16), text_ref[:, vals], preferred_element_type=F32
        ) + jnp.dot(wi.astype(BF16), v_ref[place, :, cols], preferred_element_type=F32)
        mixed = (mixed / total).astype(BF16)
        for i, out_ref in enumerate(out_refs):
            out_ref[:, cols] = mixed[i * size : (i + 1) * size]


def assemble_kernel(n_req, n_seq, *refs):
    out_ref = refs[-1]
    r, s = lax.axis_index("req"), lax.axis_index("seq")
    half = refs[0].shape[1]
    for k in range(n_req):
        for i in range(n_seq):
            start = ((s ^ i) * n_req + (r ^ k)) * half
            out_ref[:, pl.ds(pl.multiple_of(start, HDIM), half)] = refs[k * n_seq + i][...]


def per_device_heads(
    n_enc,
    n_req,
    n_seq,
    encoder_hidden,
    prompt_token_ids,
    context_weight,
    context_bias,
    modulation_shift,
    modulation_scale,
    key_value_weight,
    key_value_bias,
    request_prompt,
    adapter_of_request,
    adapter_down_maps,
    adapter_up_maps,
    image_stream_input,
    image_query_key,
    image_value_rows,
):
    e, r, s = lax.axis_index("enc"), lax.axis_index("req"), lax.axis_index("seq")
    model_width = context_weight.shape[1]
    features = context_bias.shape[0]
    tokens = encoder_hidden.shape[1]
    inner = key_value_weight.shape[1] // 2
    part = inner // n_seq
    half = part // n_req
    image_rows = image_query_key.shape[2]
    rank = adapter_up_maps.shape[1]
    qk, base, stream = image_query_key[0, 0], image_value_rows[0, 0], image_stream_input[0, 0]
    dma = pltpu.SemaphoreType.DMA
    stat = struct((8, tokens), F32)

    send, keep, sums = call(
        context_kernel,
        (
            struct((model_width // 2 + ROWS, tokens)),
            struct((model_width // 2, tokens), F32),
            stat,
        ),
        (encoder_hidden[0], context_weight, context_bias),
        name="context",
    )
    got = swap(send, "req", n_req, 1)

    maps = call(
        functools.partial(maps_kernel, part),
        struct((2 * rank, part)),
        (adapter_down_maps[0].T, adapter_up_maps[0], send),
        [ANY] * 3,
        [dma((2,))],
        name="maps_pack",
    )
    maps_core = swap(maps, "req", n_req, 1)
    weight = struct((features, 2 * half))
    weight_own, weight_core, weight_pair = call(
        functools.partial(weight_kernel, n_req, part, inner),
        (weight, weight, struct((2, features, 2 * half))),
        (key_value_weight, send),
        [ANY] * 2,
        [dma((2 * n_req,))],
        name="weight_pack",
    )

    send, keep, sums = call(
        functools.partial(halve_kernel, features),
        (
            struct((n_enc * features + ROWS, tokens)),
            struct((n_enc * features, tokens), F32),
            stat,
        ),
        (got, keep, sums),
        name="halve",
    )
    got = swap(send, "req", n_req, 2)
    packed = [
        call(
            functools.partial(image_kernel, part, inner, k),
            struct((4, image_rows, part)),
            (qk, base, stream, keep),
            [ANY] * 4,
            [dma((4,))],
            name="image_pack",
        )
        for k in range(1, n_seq)
    ]
    image_got = [swap(packed[k - 1], "seq", n_seq, k) for k in range(1, n_seq)]
    keep, sums, *sends = call(
        functools.partial(scatter_kernel, features, 1),
        (struct((features, tokens), F32), stat)
        + tuple(struct((features + ROWS, tokens)) for _ in range(1, n_enc)),
        (got, keep, sums, weight_pair),
        [VMEM] * 3 + [ANY],
        name="scatter",
    )
    arrived = partners(lambda k: sends[k - 1], "enc", n_enc).values()
    weight_pair = lax.optimization_barrier((weight_pair, keep))[0]
    weight_pair_got = swap(weight_pair, "req", n_req, 2)

    bias_columns = jnp.broadcast_to(context_bias.astype(F32)[:, None], (features, tokens))
    scale_columns = jnp.broadcast_to(
        1.0 + modulation_scale[0].astype(F32)[:, None], (features, tokens)
    )
    own = call(
        functools.partial(centre_kernel, model_width),
        struct((features + ROWS, tokens)),
        (
            request_prompt,
            maps_core,
            keep,
            sums,
            bias_columns,
            scale_columns,
            modulation_shift,
            *arrived,
        ),
        [SMEM, ANY] + [VMEM] * (5 + len(arrived)),
        name="centre",
    )
    joined = call(
        join_kernel,
        struct((n_seq * (features + ROWS), tokens)),
        (own, swap(own, "seq", n_seq, 1), image_got[0]),
        [VMEM, VMEM, ANY],
        name="join",
    )
    payloads = partners(lambda k: joined, "req", n_req)
    weight_own_pair, weight_next = call(
        pass_on_kernel,
        (weight, struct((2, features, 2 * half))),
        (weight_core, weight_pair_got, joined),
        [VMEM, VMEM, ANY],
        name="pass_on",
    )
    weight_next = swap(weight_next, "req", n_req, 1)

    size = n_seq * tokens // n_enc
    step = 2 * half // HDIM * size + ROWS
    ids, keep, *sends = call(
        functools.partial(project_kernel, n_seq, n_req, n_enc),
        (struct((n_req,), jnp.int32), struct((step, HDIM), F32))
        + tuple(struct((step, HDIM)) for _ in range(1, n_enc)),
        (weight_own, weight_own_pair, weight_next, joined, *payloads.values()),
        scratch=[pltpu.VMEM((n_enc * step, HDIM), F32)],
        out_specs=(SMEM,) + (VMEM,) * n_enc,
        name="project",
    )
    arrived = partners(lambda k: sends[k - 1], "enc", n_enc).values()

    maps = call(
        join_maps_kernel,
        struct((2, 2 * rank, part)),
        (maps, maps_core, joined),
        [VMEM, VMEM, ANY],
        name="maps_join",
    )
    maps = lax.optimization_barrier((maps, keep))[0]
    maps_pair = swap(maps, "req", n_req, 2)

    text = call(
        functools.partial(finish_kernel, n_req, model_width),
        struct((size, 2 * half)),
        (keep, key_value_bias[None], *arrived),
        [VMEM] * (2 + len(arrived)),
        name="finish",
    )
    low, chosen_maps = call(
        functools.partial(lowrank_kernel, part),
        (struct((n_seq, image_rows, rank), F32), struct((rank, part))),
        (
            adapter_of_request,
            stream,
            image_got[0],
            maps,
            maps_pair,
        ),
        [SMEM] + [VMEM] * 4,
        name="lowrank",
    )
    arranged = struct((n_req, n_seq * image_rows, half))
    queries, image_keys, image_values = call(
        functools.partial(arrange_kernel, n_req, part, inner),
        (arranged, arranged, arranged),
        (low, swap(low, "seq", n_seq, 1), chosen_maps, qk, base, *image_got),
        name="arrange",
    )
    parts = partners(lambda k: text, "enc", n_enc)
    rows = call(
        functools.partial(choose_kernel, n_seq, n_enc),
        [struct((tokens, 2 * half)) for _ in range(n_req)],
        (ids, image_values, text, *parts.values()),
        [SMEM, ANY] + [VMEM] * n_enc,
        name="choose",
    )
    rows = {0: rows[0], **partners(lambda k: rows[k], "req", n_req)}
    live = lax.dynamic_slice_in_dim(prompt_token_ids, request_prompt[0, 0], 1, 0)
    pieces = [None] * n_req
    last = (live, live)
    for k in range(n_req):
        mixed = call(
            functools.partial(heads_kernel, k, HDIM ** (-0.5)),
            [struct((image_rows, half))] * n_seq,
            (live, rows[k], queries, image_keys, image_values, *last),
            [VMEM] * 5 + [ANY] * 2,
            name="heads",
        )
        pieces[k] = [mixed[0], swap(mixed[1], "seq", n_seq, 1)]
        last = (mixed[0], pieces[k - 1][1] if k else live)
    result = call(
        functools.partial(assemble_kernel, n_req, n_seq),
        struct((image_rows, inner)),
        tuple(p for group in pieces for p in group),
        name="assemble",
    )
    return result[None, None]


def solution(mesh):
    sizes = mesh.shape
    n_enc, n_req, n_seq = sizes["enc"], sizes["req"], sizes["seq"]

    def run(*arrays):
        heads = arrays[6].shape[1] // (2 * HDIM)
        fits = n_seq == 2 and n_req == 4 and heads % (n_seq * n_req) == 0
        return (per_device_heads if fits else per_device)(n_enc, n_req, n_seq, *arrays)

    return jax.shard_map(
        run,
        mesh=mesh,
        in_specs=(
            P("seq", None, ("enc", "req")),
            P(),
            P(("enc", "req"), None),
            P(("enc", "req")),
            P("seq", ("enc", "req")),
            P("seq", ("enc", "req")),
            P(("enc", "req"), None),
            P(),
            P("enc", "req"),
            P("enc", "req"),
            P("req", None, None),
            P("req", None, None),
            P("enc", "req", "seq", None),
            P("enc", "req", "seq", None),
            P("enc", "req", "seq", None),
        ),
        out_specs=P("enc", "req", "seq", None),
        check_vma=False,
    )
```

```python
import functools

import jax
import jax.numpy as jnp
from jax import lax
from jax.experimental import pallas as pl
from jax.experimental.pallas import tpu as pltpu
from jax.sharding import PartitionSpec as P

HDIM = 128
ROWS = 16

epsilon_norm = 1e-06


def swap(block, axis, size, step):
    return lax.ppermute(block, axis, [(i, i ^ step) for i in range(size)])


def pick(array, index, dim):
    return lax.dynamic_index_in_dim(array, index, dim, keepdims=False)


def split_two(value):
    high = lax.reduce_precision(value, 8, 7)
    return high.astype(jnp.bfloat16), (value - high).astype(jnp.bfloat16)


def bits_of(size):
    return [1 << b for b in range(size.bit_length() - 1)]


def with_stat_rows(data, stat):
    high, low = split_two(stat)
    rows = jnp.concatenate(
        [high[None], low[None], jnp.zeros((ROWS - 2, stat.shape[0]), jnp.bfloat16)], axis=0
    )
    rows = jnp.broadcast_to(rows, data.shape[:-2] + rows.shape)
    return jnp.concatenate([data.astype(jnp.bfloat16), rows], axis=-2)


def attention_kernel(heads, inner, scale, mask_ref, q_ref, kt_ref, vt_ref, ki_ref, vi_ref, o_ref):
    live = mask_ref[...] != 0
    for h in range(heads):
        cols = slice(h * HDIM, (h + 1) * HDIM)
        q = q_ref[:, cols]
        dims = (((1,), (1,)), ((), ()))
        st = lax.dot_general(q, kt_ref[:, cols], dims, preferred_element_type=jnp.float32) * scale
        si = lax.dot_general(q, ki_ref[:, cols], dims, preferred_element_type=jnp.float32) * scale
        st = jnp.where(live, st, -jnp.inf)
        top = jnp.maximum(
            jnp.max(st, axis=1, keepdims=True), jnp.max(si, axis=1, keepdims=True)
        )
        wt = jnp.exp(st - top)
        wi = jnp.exp(si - top)
        total = jnp.sum(wt, axis=1, keepdims=True) + jnp.sum(wi, axis=1, keepdims=True)
        mixed = jnp.dot(
            wt.astype(jnp.bfloat16), vt_ref[:, cols], preferred_element_type=jnp.float32
        ) + jnp.dot(wi.astype(jnp.bfloat16), vi_ref[:, cols], preferred_element_type=jnp.float32)
        o_ref[:, cols] = (mixed / total).astype(o_ref.dtype)


def attention(queries, text_keys, text_values, image_keys, image_values, live):
    width = queries.shape[1]
    heads = width // HDIM
    rows = queries.shape[0]
    mask = jnp.broadcast_to(live.astype(jnp.int32)[None, :], (8, live.shape[0]))[:1]
    return pl.pallas_call(
        functools.partial(attention_kernel, heads, width, HDIM ** (-0.5)),
        out_shape=jax.ShapeDtypeStruct((rows, width), jnp.bfloat16),
        compiler_params=pltpu.CompilerParams(vmem_limit_bytes=48 * 1024 * 1024),
        name="attention",
    )(mask, queries, text_keys, text_values, image_keys, image_values)


def per_device(
    n_enc,
    n_req,
    n_seq,
    encoder_hidden,
    prompt_token_ids,
    context_weight,
    context_bias,
    modulation_shift,
    modulation_scale,
    key_value_weight,
    key_value_bias,
    request_prompt,
    adapter_of_request,
    adapter_down_maps,
    adapter_up_maps,
    image_stream_input,
    image_query_key,
    image_value_rows,
):
    f32, bf16 = jnp.float32, jnp.bfloat16
    e, r, s = lax.axis_index("enc"), lax.axis_index("req"), lax.axis_index("seq")
    req_bits = bits_of(n_req)
    model_width = context_weight.shape[1]
    features = context_bias.shape[0]
    tokens = encoder_hidden.shape[1]
    inner = key_value_weight.shape[1] // 2
    part = inner // n_seq

    def heads_of(array, share):
        return lax.dynamic_slice_in_dim(array, share * part, part, 1)

    qk = image_query_key[0, 0]
    sources = [qk[:, :inner], qk[:, inner:], image_value_rows[0, 0], image_stream_input[0, 0]]
    image_parts = [
        jnp.stack([heads_of(a, s ^ k) for a in sources]) for k in range(n_seq)
    ]
    image_parts = [image_parts[0]] + [
        swap(image_parts[k], "seq", n_seq, k) for k in range(1, n_seq)
    ]
    image_all = jnp.concatenate(image_parts, axis=1)
    queries, image_keys, base_values, stream = [image_all[i] for i in range(4)]

    partial_value = lax.dot_general(
        context_weight, encoder_hidden[0], (((0,), (1,)), ((), ())), preferred_element_type=f32
    )
    stat = jnp.sum(partial_value, axis=0) + jnp.sum(context_bias.astype(f32))
    acc = partial_value.reshape((n_enc,) + (2,) * len(req_bits) + (features, tokens))
    for i, bit in enumerate(req_bits):
        mine = (r // bit) % 2
        dim = len(req_bits) - i
        got = swap(with_stat_rows(pick(acc, 1 - mine, dim), stat), "req", n_req, bit).astype(f32)
        acc = pick(acc, mine, dim) + got[..., :features, :]
        got_stat = got.reshape((-1,) + got.shape[-2:])[0, features:]
        stat = stat + got_stat[0] + got_stat[1]
    arrived = [
        swap(with_stat_rows(pick(acc, e ^ k, 0), stat), "enc", n_enc, k).astype(f32)
        for k in range(1, n_enc)
    ]
    embedded = pick(acc, e, 0)
    for got in arrived:
        embedded = embedded + got[:features]
        stat = stat + got[features] + got[features + 1]
    embedded = embedded + context_bias.astype(f32)[:, None]
    centred = embedded - (stat / model_width)[None, :]
    squares = jnp.sum(centred * centred, axis=0)
    scaled = (1.0 + modulation_scale[0].astype(f32))[:, None] * centred

    own = with_stat_rows(scaled, squares)
    blocks = [own] + [swap(own, "seq", n_seq, k) for k in range(1, n_seq)]
    scaled_all = jnp.concatenate([b[:features] for b in blocks], axis=1)
    squares_all = jnp.concatenate(
        [b[features].astype(f32) + b[features + 1].astype(f32) for b in blocks]
    )
    weight_own = jnp.concatenate(
        [heads_of(key_value_weight[:, :inner], s), heads_of(key_value_weight[:, inner:], s)], axis=1
    )
    width = 2 * part
    projected = lax.dot_general(
        scaled_all, weight_own, (((0,), (0,)), ((), ())), preferred_element_type=f32
    )

    shift_part = jnp.dot(modulation_shift, key_value_weight, preferred_element_type=f32)
    for bit in req_bits:
        shift_part = shift_part + swap(shift_part, "req", n_req, bit)
    for bit in bits_of(n_enc):
        shift_part = shift_part + swap(shift_part, "enc", n_enc, bit)
    shift_part = shift_part + key_value_bias.astype(f32)[None]

    def columns_of(row, share):
        return jnp.concatenate(
            [heads_of(row[:, :inner], share), heads_of(row[:, inner:], share)], axis=1
        )

    shift_rows = jnp.concatenate(
        [columns_of(shift_part, s)]
        + [swap(columns_of(shift_part, s ^ k), "seq", n_seq, k) for k in range(1, n_seq)],
        axis=0,
    )

    halves = tokens // n_req // ROWS
    split = (n_seq,) + (2,) * len(req_bits) + (halves, ROWS)
    acc = projected.reshape(split + (width,))
    acc_stat = squares_all.reshape(split)

    def with_stat_columns(data, stat):
        high, low = split_two(stat)
        lane = lax.broadcasted_iota(jnp.int32, stat.shape + (HDIM,), stat.ndim)
        columns = jnp.where(
            lane == 0, high[..., None], jnp.where(lane == 1, low[..., None], jnp.zeros((), bf16))
        )
        return jnp.concatenate([data.astype(bf16), columns], axis=-1)

    for i, bit in enumerate(req_bits):
        mine = (r // bit) % 2
        dim = len(req_bits) - i
        got = swap(
            with_stat_columns(pick(acc, 1 - mine, dim), pick(acc_stat, 1 - mine, dim)),
            "req", n_req, bit,
        ).astype(f32)
        acc = pick(acc, mine, dim) + got[..., :width]
        acc_stat = pick(acc_stat, mine, dim) + got[..., width] + got[..., width + 1]
    acc = acc.reshape(n_enc, ROWS, width)
    acc_stat = acc_stat.reshape(n_enc, ROWS)
    arrived = [
        swap(with_stat_columns(pick(acc, e ^ k, 0), pick(acc_stat, e ^ k, 0)), "enc", n_enc, k)
        .astype(f32)
        for k in range(1, n_enc)
    ]
    rows = pick(acc, e, 0)
    row_squares = pick(acc_stat, e, 0)
    for got in arrived:
        rows = rows + got[:, :width]
        row_squares = row_squares + got[:, width] + got[:, width + 1]
    rows = rows * lax.rsqrt(row_squares / model_width + epsilon_norm)[:, None]
    rows = rows + pick(shift_rows, e // halves, 0)[None]
    keys = rows[:, :part].reshape(ROWS, part // HDIM, HDIM)
    keys = keys * lax.rsqrt(jnp.mean(keys * keys, axis=2, keepdims=True) + epsilon_norm)
    text = jnp.concatenate([keys.reshape(ROWS, part), rows[:, part:]], axis=1).astype(bf16)

    chosen = request_prompt[0, 0]
    relative = s ^ chosen
    by_enc = [text] + [swap(text, "enc", n_enc, k) for k in range(1, n_enc)]
    by_enc = jnp.stack(by_enc)
    by_enc = jnp.stack([pick(by_enc, k ^ e, 0) for k in range(n_enc)])
    held = by_enc.reshape(1, n_seq, halves, ROWS, width)
    first = req_bits[0]
    held = jnp.concatenate([held, swap(held, "req", n_req, first)], axis=0)
    groups = [pick(held, relative, 1)]
    for step in range(2, n_req, 2):
        wanted = swap(relative, "req", n_req, step)
        groups.append(swap(pick(held, wanted, 1), "req", n_req, step))
    text_rows = jnp.concatenate(groups, axis=0).reshape(-1, width)
    live = pick(prompt_token_ids, chosen, 0) != 0
    live = live.reshape(n_req, halves * ROWS)
    live = jnp.concatenate([pick(live, r ^ k, 0) for k in range(n_req)])

    down = lax.dynamic_slice_in_dim(adapter_down_maps[0], s * part, part, 0).T
    up = heads_of(adapter_up_maps[0], s)
    maps = jnp.concatenate([down, up], axis=0)[None]
    for bit in reversed(req_bits):
        maps = jnp.concatenate([maps, swap(maps, "req", n_req, bit)], axis=0)
    other = adapter_of_request[0, 0] ^ r
    index = 0
    for bit in req_bits:
        index = index * 2 + (other // bit) % 2
    chosen_maps = pick(maps, index, 0)
    rank = up.shape[0]
    lowrank = lax.dot_general(
        stream, chosen_maps[:rank], (((1,), (1,)), ((), ())), preferred_element_type=f32
    ).reshape(n_seq, -1, rank)
    for bit in bits_of(n_seq):
        got = swap(lowrank, "seq", n_seq, bit)
        lowrank = lowrank + jnp.stack([got[k ^ bit] for k in range(n_seq)])
    lowrank = lowrank.reshape(-1, rank).astype(bf16)
    image_values = (
        base_values.astype(f32) + jnp.dot(lowrank, chosen_maps[rank:], preferred_element_type=f32)
    ).astype(bf16)

    mixed = attention(
        queries, text_rows[:, :part], text_rows[:, part:], image_keys, image_values, live
    ).reshape(n_seq, -1, part)
    pieces = jnp.stack([mixed[0]] + [swap(mixed[k], "seq", n_seq, k) for k in range(1, n_seq)])
    result = jnp.concatenate([pick(pieces, s ^ k, 0) for k in range(n_seq)], axis=1)
    return result[None, None]


F32, BF16 = jnp.float32, jnp.bfloat16
ANY = pl.BlockSpec(memory_space=pl.ANY)
VMEM = pl.BlockSpec(memory_space=pltpu.VMEM)
SMEM = pl.BlockSpec(memory_space=pltpu.SMEM)
NT = (((1,), (1,)), ((), ()))
TN = (((0,), (0,)), ((), ()))


def partners(send, axis, size):
    return {k: swap(send(k), axis, size, k) for k in far_first(size)}


def far_first(size):
    return [k for k in range(2, size)] + [1]


def call(kernel, outs, ins, specs=None, scratch=(), name=None, out_specs=None, vmem=16):
    return pl.pallas_call(
        kernel,
        out_shape=outs,
        in_specs=specs if specs is not None else [VMEM] * len(ins),
        out_specs=out_specs if out_specs is not None else jax.tree.map(lambda _: VMEM, outs),
        scratch_shapes=list(scratch),
        compiler_params=pltpu.CompilerParams(vmem_limit_bytes=int(vmem * 1024 * 1024)),
        name=name,
    )(*ins)


def struct(shape, dtype=BF16):
    return jax.ShapeDtypeStruct(shape, dtype)


def at(index, size):
    return pl.ds(pl.multiple_of(index * size, size), size)


def stat_rows(stat):
    high = stat.astype(BF16).astype(F32)
    row = lax.broadcasted_iota(jnp.int32, (ROWS, stat.shape[1]), 0)
    return jnp.where(row == 0, high, jnp.where(row == 1, stat - high, 0.0)).astype(BF16)


def stat_of(rows):
    rows = rows.astype(F32)
    return rows[0:1] + rows[1:2]


def context_kernel(h_ref, w_ref, b_ref, send_ref, keep_ref, stat_ref):
    mine = lax.rem(lax.axis_index("req"), 2)
    features = b_ref.shape[0]
    pairs = w_ref.shape[1] // (2 * features)
    total = jnp.zeros((1, h_ref.shape[0]), F32)
    for p in range(pairs):
        product = jnp.dot(
            h_ref[...], w_ref[:, p * 2 * features : (p + 1) * 2 * features],
            preferred_element_type=F32,
        ).T
        total = total + jnp.sum(product, axis=0, keepdims=True)
        low, high = product[:features], product[features:]
        rows = slice(p * features, (p + 1) * features)
        keep_ref[rows] = jnp.where(mine == 0, low, high)
        send_ref[rows] = jnp.where(mine == 0, high, low).astype(BF16)
    stat = total + jnp.sum(b_ref[...].astype(F32))
    send_ref[pairs * features :] = stat_rows(stat)
    stat_ref[...] = jnp.broadcast_to(stat, stat_ref.shape)


def halve_kernel(features, got_ref, keep_ref, stat_ref, send_ref, kept_ref, out_stat_ref):
    mine = lax.rem(lax.axis_index("req") // 2, 2)
    count = keep_ref.shape[0] // (2 * features)
    for i in range(count):
        rows = slice(i * features, (i + 1) * features)
        own, other = at(2 * i + mine, features), at(2 * i + 1 - mine, features)
        kept_ref[rows] = keep_ref[own] + got_ref[own].astype(F32)
        send_ref[rows] = (keep_ref[other] + got_ref[other].astype(F32)).astype(BF16)
    stat = stat_ref[0:1] + stat_of(got_ref[2 * count * features :])
    send_ref[count * features :] = stat_rows(stat)
    out_stat_ref[...] = jnp.broadcast_to(stat, out_stat_ref.shape)


def scatter_kernel(features, deps, got_ref, keep_ref, stat_ref, *refs):
    kept_ref, out_stat_ref, *send_refs = refs[deps:]
    e = lax.axis_index("enc")
    count = keep_ref.shape[0] // features
    stat = stat_ref[0:1] + stat_of(got_ref[count * features :])
    own = at(e, features)
    for k, send_ref in enumerate(send_refs):
        other = at(e ^ (k + 1), features)
        send_ref[:features] = (keep_ref[other] + got_ref[other].astype(F32)).astype(BF16)
        send_ref[features:] = stat_rows(stat)
    kept_ref[...] = keep_ref[own] + got_ref[own].astype(F32)
    out_stat_ref[...] = jnp.broadcast_to(stat, out_stat_ref.shape)


def centre_kernel(width, prompt_ref, maps_ref, image_ref, keep_ref, stat_ref, bias_ref, scale_ref, shift_ref, *refs):
    got_refs, out_ref = refs[:-1], refs[-1]
    features, tokens = keep_ref.shape
    total = keep_ref[...] + bias_ref[...]
    stat = stat_ref[0:1]
    for got_ref in got_refs:
        total = total + got_ref[:features].astype(F32)
        stat = stat + stat_of(got_ref[features:])
    centred = total - stat * (1.0 / width)
    out_ref[:features] = (scale_ref[...] * centred).astype(BF16)
    squares = jnp.sum(centred * centred, axis=0, keepdims=True)
    high = squares.astype(BF16).astype(F32)
    row = lax.broadcasted_iota(jnp.int32, (ROWS, tokens), 0)
    extra = jnp.where(row == 0, high, jnp.where(row == 1, squares - high, 0.0))
    for j in range(pl.cdiv(features, tokens)):
        piece = shift_ref[:, j * tokens : min((j + 1) * tokens, features)].astype(F32)
        gap = tokens - piece.shape[1]
        if gap:
            piece = jnp.concatenate([piece, jnp.zeros((1, gap), F32)], axis=1)
        extra = jnp.where(row == 2 + j, piece, extra)
    extra = jnp.where(row == ROWS - 1, prompt_ref[0, 0].astype(F32), extra)
    out_ref[features:] = extra.astype(BF16)


def pass_on_kernel(core_ref, got_ref, dep_ref, own_ref, next_ref):
    own_ref[...] = got_ref[0]
    next_ref[0] = core_ref[...]
    next_ref[1] = got_ref[1]


def join_kernel(own_ref, got_ref, out_ref):
    size = own_ref.shape[0]
    out_ref[:size] = own_ref[...]
    out_ref[size:] = got_ref[...]


def project_kernel(n_seq, n_req, n_enc, own_ref, pair_ref, next_ref, *refs):
    payload_refs = dict(zip([0] + far_first(n_req), refs))
    weight_refs = (own_ref, next_ref.at[0], pair_ref, next_ref.at[1])
    prompts_ref, keep_ref = refs[n_req : n_req + 2]
    send_refs = refs[n_req + 2 : -1]
    rows_ref = refs[-1]
    features, width = weight_refs[0].shape
    tokens = payload_refs[0].shape[1]
    stride = features + ROWS
    total = None
    squares = [jnp.zeros((1, tokens), F32) for _ in range(n_seq)]
    for k in range(n_req):
        left = []
        shifts = []
        for p in range(n_seq):
            payload = payload_refs[k]
            left.append(payload[p * stride : p * stride + features].T)
            extra = payload[p * stride + features : (p + 1) * stride].astype(F32)
            squares[p] = squares[p] + extra[0:1] + extra[1:2]
            pieces = [extra[2 + j : 3 + j] for j in range(pl.cdiv(features, tokens))]
            shifts.append(jnp.concatenate(pieces, axis=1)[:, :features])
            if p == 0:
                prompts_ref[k] = jnp.max(extra[ROWS - 1 : ROWS]).astype(jnp.int32)
        shifts.append(jnp.zeros((ROWS - n_seq, features), F32))
        left.append(jnp.concatenate(shifts, axis=0).astype(BF16))
        term = jnp.dot(
            jnp.concatenate(left, axis=0), weight_refs[k][...], preferred_element_type=F32
        )
        total = term if total is None else total + term
    size = n_seq * tokens // n_enc
    heads = width // HDIM
    step = heads * size + ROWS
    row = lax.broadcasted_iota(jnp.int32, (ROWS, HDIM), 0)
    for z in range(n_enc):
        p, first = divmod(z * size, tokens)
        shift = total[n_seq * tokens + p : n_seq * tokens + p + 1]
        square = squares[p][:, first : first + size]
        square = jnp.concatenate([square, jnp.zeros((1, HDIM - size), F32)], axis=1)
        high = square.astype(BF16).astype(F32)
        extra = jnp.where(
            row == 2 * heads, high, jnp.where(row == 2 * heads + 1, square - high, 0.0)
        )
        for h in range(heads):
            cols = slice(h * HDIM, (h + 1) * HDIM)
            rows_ref[z * step + h * size : z * step + (h + 1) * size] = total[
                z * size : (z + 1) * size, cols
            ]
            high = shift[:, cols].astype(BF16).astype(F32)
            extra = jnp.where(
                row == h, high, jnp.where(row == heads + h, shift[:, cols] - high, extra)
            )
        rows_ref[z * step + heads * size : (z + 1) * step] = extra
    e = lax.axis_index("enc")
    keep_ref[...] = rows_ref[at(e, step)]
    for k, send_ref in enumerate(send_refs):
        send_ref[...] = rows_ref[at(e ^ (k + 1), step)].astype(BF16)


def finish_kernel(n_req, model_width, keep_ref, bias_ref, *refs):
    got_refs, out_ref = refs[:-1], refs[-1]
    r, s = lax.axis_index("req"), lax.axis_index("seq")
    size, width = out_ref.shape
    heads = width // HDIM
    half = width // 2
    inner = bias_ref.shape[1] // 2
    total = keep_ref[...]
    for got_ref in got_refs:
        total = total + got_ref[...].astype(F32)
    extra = total[heads * size :]
    squares = extra[2 * heads : 2 * heads + 1] + extra[2 * heads + 1 : 2 * heads + 2]
    squares = jnp.broadcast_to(squares, (HDIM, HDIM)).T[:size]
    factor = lax.rsqrt(squares * (1.0 / model_width) + epsilon_norm)
    for h in range(heads):
        start = (h * HDIM // half) * inner + (s * n_req + r) * half + h * HDIM % half
        bias = bias_ref[:, pl.ds(pl.multiple_of(start, HDIM), HDIM)].astype(F32)
        shift = extra[h : h + 1] + extra[heads + h : heads + h + 1] + bias
        head = total[h * size : (h + 1) * size] * factor + shift
        if h * HDIM < half:
            head = head * lax.rsqrt(jnp.mean(head * head, axis=1, keepdims=True) + epsilon_norm)
        out_ref[:, h * HDIM : (h + 1) * HDIM] = head.astype(BF16)


def choose_kernel(n_seq, n_enc, chosen_ref, dep_ref, *refs):
    part_refs, out_refs = dict(zip([0] + far_first(n_enc), refs)), refs[n_enc:]
    e, r, s = lax.axis_index("enc"), lax.axis_index("req"), lax.axis_index("seq")
    halves = n_enc // n_seq
    size = part_refs[0].shape[0]
    for k, out_ref in enumerate(out_refs):
        prompt = s ^ chosen_ref[k]
        for h in range(halves):
            place = e ^ (prompt * halves + h)
            for j in range(n_enc):
                @pl.when(place == j)
                def _():
                    out_ref[h * size : (h + 1) * size] = part_refs[j][...]


def weight_kernel(n_req, part, inner, w_ref, dep_ref, own_ref, core_ref, pair_ref, sems):
    r, s = lax.axis_index("req"), lax.axis_index("seq")
    half = part // n_req
    copies = []
    for k, out_ref in enumerate((own_ref, core_ref, pair_ref.at[0], pair_ref.at[1])):
        for side in range(2):
            columns = pl.ds(
                pl.multiple_of(side * inner + (s * n_req + (r ^ k)) * half, HDIM), half
            )
            copies.append(
                pltpu.make_async_copy(
                    w_ref.at[:, columns],
                    out_ref.at[:, pl.ds(side * half, half)],
                    sems.at[2 * k + side],
                )
            )
    for copy in copies:
        copy.start()
    for copy in copies:
        copy.wait()


def image_kernel(part, inner, step, qk_ref, v_ref, x_ref, dep_ref, out_ref, sems):
    start = (lax.axis_index("seq") ^ step) * part
    copies = []
    for i, (ref, base) in enumerate(((qk_ref, 0), (qk_ref, inner), (v_ref, 0), (x_ref, 0))):
        columns = pl.ds(pl.multiple_of(base + start, HDIM), part)
        copies.append(pltpu.make_async_copy(ref.at[:, columns], out_ref.at[i], sems.at[i]))
    for copy in copies:
        copy.start()
    for copy in copies:
        copy.wait()


def maps_kernel(part, down_ref, up_ref, dep_ref, out_ref, sems):
    rank = down_ref.shape[0]
    columns = pl.ds(pl.multiple_of(lax.axis_index("seq") * part, HDIM), part)
    copies = [
        pltpu.make_async_copy(down_ref.at[:, columns], out_ref.at[pl.ds(0, rank)], sems.at[0]),
        pltpu.make_async_copy(up_ref.at[:, columns], out_ref.at[pl.ds(rank, rank)], sems.at[1]),
    ]
    for copy in copies:
        copy.start()
    for copy in copies:
        copy.wait()


def join_maps_kernel(own_ref, core_ref, dep_ref, out_ref):
    out_ref[0] = own_ref[...]
    out_ref[1] = core_ref[...]


def lowrank_kernel(part, adapter_ref, x_ref, got_ref, *refs):
    own_ref, pair_ref, out_ref, chosen_ref = refs
    map_refs = (own_ref.at[0], own_ref.at[1], pair_ref.at[0], pair_ref.at[1])
    place = adapter_ref[0, 0] ^ lax.axis_index("req")
    rank = out_ref.shape[-1]
    for k, ref in enumerate(map_refs):
        @pl.when(place == k)
        def _():
            chosen_ref[...] = ref[rank:]
            own = x_ref[:, pl.ds(pl.multiple_of(lax.axis_index("seq") * part, HDIM), part)]
            for i, rows in enumerate((own, got_ref[3])):
                out_ref[i] = lax.dot_general(
                    rows, ref[:rank], NT, preferred_element_type=F32
                )


def arrange_kernel(n_req, part, inner, low_ref, other_ref, maps_ref, qk_ref, v_ref, *refs):
    got_refs, (q_out, k_out, v_out) = refs[:-3], refs[-3:]
    r, s = lax.axis_index("req"), lax.axis_index("seq")
    half = part // n_req
    tokens = qk_ref.shape[0]
    low = [(low_ref[i] + other_ref[i ^ 1]).astype(BF16) for i in range(2)]
    for k in range(n_req):
        place = (r ^ k) * half
        up = maps_ref[:, pl.ds(pl.multiple_of(place, HDIM), half)]
        for i in range(len(got_refs) + 1):
            rows = slice(i * tokens, (i + 1) * tokens)
            if i == 0:
                own = s * part + place
                q = qk_ref[:, pl.ds(pl.multiple_of(own, HDIM), half)]
                key = qk_ref[:, pl.ds(pl.multiple_of(inner + own, HDIM), half)]
                base = v_ref[:, pl.ds(pl.multiple_of(own, HDIM), half)]
            else:
                columns = pl.ds(pl.multiple_of(place, HDIM), half)
                q = got_refs[i - 1][0, :, columns]
                key = got_refs[i - 1][1, :, columns]
                base = got_refs[i - 1][2, :, columns]
            q_out[k, rows] = q
            k_out[k, rows] = key
            v_out[k, rows] = (
                base.astype(F32) + jnp.dot(low[i], up, preferred_element_type=F32)
            ).astype(BF16)


def heads_kernel(place, scale, live_ref, text_ref, q_ref, k_ref, v_ref, *refs):
    out_refs = refs[2:]
    live = live_ref[...] != 0
    half = q_ref.shape[2]
    size = out_refs[0].shape[0]
    for h in range(half // HDIM):
        cols = slice(h * HDIM, (h + 1) * HDIM)
        vals = slice(half + h * HDIM, half + (h + 1) * HDIM)
        q = q_ref[place, :, cols]
        st = lax.dot_general(q, text_ref[:, cols], NT, preferred_element_type=F32) * scale
        si = lax.dot_general(q, k_ref[place, :, cols], NT, preferred_element_type=F32) * scale
        st = jnp.where(live, st, -jnp.inf)
        top = jnp.maximum(
            jnp.max(st, axis=1, keepdims=True), jnp.max(si, axis=1, keepdims=True)
        )
        wt = jnp.exp(st - top)
        wi = jnp.exp(si - top)
        total = jnp.sum(wt, axis=1, keepdims=True) + jnp.sum(wi, axis=1, keepdims=True)
        mixed = jnp.dot(
            wt.astype(BF16), text_ref[:, vals], preferred_element_type=F32
        ) + jnp.dot(wi.astype(BF16), v_ref[place, :, cols], preferred_element_type=F32)
        mixed = (mixed / total).astype(BF16)
        for i, out_ref in enumerate(out_refs):
            out_ref[:, cols] = mixed[i * size : (i + 1) * size]


def assemble_kernel(n_req, n_seq, *refs):
    out_ref = refs[-1]
    r, s = lax.axis_index("req"), lax.axis_index("seq")
    half = refs[0].shape[1]
    for k in range(n_req):
        for i in range(n_seq):
            start = ((s ^ i) * n_req + (r ^ k)) * half
            out_ref[:, pl.ds(pl.multiple_of(start, HDIM), half)] = refs[k * n_seq + i][...]


def per_device_heads(
    n_enc,
    n_req,
    n_seq,
    encoder_hidden,
    prompt_token_ids,
    context_weight,
    context_bias,
    modulation_shift,
    modulation_scale,
    key_value_weight,
    key_value_bias,
    request_prompt,
    adapter_of_request,
    adapter_down_maps,
    adapter_up_maps,
    image_stream_input,
    image_query_key,
    image_value_rows,
):
    e, r, s = lax.axis_index("enc"), lax.axis_index("req"), lax.axis_index("seq")
    model_width = context_weight.shape[1]
    features = context_bias.shape[0]
    tokens = encoder_hidden.shape[1]
    inner = key_value_weight.shape[1] // 2
    part = inner // n_seq
    half = part // n_req
    image_rows = image_query_key.shape[2]
    rank = adapter_up_maps.shape[1]
    qk, base, stream = image_query_key[0, 0], image_value_rows[0, 0], image_stream_input[0, 0]
    dma = pltpu.SemaphoreType.DMA
    stat = struct((8, tokens), F32)

    send, keep, sums = call(
        context_kernel,
        (
            struct((model_width // 2 + ROWS, tokens)),
            struct((model_width // 2, tokens), F32),
            stat,
        ),
        (encoder_hidden[0], context_weight, context_bias),
        name="context",
    )
    got = swap(send, "req", n_req, 1)

    packed = [
        call(
            functools.partial(image_kernel, part, inner, k),
            struct((4, image_rows, part)),
            (qk, base, stream, send),
            [ANY] * 4,
            [dma((4,))],
            name="image_pack",
        )
        for k in range(1, n_seq)
    ]
    image_got = [swap(packed[k - 1], "seq", n_seq, k) for k in range(1, n_seq)]
    maps = call(
        functools.partial(maps_kernel, part),
        struct((2 * rank, part)),
        (adapter_down_maps[0].T, adapter_up_maps[0], send),
        [ANY] * 3,
        [dma((2,))],
        name="maps_pack",
    )
    maps_core = swap(maps, "req", n_req, 1)
    weight = struct((features, 2 * half))
    weight_own, weight_core, weight_pair = call(
        functools.partial(weight_kernel, n_req, part, inner),
        (weight, weight, struct((2, features, 2 * half))),
        (key_value_weight, send),
        [ANY] * 2,
        [dma((2 * n_req,))],
        name="weight_pack",
    )

    send, keep, sums = call(
        functools.partial(halve_kernel, features),
        (
            struct((n_enc * features + ROWS, tokens)),
            struct((n_enc * features, tokens), F32),
            stat,
        ),
        (got, keep, sums),
        name="halve",
    )
    got = swap(send, "req", n_req, 2)
    keep, sums, *sends = call(
        functools.partial(scatter_kernel, features, 1),
        (struct((features, tokens), F32), stat)
        + tuple(struct((features + ROWS, tokens)) for _ in range(1, n_enc)),
        (got, keep, sums, weight_pair),
        [VMEM] * 3 + [ANY],
        name="scatter",
    )
    arrived = partners(lambda k: sends[k - 1], "enc", n_enc).values()
    weight_pair = lax.optimization_barrier((weight_pair, keep))[0]
    weight_pair_got = swap(weight_pair, "req", n_req, 2)

    bias_columns = jnp.broadcast_to(context_bias.astype(F32)[:, None], (features, tokens))
    scale_columns = jnp.broadcast_to(
        1.0 + modulation_scale[0].astype(F32)[:, None], (features, tokens)
    )
    own = call(
        functools.partial(centre_kernel, model_width),
        struct((features + ROWS, tokens)),
        (
            request_prompt,
            maps_core,
            image_got[0],
            keep,
            sums,
            bias_columns,
            scale_columns,
            modulation_shift,
            *arrived,
        ),
        [SMEM] + [ANY] * 2 + [VMEM] * (5 + len(arrived)),
        name="centre",
    )
    joined = call(
        join_kernel,
        struct((n_seq * (features + ROWS), tokens)),
        (own, swap(own, "seq", n_seq, 1)),
        name="join",
    )
    payloads = partners(lambda k: joined, "req", n_req)
    weight_own_pair, weight_next = call(
        pass_on_kernel,
        (weight, struct((2, features, 2 * half))),
        (weight_core, weight_pair_got, joined),
        [VMEM, VMEM, ANY],
        name="pass_on",
    )
    weight_next = swap(weight_next, "req", n_req, 1)

    size = n_seq * tokens // n_enc
    step = 2 * half // HDIM * size + ROWS
    ids, keep, *sends = call(
        functools.partial(project_kernel, n_seq, n_req, n_enc),
        (struct((n_req,), jnp.int32), struct((step, HDIM), F32))
        + tuple(struct((step, HDIM)) for _ in range(1, n_enc)),
        (weight_own, weight_own_pair, weight_next, joined, *payloads.values()),
        scratch=[pltpu.VMEM((n_enc * step, HDIM), F32)],
        out_specs=(SMEM,) + (VMEM,) * n_enc,
        name="project",
    )
    arrived = partners(lambda k: sends[k - 1], "enc", n_enc).values()

    maps = call(
        join_maps_kernel,
        struct((2, 2 * rank, part)),
        (maps, maps_core, joined),
        [VMEM, VMEM, ANY],
        name="maps_join",
    )
    maps = lax.optimization_barrier((maps, keep))[0]
    maps_pair = swap(maps, "req", n_req, 2)

    text = call(
        functools.partial(finish_kernel, n_req, model_width),
        struct((size, 2 * half)),
        (keep, key_value_bias[None], *arrived),
        [VMEM] * (2 + len(arrived)),
        name="finish",
    )
    low, chosen_maps = call(
        functools.partial(lowrank_kernel, part),
        (struct((n_seq, image_rows, rank), F32), struct((rank, part))),
        (
            adapter_of_request,
            stream,
            image_got[0],
            maps,
            maps_pair,
        ),
        [SMEM] + [VMEM] * 4,
        name="lowrank",
    )
    arranged = struct((n_req, n_seq * image_rows, half))
    queries, image_keys, image_values = call(
        functools.partial(arrange_kernel, n_req, part, inner),
        (arranged, arranged, arranged),
        (low, swap(low, "seq", n_seq, 1), chosen_maps, qk, base, *image_got),
        name="arrange",
    )
    parts = partners(lambda k: text, "enc", n_enc)
    rows = call(
        functools.partial(choose_kernel, n_seq, n_enc),
        [struct((tokens, 2 * half)) for _ in range(n_req)],
        (ids, low, text, *parts.values()),
        [SMEM, ANY] + [VMEM] * n_enc,
        name="choose",
    )
    rows = {0: rows[0], **partners(lambda k: rows[k], "req", n_req)}
    live = lax.dynamic_slice_in_dim(prompt_token_ids, request_prompt[0, 0], 1, 0)
    pieces = [None] * n_req
    last = (live, live)
    for k in range(n_req):
        mixed = call(
            functools.partial(heads_kernel, k, HDIM ** (-0.5)),
            [struct((image_rows, half))] * n_seq,
            (live, rows[k], queries, image_keys, image_values, *last),
            [VMEM] * 5 + [ANY] * 2,
            name="heads",
        )
        pieces[k] = [mixed[0], swap(mixed[1], "seq", n_seq, 1)]
        last = (mixed[0], pieces[k - 1][1] if k else live)
    result = call(
        functools.partial(assemble_kernel, n_req, n_seq),
        struct((image_rows, inner)),
        tuple(p for group in pieces for p in group),
        name="assemble",
    )
    return result[None, None]


def solution(mesh):
    sizes = mesh.shape
    n_enc, n_req, n_seq = sizes["enc"], sizes["req"], sizes["seq"]

    def run(*arrays):
        heads = arrays[6].shape[1] // (2 * HDIM)
        fits = n_seq == 2 and n_req == 4 and heads % (n_seq * n_req) == 0
        return (per_device_heads if fits else per_device)(n_enc, n_req, n_seq, *arrays)

    return jax.shard_map(
        run,
        mesh=mesh,
        in_specs=(
            P("seq", None, ("enc", "req")),
            P(),
            P(("enc", "req"), None),
            P(("enc", "req")),
            P("seq", ("enc", "req")),
            P("seq", ("enc", "req")),
            P(("enc", "req"), None),
            P(),
            P("enc", "req"),
            P("enc", "req"),
            P("req", None, None),
            P("req", None, None),
            P("enc", "req", "seq", None),
            P("enc", "req", "seq", None),
            P("enc", "req", "seq", None),
        ),
        out_specs=P("enc", "req", "seq", None),
        check_vma=False,
    )
```

```python
import functools

import jax
import jax.numpy as jnp
from jax import lax
from jax.experimental import pallas as pl
from jax.experimental.pallas import tpu as pltpu
from jax.sharding import PartitionSpec as P

HDIM = 128
ROWS = 16

epsilon_norm = 1e-06


def swap(block, axis, size, step):
    return lax.ppermute(block, axis, [(i, i ^ step) for i in range(size)])


def pick(array, index, dim):
    return lax.dynamic_index_in_dim(array, index, dim, keepdims=False)


def split_two(value):
    high = lax.reduce_precision(value, 8, 7)
    return high.astype(jnp.bfloat16), (value - high).astype(jnp.bfloat16)


def bits_of(size):
    return [1 << b for b in range(size.bit_length() - 1)]


def with_stat_rows(data, stat):
    high, low = split_two(stat)
    rows = jnp.concatenate(
        [high[None], low[None], jnp.zeros((ROWS - 2, stat.shape[0]), jnp.bfloat16)], axis=0
    )
    rows = jnp.broadcast_to(rows, data.shape[:-2] + rows.shape)
    return jnp.concatenate([data.astype(jnp.bfloat16), rows], axis=-2)


def attention_kernel(heads, inner, scale, mask_ref, q_ref, kt_ref, vt_ref, ki_ref, vi_ref, o_ref):
    live = mask_ref[...] != 0
    for h in range(heads):
        cols = slice(h * HDIM, (h + 1) * HDIM)
        q = q_ref[:, cols]
        dims = (((1,), (1,)), ((), ()))
        st = lax.dot_general(q, kt_ref[:, cols], dims, preferred_element_type=jnp.float32) * scale
        si = lax.dot_general(q, ki_ref[:, cols], dims, preferred_element_type=jnp.float32) * scale
        st = jnp.where(live, st, -jnp.inf)
        top = jnp.maximum(
            jnp.max(st, axis=1, keepdims=True), jnp.max(si, axis=1, keepdims=True)
        )
        wt = jnp.exp(st - top)
        wi = jnp.exp(si - top)
        total = jnp.sum(wt, axis=1, keepdims=True) + jnp.sum(wi, axis=1, keepdims=True)
        mixed = jnp.dot(
            wt.astype(jnp.bfloat16), vt_ref[:, cols], preferred_element_type=jnp.float32
        ) + jnp.dot(wi.astype(jnp.bfloat16), vi_ref[:, cols], preferred_element_type=jnp.float32)
        o_ref[:, cols] = (mixed / total).astype(o_ref.dtype)


def attention(queries, text_keys, text_values, image_keys, image_values, live):
    width = queries.shape[1]
    heads = width // HDIM
    rows = queries.shape[0]
    mask = jnp.broadcast_to(live.astype(jnp.int32)[None, :], (8, live.shape[0]))[:1]
    return pl.pallas_call(
        functools.partial(attention_kernel, heads, width, HDIM ** (-0.5)),
        out_shape=jax.ShapeDtypeStruct((rows, width), jnp.bfloat16),
        compiler_params=pltpu.CompilerParams(vmem_limit_bytes=48 * 1024 * 1024),
        name="attention",
    )(mask, queries, text_keys, text_values, image_keys, image_values)


def per_device(
    n_enc,
    n_req,
    n_seq,
    encoder_hidden,
    prompt_token_ids,
    context_weight,
    context_bias,
    modulation_shift,
    modulation_scale,
    key_value_weight,
    key_value_bias,
    request_prompt,
    adapter_of_request,
    adapter_down_maps,
    adapter_up_maps,
    image_stream_input,
    image_query_key,
    image_value_rows,
):
    f32, bf16 = jnp.float32, jnp.bfloat16
    e, r, s = lax.axis_index("enc"), lax.axis_index("req"), lax.axis_index("seq")
    req_bits = bits_of(n_req)
    model_width = context_weight.shape[1]
    features = context_bias.shape[0]
    tokens = encoder_hidden.shape[1]
    inner = key_value_weight.shape[1] // 2
    part = inner // n_seq

    def heads_of(array, share):
        return lax.dynamic_slice_in_dim(array, share * part, part, 1)

    qk = image_query_key[0, 0]
    sources = [qk[:, :inner], qk[:, inner:], image_value_rows[0, 0], image_stream_input[0, 0]]
    image_parts = [
        jnp.stack([heads_of(a, s ^ k) for a in sources]) for k in range(n_seq)
    ]
    image_parts = [image_parts[0]] + [
        swap(image_parts[k], "seq", n_seq, k) for k in range(1, n_seq)
    ]
    image_all = jnp.concatenate(image_parts, axis=1)
    queries, image_keys, base_values, stream = [image_all[i] for i in range(4)]

    partial_value = lax.dot_general(
        context_weight, encoder_hidden[0], (((0,), (1,)), ((), ())), preferred_element_type=f32
    )
    stat = jnp.sum(partial_value, axis=0) + jnp.sum(context_bias.astype(f32))
    acc = partial_value.reshape((n_enc,) + (2,) * len(req_bits) + (features, tokens))
    for i, bit in enumerate(req_bits):
        mine = (r // bit) % 2
        dim = len(req_bits) - i
        got = swap(with_stat_rows(pick(acc, 1 - mine, dim), stat), "req", n_req, bit).astype(f32)
        acc = pick(acc, mine, dim) + got[..., :features, :]
        got_stat = got.reshape((-1,) + got.shape[-2:])[0, features:]
        stat = stat + got_stat[0] + got_stat[1]
    arrived = [
        swap(with_stat_rows(pick(acc, e ^ k, 0), stat), "enc", n_enc, k).astype(f32)
        for k in range(1, n_enc)
    ]
    embedded = pick(acc, e, 0)
    for got in arrived:
        embedded = embedded + got[:features]
        stat = stat + got[features] + got[features + 1]
    embedded = embedded + context_bias.astype(f32)[:, None]
    centred = embedded - (stat / model_width)[None, :]
    squares = jnp.sum(centred * centred, axis=0)
    scaled = (1.0 + modulation_scale[0].astype(f32))[:, None] * centred

    own = with_stat_rows(scaled, squares)
    blocks = [own] + [swap(own, "seq", n_seq, k) for k in range(1, n_seq)]
    scaled_all = jnp.concatenate([b[:features] for b in blocks], axis=1)
    squares_all = jnp.concatenate(
        [b[features].astype(f32) + b[features + 1].astype(f32) for b in blocks]
    )
    weight_own = jnp.concatenate(
        [heads_of(key_value_weight[:, :inner], s), heads_of(key_value_weight[:, inner:], s)], axis=1
    )
    width = 2 * part
    projected = lax.dot_general(
        scaled_all, weight_own, (((0,), (0,)), ((), ())), preferred_element_type=f32
    )

    shift_part = jnp.dot(modulation_shift, key_value_weight, preferred_element_type=f32)
    for bit in req_bits:
        shift_part = shift_part + swap(shift_part, "req", n_req, bit)
    for bit in bits_of(n_enc):
        shift_part = shift_part + swap(shift_part, "enc", n_enc, bit)
    shift_part = shift_part + key_value_bias.astype(f32)[None]

    def columns_of(row, share):
        return jnp.concatenate(
            [heads_of(row[:, :inner], share), heads_of(row[:, inner:], share)], axis=1
        )

    shift_rows = jnp.concatenate(
        [columns_of(shift_part, s)]
        + [swap(columns_of(shift_part, s ^ k), "seq", n_seq, k) for k in range(1, n_seq)],
        axis=0,
    )

    halves = tokens // n_req // ROWS
    split = (n_seq,) + (2,) * len(req_bits) + (halves, ROWS)
    acc = projected.reshape(split + (width,))
    acc_stat = squares_all.reshape(split)

    def with_stat_columns(data, stat):
        high, low = split_two(stat)
        lane = lax.broadcasted_iota(jnp.int32, stat.shape + (HDIM,), stat.ndim)
        columns = jnp.where(
            lane == 0, high[..., None], jnp.where(lane == 1, low[..., None], jnp.zeros((), bf16))
        )
        return jnp.concatenate([data.astype(bf16), columns], axis=-1)

    for i, bit in enumerate(req_bits):
        mine = (r // bit) % 2
        dim = len(req_bits) - i
        got = swap(
            with_stat_columns(pick(acc, 1 - mine, dim), pick(acc_stat, 1 - mine, dim)),
            "req", n_req, bit,
        ).astype(f32)
        acc = pick(acc, mine, dim) + got[..., :width]
        acc_stat = pick(acc_stat, mine, dim) + got[..., width] + got[..., width + 1]
    acc = acc.reshape(n_enc, ROWS, width)
    acc_stat = acc_stat.reshape(n_enc, ROWS)
    arrived = [
        swap(with_stat_columns(pick(acc, e ^ k, 0), pick(acc_stat, e ^ k, 0)), "enc", n_enc, k)
        .astype(f32)
        for k in range(1, n_enc)
    ]
    rows = pick(acc, e, 0)
    row_squares = pick(acc_stat, e, 0)
    for got in arrived:
        rows = rows + got[:, :width]
        row_squares = row_squares + got[:, width] + got[:, width + 1]
    rows = rows * lax.rsqrt(row_squares / model_width + epsilon_norm)[:, None]
    rows = rows + pick(shift_rows, e // halves, 0)[None]
    keys = rows[:, :part].reshape(ROWS, part // HDIM, HDIM)
    keys = keys * lax.rsqrt(jnp.mean(keys * keys, axis=2, keepdims=True) + epsilon_norm)
    text = jnp.concatenate([keys.reshape(ROWS, part), rows[:, part:]], axis=1).astype(bf16)

    chosen = request_prompt[0, 0]
    relative = s ^ chosen
    by_enc = [text] + [swap(text, "enc", n_enc, k) for k in range(1, n_enc)]
    by_enc = jnp.stack(by_enc)
    by_enc = jnp.stack([pick(by_enc, k ^ e, 0) for k in range(n_enc)])
    held = by_enc.reshape(1, n_seq, halves, ROWS, width)
    first = req_bits[0]
    held = jnp.concatenate([held, swap(held, "req", n_req, first)], axis=0)
    groups = [pick(held, relative, 1)]
    for step in range(2, n_req, 2):
        wanted = swap(relative, "req", n_req, step)
        groups.append(swap(pick(held, wanted, 1), "req", n_req, step))
    text_rows = jnp.concatenate(groups, axis=0).reshape(-1, width)
    live = pick(prompt_token_ids, chosen, 0) != 0
    live = live.reshape(n_req, halves * ROWS)
    live = jnp.concatenate([pick(live, r ^ k, 0) for k in range(n_req)])

    down = lax.dynamic_slice_in_dim(adapter_down_maps[0], s * part, part, 0).T
    up = heads_of(adapter_up_maps[0], s)
    maps = jnp.concatenate([down, up], axis=0)[None]
    for bit in reversed(req_bits):
        maps = jnp.concatenate([maps, swap(maps, "req", n_req, bit)], axis=0)
    other = adapter_of_request[0, 0] ^ r
    index = 0
    for bit in req_bits:
        index = index * 2 + (other // bit) % 2
    chosen_maps = pick(maps, index, 0)
    rank = up.shape[0]
    lowrank = lax.dot_general(
        stream, chosen_maps[:rank], (((1,), (1,)), ((), ())), preferred_element_type=f32
    ).reshape(n_seq, -1, rank)
    for bit in bits_of(n_seq):
        got = swap(lowrank, "seq", n_seq, bit)
        lowrank = lowrank + jnp.stack([got[k ^ bit] for k in range(n_seq)])
    lowrank = lowrank.reshape(-1, rank).astype(bf16)
    image_values = (
        base_values.astype(f32) + jnp.dot(lowrank, chosen_maps[rank:], preferred_element_type=f32)
    ).astype(bf16)

    mixed = attention(
        queries, text_rows[:, :part], text_rows[:, part:], image_keys, image_values, live
    ).reshape(n_seq, -1, part)
    pieces = jnp.stack([mixed[0]] + [swap(mixed[k], "seq", n_seq, k) for k in range(1, n_seq)])
    result = jnp.concatenate([pick(pieces, s ^ k, 0) for k in range(n_seq)], axis=1)
    return result[None, None]


F32, BF16 = jnp.float32, jnp.bfloat16
ANY = pl.BlockSpec(memory_space=pl.ANY)
VMEM = pl.BlockSpec(memory_space=pltpu.VMEM)
SMEM = pl.BlockSpec(memory_space=pltpu.SMEM)
NT = (((1,), (1,)), ((), ()))
TN = (((0,), (0,)), ((), ()))


def partners(send, axis, size):
    return {k: swap(send(k), axis, size, k) for k in far_first(size)}


def far_first(size):
    return [k for k in range(2, size)] + [1]


def call(kernel, outs, ins, specs=None, scratch=(), name=None, out_specs=None, vmem=16):
    return pl.pallas_call(
        kernel,
        out_shape=outs,
        in_specs=specs if specs is not None else [VMEM] * len(ins),
        out_specs=out_specs if out_specs is not None else jax.tree.map(lambda _: VMEM, outs),
        scratch_shapes=list(scratch),
        compiler_params=pltpu.CompilerParams(vmem_limit_bytes=int(vmem * 1024 * 1024)),
        name=name,
    )(*ins)


def struct(shape, dtype=BF16):
    return jax.ShapeDtypeStruct(shape, dtype)


def at(index, size):
    return pl.ds(pl.multiple_of(index * size, size), size)


def stat_rows(stat):
    high = stat.astype(BF16).astype(F32)
    row = lax.broadcasted_iota(jnp.int32, (ROWS, stat.shape[1]), 0)
    return jnp.where(row == 0, high, jnp.where(row == 1, stat - high, 0.0)).astype(BF16)


def stat_of(rows):
    rows = rows.astype(F32)
    return rows[0:1] + rows[1:2]


def context_kernel(h_ref, w_ref, b_ref, send_ref, keep_ref, stat_ref):
    mine = lax.rem(lax.axis_index("req"), 2)
    features = b_ref.shape[0]
    pairs = w_ref.shape[1] // (2 * features)
    total = jnp.zeros((1, h_ref.shape[0]), F32)
    for p in range(pairs):
        product = jnp.dot(
            h_ref[...], w_ref[:, p * 2 * features : (p + 1) * 2 * features],
            preferred_element_type=F32,
        ).T
        total = total + jnp.sum(product, axis=0, keepdims=True)
        low, high = product[:features], product[features:]
        rows = slice(p * features, (p + 1) * features)
        keep_ref[rows] = jnp.where(mine == 0, low, high)
        send_ref[rows] = jnp.where(mine == 0, high, low).astype(BF16)
    stat = total + jnp.sum(b_ref[...].astype(F32))
    send_ref[pairs * features :] = stat_rows(stat)
    stat_ref[...] = jnp.broadcast_to(stat, stat_ref.shape)


def halve_kernel(features, got_ref, keep_ref, stat_ref, send_ref, kept_ref, out_stat_ref):
    mine = lax.rem(lax.axis_index("req") // 2, 2)
    count = keep_ref.shape[0] // (2 * features)
    for i in range(count):
        rows = slice(i * features, (i + 1) * features)
        own, other = at(2 * i + mine, features), at(2 * i + 1 - mine, features)
        kept_ref[rows] = keep_ref[own] + got_ref[own].astype(F32)
        send_ref[rows] = (keep_ref[other] + got_ref[other].astype(F32)).astype(BF16)
    stat = stat_ref[0:1] + stat_of(got_ref[2 * count * features :])
    send_ref[count * features :] = stat_rows(stat)
    out_stat_ref[...] = jnp.broadcast_to(stat, out_stat_ref.shape)


def scatter_kernel(features, deps, got_ref, keep_ref, stat_ref, *refs):
    kept_ref, out_stat_ref, *send_refs = refs[deps:]
    e = lax.axis_index("enc")
    count = keep_ref.shape[0] // features
    stat = stat_ref[0:1] + stat_of(got_ref[count * features :])
    own = at(e, features)
    for k, send_ref in enumerate(send_refs):
        other = at(e ^ (k + 1), features)
        send_ref[:features] = (keep_ref[other] + got_ref[other].astype(F32)).astype(BF16)
        send_ref[features:] = stat_rows(stat)
    kept_ref[...] = keep_ref[own] + got_ref[own].astype(F32)
    out_stat_ref[...] = jnp.broadcast_to(stat, out_stat_ref.shape)


def centre_kernel(width, prompt_ref, dep_ref, keep_ref, stat_ref, bias_ref, scale_ref, shift_ref, *refs):
    got_refs, out_ref = refs[:-1], refs[-1]
    features, tokens = keep_ref.shape
    total = keep_ref[...] + bias_ref[...]
    stat = stat_ref[0:1]
    for got_ref in got_refs:
        total = total + got_ref[:features].astype(F32)
        stat = stat + stat_of(got_ref[features:])
    centred = total - stat * (1.0 / width)
    out_ref[:features] = (scale_ref[...] * centred).astype(BF16)
    squares = jnp.sum(centred * centred, axis=0, keepdims=True)
    high = squares.astype(BF16).astype(F32)
    row = lax.broadcasted_iota(jnp.int32, (ROWS, tokens), 0)
    extra = jnp.where(row == 0, high, jnp.where(row == 1, squares - high, 0.0))
    for j in range(pl.cdiv(features, tokens)):
        piece = shift_ref[:, j * tokens : min((j + 1) * tokens, features)].astype(F32)
        gap = tokens - piece.shape[1]
        if gap:
            piece = jnp.concatenate([piece, jnp.zeros((1, gap), F32)], axis=1)
        extra = jnp.where(row == 2 + j, piece, extra)
    extra = jnp.where(row == ROWS - 1, prompt_ref[0, 0].astype(F32), extra)
    out_ref[features:] = extra.astype(BF16)


def pass_on_kernel(core_ref, got_ref, *refs):
    own_ref, next_ref = refs[-2:]
    own_ref[...] = got_ref[0]
    next_ref[0] = core_ref[...]
    next_ref[1] = got_ref[1]


def project_kernel(n_seq, n_req, n_enc, order, own_ref, pair_ref, next_ref, *refs):
    payload_refs = dict(zip([(0, 0)] + order, refs))
    weight_refs = (own_ref, next_ref.at[0], pair_ref, next_ref.at[1])
    prompts_ref, keep_ref, *send_refs = refs[n_seq * n_req : -1]
    rows_ref = refs[-1]
    features, width = weight_refs[0].shape
    tokens = payload_refs[0, 0].shape[1]
    total = None
    squares = [jnp.zeros((1, tokens), F32) for _ in range(n_seq)]
    for k in range(n_req):
        left = []
        shifts = []
        for p in range(n_seq):
            payload = payload_refs[p, k]
            left.append(payload[:features].T)
            extra = payload[features:].astype(F32)
            squares[p] = squares[p] + extra[0:1] + extra[1:2]
            pieces = [extra[2 + j : 3 + j] for j in range(pl.cdiv(features, tokens))]
            shifts.append(jnp.concatenate(pieces, axis=1)[:, :features])
            if p == 0:
                prompts_ref[k] = jnp.max(extra[ROWS - 1 : ROWS]).astype(jnp.int32)
        shifts.append(jnp.zeros((ROWS - n_seq, features), F32))
        left.append(jnp.concatenate(shifts, axis=0).astype(BF16))
        term = jnp.dot(
            jnp.concatenate(left, axis=0), weight_refs[k][...], preferred_element_type=F32
        )
        total = term if total is None else total + term
    size = n_seq * tokens // n_enc
    heads = width // HDIM
    step = heads * size + ROWS
    row = lax.broadcasted_iota(jnp.int32, (ROWS, HDIM), 0)
    for z in range(n_enc):
        p, first = divmod(z * size, tokens)
        shift = total[n_seq * tokens + p : n_seq * tokens + p + 1]
        square = squares[p][:, first : first + size]
        square = jnp.concatenate([square, jnp.zeros((1, HDIM - size), F32)], axis=1)
        high = square.astype(BF16).astype(F32)
        extra = jnp.where(
            row == 2 * heads, high, jnp.where(row == 2 * heads + 1, square - high, 0.0)
        )
        for h in range(heads):
            cols = slice(h * HDIM, (h + 1) * HDIM)
            rows_ref[z * step + h * size : z * step + (h + 1) * size] = total[
                z * size : (z + 1) * size, cols
            ]
            high = shift[:, cols].astype(BF16).astype(F32)
            extra = jnp.where(
                row == h, high, jnp.where(row == heads + h, shift[:, cols] - high, extra)
            )
        rows_ref[z * step + heads * size : (z + 1) * step] = extra
    e = lax.axis_index("enc")
    keep_ref[...] = rows_ref[at(e, step)]
    for k, send_ref in enumerate(send_refs):
        send_ref[...] = rows_ref[at(e ^ (k + 1), step)].astype(BF16)


def finish_kernel(n_req, model_width, keep_ref, bias_ref, *refs):
    got_refs, out_ref = refs[:-1], refs[-1]
    r, s = lax.axis_index("req"), lax.axis_index("seq")
    size, width = out_ref.shape
    heads = width // HDIM
    half = width // 2
    inner = bias_ref.shape[1] // 2
    total = keep_ref[...]
    for got_ref in got_refs:
        total = total + got_ref[...].astype(F32)
    extra = total[heads * size :]
    squares = extra[2 * heads : 2 * heads + 1] + extra[2 * heads + 1 : 2 * heads + 2]
    squares = jnp.broadcast_to(squares, (HDIM, HDIM)).T[:size]
    factor = lax.rsqrt(squares * (1.0 / model_width) + epsilon_norm)
    for h in range(heads):
        start = (h * HDIM // half) * inner + (s * n_req + r) * half + h * HDIM % half
        bias = bias_ref[:, pl.ds(pl.multiple_of(start, HDIM), HDIM)].astype(F32)
        shift = extra[h : h + 1] + extra[heads + h : heads + h + 1] + bias
        head = total[h * size : (h + 1) * size] * factor + shift
        if h * HDIM < half:
            head = head * lax.rsqrt(jnp.mean(head * head, axis=1, keepdims=True) + epsilon_norm)
        out_ref[:, h * HDIM : (h + 1) * HDIM] = head.astype(BF16)


def choose_kernel(n_seq, n_enc, chosen_ref, dep_ref, *refs):
    part_refs, out_refs = dict(zip([0] + far_first(n_enc), refs)), refs[n_enc:]
    e, r, s = lax.axis_index("enc"), lax.axis_index("req"), lax.axis_index("seq")
    halves = n_enc // n_seq
    size = part_refs[0].shape[0]
    for k, out_ref in enumerate(out_refs):
        prompt = s ^ chosen_ref[k]
        for h in range(halves):
            place = e ^ (prompt * halves + h)
            for j in range(n_enc):
                @pl.when(place == j)
                def _():
                    out_ref[h * size : (h + 1) * size] = part_refs[j][...]


def weight_kernel(n_req, part, inner, w_ref, dep_ref, own_ref, core_ref, pair_ref, sems):
    r, s = lax.axis_index("req"), lax.axis_index("seq")
    half = part // n_req
    copies = []
    for k, out_ref in enumerate((own_ref, core_ref, pair_ref.at[0], pair_ref.at[1])):
        for side in range(2):
            columns = pl.ds(
                pl.multiple_of(side * inner + (s * n_req + (r ^ k)) * half, HDIM), half
            )
            copies.append(
                pltpu.make_async_copy(
                    w_ref.at[:, columns],
                    out_ref.at[:, pl.ds(side * half, half)],
                    sems.at[2 * k + side],
                )
            )
    for copy in copies:
        copy.start()
    for copy in copies:
        copy.wait()


def image_kernel(part, inner, step, qk_ref, v_ref, x_ref, dep_ref, out_ref, sems):
    start = (lax.axis_index("seq") ^ step) * part
    copies = []
    for i, (ref, base) in enumerate(((qk_ref, 0), (qk_ref, inner), (v_ref, 0), (x_ref, 0))):
        columns = pl.ds(pl.multiple_of(base + start, HDIM), part)
        copies.append(pltpu.make_async_copy(ref.at[:, columns], out_ref.at[i], sems.at[i]))
    for copy in copies:
        copy.start()
    for copy in copies:
        copy.wait()


def maps_kernel(part, down_ref, up_ref, dep_ref, out_ref, sems):
    rank = down_ref.shape[0]
    columns = pl.ds(pl.multiple_of(lax.axis_index("seq") * part, HDIM), part)
    copies = [
        pltpu.make_async_copy(down_ref.at[:, columns], out_ref.at[pl.ds(0, rank)], sems.at[0]),
        pltpu.make_async_copy(up_ref.at[:, columns], out_ref.at[pl.ds(rank, rank)], sems.at[1]),
    ]
    for copy in copies:
        copy.start()
    for copy in copies:
        copy.wait()


def join_maps_kernel(own_ref, core_ref, dep_ref, out_ref):
    out_ref[0] = own_ref[...]
    out_ref[1] = core_ref[...]


def lowrank_kernel(part, adapter_ref, x_ref, got_ref, *refs):
    own_ref, pair_ref, out_ref, chosen_ref = refs
    map_refs = (own_ref.at[0], own_ref.at[1], pair_ref.at[0], pair_ref.at[1])
    place = adapter_ref[0, 0] ^ lax.axis_index("req")
    rank = out_ref.shape[-1]
    for k, ref in enumerate(map_refs):
        @pl.when(place == k)
        def _():
            chosen_ref[...] = ref[rank:]
            own = x_ref[:, pl.ds(pl.multiple_of(lax.axis_index("seq") * part, HDIM), part)]
            for i, rows in enumerate((own, got_ref[3])):
                out_ref[i] = lax.dot_general(
                    rows, ref[:rank], NT, preferred_element_type=F32
                )


def arrange_kernel(n_req, part, inner, low_ref, other_ref, maps_ref, qk_ref, v_ref, *refs):
    got_refs, (q_out, k_out, v_out) = refs[:-3], refs[-3:]
    r, s = lax.axis_index("req"), lax.axis_index("seq")
    half = part // n_req
    tokens = qk_ref.shape[0]
    low = [(low_ref[i] + other_ref[i ^ 1]).astype(BF16) for i in range(2)]
    for k in range(n_req):
        place = (r ^ k) * half
        up = maps_ref[:, pl.ds(pl.multiple_of(place, HDIM), half)]
        for i in range(len(got_refs) + 1):
            rows = slice(i * tokens, (i + 1) * tokens)
            if i == 0:
                own = s * part + place
                q = qk_ref[:, pl.ds(pl.multiple_of(own, HDIM), half)]
                key = qk_ref[:, pl.ds(pl.multiple_of(inner + own, HDIM), half)]
                base = v_ref[:, pl.ds(pl.multiple_of(own, HDIM), half)]
            else:
                columns = pl.ds(pl.multiple_of(place, HDIM), half)
                q = got_refs[i - 1][0, :, columns]
                key = got_refs[i - 1][1, :, columns]
                base = got_refs[i - 1][2, :, columns]
            q_out[k, rows] = q
            k_out[k, rows] = key
            v_out[k, rows] = (
                base.astype(F32) + jnp.dot(low[i], up, preferred_element_type=F32)
            ).astype(BF16)


def heads_kernel(place, scale, live_ref, text_ref, q_ref, k_ref, v_ref, *refs):
    out_refs = refs[2:]
    live = live_ref[...] != 0
    half = q_ref.shape[2]
    size = out_refs[0].shape[0]
    for h in range(half // HDIM):
        cols = slice(h * HDIM, (h + 1) * HDIM)
        vals = slice(half + h * HDIM, half + (h + 1) * HDIM)
        q = q_ref[place, :, cols]
        st = lax.dot_general(q, text_ref[:, cols], NT, preferred_element_type=F32) * scale
        si = lax.dot_general(q, k_ref[place, :, cols], NT, preferred_element_type=F32) * scale
        st = jnp.where(live, st, -jnp.inf)
        top = jnp.maximum(
            jnp.max(st, axis=1, keepdims=True), jnp.max(si, axis=1, keepdims=True)
        )
        wt = jnp.exp(st - top)
        wi = jnp.exp(si - top)
        total = jnp.sum(wt, axis=1, keepdims=True) + jnp.sum(wi, axis=1, keepdims=True)
        mixed = jnp.dot(
            wt.astype(BF16), text_ref[:, vals], preferred_element_type=F32
        ) + jnp.dot(wi.astype(BF16), v_ref[place, :, cols], preferred_element_type=F32)
        mixed = (mixed / total).astype(BF16)
        for i, out_ref in enumerate(out_refs):
            out_ref[:, cols] = mixed[i * size : (i + 1) * size]


def assemble_kernel(n_req, n_seq, *refs):
    out_ref = refs[-1]
    r, s = lax.axis_index("req"), lax.axis_index("seq")
    half = refs[0].shape[1]
    for k in range(n_req):
        for i in range(n_seq):
            start = ((s ^ i) * n_req + (r ^ k)) * half
            out_ref[:, pl.ds(pl.multiple_of(start, HDIM), half)] = refs[k * n_seq + i][...]


def per_device_heads(
    n_enc,
    n_req,
    n_seq,
    encoder_hidden,
    prompt_token_ids,
    context_weight,
    context_bias,
    modulation_shift,
    modulation_scale,
    key_value_weight,
    key_value_bias,
    request_prompt,
    adapter_of_request,
    adapter_down_maps,
    adapter_up_maps,
    image_stream_input,
    image_query_key,
    image_value_rows,
):
    e, r, s = lax.axis_index("enc"), lax.axis_index("req"), lax.axis_index("seq")
    model_width = context_weight.shape[1]
    features = context_bias.shape[0]
    tokens = encoder_hidden.shape[1]
    inner = key_value_weight.shape[1] // 2
    part = inner // n_seq
    half = part // n_req
    image_rows = image_query_key.shape[2]
    rank = adapter_up_maps.shape[1]
    qk, base, stream = image_query_key[0, 0], image_value_rows[0, 0], image_stream_input[0, 0]
    dma = pltpu.SemaphoreType.DMA
    stat = struct((8, tokens), F32)

    send, keep, sums = call(
        context_kernel,
        (
            struct((model_width // 2 + ROWS, tokens)),
            struct((model_width // 2, tokens), F32),
            stat,
        ),
        (encoder_hidden[0], context_weight, context_bias),
        name="context",
    )
    got = swap(send, "req", n_req, 1)

    maps = call(
        functools.partial(maps_kernel, part),
        struct((2 * rank, part)),
        (adapter_down_maps[0].T, adapter_up_maps[0], send),
        [ANY] * 3,
        [dma((2,))],
        name="maps_pack",
    )
    maps_core = swap(maps, "req", n_req, 1)
    weight = struct((features, 2 * half))
    weight_own, weight_core, weight_pair = call(
        functools.partial(weight_kernel, n_req, part, inner),
        (weight, weight, struct((2, features, 2 * half))),
        (key_value_weight, send),
        [ANY] * 2,
        [dma((2 * n_req,))],
        name="weight_pack",
    )

    send, keep, sums = call(
        functools.partial(halve_kernel, features),
        (
            struct((n_enc * features + ROWS, tokens)),
            struct((n_enc * features, tokens), F32),
            stat,
        ),
        (got, keep, sums),
        name="halve",
    )
    got = swap(send, "req", n_req, 2)
    packed = [
        call(
            functools.partial(image_kernel, part, inner, k),
            struct((4, image_rows, part)),
            (qk, base, stream, keep),
            [ANY] * 4,
            [dma((4,))],
            name="image_pack",
        )
        for k in range(1, n_seq)
    ]
    image_got = [swap(packed[k - 1], "seq", n_seq, k) for k in range(1, n_seq)]
    keep, sums, *sends = call(
        functools.partial(scatter_kernel, features, 1),
        (struct((features, tokens), F32), stat)
        + tuple(struct((features + ROWS, tokens)) for _ in range(1, n_enc)),
        (got, keep, sums, weight_pair),
        [VMEM] * 3 + [ANY],
        name="scatter",
    )
    arrived = partners(lambda k: sends[k - 1], "enc", n_enc).values()
    weight_pair = lax.optimization_barrier((weight_pair, keep))[0]
    weight_pair_got = swap(weight_pair, "req", n_req, 2)

    bias_columns = jnp.broadcast_to(context_bias.astype(F32)[:, None], (features, tokens))
    scale_columns = jnp.broadcast_to(
        1.0 + modulation_scale[0].astype(F32)[:, None], (features, tokens)
    )
    own = call(
        functools.partial(centre_kernel, model_width),
        struct((features + ROWS, tokens)),
        (
            request_prompt,
            maps_core,
            keep,
            sums,
            bias_columns,
            scale_columns,
            modulation_shift,
            *arrived,
        ),
        [SMEM, ANY] + [VMEM] * (5 + len(arrived)),
        name="centre",
    )
    order = [(i, k) for k in far_first(n_req) + [0] for i in (1, 0) if i or k]
    payloads = {
        (i, k): lax.ppermute(
            own,
            ("seq", "req"),
            [
                (a * n_req + b, (a ^ i) * n_req + (b ^ k))
                for a in range(n_seq)
                for b in range(n_req)
            ],
        )
        for i, k in order
    }
    early = [payloads[place] for place in order[:5]]
    weight_own_pair, weight_next = call(
        pass_on_kernel,
        (weight, struct((2, features, 2 * half))),
        (weight_core, weight_pair_got, image_got[0], *early),
        [VMEM, VMEM] + [ANY] * (1 + len(early)),
        name="pass_on",
    )
    weight_next = swap(weight_next, "req", n_req, 1)

    size = n_seq * tokens // n_enc
    step = 2 * half // HDIM * size + ROWS
    ids, keep, *sends = call(
        functools.partial(project_kernel, n_seq, n_req, n_enc, order),
        (struct((n_req,), jnp.int32), struct((step, HDIM), F32))
        + tuple(struct((step, HDIM)) for _ in range(1, n_enc)),
        (weight_own, weight_own_pair, weight_next, own, *payloads.values()),
        scratch=[pltpu.VMEM((n_enc * step, HDIM), F32)],
        out_specs=(SMEM,) + (VMEM,) * n_enc,
        name="project",
    )
    arrived = partners(lambda k: sends[k - 1], "enc", n_enc).values()

    maps = call(
        join_maps_kernel,
        struct((2, 2 * rank, part)),
        (maps, maps_core, own),
        [VMEM, VMEM, ANY],
        name="maps_join",
    )
    maps = lax.optimization_barrier((maps, keep))[0]
    maps_pair = swap(maps, "req", n_req, 2)

    text = call(
        functools.partial(finish_kernel, n_req, model_width),
        struct((size, 2 * half)),
        (keep, key_value_bias[None], *arrived),
        [VMEM] * (2 + len(arrived)),
        name="finish",
    )
    low, chosen_maps = call(
        functools.partial(lowrank_kernel, part),
        (struct((n_seq, image_rows, rank), F32), struct((rank, part))),
        (
            adapter_of_request,
            stream,
            image_got[0],
            maps,
            maps_pair,
        ),
        [SMEM] + [VMEM] * 4,
        name="lowrank",
    )
    arranged = struct((n_req, n_seq * image_rows, half))
    queries, image_keys, image_values = call(
        functools.partial(arrange_kernel, n_req, part, inner),
        (arranged, arranged, arranged),
        (low, swap(low, "seq", n_seq, 1), chosen_maps, qk, base, *image_got),
        name="arrange",
    )
    parts = partners(lambda k: text, "enc", n_enc)
    rows = call(
        functools.partial(choose_kernel, n_seq, n_enc),
        [struct((tokens, 2 * half)) for _ in range(n_req)],
        (ids, image_values, text, *parts.values()),
        [SMEM, ANY] + [VMEM] * n_enc,
        name="choose",
    )
    rows = {0: rows[0], **partners(lambda k: rows[k], "req", n_req)}
    live = lax.dynamic_slice_in_dim(prompt_token_ids, request_prompt[0, 0], 1, 0)
    pieces = [None] * n_req
    last = (live, live)
    for k in range(n_req):
        mixed = call(
            functools.partial(heads_kernel, k, HDIM ** (-0.5)),
            [struct((image_rows, half))] * n_seq,
            (live, rows[k], queries, image_keys, image_values, *last),
            [VMEM] * 5 + [ANY] * 2,
            name="heads",
        )
        pieces[k] = [mixed[0], swap(mixed[1], "seq", n_seq, 1)]
        last = (mixed[0], pieces[k - 1][1] if k else live)
    result = call(
        functools.partial(assemble_kernel, n_req, n_seq),
        struct((image_rows, inner)),
        tuple(p for group in pieces for p in group),
        name="assemble",
    )
    return result[None, None]


def solution(mesh):
    sizes = mesh.shape
    n_enc, n_req, n_seq = sizes["enc"], sizes["req"], sizes["seq"]

    def run(*arrays):
        heads = arrays[6].shape[1] // (2 * HDIM)
        fits = n_seq == 2 and n_req == 4 and heads % (n_seq * n_req) == 0
        return (per_device_heads if fits else per_device)(n_enc, n_req, n_seq, *arrays)

    return jax.shard_map(
        run,
        mesh=mesh,
        in_specs=(
            P("seq", None, ("enc", "req")),
            P(),
            P(("enc", "req"), None),
            P(("enc", "req")),
            P("seq", ("enc", "req")),
            P("seq", ("enc", "req")),
            P(("enc", "req"), None),
            P(),
            P("enc", "req"),
            P("enc", "req"),
            P("req", None, None),
            P("req", None, None),
            P("enc", "req", "seq", None),
            P("enc", "req", "seq", None),
            P("enc", "req", "seq", None),
        ),
        out_specs=P("enc", "req", "seq", None),
        check_vma=False,
    )
```

```python
import functools

import jax
import jax.numpy as jnp
from jax import lax
from jax.experimental import pallas as pl
from jax.experimental.pallas import tpu as pltpu
from jax.sharding import PartitionSpec as P

HDIM = 128
ROWS = 16

epsilon_norm = 1e-06


def swap(block, axis, size, step):
    return lax.ppermute(block, axis, [(i, i ^ step) for i in range(size)])


def pick(array, index, dim):
    return lax.dynamic_index_in_dim(array, index, dim, keepdims=False)


def split_two(value):
    high = lax.reduce_precision(value, 8, 7)
    return high.astype(jnp.bfloat16), (value - high).astype(jnp.bfloat16)


def bits_of(size):
    return [1 << b for b in range(size.bit_length() - 1)]


def with_stat_rows(data, stat):
    high, low = split_two(stat)
    rows = jnp.concatenate(
        [high[None], low[None], jnp.zeros((ROWS - 2, stat.shape[0]), jnp.bfloat16)], axis=0
    )
    rows = jnp.broadcast_to(rows, data.shape[:-2] + rows.shape)
    return jnp.concatenate([data.astype(jnp.bfloat16), rows], axis=-2)


def attention_kernel(heads, inner, scale, mask_ref, q_ref, kt_ref, vt_ref, ki_ref, vi_ref, o_ref):
    live = mask_ref[...] != 0
    for h in range(heads):
        cols = slice(h * HDIM, (h + 1) * HDIM)
        q = q_ref[:, cols]
        dims = (((1,), (1,)), ((), ()))
        st = lax.dot_general(q, kt_ref[:, cols], dims, preferred_element_type=jnp.float32) * scale
        si = lax.dot_general(q, ki_ref[:, cols], dims, preferred_element_type=jnp.float32) * scale
        st = jnp.where(live, st, -jnp.inf)
        top = jnp.maximum(
            jnp.max(st, axis=1, keepdims=True), jnp.max(si, axis=1, keepdims=True)
        )
        wt = jnp.exp(st - top)
        wi = jnp.exp(si - top)
        total = jnp.sum(wt, axis=1, keepdims=True) + jnp.sum(wi, axis=1, keepdims=True)
        mixed = jnp.dot(
            wt.astype(jnp.bfloat16), vt_ref[:, cols], preferred_element_type=jnp.float32
        ) + jnp.dot(wi.astype(jnp.bfloat16), vi_ref[:, cols], preferred_element_type=jnp.float32)
        o_ref[:, cols] = (mixed / total).astype(o_ref.dtype)


def attention(queries, text_keys, text_values, image_keys, image_values, live):
    width = queries.shape[1]
    heads = width // HDIM
    rows = queries.shape[0]
    mask = jnp.broadcast_to(live.astype(jnp.int32)[None, :], (8, live.shape[0]))[:1]
    return pl.pallas_call(
        functools.partial(attention_kernel, heads, width, HDIM ** (-0.5)),
        out_shape=jax.ShapeDtypeStruct((rows, width), jnp.bfloat16),
        compiler_params=pltpu.CompilerParams(vmem_limit_bytes=48 * 1024 * 1024),
        name="attention",
    )(mask, queries, text_keys, text_values, image_keys, image_values)


def per_device(
    n_enc,
    n_req,
    n_seq,
    encoder_hidden,
    prompt_token_ids,
    context_weight,
    context_bias,
    modulation_shift,
    modulation_scale,
    key_value_weight,
    key_value_bias,
    request_prompt,
    adapter_of_request,
    adapter_down_maps,
    adapter_up_maps,
    image_stream_input,
    image_query_key,
    image_value_rows,
):
    f32, bf16 = jnp.float32, jnp.bfloat16
    e, r, s = lax.axis_index("enc"), lax.axis_index("req"), lax.axis_index("seq")
    req_bits = bits_of(n_req)
    model_width = context_weight.shape[1]
    features = context_bias.shape[0]
    tokens = encoder_hidden.shape[1]
    inner = key_value_weight.shape[1] // 2
    part = inner // n_seq

    def heads_of(array, share):
        return lax.dynamic_slice_in_dim(array, share * part, part, 1)

    qk = image_query_key[0, 0]
    sources = [qk[:, :inner], qk[:, inner:], image_value_rows[0, 0], image_stream_input[0, 0]]
    image_parts = [
        jnp.stack([heads_of(a, s ^ k) for a in sources]) for k in range(n_seq)
    ]
    image_parts = [image_parts[0]] + [
        swap(image_parts[k], "seq", n_seq, k) for k in range(1, n_seq)
    ]
    image_all = jnp.concatenate(image_parts, axis=1)
    queries, image_keys, base_values, stream = [image_all[i] for i in range(4)]

    partial_value = lax.dot_general(
        context_weight, encoder_hidden[0], (((0,), (1,)), ((), ())), preferred_element_type=f32
    )
    stat = jnp.sum(partial_value, axis=0) + jnp.sum(context_bias.astype(f32))
    acc = partial_value.reshape((n_enc,) + (2,) * len(req_bits) + (features, tokens))
    for i, bit in enumerate(req_bits):
        mine = (r // bit) % 2
        dim = len(req_bits) - i
        got = swap(with_stat_rows(pick(acc, 1 - mine, dim), stat), "req", n_req, bit).astype(f32)
        acc = pick(acc, mine, dim) + got[..., :features, :]
        got_stat = got.reshape((-1,) + got.shape[-2:])[0, features:]
        stat = stat + got_stat[0] + got_stat[1]
    arrived = [
        swap(with_stat_rows(pick(acc, e ^ k, 0), stat), "enc", n_enc, k).astype(f32)
        for k in range(1, n_enc)
    ]
    embedded = pick(acc, e, 0)
    for got in arrived:
        embedded = embedded + got[:features]
        stat = stat + got[features] + got[features + 1]
    embedded = embedded + context_bias.astype(f32)[:, None]
    centred = embedded - (stat / model_width)[None, :]
    squares = jnp.sum(centred * centred, axis=0)
    scaled = (1.0 + modulation_scale[0].astype(f32))[:, None] * centred

    own = with_stat_rows(scaled, squares)
    blocks = [own] + [swap(own, "seq", n_seq, k) for k in range(1, n_seq)]
    scaled_all = jnp.concatenate([b[:features] for b in blocks], axis=1)
    squares_all = jnp.concatenate(
        [b[features].astype(f32) + b[features + 1].astype(f32) for b in blocks]
    )
    weight_own = jnp.concatenate(
        [heads_of(key_value_weight[:, :inner], s), heads_of(key_value_weight[:, inner:], s)], axis=1
    )
    width = 2 * part
    projected = lax.dot_general(
        scaled_all, weight_own, (((0,), (0,)), ((), ())), preferred_element_type=f32
    )

    shift_part = jnp.dot(modulation_shift, key_value_weight, preferred_element_type=f32)
    for bit in req_bits:
        shift_part = shift_part + swap(shift_part, "req", n_req, bit)
    for bit in bits_of(n_enc):
        shift_part = shift_part + swap(shift_part, "enc", n_enc, bit)
    shift_part = shift_part + key_value_bias.astype(f32)[None]

    def columns_of(row, share):
        return jnp.concatenate(
            [heads_of(row[:, :inner], share), heads_of(row[:, inner:], share)], axis=1
        )

    shift_rows = jnp.concatenate(
        [columns_of(shift_part, s)]
        + [swap(columns_of(shift_part, s ^ k), "seq", n_seq, k) for k in range(1, n_seq)],
        axis=0,
    )

    halves = tokens // n_req // ROWS
    split = (n_seq,) + (2,) * len(req_bits) + (halves, ROWS)
    acc = projected.reshape(split + (width,))
    acc_stat = squares_all.reshape(split)

    def with_stat_columns(data, stat):
        high, low = split_two(stat)
        lane = lax.broadcasted_iota(jnp.int32, stat.shape + (HDIM,), stat.ndim)
        columns = jnp.where(
            lane == 0, high[..., None], jnp.where(lane == 1, low[..., None], jnp.zeros((), bf16))
        )
        return jnp.concatenate([data.astype(bf16), columns], axis=-1)

    for i, bit in enumerate(req_bits):
        mine = (r // bit) % 2
        dim = len(req_bits) - i
        got = swap(
            with_stat_columns(pick(acc, 1 - mine, dim), pick(acc_stat, 1 - mine, dim)),
            "req", n_req, bit,
        ).astype(f32)
        acc = pick(acc, mine, dim) + got[..., :width]
        acc_stat = pick(acc_stat, mine, dim) + got[..., width] + got[..., width + 1]
    acc = acc.reshape(n_enc, ROWS, width)
    acc_stat = acc_stat.reshape(n_enc, ROWS)
    arrived = [
        swap(with_stat_columns(pick(acc, e ^ k, 0), pick(acc_stat, e ^ k, 0)), "enc", n_enc, k)
        .astype(f32)
        for k in range(1, n_enc)
    ]
    rows = pick(acc, e, 0)
    row_squares = pick(acc_stat, e, 0)
    for got in arrived:
        rows = rows + got[:, :width]
        row_squares = row_squares + got[:, width] + got[:, width + 1]
    rows = rows * lax.rsqrt(row_squares / model_width + epsilon_norm)[:, None]
    rows = rows + pick(shift_rows, e // halves, 0)[None]
    keys = rows[:, :part].reshape(ROWS, part // HDIM, HDIM)
    keys = keys * lax.rsqrt(jnp.mean(keys * keys, axis=2, keepdims=True) + epsilon_norm)
    text = jnp.concatenate([keys.reshape(ROWS, part), rows[:, part:]], axis=1).astype(bf16)

    chosen = request_prompt[0, 0]
    relative = s ^ chosen
    by_enc = [text] + [swap(text, "enc", n_enc, k) for k in range(1, n_enc)]
    by_enc = jnp.stack(by_enc)
    by_enc = jnp.stack([pick(by_enc, k ^ e, 0) for k in range(n_enc)])
    held = by_enc.reshape(1, n_seq, halves, ROWS, width)
    first = req_bits[0]
    held = jnp.concatenate([held, swap(held, "req", n_req, first)], axis=0)
    groups = [pick(held, relative, 1)]
    for step in range(2, n_req, 2):
        wanted = swap(relative, "req", n_req, step)
        groups.append(swap(pick(held, wanted, 1), "req", n_req, step))
    text_rows = jnp.concatenate(groups, axis=0).reshape(-1, width)
    live = pick(prompt_token_ids, chosen, 0) != 0
    live = live.reshape(n_req, halves * ROWS)
    live = jnp.concatenate([pick(live, r ^ k, 0) for k in range(n_req)])

    down = lax.dynamic_slice_in_dim(adapter_down_maps[0], s * part, part, 0).T
    up = heads_of(adapter_up_maps[0], s)
    maps = jnp.concatenate([down, up], axis=0)[None]
    for bit in reversed(req_bits):
        maps = jnp.concatenate([maps, swap(maps, "req", n_req, bit)], axis=0)
    other = adapter_of_request[0, 0] ^ r
    index = 0
    for bit in req_bits:
        index = index * 2 + (other // bit) % 2
    chosen_maps = pick(maps, index, 0)
    rank = up.shape[0]
    lowrank = lax.dot_general(
        stream, chosen_maps[:rank], (((1,), (1,)), ((), ())), preferred_element_type=f32
    ).reshape(n_seq, -1, rank)
    for bit in bits_of(n_seq):
        got = swap(lowrank, "seq", n_seq, bit)
        lowrank = lowrank + jnp.stack([got[k ^ bit] for k in range(n_seq)])
    lowrank = lowrank.reshape(-1, rank).astype(bf16)
    image_values = (
        base_values.astype(f32) + jnp.dot(lowrank, chosen_maps[rank:], preferred_element_type=f32)
    ).astype(bf16)

    mixed = attention(
        queries, text_rows[:, :part], text_rows[:, part:], image_keys, image_values, live
    ).reshape(n_seq, -1, part)
    pieces = jnp.stack([mixed[0]] + [swap(mixed[k], "seq", n_seq, k) for k in range(1, n_seq)])
    result = jnp.concatenate([pick(pieces, s ^ k, 0) for k in range(n_seq)], axis=1)
    return result[None, None]


F32, BF16 = jnp.float32, jnp.bfloat16
ANY = pl.BlockSpec(memory_space=pl.ANY)
VMEM = pl.BlockSpec(memory_space=pltpu.VMEM)
SMEM = pl.BlockSpec(memory_space=pltpu.SMEM)
NT = (((1,), (1,)), ((), ()))
TN = (((0,), (0,)), ((), ()))


def partners(send, axis, size):
    return {k: swap(send(k), axis, size, k) for k in far_first(size)}


def far_first(size):
    return [k for k in range(2, size)] + [1]


def call(kernel, outs, ins, specs=None, scratch=(), name=None, out_specs=None, vmem=16):
    return pl.pallas_call(
        kernel,
        out_shape=outs,
        in_specs=specs if specs is not None else [VMEM] * len(ins),
        out_specs=out_specs if out_specs is not None else jax.tree.map(lambda _: VMEM, outs),
        scratch_shapes=list(scratch),
        compiler_params=pltpu.CompilerParams(vmem_limit_bytes=int(vmem * 1024 * 1024)),
        name=name,
    )(*ins)


def struct(shape, dtype=BF16):
    return jax.ShapeDtypeStruct(shape, dtype)


def at(index, size):
    return pl.ds(pl.multiple_of(index * size, size), size)


def stat_rows(stat):
    high = stat.astype(BF16).astype(F32)
    row = lax.broadcasted_iota(jnp.int32, (ROWS, stat.shape[1]), 0)
    return jnp.where(row == 0, high, jnp.where(row == 1, stat - high, 0.0)).astype(BF16)


def stat_of(rows):
    rows = rows.astype(F32)
    return rows[0:1] + rows[1:2]


def context_kernel(h_ref, w_ref, b_ref, send_ref, keep_ref, stat_ref):
    mine = lax.rem(lax.axis_index("req"), 2)
    features = b_ref.shape[0]
    pairs = w_ref.shape[1] // (2 * features)
    total = jnp.zeros((1, h_ref.shape[0]), F32)
    for p in range(pairs):
        product = jnp.dot(
            h_ref[...], w_ref[:, p * 2 * features : (p + 1) * 2 * features],
            preferred_element_type=F32,
        ).T
        total = total + jnp.sum(product, axis=0, keepdims=True)
        low, high = product[:features], product[features:]
        rows = slice(p * features, (p + 1) * features)
        keep_ref[rows] = jnp.where(mine == 0, low, high)
        send_ref[rows] = jnp.where(mine == 0, high, low).astype(BF16)
    stat = total + jnp.sum(b_ref[...].astype(F32))
    send_ref[pairs * features :] = stat_rows(stat)
    stat_ref[...] = jnp.broadcast_to(stat, stat_ref.shape)


def scatter_kernel(features, deps, got_ref, keep_ref, stat_ref, *refs):
    kept_ref, out_stat_ref, *send_refs = refs[deps:]
    e = lax.axis_index("enc")
    count = keep_ref.shape[0] // features
    stat = stat_ref[0:1] + stat_of(got_ref[count * features :])
    own = at(e, features)
    for k, send_ref in enumerate(send_refs):
        other = at(e ^ (k + 1), features)
        send_ref[:features] = (keep_ref[other] + got_ref[other].astype(F32)).astype(BF16)
        send_ref[features:] = stat_rows(stat)
    kept_ref[...] = keep_ref[own] + got_ref[own].astype(F32)
    out_stat_ref[...] = jnp.broadcast_to(stat, out_stat_ref.shape)


def lane_rows(rows, first, values, extra):
    tokens = extra.shape[1]
    for j in range(pl.cdiv(values.shape[1], tokens)):
        piece = values[:, j * tokens : min((j + 1) * tokens, values.shape[1])]
        gap = tokens - piece.shape[1]
        if gap:
            piece = jnp.concatenate([piece, jnp.zeros((1, gap), F32)], axis=1)
        extra = jnp.where(rows == first + j, piece, extra)
    return extra


def from_rows(extra, first, count):
    tokens = extra.shape[1]
    pieces = [extra[first + j : first + j + 1] for j in range(pl.cdiv(count, tokens))]
    return jnp.concatenate(pieces, axis=1)[:, :count]


def merge_kernel(deps, prompt_ref, keep_ref, stat_ref, bias_ref, scale_ref, shift_ref, *refs):
    got_refs, (send_ref, kept_ref, out_stat_ref) = refs[deps:-3], refs[-3:]
    features, tokens = bias_ref.shape
    mine = lax.rem(lax.axis_index("req") // 2, 2)
    total = keep_ref[...]
    stat = stat_ref[0:1]
    for got_ref in got_refs:
        total = total + got_ref[: 2 * features].astype(F32)
        stat = stat + stat_of(got_ref[2 * features :])
    kept_ref[...] = total
    own = at(mine, features)
    kept_ref[own] = kept_ref[own] + bias_ref[...]
    send_ref[: 2 * features] = kept_ref[...].astype(BF16)
    rows = lax.broadcasted_iota(jnp.int32, (ROWS, tokens), 0)
    extra = stat_rows(stat).astype(F32)
    extra = lane_rows(rows, 2, scale_ref[...].astype(F32), extra)
    extra = lane_rows(rows, 6, shift_ref[...].astype(F32), extra)
    extra = jnp.where(rows == ROWS - 1, prompt_ref[0, 0].astype(F32), extra)
    send_ref[2 * features :] = extra.astype(BF16)
    out_stat_ref[...] = jnp.broadcast_to(stat, out_stat_ref.shape)


def centre_kernel(
    width, prompt_ref, dep_ref, keep_ref, stat_ref, got_ref, scale_ref, shift_ref, out_ref
):
    features, tokens = scale_ref.shape
    mine = lax.rem(lax.axis_index("req") // 2, 2)
    extra = got_ref[2 * features :].astype(F32)
    stat = stat_ref[0:1] + extra[0:1] + extra[1:2]
    average = stat * (1.0 / width)
    scale = from_rows(extra, 2, features)
    columns = []
    for first in range(0, features, tokens):
        piece = scale[:, first : min(first + tokens, features)]
        piece = jnp.broadcast_to(piece, (tokens, piece.shape[1]))
        gap = tokens - piece.shape[1]
        if gap:
            piece = jnp.concatenate([piece, jnp.zeros((tokens, gap), F32)], axis=1)
        columns.append(piece.T[: min(tokens, features - first)])
    scales = (scale_ref[...], 1.0 + jnp.concatenate(columns, axis=0))
    squares = jnp.zeros((1, tokens), F32)
    for i in range(2):
        block = at(mine ^ i, features)
        centred = keep_ref[block] + got_ref[block].astype(F32) - average
        squares = squares + jnp.sum(centred * centred, axis=0, keepdims=True)
        out_ref[i * features : (i + 1) * features] = (scales[i] * centred).astype(BF16)
    shift = jnp.concatenate([shift_ref[...].astype(F32), from_rows(extra, 6, features)], axis=1)
    other_prompt = extra[ROWS - 1 : ROWS]
    rows = lax.broadcasted_iota(jnp.int32, (ROWS, tokens), 0)
    extra = stat_rows(squares).astype(F32)
    extra = lane_rows(rows, 2, shift, extra)
    extra = jnp.where(rows == ROWS - 1, prompt_ref[0, 0].astype(F32), extra)
    extra = jnp.where(rows == ROWS - 2, other_prompt, extra)
    out_ref[2 * features :] = extra.astype(BF16)


def pass_on_kernel(own_ref, core_ref, got_ref, dep_ref, mine_ref, next_ref):
    features = own_ref.shape[0]
    mine_ref[:features] = own_ref[...]
    mine_ref[features:] = got_ref[0]
    next_ref[:features] = core_ref[...]
    next_ref[features:] = got_ref[1]


def join_kernel(own_ref, got_ref, out_ref):
    size = own_ref.shape[0]
    out_ref[:size] = own_ref[...]
    out_ref[size:] = got_ref[...]


def project_kernel(n_seq, n_enc, *refs):
    payload_refs, weight_refs, refs = refs[:2], refs[2:4], refs[4:]
    prompts_ref, keep_ref, *send_refs = refs[:-1]
    rows_ref = refs[-1]
    features, width = weight_refs[0].shape
    tokens = payload_refs[0].shape[1]
    stride = features + ROWS
    total = None
    squares = [jnp.zeros((1, tokens), F32) for _ in range(n_seq)]
    for k, (payload, weight_ref) in enumerate(zip(payload_refs, weight_refs)):
        left = []
        shifts = []
        for p in range(n_seq):
            left.append(payload[p * stride : p * stride + features].T)
            extra = payload[p * stride + features : (p + 1) * stride].astype(F32)
            squares[p] = squares[p] + extra[0:1] + extra[1:2]
            shifts.append(from_rows(extra, 2, features))
            if p == 0:
                prompts_ref[k] = jnp.max(extra[ROWS - 1 : ROWS]).astype(jnp.int32)
                prompts_ref[2 + k] = jnp.max(extra[ROWS - 2 : ROWS - 1]).astype(jnp.int32)
        shifts.append(jnp.zeros((ROWS - n_seq, features), F32))
        left.append(jnp.concatenate(shifts, axis=0).astype(BF16))
        term = jnp.dot(
            jnp.concatenate(left, axis=0), weight_ref[...], preferred_element_type=F32
        )
        total = term if total is None else total + term
    size = n_seq * tokens // n_enc
    heads = width // HDIM
    step = heads * size + ROWS
    row = lax.broadcasted_iota(jnp.int32, (ROWS, HDIM), 0)
    for z in range(n_enc):
        p, first = divmod(z * size, tokens)
        shift = total[n_seq * tokens + p : n_seq * tokens + p + 1]
        square = squares[p][:, first : first + size]
        square = jnp.concatenate([square, jnp.zeros((1, HDIM - size), F32)], axis=1)
        high = square.astype(BF16).astype(F32)
        extra = jnp.where(
            row == 2 * heads, high, jnp.where(row == 2 * heads + 1, square - high, 0.0)
        )
        for h in range(heads):
            cols = slice(h * HDIM, (h + 1) * HDIM)
            rows_ref[z * step + h * size : z * step + (h + 1) * size] = total[
                z * size : (z + 1) * size, cols
            ]
            high = shift[:, cols].astype(BF16).astype(F32)
            extra = jnp.where(
                row == h, high, jnp.where(row == heads + h, shift[:, cols] - high, extra)
            )
        rows_ref[z * step + heads * size : (z + 1) * step] = extra
    e = lax.axis_index("enc")
    keep_ref[...] = rows_ref[at(e, step)]
    for k, send_ref in enumerate(send_refs):
        send_ref[...] = rows_ref[at(e ^ (k + 1), step)].astype(BF16)


def finish_kernel(n_req, model_width, keep_ref, bias_ref, *refs):
    got_refs, out_ref = refs[:-1], refs[-1]
    r, s = lax.axis_index("req"), lax.axis_index("seq")
    size, width = out_ref.shape
    heads = width // HDIM
    half = width // 2
    inner = bias_ref.shape[1] // 2
    total = keep_ref[...]
    for got_ref in got_refs:
        total = total + got_ref[...].astype(F32)
    extra = total[heads * size :]
    squares = extra[2 * heads : 2 * heads + 1] + extra[2 * heads + 1 : 2 * heads + 2]
    squares = jnp.broadcast_to(squares, (HDIM, HDIM)).T[:size]
    factor = lax.rsqrt(squares * (1.0 / model_width) + epsilon_norm)
    for h in range(heads):
        start = (h * HDIM // half) * inner + (s * n_req + r) * half + h * HDIM % half
        bias = bias_ref[:, pl.ds(pl.multiple_of(start, HDIM), HDIM)].astype(F32)
        shift = extra[h : h + 1] + extra[heads + h : heads + h + 1] + bias
        head = total[h * size : (h + 1) * size] * factor + shift
        if h * HDIM < half:
            head = head * lax.rsqrt(jnp.mean(head * head, axis=1, keepdims=True) + epsilon_norm)
        out_ref[:, h * HDIM : (h + 1) * HDIM] = head.astype(BF16)


def choose_kernel(n_seq, n_enc, chosen_ref, dep_ref, *refs):
    part_refs, out_refs = dict(zip([0] + far_first(n_enc), refs)), refs[n_enc:]
    e, r, s = lax.axis_index("enc"), lax.axis_index("req"), lax.axis_index("seq")
    halves = n_enc // n_seq
    size = part_refs[0].shape[0]
    for k, out_ref in enumerate(out_refs):
        prompt = s ^ chosen_ref[k]
        for h in range(halves):
            place = e ^ (prompt * halves + h)
            for j in range(n_enc):
                @pl.when(place == j)
                def _():
                    out_ref[h * size : (h + 1) * size] = part_refs[j][...]


def weight_kernel(n_req, part, inner, w_ref, dep_ref, own_ref, core_ref, pair_ref, sems):
    r, s = lax.axis_index("req"), lax.axis_index("seq")
    half = part // n_req
    copies = []
    for k, out_ref in enumerate((own_ref, core_ref, pair_ref.at[0], pair_ref.at[1])):
        for side in range(2):
            columns = pl.ds(
                pl.multiple_of(side * inner + (s * n_req + (r ^ k)) * half, HDIM), half
            )
            copies.append(
                pltpu.make_async_copy(
                    w_ref.at[:, columns],
                    out_ref.at[:, pl.ds(side * half, half)],
                    sems.at[2 * k + side],
                )
            )
    for copy in copies:
        copy.start()
    for copy in copies:
        copy.wait()


def image_kernel(part, inner, step, qk_ref, v_ref, x_ref, dep_ref, out_ref, sems):
    start = (lax.axis_index("seq") ^ step) * part
    copies = []
    for i, (ref, base) in enumerate(((qk_ref, 0), (qk_ref, inner), (v_ref, 0), (x_ref, 0))):
        columns = pl.ds(pl.multiple_of(base + start, HDIM), part)
        copies.append(pltpu.make_async_copy(ref.at[:, columns], out_ref.at[i], sems.at[i]))
    for copy in copies:
        copy.start()
    for copy in copies:
        copy.wait()


def maps_kernel(part, down_ref, up_ref, dep_ref, out_ref, sems):
    rank = down_ref.shape[0]
    columns = pl.ds(pl.multiple_of(lax.axis_index("seq") * part, HDIM), part)
    copies = [
        pltpu.make_async_copy(down_ref.at[:, columns], out_ref.at[pl.ds(0, rank)], sems.at[0]),
        pltpu.make_async_copy(up_ref.at[:, columns], out_ref.at[pl.ds(rank, rank)], sems.at[1]),
    ]
    for copy in copies:
        copy.start()
    for copy in copies:
        copy.wait()


def join_maps_kernel(own_ref, core_ref, dep_ref, out_ref):
    out_ref[0] = own_ref[...]
    out_ref[1] = core_ref[...]


def lowrank_kernel(part, adapter_ref, x_ref, got_ref, *refs):
    own_ref, pair_ref, out_ref, chosen_ref = refs
    map_refs = (own_ref.at[0], own_ref.at[1], pair_ref.at[0], pair_ref.at[1])
    place = adapter_ref[0, 0] ^ lax.axis_index("req")
    rank = out_ref.shape[-1]
    for k, ref in enumerate(map_refs):
        @pl.when(place == k)
        def _():
            chosen_ref[...] = ref[rank:]
            own = x_ref[:, pl.ds(pl.multiple_of(lax.axis_index("seq") * part, HDIM), part)]
            for i, rows in enumerate((own, got_ref[3])):
                out_ref[i] = lax.dot_general(
                    rows, ref[:rank], NT, preferred_element_type=F32
                )


def arrange_kernel(n_req, part, inner, low_ref, other_ref, maps_ref, qk_ref, v_ref, *refs):
    got_refs, (q_out, k_out, v_out) = refs[:-3], refs[-3:]
    r, s = lax.axis_index("req"), lax.axis_index("seq")
    half = part // n_req
    tokens = qk_ref.shape[0]
    low = [(low_ref[i] + other_ref[i ^ 1]).astype(BF16) for i in range(2)]
    for k in range(n_req):
        place = (r ^ k) * half
        up = maps_ref[:, pl.ds(pl.multiple_of(place, HDIM), half)]
        for i in range(len(got_refs) + 1):
            rows = slice(i * tokens, (i + 1) * tokens)
            if i == 0:
                own = s * part + place
                q = qk_ref[:, pl.ds(pl.multiple_of(own, HDIM), half)]
                key = qk_ref[:, pl.ds(pl.multiple_of(inner + own, HDIM), half)]
                base = v_ref[:, pl.ds(pl.multiple_of(own, HDIM), half)]
            else:
                columns = pl.ds(pl.multiple_of(place, HDIM), half)
                q = got_refs[i - 1][0, :, columns]
                key = got_refs[i - 1][1, :, columns]
                base = got_refs[i - 1][2, :, columns]
            q_out[k, rows] = q
            k_out[k, rows] = key
            v_out[k, rows] = (
                base.astype(F32) + jnp.dot(low[i], up, preferred_element_type=F32)
            ).astype(BF16)


def heads_kernel(place, scale, live_ref, text_ref, q_ref, k_ref, v_ref, *refs):
    out_refs = refs[2:]
    live = live_ref[...] != 0
    half = q_ref.shape[2]
    size = out_refs[0].shape[0]
    for h in range(half // HDIM):
        cols = slice(h * HDIM, (h + 1) * HDIM)
        vals = slice(half + h * HDIM, half + (h + 1) * HDIM)
        q = q_ref[place, :, cols]
        st = lax.dot_general(q, text_ref[:, cols], NT, preferred_element_type=F32) * scale
        si = lax.dot_general(q, k_ref[place, :, cols], NT, preferred_element_type=F32) * scale
        st = jnp.where(live, st, -jnp.inf)
        top = jnp.maximum(
            jnp.max(st, axis=1, keepdims=True), jnp.max(si, axis=1, keepdims=True)
        )
        wt = jnp.exp(st - top)
        wi = jnp.exp(si - top)
        total = jnp.sum(wt, axis=1, keepdims=True) + jnp.sum(wi, axis=1, keepdims=True)
        mixed = jnp.dot(
            wt.astype(BF16), text_ref[:, vals], preferred_element_type=F32
        ) + jnp.dot(wi.astype(BF16), v_ref[place, :, cols], preferred_element_type=F32)
        mixed = (mixed / total).astype(BF16)
        for i, out_ref in enumerate(out_refs):
            out_ref[:, cols] = mixed[i * size : (i + 1) * size]


def assemble_kernel(n_req, n_seq, *refs):
    out_ref = refs[-1]
    r, s = lax.axis_index("req"), lax.axis_index("seq")
    half = refs[0].shape[1]
    for k in range(n_req):
        for i in range(n_seq):
            start = ((s ^ i) * n_req + (r ^ k)) * half
            out_ref[:, pl.ds(pl.multiple_of(start, HDIM), half)] = refs[k * n_seq + i][...]


def per_device_heads(
    n_enc,
    n_req,
    n_seq,
    encoder_hidden,
    prompt_token_ids,
    context_weight,
    context_bias,
    modulation_shift,
    modulation_scale,
    key_value_weight,
    key_value_bias,
    request_prompt,
    adapter_of_request,
    adapter_down_maps,
    adapter_up_maps,
    image_stream_input,
    image_query_key,
    image_value_rows,
):
    e, r, s = lax.axis_index("enc"), lax.axis_index("req"), lax.axis_index("seq")
    model_width = context_weight.shape[1]
    features = context_bias.shape[0]
    tokens = encoder_hidden.shape[1]
    inner = key_value_weight.shape[1] // 2
    part = inner // n_seq
    half = part // n_req
    image_rows = image_query_key.shape[2]
    rank = adapter_up_maps.shape[1]
    qk, base, stream = image_query_key[0, 0], image_value_rows[0, 0], image_stream_input[0, 0]
    dma = pltpu.SemaphoreType.DMA
    stat = struct((8, tokens), F32)

    send, keep, sums = call(
        context_kernel,
        (
            struct((model_width // 2 + ROWS, tokens)),
            struct((model_width // 2, tokens), F32),
            stat,
        ),
        (encoder_hidden[0], context_weight, context_bias),
        name="context",
    )
    got = swap(send, "req", n_req, 1)

    keep, sums, *sends = call(
        functools.partial(scatter_kernel, 2 * features, 0),
        (struct((2 * features, tokens), F32), stat)
        + tuple(struct((2 * features + ROWS, tokens)) for _ in range(1, n_enc)),
        (got, keep, sums),
        name="scatter",
    )
    arrived = partners(lambda k: sends[k - 1], "enc", n_enc).values()
    weight = struct((features, 2 * half))
    weight_own, weight_core, weight_pair = call(
        functools.partial(weight_kernel, n_req, part, inner),
        (weight, weight, struct((2, features, 2 * half))),
        (key_value_weight, keep),
        [ANY] * 2,
        [dma((2 * n_req,))],
        name="weight_pack",
        vmem=16,
    )

    weight_pair_got = swap(weight_pair, "req", n_req, 2)
    bias_columns = jnp.broadcast_to(context_bias.astype(F32)[:, None], (features, tokens))
    scale_columns = jnp.broadcast_to(
        1.0 + modulation_scale[0].astype(F32)[:, None], (features, tokens)
    )
    deps = ()
    send, keep, sums = call(
        functools.partial(merge_kernel, len(deps)),
        (
            struct((2 * features + ROWS, tokens)),
            struct((2 * features, tokens), F32),
            stat,
        ),
        (
            request_prompt,
            keep,
            sums,
            bias_columns,
            modulation_scale,
            modulation_shift,
            *deps,
            *arrived,
        ),
        [SMEM] + [VMEM] * 5 + [ANY] * len(deps) + [VMEM] * len(arrived),
        name="merge",
    )
    got = swap(send, "req", n_req, 2)
    weights = struct((2 * features, 2 * half))
    weight_mine, weight_next = call(
        pass_on_kernel,
        (weights, weights),
        (weight_own, weight_core, weight_pair_got, keep),
        [VMEM] * 3 + [ANY],
        name="pass_on",
    )
    weight_next = swap(weight_next, "req", n_req, 1)
    own = call(
        functools.partial(centre_kernel, model_width),
        struct((2 * features + ROWS, tokens)),
        (request_prompt, weight_mine, keep, sums, got, scale_columns, modulation_shift),
        [SMEM, ANY] + [VMEM] * 5,
        name="centre",
    )
    joined = call(
        join_kernel,
        struct((n_seq * (2 * features + ROWS), tokens)),
        (own, swap(own, "seq", n_seq, 1)),
        name="join",
    )
    packed = [
        call(
            functools.partial(image_kernel, part, inner, k),
            struct((4, image_rows, part)),
            (qk, base, stream, joined),
            [ANY] * 4,
            [dma((4,))],
            name="image_pack",
        )
        for k in range(1, n_seq)
    ]
    image_got = [swap(packed[k - 1], "seq", n_seq, k) for k in range(1, n_seq)]
    weight_pair = lax.optimization_barrier((weight_pair, keep))[0]
    joined_core = swap(joined, "req", n_req, 1)
    maps = call(
        functools.partial(maps_kernel, part),
        struct((2 * rank, part)),
        (adapter_down_maps[0].T, adapter_up_maps[0], joined),
        [ANY] * 3,
        [dma((2,))],
        name="maps_pack",
    )
    maps_core = swap(maps, "req", n_req, 1)
    maps = call(
        join_maps_kernel,
        struct((2, 2 * rank, part)),
        (maps, maps_core, joined),
        [VMEM, VMEM, ANY],
        name="maps_join",
    )

    size = n_seq * tokens // n_enc
    step = 2 * half // HDIM * size + ROWS
    ids, keep, *sends = call(
        functools.partial(project_kernel, n_seq, n_enc),
        (struct((n_req,), jnp.int32), struct((step, HDIM), F32))
        + tuple(struct((step, HDIM)) for _ in range(1, n_enc)),
        (joined, joined_core, weight_mine, weight_next),
        scratch=[pltpu.VMEM((n_enc * step, HDIM), F32)],
        out_specs=(SMEM,) + (VMEM,) * n_enc,
        name="project",
    )
    arrived = partners(lambda k: sends[k - 1], "enc", n_enc).values()

    maps = lax.optimization_barrier((maps, keep))[0]
    maps_pair = swap(maps, "req", n_req, 2)

    text = call(
        functools.partial(finish_kernel, n_req, model_width),
        struct((size, 2 * half)),
        (keep, key_value_bias[None], *arrived),
        [VMEM] * (2 + len(arrived)),
        name="finish",
    )
    low, chosen_maps = call(
        functools.partial(lowrank_kernel, part),
        (struct((n_seq, image_rows, rank), F32), struct((rank, part))),
        (
            adapter_of_request,
            stream,
            image_got[0],
            maps,
            maps_pair,
        ),
        [SMEM] + [VMEM] * 4,
        name="lowrank",
    )
    arranged = struct((n_req, n_seq * image_rows, half))
    queries, image_keys, image_values = call(
        functools.partial(arrange_kernel, n_req, part, inner),
        (arranged, arranged, arranged),
        (low, swap(low, "seq", n_seq, 1), chosen_maps, qk, base, *image_got),
        name="arrange",
    )
    parts = partners(lambda k: text, "enc", n_enc)
    rows = call(
        functools.partial(choose_kernel, n_seq, n_enc),
        [struct((tokens, 2 * half)) for _ in range(n_req)],
        (ids, image_values, text, *parts.values()),
        [SMEM, ANY] + [VMEM] * n_enc,
        name="choose",
    )
    rows = {0: rows[0], **partners(lambda k: rows[k], "req", n_req)}
    live = lax.dynamic_slice_in_dim(prompt_token_ids, request_prompt[0, 0], 1, 0)
    pieces = [None] * n_req
    last = (live, live)
    for k in range(n_req):
        mixed = call(
            functools.partial(heads_kernel, k, HDIM ** (-0.5)),
            [struct((image_rows, half))] * n_seq,
            (live, rows[k], queries, image_keys, image_values, *last),
            [VMEM] * 5 + [ANY] * 2,
            name="heads",
        )
        pieces[k] = [mixed[0], swap(mixed[1], "seq", n_seq, 1)]
        last = (mixed[0], pieces[k - 1][1] if k else live)
    result = call(
        functools.partial(assemble_kernel, n_req, n_seq),
        struct((image_rows, inner)),
        tuple(p for group in pieces for p in group),
        name="assemble",
    )
    return result[None, None]


def solution(mesh):
    sizes = mesh.shape
    n_enc, n_req, n_seq = sizes["enc"], sizes["req"], sizes["seq"]

    def run(*arrays):
        heads = arrays[6].shape[1] // (2 * HDIM)
        fits = n_seq == 2 and n_req == 4 and heads % (n_seq * n_req) == 0
        return (per_device_heads if fits else per_device)(n_enc, n_req, n_seq, *arrays)

    return jax.shard_map(
        run,
        mesh=mesh,
        in_specs=(
            P("seq", None, ("enc", "req")),
            P(),
            P(("enc", "req"), None),
            P(("enc", "req")),
            P("seq", ("enc", "req")),
            P("seq", ("enc", "req")),
            P(("enc", "req"), None),
            P(),
            P("enc", "req"),
            P("enc", "req"),
            P("req", None, None),
            P("req", None, None),
            P("enc", "req", "seq", None),
            P("enc", "req", "seq", None),
            P("enc", "req", "seq", None),
        ),
        out_specs=P("enc", "req", "seq", None),
        check_vma=False,
    )
```

```python
import functools

import jax
import jax.numpy as jnp
from jax import lax
from jax.experimental import pallas as pl
from jax.experimental.pallas import tpu as pltpu
from jax.sharding import PartitionSpec as P

HDIM = 128
ROWS = 16

epsilon_norm = 1e-06


def swap(block, axis, size, step):
    return lax.ppermute(block, axis, [(i, i ^ step) for i in range(size)])


def pick(array, index, dim):
    return lax.dynamic_index_in_dim(array, index, dim, keepdims=False)


def split_two(value):
    high = lax.reduce_precision(value, 8, 7)
    return high.astype(jnp.bfloat16), (value - high).astype(jnp.bfloat16)


def bits_of(size):
    return [1 << b for b in range(size.bit_length() - 1)]


def with_stat_rows(data, stat):
    high, low = split_two(stat)
    rows = jnp.concatenate(
        [high[None], low[None], jnp.zeros((ROWS - 2, stat.shape[0]), jnp.bfloat16)], axis=0
    )
    rows = jnp.broadcast_to(rows, data.shape[:-2] + rows.shape)
    return jnp.concatenate([data.astype(jnp.bfloat16), rows], axis=-2)


def attention_kernel(heads, inner, scale, mask_ref, q_ref, kt_ref, vt_ref, ki_ref, vi_ref, o_ref):
    live = mask_ref[...] != 0
    for h in range(heads):
        cols = slice(h * HDIM, (h + 1) * HDIM)
        q = q_ref[:, cols]
        dims = (((1,), (1,)), ((), ()))
        st = lax.dot_general(q, kt_ref[:, cols], dims, preferred_element_type=jnp.float32) * scale
        si = lax.dot_general(q, ki_ref[:, cols], dims, preferred_element_type=jnp.float32) * scale
        st = jnp.where(live, st, -jnp.inf)
        top = jnp.maximum(
            jnp.max(st, axis=1, keepdims=True), jnp.max(si, axis=1, keepdims=True)
        )
        wt = jnp.exp(st - top)
        wi = jnp.exp(si - top)
        total = jnp.sum(wt, axis=1, keepdims=True) + jnp.sum(wi, axis=1, keepdims=True)
        mixed = jnp.dot(
            wt.astype(jnp.bfloat16), vt_ref[:, cols], preferred_element_type=jnp.float32
        ) + jnp.dot(wi.astype(jnp.bfloat16), vi_ref[:, cols], preferred_element_type=jnp.float32)
        o_ref[:, cols] = (mixed / total).astype(o_ref.dtype)


def attention(queries, text_keys, text_values, image_keys, image_values, live):
    width = queries.shape[1]
    heads = width // HDIM
    rows = queries.shape[0]
    mask = jnp.broadcast_to(live.astype(jnp.int32)[None, :], (8, live.shape[0]))[:1]
    return pl.pallas_call(
        functools.partial(attention_kernel, heads, width, HDIM ** (-0.5)),
        out_shape=jax.ShapeDtypeStruct((rows, width), jnp.bfloat16),
        compiler_params=pltpu.CompilerParams(vmem_limit_bytes=48 * 1024 * 1024),
        name="attention",
    )(mask, queries, text_keys, text_values, image_keys, image_values)


def per_device(
    n_enc,
    n_req,
    n_seq,
    encoder_hidden,
    prompt_token_ids,
    context_weight,
    context_bias,
    modulation_shift,
    modulation_scale,
    key_value_weight,
    key_value_bias,
    request_prompt,
    adapter_of_request,
    adapter_down_maps,
    adapter_up_maps,
    image_stream_input,
    image_query_key,
    image_value_rows,
):
    f32, bf16 = jnp.float32, jnp.bfloat16
    e, r, s = lax.axis_index("enc"), lax.axis_index("req"), lax.axis_index("seq")
    req_bits = bits_of(n_req)
    model_width = context_weight.shape[1]
    features = context_bias.shape[0]
    tokens = encoder_hidden.shape[1]
    inner = key_value_weight.shape[1] // 2
    part = inner // n_seq

    def heads_of(array, share):
        return lax.dynamic_slice_in_dim(array, share * part, part, 1)

    qk = image_query_key[0, 0]
    sources = [qk[:, :inner], qk[:, inner:], image_value_rows[0, 0], image_stream_input[0, 0]]
    image_parts = [
        jnp.stack([heads_of(a, s ^ k) for a in sources]) for k in range(n_seq)
    ]
    image_parts = [image_parts[0]] + [
        swap(image_parts[k], "seq", n_seq, k) for k in range(1, n_seq)
    ]
    image_all = jnp.concatenate(image_parts, axis=1)
    queries, image_keys, base_values, stream = [image_all[i] for i in range(4)]

    partial_value = lax.dot_general(
        context_weight, encoder_hidden[0], (((0,), (1,)), ((), ())), preferred_element_type=f32
    )
    stat = jnp.sum(partial_value, axis=0) + jnp.sum(context_bias.astype(f32))
    acc = partial_value.reshape((n_enc,) + (2,) * len(req_bits) + (features, tokens))
    for i, bit in enumerate(req_bits):
        mine = (r // bit) % 2
        dim = len(req_bits) - i
        got = swap(with_stat_rows(pick(acc, 1 - mine, dim), stat), "req", n_req, bit).astype(f32)
        acc = pick(acc, mine, dim) + got[..., :features, :]
        got_stat = got.reshape((-1,) + got.shape[-2:])[0, features:]
        stat = stat + got_stat[0] + got_stat[1]
    arrived = [
        swap(with_stat_rows(pick(acc, e ^ k, 0), stat), "enc", n_enc, k).astype(f32)
        for k in range(1, n_enc)
    ]
    embedded = pick(acc, e, 0)
    for got in arrived:
        embedded = embedded + got[:features]
        stat = stat + got[features] + got[features + 1]
    embedded = embedded + context_bias.astype(f32)[:, None]
    centred = embedded - (stat / model_width)[None, :]
    squares = jnp.sum(centred * centred, axis=0)
    scaled = (1.0 + modulation_scale[0].astype(f32))[:, None] * centred

    own = with_stat_rows(scaled, squares)
    blocks = [own] + [swap(own, "seq", n_seq, k) for k in range(1, n_seq)]
    scaled_all = jnp.concatenate([b[:features] for b in blocks], axis=1)
    squares_all = jnp.concatenate(
        [b[features].astype(f32) + b[features + 1].astype(f32) for b in blocks]
    )
    weight_own = jnp.concatenate(
        [heads_of(key_value_weight[:, :inner], s), heads_of(key_value_weight[:, inner:], s)], axis=1
    )
    width = 2 * part
    projected = lax.dot_general(
        scaled_all, weight_own, (((0,), (0,)), ((), ())), preferred_element_type=f32
    )

    shift_part = jnp.dot(modulation_shift, key_value_weight, preferred_element_type=f32)
    for bit in req_bits:
        shift_part = shift_part + swap(shift_part, "req", n_req, bit)
    for bit in bits_of(n_enc):
        shift_part = shift_part + swap(shift_part, "enc", n_enc, bit)
    shift_part = shift_part + key_value_bias.astype(f32)[None]

    def columns_of(row, share):
        return jnp.concatenate(
            [heads_of(row[:, :inner], share), heads_of(row[:, inner:], share)], axis=1
        )

    shift_rows = jnp.concatenate(
        [columns_of(shift_part, s)]
        + [swap(columns_of(shift_part, s ^ k), "seq", n_seq, k) for k in range(1, n_seq)],
        axis=0,
    )

    halves = tokens // n_req // ROWS
    split = (n_seq,) + (2,) * len(req_bits) + (halves, ROWS)
    acc = projected.reshape(split + (width,))
    acc_stat = squares_all.reshape(split)

    def with_stat_columns(data, stat):
        high, low = split_two(stat)
        lane = lax.broadcasted_iota(jnp.int32, stat.shape + (HDIM,), stat.ndim)
        columns = jnp.where(
            lane == 0, high[..., None], jnp.where(lane == 1, low[..., None], jnp.zeros((), bf16))
        )
        return jnp.concatenate([data.astype(bf16), columns], axis=-1)

    for i, bit in enumerate(req_bits):
        mine = (r // bit) % 2
        dim = len(req_bits) - i
        got = swap(
            with_stat_columns(pick(acc, 1 - mine, dim), pick(acc_stat, 1 - mine, dim)),
            "req", n_req, bit,
        ).astype(f32)
        acc = pick(acc, mine, dim) + got[..., :width]
        acc_stat = pick(acc_stat, mine, dim) + got[..., width] + got[..., width + 1]
    acc = acc.reshape(n_enc, ROWS, width)
    acc_stat = acc_stat.reshape(n_enc, ROWS)
    arrived = [
        swap(with_stat_columns(pick(acc, e ^ k, 0), pick(acc_stat, e ^ k, 0)), "enc", n_enc, k)
        .astype(f32)
        for k in range(1, n_enc)
    ]
    rows = pick(acc, e, 0)
    row_squares = pick(acc_stat, e, 0)
    for got in arrived:
        rows = rows + got[:, :width]
        row_squares = row_squares + got[:, width] + got[:, width + 1]
    rows = rows * lax.rsqrt(row_squares / model_width + epsilon_norm)[:, None]
    rows = rows + pick(shift_rows, e // halves, 0)[None]
    keys = rows[:, :part].reshape(ROWS, part // HDIM, HDIM)
    keys = keys * lax.rsqrt(jnp.mean(keys * keys, axis=2, keepdims=True) + epsilon_norm)
    text = jnp.concatenate([keys.reshape(ROWS, part), rows[:, part:]], axis=1).astype(bf16)

    chosen = request_prompt[0, 0]
    relative = s ^ chosen
    by_enc = [text] + [swap(text, "enc", n_enc, k) for k in range(1, n_enc)]
    by_enc = jnp.stack(by_enc)
    by_enc = jnp.stack([pick(by_enc, k ^ e, 0) for k in range(n_enc)])
    held = by_enc.reshape(1, n_seq, halves, ROWS, width)
    first = req_bits[0]
    held = jnp.concatenate([held, swap(held, "req", n_req, first)], axis=0)
    groups = [pick(held, relative, 1)]
    for step in range(2, n_req, 2):
        wanted = swap(relative, "req", n_req, step)
        groups.append(swap(pick(held, wanted, 1), "req", n_req, step))
    text_rows = jnp.concatenate(groups, axis=0).reshape(-1, width)
    live = pick(prompt_token_ids, chosen, 0) != 0
    live = live.reshape(n_req, halves * ROWS)
    live = jnp.concatenate([pick(live, r ^ k, 0) for k in range(n_req)])

    down = lax.dynamic_slice_in_dim(adapter_down_maps[0], s * part, part, 0).T
    up = heads_of(adapter_up_maps[0], s)
    maps = jnp.concatenate([down, up], axis=0)[None]
    for bit in reversed(req_bits):
        maps = jnp.concatenate([maps, swap(maps, "req", n_req, bit)], axis=0)
    other = adapter_of_request[0, 0] ^ r
    index = 0
    for bit in req_bits:
        index = index * 2 + (other // bit) % 2
    chosen_maps = pick(maps, index, 0)
    rank = up.shape[0]
    lowrank = lax.dot_general(
        stream, chosen_maps[:rank], (((1,), (1,)), ((), ())), preferred_element_type=f32
    ).reshape(n_seq, -1, rank)
    for bit in bits_of(n_seq):
        got = swap(lowrank, "seq", n_seq, bit)
        lowrank = lowrank + jnp.stack([got[k ^ bit] for k in range(n_seq)])
    lowrank = lowrank.reshape(-1, rank).astype(bf16)
    image_values = (
        base_values.astype(f32) + jnp.dot(lowrank, chosen_maps[rank:], preferred_element_type=f32)
    ).astype(bf16)

    mixed = attention(
        queries, text_rows[:, :part], text_rows[:, part:], image_keys, image_values, live
    ).reshape(n_seq, -1, part)
    pieces = jnp.stack([mixed[0]] + [swap(mixed[k], "seq", n_seq, k) for k in range(1, n_seq)])
    result = jnp.concatenate([pick(pieces, s ^ k, 0) for k in range(n_seq)], axis=1)
    return result[None, None]


F32, BF16 = jnp.float32, jnp.bfloat16
ANY = pl.BlockSpec(memory_space=pl.ANY)
VMEM = pl.BlockSpec(memory_space=pltpu.VMEM)
SMEM = pl.BlockSpec(memory_space=pltpu.SMEM)
NT = (((1,), (1,)), ((), ()))
TN = (((0,), (0,)), ((), ()))


def partners(send, axis, size):
    return {k: swap(send(k), axis, size, k) for k in far_first(size)}


def far_first(size):
    return [k for k in range(2, size)] + [1]


def call(kernel, outs, ins, specs=None, scratch=(), name=None, out_specs=None, vmem=16):
    return pl.pallas_call(
        kernel,
        out_shape=outs,
        in_specs=specs if specs is not None else [VMEM] * len(ins),
        out_specs=out_specs if out_specs is not None else jax.tree.map(lambda _: VMEM, outs),
        scratch_shapes=list(scratch),
        compiler_params=pltpu.CompilerParams(vmem_limit_bytes=int(vmem * 1024 * 1024)),
        name=name,
    )(*ins)


def struct(shape, dtype=BF16):
    return jax.ShapeDtypeStruct(shape, dtype)


def at(index, size):
    return pl.ds(pl.multiple_of(index * size, size), size)


def stat_rows(stat):
    high = stat.astype(BF16).astype(F32)
    row = lax.broadcasted_iota(jnp.int32, (ROWS, stat.shape[1]), 0)
    return jnp.where(row == 0, high, jnp.where(row == 1, stat - high, 0.0)).astype(BF16)


def stat_of(rows):
    rows = rows.astype(F32)
    return rows[0:1] + rows[1:2]


def context_kernel(h_ref, w_ref, b_ref, send_ref, keep_ref, stat_ref):
    mine = lax.rem(lax.axis_index("req"), 2)
    features = b_ref.shape[0]
    pairs = w_ref.shape[1] // (2 * features)
    total = jnp.zeros((1, h_ref.shape[0]), F32)
    for p in range(pairs):
        product = jnp.dot(
            h_ref[...], w_ref[:, p * 2 * features : (p + 1) * 2 * features],
            preferred_element_type=F32,
        ).T
        total = total + jnp.sum(product, axis=0, keepdims=True)
        low, high = product[:features], product[features:]
        rows = slice(p * features, (p + 1) * features)
        keep_ref[rows] = jnp.where(mine == 0, low, high)
        send_ref[rows] = jnp.where(mine == 0, high, low).astype(BF16)
    stat = total + jnp.sum(b_ref[...].astype(F32))
    send_ref[pairs * features :] = stat_rows(stat)
    stat_ref[...] = jnp.broadcast_to(stat, stat_ref.shape)


def scatter_kernel(features, deps, got_ref, keep_ref, stat_ref, *refs):
    kept_ref, out_stat_ref, *send_refs = refs[deps:]
    e = lax.axis_index("enc")
    count = keep_ref.shape[0] // features
    stat = stat_ref[0:1] + stat_of(got_ref[count * features :])
    own = at(e, features)
    for k, send_ref in enumerate(send_refs):
        other = at(e ^ (k + 1), features)
        send_ref[:features] = (keep_ref[other] + got_ref[other].astype(F32)).astype(BF16)
        send_ref[features:] = stat_rows(stat)
    kept_ref[...] = keep_ref[own] + got_ref[own].astype(F32)
    out_stat_ref[...] = jnp.broadcast_to(stat, out_stat_ref.shape)


def lane_rows(rows, first, values, extra):
    tokens = extra.shape[1]
    for j in range(pl.cdiv(values.shape[1], tokens)):
        piece = values[:, j * tokens : min((j + 1) * tokens, values.shape[1])]
        gap = tokens - piece.shape[1]
        if gap:
            piece = jnp.concatenate([piece, jnp.zeros((1, gap), F32)], axis=1)
        extra = jnp.where(rows == first + j, piece, extra)
    return extra


def from_rows(extra, first, count):
    tokens = extra.shape[1]
    pieces = [extra[first + j : first + j + 1] for j in range(pl.cdiv(count, tokens))]
    return jnp.concatenate(pieces, axis=1)[:, :count]


def merge_kernel(deps, prompt_ref, keep_ref, stat_ref, bias_ref, scale_ref, shift_ref, *refs):
    got_refs, (send_ref, kept_ref, out_stat_ref) = refs[deps:-3], refs[-3:]
    features, tokens = bias_ref.shape
    mine = lax.rem(lax.axis_index("req") // 2, 2)
    total = keep_ref[...]
    stat = stat_ref[0:1]
    for got_ref in got_refs:
        total = total + got_ref[: 2 * features].astype(F32)
        stat = stat + stat_of(got_ref[2 * features :])
    kept_ref[...] = total
    own = at(mine, features)
    kept_ref[own] = kept_ref[own] + bias_ref[...]
    send_ref[: 2 * features] = kept_ref[...].astype(BF16)
    rows = lax.broadcasted_iota(jnp.int32, (ROWS, tokens), 0)
    extra = stat_rows(stat).astype(F32)
    extra = lane_rows(rows, 2, scale_ref[...].astype(F32), extra)
    extra = lane_rows(rows, 6, shift_ref[...].astype(F32), extra)
    extra = jnp.where(rows == ROWS - 1, prompt_ref[0, 0].astype(F32), extra)
    send_ref[2 * features :] = extra.astype(BF16)
    out_stat_ref[...] = jnp.broadcast_to(stat, out_stat_ref.shape)


def centre_kernel(
    width, prompt_ref, dep_ref, keep_ref, stat_ref, got_ref, scale_ref, shift_ref, out_ref
):
    features, tokens = scale_ref.shape
    mine = lax.rem(lax.axis_index("req") // 2, 2)
    extra = got_ref[2 * features :].astype(F32)
    stat = stat_ref[0:1] + extra[0:1] + extra[1:2]
    average = stat * (1.0 / width)
    scale = from_rows(extra, 2, features)
    columns = []
    for first in range(0, features, tokens):
        piece = scale[:, first : min(first + tokens, features)]
        piece = jnp.broadcast_to(piece, (tokens, piece.shape[1]))
        gap = tokens - piece.shape[1]
        if gap:
            piece = jnp.concatenate([piece, jnp.zeros((tokens, gap), F32)], axis=1)
        columns.append(piece.T[: min(tokens, features - first)])
    scales = (scale_ref[...], 1.0 + jnp.concatenate(columns, axis=0))
    squares = jnp.zeros((1, tokens), F32)
    for i in range(2):
        block = at(mine ^ i, features)
        centred = keep_ref[block] + got_ref[block].astype(F32) - average
        squares = squares + jnp.sum(centred * centred, axis=0, keepdims=True)
        out_ref[i * features : (i + 1) * features] = (scales[i] * centred).astype(BF16)
    shift = jnp.concatenate([shift_ref[...].astype(F32), from_rows(extra, 6, features)], axis=1)
    other_prompt = extra[ROWS - 1 : ROWS]
    rows = lax.broadcasted_iota(jnp.int32, (ROWS, tokens), 0)
    extra = stat_rows(squares).astype(F32)
    extra = lane_rows(rows, 2, shift, extra)
    extra = jnp.where(rows == ROWS - 1, prompt_ref[0, 0].astype(F32), extra)
    extra = jnp.where(rows == ROWS - 2, other_prompt, extra)
    out_ref[2 * features :] = extra.astype(BF16)


def pass_on_kernel(own_ref, core_ref, got_ref, dep_ref, mine_ref, next_ref):
    features = own_ref.shape[0]
    mine_ref[:features] = own_ref[...]
    mine_ref[features:] = got_ref[0]
    next_ref[:features] = core_ref[...]
    next_ref[features:] = got_ref[1]


def join_kernel(own_ref, got_ref, out_ref):
    size = own_ref.shape[0]
    out_ref[:size] = own_ref[...]
    out_ref[size:] = got_ref[...]


def project_kernel(n_seq, n_enc, *refs):
    payload_refs, weight_refs, refs = refs[:2], refs[2:4], refs[4:]
    prompts_ref, keep_ref, *send_refs = refs[:-1]
    rows_ref = refs[-1]
    features, width = weight_refs[0].shape
    tokens = payload_refs[0].shape[1]
    stride = features + ROWS
    total = None
    squares = [jnp.zeros((1, tokens), F32) for _ in range(n_seq)]
    for k, (payload, weight_ref) in enumerate(zip(payload_refs, weight_refs)):
        left = []
        shifts = []
        for p in range(n_seq):
            left.append(payload[p * stride : p * stride + features].T)
            extra = payload[p * stride + features : (p + 1) * stride].astype(F32)
            squares[p] = squares[p] + extra[0:1] + extra[1:2]
            shifts.append(from_rows(extra, 2, features))
            if p == 0:
                prompts_ref[k] = jnp.max(extra[ROWS - 1 : ROWS]).astype(jnp.int32)
                prompts_ref[2 + k] = jnp.max(extra[ROWS - 2 : ROWS - 1]).astype(jnp.int32)
        shifts.append(jnp.zeros((ROWS - n_seq, features), F32))
        left.append(jnp.concatenate(shifts, axis=0).astype(BF16))
        term = jnp.dot(
            jnp.concatenate(left, axis=0), weight_ref[...], preferred_element_type=F32
        )
        total = term if total is None else total + term
    size = n_seq * tokens // n_enc
    heads = width // HDIM
    step = heads * size + ROWS
    row = lax.broadcasted_iota(jnp.int32, (ROWS, HDIM), 0)
    for z in range(n_enc):
        p, first = divmod(z * size, tokens)
        shift = total[n_seq * tokens + p : n_seq * tokens + p + 1]
        square = squares[p][:, first : first + size]
        square = jnp.concatenate([square, jnp.zeros((1, HDIM - size), F32)], axis=1)
        high = square.astype(BF16).astype(F32)
        extra = jnp.where(
            row == 2 * heads, high, jnp.where(row == 2 * heads + 1, square - high, 0.0)
        )
        for h in range(heads):
            cols = slice(h * HDIM, (h + 1) * HDIM)
            rows_ref[z * step + h * size : z * step + (h + 1) * size] = total[
                z * size : (z + 1) * size, cols
            ]
            high = shift[:, cols].astype(BF16).astype(F32)
            extra = jnp.where(
                row == h, high, jnp.where(row == heads + h, shift[:, cols] - high, extra)
            )
        rows_ref[z * step + heads * size : (z + 1) * step] = extra
    e = lax.axis_index("enc")
    keep_ref[...] = rows_ref[at(e, step)]
    for k, send_ref in enumerate(send_refs):
        send_ref[...] = rows_ref[at(e ^ (k + 1), step)].astype(BF16)


def finish_kernel(n_req, model_width, keep_ref, bias_ref, *refs):
    got_refs, out_ref = refs[:-1], refs[-1]
    r, s = lax.axis_index("req"), lax.axis_index("seq")
    size, width = out_ref.shape
    heads = width // HDIM
    half = width // 2
    inner = bias_ref.shape[1] // 2
    total = keep_ref[...]
    for got_ref in got_refs:
        total = total + got_ref[...].astype(F32)
    extra = total[heads * size :]
    squares = extra[2 * heads : 2 * heads + 1] + extra[2 * heads + 1 : 2 * heads + 2]
    squares = jnp.broadcast_to(squares, (HDIM, HDIM)).T[:size]
    factor = lax.rsqrt(squares * (1.0 / model_width) + epsilon_norm)
    for h in range(heads):
        start = (h * HDIM // half) * inner + (s * n_req + r) * half + h * HDIM % half
        bias = bias_ref[:, pl.ds(pl.multiple_of(start, HDIM), HDIM)].astype(F32)
        shift = extra[h : h + 1] + extra[heads + h : heads + h + 1] + bias
        head = total[h * size : (h + 1) * size] * factor + shift
        if h * HDIM < half:
            head = head * lax.rsqrt(jnp.mean(head * head, axis=1, keepdims=True) + epsilon_norm)
        out_ref[:, h * HDIM : (h + 1) * HDIM] = head.astype(BF16)


def choose_kernel(n_seq, n_enc, chosen_ref, dep_ref, *refs):
    part_refs, out_refs = dict(zip([0] + far_first(n_enc), refs)), refs[n_enc:]
    e, r, s = lax.axis_index("enc"), lax.axis_index("req"), lax.axis_index("seq")
    halves = n_enc // n_seq
    size = part_refs[0].shape[0]
    for k, out_ref in enumerate(out_refs):
        prompt = s ^ chosen_ref[k]
        for h in range(halves):
            place = e ^ (prompt * halves + h)
            for j in range(n_enc):
                @pl.when(place == j)
                def _():
                    out_ref[h * size : (h + 1) * size] = part_refs[j][...]


def weight_kernel(n_req, part, inner, w_ref, dep_ref, own_ref, core_ref, pair_ref, sems):
    r, s = lax.axis_index("req"), lax.axis_index("seq")
    half = part // n_req
    copies = []
    for k, out_ref in enumerate((own_ref, core_ref, pair_ref.at[0], pair_ref.at[1])):
        for side in range(2):
            columns = pl.ds(
                pl.multiple_of(side * inner + (s * n_req + (r ^ k)) * half, HDIM), half
            )
            copies.append(
                pltpu.make_async_copy(
                    w_ref.at[:, columns],
                    out_ref.at[:, pl.ds(side * half, half)],
                    sems.at[2 * k + side],
                )
            )
    for copy in copies:
        copy.start()
    for copy in copies:
        copy.wait()


def image_kernel(part, inner, step, qk_ref, v_ref, x_ref, dep_ref, out_ref, sems):
    start = (lax.axis_index("seq") ^ step) * part
    copies = []
    for i, (ref, base) in enumerate(((qk_ref, 0), (qk_ref, inner), (v_ref, 0), (x_ref, 0))):
        columns = pl.ds(pl.multiple_of(base + start, HDIM), part)
        copies.append(pltpu.make_async_copy(ref.at[:, columns], out_ref.at[i], sems.at[i]))
    for copy in copies:
        copy.start()
    for copy in copies:
        copy.wait()


def maps_kernel(part, down_ref, up_ref, dep_ref, out_ref, sems):
    rank = down_ref.shape[0]
    columns = pl.ds(pl.multiple_of(lax.axis_index("seq") * part, HDIM), part)
    copies = [
        pltpu.make_async_copy(down_ref.at[:, columns], out_ref.at[pl.ds(0, rank)], sems.at[0]),
        pltpu.make_async_copy(up_ref.at[:, columns], out_ref.at[pl.ds(rank, rank)], sems.at[1]),
    ]
    for copy in copies:
        copy.start()
    for copy in copies:
        copy.wait()


def join_maps_kernel(own_ref, core_ref, dep_ref, out_ref):
    out_ref[0] = own_ref[...]
    out_ref[1] = core_ref[...]


def lowrank_kernel(part, adapter_ref, x_ref, got_ref, *refs):
    own_ref, pair_ref, out_ref, chosen_ref = refs
    map_refs = (own_ref.at[0], own_ref.at[1], pair_ref.at[0], pair_ref.at[1])
    place = adapter_ref[0, 0] ^ lax.axis_index("req")
    rank = out_ref.shape[-1]
    for k, ref in enumerate(map_refs):
        @pl.when(place == k)
        def _():
            chosen_ref[...] = ref[rank:]
            own = x_ref[:, pl.ds(pl.multiple_of(lax.axis_index("seq") * part, HDIM), part)]
            for i, rows in enumerate((own, got_ref[3])):
                out_ref[i] = lax.dot_general(
                    rows, ref[:rank], NT, preferred_element_type=F32
                )


def arrange_kernel(n_req, part, inner, low_ref, other_ref, maps_ref, qk_ref, v_ref, *refs):
    got_refs, (q_out, k_out, v_out) = refs[:-3], refs[-3:]
    r, s = lax.axis_index("req"), lax.axis_index("seq")
    half = part // n_req
    tokens = qk_ref.shape[0]
    low = [(low_ref[i] + other_ref[i ^ 1]).astype(BF16) for i in range(2)]
    for k in range(n_req):
        place = (r ^ k) * half
        up = maps_ref[:, pl.ds(pl.multiple_of(place, HDIM), half)]
        for i in range(len(got_refs) + 1):
            rows = slice(i * tokens, (i + 1) * tokens)
            if i == 0:
                own = s * part + place
                q = qk_ref[:, pl.ds(pl.multiple_of(own, HDIM), half)]
                key = qk_ref[:, pl.ds(pl.multiple_of(inner + own, HDIM), half)]
                base = v_ref[:, pl.ds(pl.multiple_of(own, HDIM), half)]
            else:
                columns = pl.ds(pl.multiple_of(place, HDIM), half)
                q = got_refs[i - 1][0, :, columns]
                key = got_refs[i - 1][1, :, columns]
                base = got_refs[i - 1][2, :, columns]
            q_out[k, rows] = q
            k_out[k, rows] = key
            v_out[k, rows] = (
                base.astype(F32) + jnp.dot(low[i], up, preferred_element_type=F32)
            ).astype(BF16)


def heads_kernel(place, scale, live_ref, text_ref, q_ref, k_ref, v_ref, *refs):
    out_refs = refs[2:]
    live = live_ref[...] != 0
    half = q_ref.shape[2]
    size = out_refs[0].shape[0]
    for h in range(half // HDIM):
        cols = slice(h * HDIM, (h + 1) * HDIM)
        vals = slice(half + h * HDIM, half + (h + 1) * HDIM)
        q = q_ref[place, :, cols]
        st = lax.dot_general(q, text_ref[:, cols], NT, preferred_element_type=F32) * scale
        si = lax.dot_general(q, k_ref[place, :, cols], NT, preferred_element_type=F32) * scale
        st = jnp.where(live, st, -jnp.inf)
        top = jnp.maximum(
            jnp.max(st, axis=1, keepdims=True), jnp.max(si, axis=1, keepdims=True)
        )
        wt = jnp.exp(st - top)
        wi = jnp.exp(si - top)
        total = jnp.sum(wt, axis=1, keepdims=True) + jnp.sum(wi, axis=1, keepdims=True)
        mixed = jnp.dot(
            wt.astype(BF16), text_ref[:, vals], preferred_element_type=F32
        ) + jnp.dot(wi.astype(BF16), v_ref[place, :, cols], preferred_element_type=F32)
        mixed = (mixed / total).astype(BF16)
        for i, out_ref in enumerate(out_refs):
            out_ref[:, cols] = mixed[i * size : (i + 1) * size]


def assemble_kernel(n_req, n_seq, *refs):
    piece_refs, out_ref, sems = refs[:-2], refs[-2], refs[-1]
    r, s = lax.axis_index("req"), lax.axis_index("seq")
    half = piece_refs[0].shape[1]
    copies = []
    for k in range(n_req):
        for i in range(n_seq):
            start = ((s ^ i) * n_req + (r ^ k)) * half
            columns = pl.ds(pl.multiple_of(start, HDIM), half)
            copies.append(
                pltpu.make_async_copy(
                    piece_refs[k * n_seq + i], out_ref.at[:, columns], sems.at[k * n_seq + i]
                )
            )
    for copy in copies:
        copy.start()
    for copy in copies:
        copy.wait()


def per_device_heads(
    n_enc,
    n_req,
    n_seq,
    encoder_hidden,
    prompt_token_ids,
    context_weight,
    context_bias,
    modulation_shift,
    modulation_scale,
    key_value_weight,
    key_value_bias,
    request_prompt,
    adapter_of_request,
    adapter_down_maps,
    adapter_up_maps,
    image_stream_input,
    image_query_key,
    image_value_rows,
):
    e, r, s = lax.axis_index("enc"), lax.axis_index("req"), lax.axis_index("seq")
    model_width = context_weight.shape[1]
    features = context_bias.shape[0]
    tokens = encoder_hidden.shape[1]
    inner = key_value_weight.shape[1] // 2
    part = inner // n_seq
    half = part // n_req
    image_rows = image_query_key.shape[2]
    rank = adapter_up_maps.shape[1]
    qk, base, stream = image_query_key[0, 0], image_value_rows[0, 0], image_stream_input[0, 0]
    dma = pltpu.SemaphoreType.DMA
    stat = struct((8, tokens), F32)

    send, keep, sums = call(
        context_kernel,
        (
            struct((model_width // 2 + ROWS, tokens)),
            struct((model_width // 2, tokens), F32),
            stat,
        ),
        (encoder_hidden[0], context_weight, context_bias),
        name="context",
    )
    got = swap(send, "req", n_req, 1)

    keep, sums, *sends = call(
        functools.partial(scatter_kernel, 2 * features, 0),
        (struct((2 * features, tokens), F32), stat)
        + tuple(struct((2 * features + ROWS, tokens)) for _ in range(1, n_enc)),
        (got, keep, sums),
        name="scatter",
    )
    arrived = partners(lambda k: sends[k - 1], "enc", n_enc).values()
    weight = struct((features, 2 * half))
    weight_own, weight_core, weight_pair = call(
        functools.partial(weight_kernel, n_req, part, inner),
        (weight, weight, struct((2, features, 2 * half))),
        (key_value_weight, keep),
        [ANY] * 2,
        [dma((2 * n_req,))],
        name="weight_pack",
        vmem=16,
    )

    weight_pair_got = swap(weight_pair, "req", n_req, 2)
    bias_columns = jnp.broadcast_to(context_bias.astype(F32)[:, None], (features, tokens))
    scale_columns = jnp.broadcast_to(
        1.0 + modulation_scale[0].astype(F32)[:, None], (features, tokens)
    )
    deps = ()
    send, keep, sums = call(
        functools.partial(merge_kernel, len(deps)),
        (
            struct((2 * features + ROWS, tokens)),
            struct((2 * features, tokens), F32),
            stat,
        ),
        (
            request_prompt,
            keep,
            sums,
            bias_columns,
            modulation_scale,
            modulation_shift,
            *deps,
            *arrived,
        ),
        [SMEM] + [VMEM] * 5 + [ANY] * len(deps) + [VMEM] * len(arrived),
        name="merge",
    )
    got = swap(send, "req", n_req, 2)
    weights = struct((2 * features, 2 * half))
    weight_mine, weight_next = call(
        pass_on_kernel,
        (weights, weights),
        (weight_own, weight_core, weight_pair_got, keep),
        [VMEM] * 3 + [ANY],
        name="pass_on",
    )
    weight_next = swap(weight_next, "req", n_req, 1)
    own = call(
        functools.partial(centre_kernel, model_width),
        struct((2 * features + ROWS, tokens)),
        (request_prompt, weight_mine, keep, sums, got, scale_columns, modulation_shift),
        [SMEM, ANY] + [VMEM] * 5,
        name="centre",
    )
    joined = call(
        join_kernel,
        struct((n_seq * (2 * features + ROWS), tokens)),
        (own, swap(own, "seq", n_seq, 1)),
        name="join",
    )
    packed = [
        call(
            functools.partial(image_kernel, part, inner, k),
            struct((4, image_rows, part)),
            (qk, base, stream, joined),
            [ANY] * 4,
            [dma((4,))],
            name="image_pack",
        )
        for k in range(1, n_seq)
    ]
    image_got = [swap(packed[k - 1], "seq", n_seq, k) for k in range(1, n_seq)]
    weight_pair = lax.optimization_barrier((weight_pair, keep))[0]
    joined_core = swap(joined, "req", n_req, 1)
    maps = call(
        functools.partial(maps_kernel, part),
        struct((2 * rank, part)),
        (adapter_down_maps[0].T, adapter_up_maps[0], joined),
        [ANY] * 3,
        [dma((2,))],
        name="maps_pack",
    )
    maps_core = swap(maps, "req", n_req, 1)
    maps = call(
        join_maps_kernel,
        struct((2, 2 * rank, part)),
        (maps, maps_core, joined),
        [VMEM, VMEM, ANY],
        name="maps_join",
    )

    size = n_seq * tokens // n_enc
    step = 2 * half // HDIM * size + ROWS
    ids, keep, *sends = call(
        functools.partial(project_kernel, n_seq, n_enc),
        (struct((n_req,), jnp.int32), struct((step, HDIM), F32))
        + tuple(struct((step, HDIM)) for _ in range(1, n_enc)),
        (joined, joined_core, weight_mine, weight_next),
        scratch=[pltpu.VMEM((n_enc * step, HDIM), F32)],
        out_specs=(SMEM,) + (VMEM,) * n_enc,
        name="project",
    )
    arrived = partners(lambda k: sends[k - 1], "enc", n_enc).values()

    maps = lax.optimization_barrier((maps, keep))[0]
    maps_pair = swap(maps, "req", n_req, 2)

    text = call(
        functools.partial(finish_kernel, n_req, model_width),
        struct((size, 2 * half)),
        (keep, key_value_bias[None], *arrived),
        [VMEM] * (2 + len(arrived)),
        name="finish",
    )
    low, chosen_maps = call(
        functools.partial(lowrank_kernel, part),
        (struct((n_seq, image_rows, rank), F32), struct((rank, part))),
        (
            adapter_of_request,
            stream,
            image_got[0],
            maps,
            maps_pair,
        ),
        [SMEM] + [VMEM] * 4,
        name="lowrank",
    )
    arranged = struct((n_req, n_seq * image_rows, half))
    queries, image_keys, image_values = call(
        functools.partial(arrange_kernel, n_req, part, inner),
        (arranged, arranged, arranged),
        (low, swap(low, "seq", n_seq, 1), chosen_maps, qk, base, *image_got),
        name="arrange",
    )
    parts = partners(lambda k: text, "enc", n_enc)
    rows = call(
        functools.partial(choose_kernel, n_seq, n_enc),
        [struct((tokens, 2 * half)) for _ in range(n_req)],
        (ids, image_values, text, *parts.values()),
        [SMEM, ANY] + [VMEM] * n_enc,
        name="choose",
    )
    rows = {0: rows[0], **partners(lambda k: rows[k], "req", n_req)}
    live = lax.dynamic_slice_in_dim(prompt_token_ids, request_prompt[0, 0], 1, 0)
    pieces = [None] * n_req
    last = (live, live)
    sent = live
    for k in (0,2,1,3):
        mixed = call(
            functools.partial(heads_kernel, k, HDIM ** (-0.5)),
            [struct((image_rows, half))] * n_seq,
            (live, rows[k], queries, image_keys, image_values, *last),
            [VMEM] * 5 + [ANY] * 2,
            name="heads",
        )
        pieces[k] = [mixed[0], swap(mixed[1], "seq", n_seq, 1)]
        last, sent = (mixed[0], sent), pieces[k][1]
    result = call(
        functools.partial(assemble_kernel, n_req, n_seq),
        struct((image_rows, inner)),
        tuple(p for group in pieces for p in group),
        scratch=[dma((n_req * n_seq,))],
        out_specs=ANY,
        name="assemble",
    )
    return result[None, None]


def solution(mesh):
    sizes = mesh.shape
    n_enc, n_req, n_seq = sizes["enc"], sizes["req"], sizes["seq"]

    def run(*arrays):
        heads = arrays[6].shape[1] // (2 * HDIM)
        fits = n_seq == 2 and n_req == 4 and heads % (n_seq * n_req) == 0
        return (per_device_heads if fits else per_device)(n_enc, n_req, n_seq, *arrays)

    return jax.shard_map(
        run,
        mesh=mesh,
        in_specs=(
            P("seq", None, ("enc", "req")),
            P(),
            P(("enc", "req"), None),
            P(("enc", "req")),
            P("seq", ("enc", "req")),
            P("seq", ("enc", "req")),
            P(("enc", "req"), None),
            P(),
            P("enc", "req"),
            P("enc", "req"),
            P("req", None, None),
            P("req", None, None),
            P("enc", "req", "seq", None),
            P("enc", "req", "seq", None),
            P("enc", "req", "seq", None),
        ),
        out_specs=P("enc", "req", "seq", None),
        check_vma=False,
    )
```

```python
import functools

import jax
import jax.numpy as jnp
from jax import lax
from jax.experimental import pallas as pl
from jax.experimental.pallas import tpu as pltpu
from jax.sharding import PartitionSpec as P

HDIM = 128
ROWS = 16

epsilon_norm = 1e-06


def swap(block, axis, size, step):
    return lax.ppermute(block, axis, [(i, i ^ step) for i in range(size)])


def pick(array, index, dim):
    return lax.dynamic_index_in_dim(array, index, dim, keepdims=False)


def split_two(value):
    high = lax.reduce_precision(value, 8, 7)
    return high.astype(jnp.bfloat16), (value - high).astype(jnp.bfloat16)


def bits_of(size):
    return [1 << b for b in range(size.bit_length() - 1)]


def with_stat_rows(data, stat):
    high, low = split_two(stat)
    rows = jnp.concatenate(
        [high[None], low[None], jnp.zeros((ROWS - 2, stat.shape[0]), jnp.bfloat16)], axis=0
    )
    rows = jnp.broadcast_to(rows, data.shape[:-2] + rows.shape)
    return jnp.concatenate([data.astype(jnp.bfloat16), rows], axis=-2)


def attention_kernel(heads, inner, scale, mask_ref, q_ref, kt_ref, vt_ref, ki_ref, vi_ref, o_ref):
    live = mask_ref[...] != 0
    for h in range(heads):
        cols = slice(h * HDIM, (h + 1) * HDIM)
        q = q_ref[:, cols]
        dims = (((1,), (1,)), ((), ()))
        st = lax.dot_general(q, kt_ref[:, cols], dims, preferred_element_type=jnp.float32) * scale
        si = lax.dot_general(q, ki_ref[:, cols], dims, preferred_element_type=jnp.float32) * scale
        st = jnp.where(live, st, -jnp.inf)
        top = jnp.maximum(
            jnp.max(st, axis=1, keepdims=True), jnp.max(si, axis=1, keepdims=True)
        )
        wt = jnp.exp(st - top)
        wi = jnp.exp(si - top)
        total = jnp.sum(wt, axis=1, keepdims=True) + jnp.sum(wi, axis=1, keepdims=True)
        mixed = jnp.dot(
            wt.astype(jnp.bfloat16), vt_ref[:, cols], preferred_element_type=jnp.float32
        ) + jnp.dot(wi.astype(jnp.bfloat16), vi_ref[:, cols], preferred_element_type=jnp.float32)
        o_ref[:, cols] = (mixed / total).astype(o_ref.dtype)


def attention(queries, text_keys, text_values, image_keys, image_values, live):
    width = queries.shape[1]
    heads = width // HDIM
    rows = queries.shape[0]
    mask = jnp.broadcast_to(live.astype(jnp.int32)[None, :], (8, live.shape[0]))[:1]
    return pl.pallas_call(
        functools.partial(attention_kernel, heads, width, HDIM ** (-0.5)),
        out_shape=jax.ShapeDtypeStruct((rows, width), jnp.bfloat16),
        compiler_params=pltpu.CompilerParams(vmem_limit_bytes=48 * 1024 * 1024),
        name="attention",
    )(mask, queries, text_keys, text_values, image_keys, image_values)


def per_device(
    n_enc,
    n_req,
    n_seq,
    encoder_hidden,
    prompt_token_ids,
    context_weight,
    context_bias,
    modulation_shift,
    modulation_scale,
    key_value_weight,
    key_value_bias,
    request_prompt,
    adapter_of_request,
    adapter_down_maps,
    adapter_up_maps,
    image_stream_input,
    image_query_key,
    image_value_rows,
):
    f32, bf16 = jnp.float32, jnp.bfloat16
    e, r, s = lax.axis_index("enc"), lax.axis_index("req"), lax.axis_index("seq")
    req_bits = bits_of(n_req)
    model_width = context_weight.shape[1]
    features = context_bias.shape[0]
    tokens = encoder_hidden.shape[1]
    inner = key_value_weight.shape[1] // 2
    part = inner // n_seq

    def heads_of(array, share):
        return lax.dynamic_slice_in_dim(array, share * part, part, 1)

    qk = image_query_key[0, 0]
    sources = [qk[:, :inner], qk[:, inner:], image_value_rows[0, 0], image_stream_input[0, 0]]
    image_parts = [
        jnp.stack([heads_of(a, s ^ k) for a in sources]) for k in range(n_seq)
    ]
    image_parts = [image_parts[0]] + [
        swap(image_parts[k], "seq", n_seq, k) for k in range(1, n_seq)
    ]
    image_all = jnp.concatenate(image_parts, axis=1)
    queries, image_keys, base_values, stream = [image_all[i] for i in range(4)]

    partial_value = lax.dot_general(
        context_weight, encoder_hidden[0], (((0,), (1,)), ((), ())), preferred_element_type=f32
    )
    stat = jnp.sum(partial_value, axis=0) + jnp.sum(context_bias.astype(f32))
    acc = partial_value.reshape((n_enc,) + (2,) * len(req_bits) + (features, tokens))
    for i, bit in enumerate(req_bits):
        mine = (r // bit) % 2
        dim = len(req_bits) - i
        got = swap(with_stat_rows(pick(acc, 1 - mine, dim), stat), "req", n_req, bit).astype(f32)
        acc = pick(acc, mine, dim) + got[..., :features, :]
        got_stat = got.reshape((-1,) + got.shape[-2:])[0, features:]
        stat = stat + got_stat[0] + got_stat[1]
    arrived = [
        swap(with_stat_rows(pick(acc, e ^ k, 0), stat), "enc", n_enc, k).astype(f32)
        for k in range(1, n_enc)
    ]
    embedded = pick(acc, e, 0)
    for got in arrived:
        embedded = embedded + got[:features]
        stat = stat + got[features] + got[features + 1]
    embedded = embedded + context_bias.astype(f32)[:, None]
    centred = embedded - (stat / model_width)[None, :]
    squares = jnp.sum(centred * centred, axis=0)
    scaled = (1.0 + modulation_scale[0].astype(f32))[:, None] * centred

    own = with_stat_rows(scaled, squares)
    blocks = [own] + [swap(own, "seq", n_seq, k) for k in range(1, n_seq)]
    scaled_all = jnp.concatenate([b[:features] for b in blocks], axis=1)
    squares_all = jnp.concatenate(
        [b[features].astype(f32) + b[features + 1].astype(f32) for b in blocks]
    )
    weight_own = jnp.concatenate(
        [heads_of(key_value_weight[:, :inner], s), heads_of(key_value_weight[:, inner:], s)], axis=1
    )
    width = 2 * part
    projected = lax.dot_general(
        scaled_all, weight_own, (((0,), (0,)), ((), ())), preferred_element_type=f32
    )

    shift_part = jnp.dot(modulation_shift, key_value_weight, preferred_element_type=f32)
    for bit in req_bits:
        shift_part = shift_part + swap(shift_part, "req", n_req, bit)
    for bit in bits_of(n_enc):
        shift_part = shift_part + swap(shift_part, "enc", n_enc, bit)
    shift_part = shift_part + key_value_bias.astype(f32)[None]

    def columns_of(row, share):
        return jnp.concatenate(
            [heads_of(row[:, :inner], share), heads_of(row[:, inner:], share)], axis=1
        )

    shift_rows = jnp.concatenate(
        [columns_of(shift_part, s)]
        + [swap(columns_of(shift_part, s ^ k), "seq", n_seq, k) for k in range(1, n_seq)],
        axis=0,
    )

    halves = tokens // n_req // ROWS
    split = (n_seq,) + (2,) * len(req_bits) + (halves, ROWS)
    acc = projected.reshape(split + (width,))
    acc_stat = squares_all.reshape(split)

    def with_stat_columns(data, stat):
        high, low = split_two(stat)
        lane = lax.broadcasted_iota(jnp.int32, stat.shape + (HDIM,), stat.ndim)
        columns = jnp.where(
            lane == 0, high[..., None], jnp.where(lane == 1, low[..., None], jnp.zeros((), bf16))
        )
        return jnp.concatenate([data.astype(bf16), columns], axis=-1)

    for i, bit in enumerate(req_bits):
        mine = (r // bit) % 2
        dim = len(req_bits) - i
        got = swap(
            with_stat_columns(pick(acc, 1 - mine, dim), pick(acc_stat, 1 - mine, dim)),
            "req", n_req, bit,
        ).astype(f32)
        acc = pick(acc, mine, dim) + got[..., :width]
        acc_stat = pick(acc_stat, mine, dim) + got[..., width] + got[..., width + 1]
    acc = acc.reshape(n_enc, ROWS, width)
    acc_stat = acc_stat.reshape(n_enc, ROWS)
    arrived = [
        swap(with_stat_columns(pick(acc, e ^ k, 0), pick(acc_stat, e ^ k, 0)), "enc", n_enc, k)
        .astype(f32)
        for k in range(1, n_enc)
    ]
    rows = pick(acc, e, 0)
    row_squares = pick(acc_stat, e, 0)
    for got in arrived:
        rows = rows + got[:, :width]
        row_squares = row_squares + got[:, width] + got[:, width + 1]
    rows = rows * lax.rsqrt(row_squares / model_width + epsilon_norm)[:, None]
    rows = rows + pick(shift_rows, e // halves, 0)[None]
    keys = rows[:, :part].reshape(ROWS, part // HDIM, HDIM)
    keys = keys * lax.rsqrt(jnp.mean(keys * keys, axis=2, keepdims=True) + epsilon_norm)
    text = jnp.concatenate([keys.reshape(ROWS, part), rows[:, part:]], axis=1).astype(bf16)

    chosen = request_prompt[0, 0]
    relative = s ^ chosen
    by_enc = [text] + [swap(text, "enc", n_enc, k) for k in range(1, n_enc)]
    by_enc = jnp.stack(by_enc)
    by_enc = jnp.stack([pick(by_enc, k ^ e, 0) for k in range(n_enc)])
    held = by_enc.reshape(1, n_seq, halves, ROWS, width)
    first = req_bits[0]
    held = jnp.concatenate([held, swap(held, "req", n_req, first)], axis=0)
    groups = [pick(held, relative, 1)]
    for step in range(2, n_req, 2):
        wanted = swap(relative, "req", n_req, step)
        groups.append(swap(pick(held, wanted, 1), "req", n_req, step))
    text_rows = jnp.concatenate(groups, axis=0).reshape(-1, width)
    live = pick(prompt_token_ids, chosen, 0) != 0
    live = live.reshape(n_req, halves * ROWS)
    live = jnp.concatenate([pick(live, r ^ k, 0) for k in range(n_req)])

    down = lax.dynamic_slice_in_dim(adapter_down_maps[0], s * part, part, 0).T
    up = heads_of(adapter_up_maps[0], s)
    maps = jnp.concatenate([down, up], axis=0)[None]
    for bit in reversed(req_bits):
        maps = jnp.concatenate([maps, swap(maps, "req", n_req, bit)], axis=0)
    other = adapter_of_request[0, 0] ^ r
    index = 0
    for bit in req_bits:
        index = index * 2 + (other // bit) % 2
    chosen_maps = pick(maps, index, 0)
    rank = up.shape[0]
    lowrank = lax.dot_general(
        stream, chosen_maps[:rank], (((1,), (1,)), ((), ())), preferred_element_type=f32
    ).reshape(n_seq, -1, rank)
    for bit in bits_of(n_seq):
        got = swap(lowrank, "seq", n_seq, bit)
        lowrank = lowrank + jnp.stack([got[k ^ bit] for k in range(n_seq)])
    lowrank = lowrank.reshape(-1, rank).astype(bf16)
    image_values = (
        base_values.astype(f32) + jnp.dot(lowrank, chosen_maps[rank:], preferred_element_type=f32)
    ).astype(bf16)

    mixed = attention(
        queries, text_rows[:, :part], text_rows[:, part:], image_keys, image_values, live
    ).reshape(n_seq, -1, part)
    pieces = jnp.stack([mixed[0]] + [swap(mixed[k], "seq", n_seq, k) for k in range(1, n_seq)])
    result = jnp.concatenate([pick(pieces, s ^ k, 0) for k in range(n_seq)], axis=1)
    return result[None, None]


F32, BF16 = jnp.float32, jnp.bfloat16
ANY = pl.BlockSpec(memory_space=pl.ANY)
VMEM = pl.BlockSpec(memory_space=pltpu.VMEM)
SMEM = pl.BlockSpec(memory_space=pltpu.SMEM)
NT = (((1,), (1,)), ((), ()))
TN = (((0,), (0,)), ((), ()))


def partners(send, axis, size):
    return {k: swap(send(k), axis, size, k) for k in far_first(size)}


def far_first(size):
    return [k for k in range(2, size)] + [1]


def call(kernel, outs, ins, specs=None, scratch=(), name=None, out_specs=None, vmem=16):
    return pl.pallas_call(
        kernel,
        out_shape=outs,
        in_specs=specs if specs is not None else [VMEM] * len(ins),
        out_specs=out_specs if out_specs is not None else jax.tree.map(lambda _: VMEM, outs),
        scratch_shapes=list(scratch),
        compiler_params=pltpu.CompilerParams(vmem_limit_bytes=int(vmem * 1024 * 1024)),
        name=name,
    )(*ins)


def struct(shape, dtype=BF16):
    return jax.ShapeDtypeStruct(shape, dtype)


def at(index, size):
    return pl.ds(pl.multiple_of(index * size, size), size)


def stat_rows(stat):
    high = stat.astype(BF16).astype(F32)
    row = lax.broadcasted_iota(jnp.int32, (ROWS, stat.shape[1]), 0)
    return jnp.where(row == 0, high, jnp.where(row == 1, stat - high, 0.0)).astype(BF16)


def stat_of(rows):
    rows = rows.astype(F32)
    return rows[0:1] + rows[1:2]


def context_kernel(h_ref, w_ref, b_ref, send_ref, keep_ref, stat_ref):
    mine = lax.rem(lax.axis_index("req"), 2)
    features = b_ref.shape[0]
    pairs = w_ref.shape[1] // (2 * features)
    total = jnp.zeros((1, h_ref.shape[0]), F32)
    for p in range(pairs):
        product = jnp.dot(
            h_ref[...], w_ref[:, p * 2 * features : (p + 1) * 2 * features],
            preferred_element_type=F32,
        ).T
        total = total + jnp.sum(product, axis=0, keepdims=True)
        low, high = product[:features], product[features:]
        rows = slice(p * features, (p + 1) * features)
        keep_ref[rows] = jnp.where(mine == 0, low, high)
        send_ref[rows] = jnp.where(mine == 0, high, low).astype(BF16)
    stat = total + jnp.sum(b_ref[...].astype(F32))
    send_ref[pairs * features :] = stat_rows(stat)
    stat_ref[...] = jnp.broadcast_to(stat, stat_ref.shape)


def scatter_kernel(features, deps, got_ref, keep_ref, stat_ref, *refs):
    kept_ref, out_stat_ref, *send_refs = refs[deps:]
    e = lax.axis_index("enc")
    count = keep_ref.shape[0] // features
    stat = stat_ref[0:1] + stat_of(got_ref[count * features :])
    own = at(e, features)
    for k, send_ref in enumerate(send_refs):
        other = at(e ^ (k + 1), features)
        send_ref[:features] = (keep_ref[other] + got_ref[other].astype(F32)).astype(BF16)
        send_ref[features:] = stat_rows(stat)
    kept_ref[...] = keep_ref[own] + got_ref[own].astype(F32)
    out_stat_ref[...] = jnp.broadcast_to(stat, out_stat_ref.shape)


def lane_rows(rows, first, values, extra):
    tokens = extra.shape[1]
    for j in range(pl.cdiv(values.shape[1], tokens)):
        piece = values[:, j * tokens : min((j + 1) * tokens, values.shape[1])]
        gap = tokens - piece.shape[1]
        if gap:
            piece = jnp.concatenate([piece, jnp.zeros((1, gap), F32)], axis=1)
        extra = jnp.where(rows == first + j, piece, extra)
    return extra


def from_rows(extra, first, count):
    tokens = extra.shape[1]
    pieces = [extra[first + j : first + j + 1] for j in range(pl.cdiv(count, tokens))]
    return jnp.concatenate(pieces, axis=1)[:, :count]


def merge_kernel(deps, prompt_ref, keep_ref, stat_ref, bias_ref, scale_ref, shift_ref, *refs):
    got_refs, (send_ref, kept_ref, out_stat_ref) = refs[deps:-3], refs[-3:]
    features, tokens = bias_ref.shape
    mine = lax.rem(lax.axis_index("req") // 2, 2)
    total = keep_ref[...]
    stat = stat_ref[0:1]
    for got_ref in got_refs:
        total = total + got_ref[: 2 * features].astype(F32)
        stat = stat + stat_of(got_ref[2 * features :])
    kept_ref[...] = total
    own = at(mine, features)
    kept_ref[own] = kept_ref[own] + bias_ref[...]
    send_ref[: 2 * features] = kept_ref[...].astype(BF16)
    rows = lax.broadcasted_iota(jnp.int32, (ROWS, tokens), 0)
    extra = stat_rows(stat).astype(F32)
    extra = lane_rows(rows, 2, scale_ref[...].astype(F32), extra)
    extra = lane_rows(rows, 6, shift_ref[...].astype(F32), extra)
    extra = jnp.where(rows == ROWS - 1, prompt_ref[0, 0].astype(F32), extra)
    send_ref[2 * features :] = extra.astype(BF16)
    out_stat_ref[...] = jnp.broadcast_to(stat, out_stat_ref.shape)


def centre_kernel(
    width, prompt_ref, dep_ref, keep_ref, stat_ref, got_ref, scale_ref, shift_ref, out_ref
):
    features, tokens = scale_ref.shape
    mine = lax.rem(lax.axis_index("req") // 2, 2)
    extra = got_ref[2 * features :].astype(F32)
    stat = stat_ref[0:1] + extra[0:1] + extra[1:2]
    average = stat * (1.0 / width)
    scale = from_rows(extra, 2, features)
    columns = []
    for first in range(0, features, tokens):
        piece = scale[:, first : min(first + tokens, features)]
        piece = jnp.broadcast_to(piece, (tokens, piece.shape[1]))
        gap = tokens - piece.shape[1]
        if gap:
            piece = jnp.concatenate([piece, jnp.zeros((tokens, gap), F32)], axis=1)
        columns.append(piece.T[: min(tokens, features - first)])
    scales = (scale_ref[...], 1.0 + jnp.concatenate(columns, axis=0))
    squares = jnp.zeros((1, tokens), F32)
    for i in range(2):
        block = at(mine ^ i, features)
        centred = keep_ref[block] + got_ref[block].astype(F32) - average
        squares = squares + jnp.sum(centred * centred, axis=0, keepdims=True)
        out_ref[i * features : (i + 1) * features] = (scales[i] * centred).astype(BF16)
    shift = jnp.concatenate([shift_ref[...].astype(F32), from_rows(extra, 6, features)], axis=1)
    other_prompt = extra[ROWS - 1 : ROWS]
    rows = lax.broadcasted_iota(jnp.int32, (ROWS, tokens), 0)
    extra = stat_rows(squares).astype(F32)
    extra = lane_rows(rows, 2, shift, extra)
    extra = jnp.where(rows == ROWS - 1, prompt_ref[0, 0].astype(F32), extra)
    extra = jnp.where(rows == ROWS - 2, other_prompt, extra)
    out_ref[2 * features :] = extra.astype(BF16)


def pass_on_kernel(own_ref, core_ref, got_ref, dep_ref, mine_ref, next_ref):
    features = own_ref.shape[0]
    mine_ref[:features] = own_ref[...]
    mine_ref[features:] = got_ref[0]
    next_ref[:features] = core_ref[...]
    next_ref[features:] = got_ref[1]


def join_kernel(own_ref, got_ref, out_ref):
    size = own_ref.shape[0]
    out_ref[:size] = own_ref[...]
    out_ref[size:] = got_ref[...]


def project_kernel(n_seq, n_enc, *refs):
    payload_refs, weight_refs, refs = refs[:2], refs[2:4], refs[4:]
    prompts_ref, keep_ref, *send_refs = refs[:-1]
    rows_ref = refs[-1]
    features, width = weight_refs[0].shape
    tokens = payload_refs[0].shape[1]
    stride = features + ROWS
    total = None
    squares = [jnp.zeros((1, tokens), F32) for _ in range(n_seq)]
    for k, (payload, weight_ref) in enumerate(zip(payload_refs, weight_refs)):
        left = []
        shifts = []
        for p in range(n_seq):
            left.append(payload[p * stride : p * stride + features].T)
            extra = payload[p * stride + features : (p + 1) * stride].astype(F32)
            squares[p] = squares[p] + extra[0:1] + extra[1:2]
            shifts.append(from_rows(extra, 2, features))
            if p == 0:
                prompts_ref[k] = jnp.max(extra[ROWS - 1 : ROWS]).astype(jnp.int32)
                prompts_ref[2 + k] = jnp.max(extra[ROWS - 2 : ROWS - 1]).astype(jnp.int32)
        shifts.append(jnp.zeros((ROWS - n_seq, features), F32))
        left.append(jnp.concatenate(shifts, axis=0).astype(BF16))
        term = jnp.dot(
            jnp.concatenate(left, axis=0), weight_ref[...], preferred_element_type=F32
        )
        total = term if total is None else total + term
    size = n_seq * tokens // n_enc
    heads = width // HDIM
    step = heads * size + ROWS
    row = lax.broadcasted_iota(jnp.int32, (ROWS, HDIM), 0)
    for z in range(n_enc):
        p, first = divmod(z * size, tokens)
        shift = total[n_seq * tokens + p : n_seq * tokens + p + 1]
        square = squares[p][:, first : first + size]
        square = jnp.concatenate([square, jnp.zeros((1, HDIM - size), F32)], axis=1)
        high = square.astype(BF16).astype(F32)
        extra = jnp.where(
            row == 2 * heads, high, jnp.where(row == 2 * heads + 1, square - high, 0.0)
        )
        for h in range(heads):
            cols = slice(h * HDIM, (h + 1) * HDIM)
            rows_ref[z * step + h * size : z * step + (h + 1) * size] = total[
                z * size : (z + 1) * size, cols
            ]
            high = shift[:, cols].astype(BF16).astype(F32)
            extra = jnp.where(
                row == h, high, jnp.where(row == heads + h, shift[:, cols] - high, extra)
            )
        rows_ref[z * step + heads * size : (z + 1) * step] = extra
    e = lax.axis_index("enc")
    keep_ref[...] = rows_ref[at(e, step)]
    for k, send_ref in enumerate(send_refs):
        send_ref[...] = rows_ref[at(e ^ (k + 1), step)].astype(BF16)


def finish_kernel(n_req, model_width, keep_ref, bias_ref, *refs):
    got_refs, out_ref = refs[:-1], refs[-1]
    r, s = lax.axis_index("req"), lax.axis_index("seq")
    size, width = out_ref.shape
    heads = width // HDIM
    half = width // 2
    inner = bias_ref.shape[1] // 2
    total = keep_ref[...]
    for got_ref in got_refs:
        total = total + got_ref[...].astype(F32)
    extra = total[heads * size :]
    squares = extra[2 * heads : 2 * heads + 1] + extra[2 * heads + 1 : 2 * heads + 2]
    squares = jnp.broadcast_to(squares, (HDIM, HDIM)).T[:size]
    factor = lax.rsqrt(squares * (1.0 / model_width) + epsilon_norm)
    for h in range(heads):
        start = (h * HDIM // half) * inner + (s * n_req + r) * half + h * HDIM % half
        bias = bias_ref[:, pl.ds(pl.multiple_of(start, HDIM), HDIM)].astype(F32)
        shift = extra[h : h + 1] + extra[heads + h : heads + h + 1] + bias
        head = total[h * size : (h + 1) * size] * factor + shift
        if h * HDIM < half:
            head = head * lax.rsqrt(jnp.mean(head * head, axis=1, keepdims=True) + epsilon_norm)
        out_ref[:, h * HDIM : (h + 1) * HDIM] = head.astype(BF16)


def choose_kernel(n_seq, n_enc, chosen_ref, dep_ref, *refs):
    part_refs, out_refs = dict(zip([0] + far_first(n_enc), refs)), refs[n_enc:]
    e, r, s = lax.axis_index("enc"), lax.axis_index("req"), lax.axis_index("seq")
    halves = n_enc // n_seq
    size = part_refs[0].shape[0]
    for k, out_ref in enumerate(out_refs):
        prompt = s ^ chosen_ref[k]
        for h in range(halves):
            place = e ^ (prompt * halves + h)
            for j in range(n_enc):
                @pl.when(place == j)
                def _():
                    out_ref[h * size : (h + 1) * size] = part_refs[j][...]


def weight_kernel(n_req, part, inner, w_ref, dep_ref, own_ref, core_ref, pair_ref, sems):
    r, s = lax.axis_index("req"), lax.axis_index("seq")
    half = part // n_req
    copies = []
    for k, out_ref in enumerate((own_ref, core_ref, pair_ref.at[0], pair_ref.at[1])):
        for side in range(2):
            columns = pl.ds(
                pl.multiple_of(side * inner + (s * n_req + (r ^ k)) * half, HDIM), half
            )
            copies.append(
                pltpu.make_async_copy(
                    w_ref.at[:, columns],
                    out_ref.at[:, pl.ds(side * half, half)],
                    sems.at[2 * k + side],
                )
            )
    for copy in copies:
        copy.start()
    for copy in copies:
        copy.wait()


def image_kernel(part, inner, step, qk_ref, v_ref, x_ref, dep_ref, out_ref, sems):
    start = (lax.axis_index("seq") ^ step) * part
    copies = []
    for i, (ref, base) in enumerate(((qk_ref, 0), (qk_ref, inner), (v_ref, 0), (x_ref, 0))):
        columns = pl.ds(pl.multiple_of(base + start, HDIM), part)
        copies.append(pltpu.make_async_copy(ref.at[:, columns], out_ref.at[i], sems.at[i]))
    for copy in copies:
        copy.start()
    for copy in copies:
        copy.wait()


def maps_kernel(part, down_ref, up_ref, dep_ref, out_ref, sems):
    rank = down_ref.shape[0]
    columns = pl.ds(pl.multiple_of(lax.axis_index("seq") * part, HDIM), part)
    copies = [
        pltpu.make_async_copy(down_ref.at[:, columns], out_ref.at[pl.ds(0, rank)], sems.at[0]),
        pltpu.make_async_copy(up_ref.at[:, columns], out_ref.at[pl.ds(rank, rank)], sems.at[1]),
    ]
    for copy in copies:
        copy.start()
    for copy in copies:
        copy.wait()


def join_maps_kernel(own_ref, core_ref, dep_ref, out_ref):
    out_ref[0] = own_ref[...]
    out_ref[1] = core_ref[...]


def lowrank_kernel(part, adapter_ref, x_ref, got_ref, *refs):
    own_ref, pair_ref, out_ref, chosen_ref = refs
    map_refs = (own_ref.at[0], own_ref.at[1], pair_ref.at[0], pair_ref.at[1])
    place = adapter_ref[0, 0] ^ lax.axis_index("req")
    rank = out_ref.shape[-1]
    for k, ref in enumerate(map_refs):
        @pl.when(place == k)
        def _():
            chosen_ref[...] = ref[rank:]
            own = x_ref[:, pl.ds(pl.multiple_of(lax.axis_index("seq") * part, HDIM), part)]
            for i, rows in enumerate((own, got_ref[3])):
                out_ref[i] = lax.dot_general(
                    rows, ref[:rank], NT, preferred_element_type=F32
                )


def arrange_kernel(n_req, part, inner, low_ref, other_ref, maps_ref, qk_ref, v_ref, *refs):
    got_refs, (q_out, k_out, v_out) = refs[:-3], refs[-3:]
    r, s = lax.axis_index("req"), lax.axis_index("seq")
    half = part // n_req
    tokens = qk_ref.shape[0]
    low = [(low_ref[i] + other_ref[i ^ 1]).astype(BF16) for i in range(2)]
    for k in range(n_req):
        place = (r ^ k) * half
        up = maps_ref[:, pl.ds(pl.multiple_of(place, HDIM), half)]
        for i in range(len(got_refs) + 1):
            rows = slice(i * tokens, (i + 1) * tokens)
            if i == 0:
                own = s * part + place
                q = qk_ref[:, pl.ds(pl.multiple_of(own, HDIM), half)]
                key = qk_ref[:, pl.ds(pl.multiple_of(inner + own, HDIM), half)]
                base = v_ref[:, pl.ds(pl.multiple_of(own, HDIM), half)]
            else:
                columns = pl.ds(pl.multiple_of(place, HDIM), half)
                q = got_refs[i - 1][0, :, columns]
                key = got_refs[i - 1][1, :, columns]
                base = got_refs[i - 1][2, :, columns]
            q_out[k, rows] = q
            k_out[k, rows] = key
            v_out[k, rows] = (
                base.astype(F32) + jnp.dot(low[i], up, preferred_element_type=F32)
            ).astype(BF16)


def heads_kernel(place, first, scale, live_ref, text_ref, q_ref, k_ref, v_ref, *refs):
    out_refs = refs[2:]
    live = live_ref[...] != 0
    half = q_ref.shape[2]
    size = out_refs[0].shape[0]
    for h in range(half // HDIM):
        cols = slice(h * HDIM, (h + 1) * HDIM)
        vals = slice(half + h * HDIM, half + (h + 1) * HDIM)
        q = q_ref[place, first * size : (first + len(out_refs)) * size, cols]
        st = lax.dot_general(q, text_ref[:, cols], NT, preferred_element_type=F32) * scale
        si = lax.dot_general(q, k_ref[place, :, cols], NT, preferred_element_type=F32) * scale
        st = jnp.where(live, st, -jnp.inf)
        top = jnp.maximum(
            jnp.max(st, axis=1, keepdims=True), jnp.max(si, axis=1, keepdims=True)
        )
        wt = jnp.exp(st - top)
        wi = jnp.exp(si - top)
        total = jnp.sum(wt, axis=1, keepdims=True) + jnp.sum(wi, axis=1, keepdims=True)
        mixed = jnp.dot(
            wt.astype(BF16), text_ref[:, vals], preferred_element_type=F32
        ) + jnp.dot(wi.astype(BF16), v_ref[place, :, cols], preferred_element_type=F32)
        mixed = (mixed / total).astype(BF16)
        for i, out_ref in enumerate(out_refs):
            out_ref[:, cols] = mixed[i * size : (i + 1) * size]


def assemble_kernel(n_req, n_seq, *refs):
    out_ref = refs[-1]
    r, s = lax.axis_index("req"), lax.axis_index("seq")
    half = refs[0].shape[1]
    for k in range(n_req):
        for i in range(n_seq):
            start = ((s ^ i) * n_req + (r ^ k)) * half
            out_ref[:, pl.ds(pl.multiple_of(start, HDIM), half)] = refs[k * n_seq + i][...]


def per_device_heads(
    n_enc,
    n_req,
    n_seq,
    encoder_hidden,
    prompt_token_ids,
    context_weight,
    context_bias,
    modulation_shift,
    modulation_scale,
    key_value_weight,
    key_value_bias,
    request_prompt,
    adapter_of_request,
    adapter_down_maps,
    adapter_up_maps,
    image_stream_input,
    image_query_key,
    image_value_rows,
):
    e, r, s = lax.axis_index("enc"), lax.axis_index("req"), lax.axis_index("seq")
    model_width = context_weight.shape[1]
    features = context_bias.shape[0]
    tokens = encoder_hidden.shape[1]
    inner = key_value_weight.shape[1] // 2
    part = inner // n_seq
    half = part // n_req
    image_rows = image_query_key.shape[2]
    rank = adapter_up_maps.shape[1]
    qk, base, stream = image_query_key[0, 0], image_value_rows[0, 0], image_stream_input[0, 0]
    dma = pltpu.SemaphoreType.DMA
    stat = struct((8, tokens), F32)

    send, keep, sums = call(
        context_kernel,
        (
            struct((model_width // 2 + ROWS, tokens)),
            struct((model_width // 2, tokens), F32),
            stat,
        ),
        (encoder_hidden[0], context_weight, context_bias),
        name="context",
    )
    got = swap(send, "req", n_req, 1)

    keep, sums, *sends = call(
        functools.partial(scatter_kernel, 2 * features, 0),
        (struct((2 * features, tokens), F32), stat)
        + tuple(struct((2 * features + ROWS, tokens)) for _ in range(1, n_enc)),
        (got, keep, sums),
        name="scatter",
    )
    arrived = partners(lambda k: sends[k - 1], "enc", n_enc).values()
    weight = struct((features, 2 * half))
    weight_own, weight_core, weight_pair = call(
        functools.partial(weight_kernel, n_req, part, inner),
        (weight, weight, struct((2, features, 2 * half))),
        (key_value_weight, keep),
        [ANY] * 2,
        [dma((2 * n_req,))],
        name="weight_pack",
        vmem=16,
    )

    weight_pair_got = swap(weight_pair, "req", n_req, 2)
    bias_columns = jnp.broadcast_to(context_bias.astype(F32)[:, None], (features, tokens))
    scale_columns = jnp.broadcast_to(
        1.0 + modulation_scale[0].astype(F32)[:, None], (features, tokens)
    )
    deps = ()
    send, keep, sums = call(
        functools.partial(merge_kernel, len(deps)),
        (
            struct((2 * features + ROWS, tokens)),
            struct((2 * features, tokens), F32),
            stat,
        ),
        (
            request_prompt,
            keep,
            sums,
            bias_columns,
            modulation_scale,
            modulation_shift,
            *deps,
            *arrived,
        ),
        [SMEM] + [VMEM] * 5 + [ANY] * len(deps) + [VMEM] * len(arrived),
        name="merge",
    )
    got = swap(send, "req", n_req, 2)
    weights = struct((2 * features, 2 * half))
    weight_mine, weight_next = call(
        pass_on_kernel,
        (weights, weights),
        (weight_own, weight_core, weight_pair_got, keep),
        [VMEM] * 3 + [ANY],
        name="pass_on",
    )
    weight_next = swap(weight_next, "req", n_req, 1)
    own = call(
        functools.partial(centre_kernel, model_width),
        struct((2 * features + ROWS, tokens)),
        (request_prompt, weight_mine, keep, sums, got, scale_columns, modulation_shift),
        [SMEM, ANY] + [VMEM] * 5,
        name="centre",
    )
    joined = call(
        join_kernel,
        struct((n_seq * (2 * features + ROWS), tokens)),
        (own, swap(own, "seq", n_seq, 1)),
        name="join",
    )
    packed = [
        call(
            functools.partial(image_kernel, part, inner, k),
            struct((4, image_rows, part)),
            (qk, base, stream, joined),
            [ANY] * 4,
            [dma((4,))],
            name="image_pack",
        )
        for k in range(1, n_seq)
    ]
    image_got = [swap(packed[k - 1], "seq", n_seq, k) for k in range(1, n_seq)]
    weight_pair = lax.optimization_barrier((weight_pair, keep))[0]
    joined_core = swap(joined, "req", n_req, 1)
    maps = call(
        functools.partial(maps_kernel, part),
        struct((2 * rank, part)),
        (adapter_down_maps[0].T, adapter_up_maps[0], joined),
        [ANY] * 3,
        [dma((2,))],
        name="maps_pack",
    )
    maps_core = swap(maps, "req", n_req, 1)
    maps = call(
        join_maps_kernel,
        struct((2, 2 * rank, part)),
        (maps, maps_core, joined),
        [VMEM, VMEM, ANY],
        name="maps_join",
    )

    size = n_seq * tokens // n_enc
    step = 2 * half // HDIM * size + ROWS
    ids, keep, *sends = call(
        functools.partial(project_kernel, n_seq, n_enc),
        (struct((n_req,), jnp.int32), struct((step, HDIM), F32))
        + tuple(struct((step, HDIM)) for _ in range(1, n_enc)),
        (joined, joined_core, weight_mine, weight_next),
        scratch=[pltpu.VMEM((n_enc * step, HDIM), F32)],
        out_specs=(SMEM,) + (VMEM,) * n_enc,
        name="project",
    )
    arrived = partners(lambda k: sends[k - 1], "enc", n_enc).values()

    maps = lax.optimization_barrier((maps, keep))[0]
    maps_pair = swap(maps, "req", n_req, 2)

    text = call(
        functools.partial(finish_kernel, n_req, model_width),
        struct((size, 2 * half)),
        (keep, key_value_bias[None], *arrived),
        [VMEM] * (2 + len(arrived)),
        name="finish",
    )
    low, chosen_maps = call(
        functools.partial(lowrank_kernel, part),
        (struct((n_seq, image_rows, rank), F32), struct((rank, part))),
        (
            adapter_of_request,
            stream,
            image_got[0],
            maps,
            maps_pair,
        ),
        [SMEM] + [VMEM] * 4,
        name="lowrank",
    )
    arranged = struct((n_req, n_seq * image_rows, half))
    queries, image_keys, image_values = call(
        functools.partial(arrange_kernel, n_req, part, inner),
        (arranged, arranged, arranged),
        (low, swap(low, "seq", n_seq, 1), chosen_maps, qk, base, *image_got),
        name="arrange",
    )
    parts = partners(lambda k: text, "enc", n_enc)
    rows = call(
        functools.partial(choose_kernel, n_seq, n_enc),
        [struct((tokens, 2 * half)) for _ in range(n_req)],
        (ids, image_values, text, *parts.values()),
        [SMEM, ANY] + [VMEM] * n_enc,
        name="choose",
    )
    rows = {0: rows[0], **partners(lambda k: rows[k], "req", n_req)}
    live = lax.dynamic_slice_in_dim(prompt_token_ids, request_prompt[0, 0], 1, 0)
    def heads(k, first, count, last):
        return call(
            functools.partial(heads_kernel, k, first, HDIM ** (-0.5)),
            [struct((image_rows, half))] * count,
            (live, rows[k], queries, image_keys, image_values, *last),
            [VMEM] * 5 + [ANY] * 2,
            name="heads",
        )

    pieces = [None] * n_req
    last = (live, live)
    for k in range(n_req):
        if k < n_req - 1:
            mixed = heads(k, 0, n_seq, last)
        else:
            (back,) = heads(k, 1, 1, last)
            (mine,) = heads(k, 0, 1, (back, last[1]))
            mixed = (mine, back)
        pieces[k] = [mixed[0], swap(mixed[1], "seq", n_seq, 1)]
        last = (mixed[0], pieces[k - 1][1] if k else live)
    result = call(
        functools.partial(assemble_kernel, n_req, n_seq),
        struct((image_rows, inner)),
        tuple(p for group in pieces for p in group),
        name="assemble",
    )
    return result[None, None]


def solution(mesh):
    sizes = mesh.shape
    n_enc, n_req, n_seq = sizes["enc"], sizes["req"], sizes["seq"]

    def run(*arrays):
        heads = arrays[6].shape[1] // (2 * HDIM)
        fits = n_seq == 2 and n_req == 4 and heads % (n_seq * n_req) == 0
        return (per_device_heads if fits else per_device)(n_enc, n_req, n_seq, *arrays)

    return jax.shard_map(
        run,
        mesh=mesh,
        in_specs=(
            P("seq", None, ("enc", "req")),
            P(),
            P(("enc", "req"), None),
            P(("enc", "req")),
            P("seq", ("enc", "req")),
            P("seq", ("enc", "req")),
            P(("enc", "req"), None),
            P(),
            P("enc", "req"),
            P("enc", "req"),
            P("req", None, None),
            P("req", None, None),
            P("enc", "req", "seq", None),
            P("enc", "req", "seq", None),
            P("enc", "req", "seq", None),
        ),
        out_specs=P("enc", "req", "seq", None),
        check_vma=False,
    )
```

```python
import functools

import jax
import jax.numpy as jnp
from jax import lax
from jax.experimental import pallas as pl
from jax.experimental.pallas import tpu as pltpu
from jax.sharding import PartitionSpec as P

HDIM = 128
ROWS = 16

epsilon_norm = 1e-06


def swap(block, axis, size, step):
    return lax.ppermute(block, axis, [(i, i ^ step) for i in range(size)])


def pick(array, index, dim):
    return lax.dynamic_index_in_dim(array, index, dim, keepdims=False)


def split_two(value):
    high = lax.reduce_precision(value, 8, 7)
    return high.astype(jnp.bfloat16), (value - high).astype(jnp.bfloat16)


def bits_of(size):
    return [1 << b for b in range(size.bit_length() - 1)]


def with_stat_rows(data, stat):
    high, low = split_two(stat)
    rows = jnp.concatenate(
        [high[None], low[None], jnp.zeros((ROWS - 2, stat.shape[0]), jnp.bfloat16)], axis=0
    )
    rows = jnp.broadcast_to(rows, data.shape[:-2] + rows.shape)
    return jnp.concatenate([data.astype(jnp.bfloat16), rows], axis=-2)


def attention_kernel(heads, inner, scale, mask_ref, q_ref, kt_ref, vt_ref, ki_ref, vi_ref, o_ref):
    live = mask_ref[...] != 0
    for h in range(heads):
        cols = slice(h * HDIM, (h + 1) * HDIM)
        q = q_ref[:, cols]
        dims = (((1,), (1,)), ((), ()))
        st = lax.dot_general(q, kt_ref[:, cols], dims, preferred_element_type=jnp.float32) * scale
        si = lax.dot_general(q, ki_ref[:, cols], dims, preferred_element_type=jnp.float32) * scale
        st = jnp.where(live, st, -jnp.inf)
        top = jnp.maximum(
            jnp.max(st, axis=1, keepdims=True), jnp.max(si, axis=1, keepdims=True)
        )
        wt = jnp.exp(st - top)
        wi = jnp.exp(si - top)
        total = jnp.sum(wt, axis=1, keepdims=True) + jnp.sum(wi, axis=1, keepdims=True)
        mixed = jnp.dot(
            wt.astype(jnp.bfloat16), vt_ref[:, cols], preferred_element_type=jnp.float32
        ) + jnp.dot(wi.astype(jnp.bfloat16), vi_ref[:, cols], preferred_element_type=jnp.float32)
        o_ref[:, cols] = (mixed / total).astype(o_ref.dtype)


def attention(queries, text_keys, text_values, image_keys, image_values, live):
    width = queries.shape[1]
    heads = width // HDIM
    rows = queries.shape[0]
    mask = jnp.broadcast_to(live.astype(jnp.int32)[None, :], (8, live.shape[0]))[:1]
    return pl.pallas_call(
        functools.partial(attention_kernel, heads, width, HDIM ** (-0.5)),
        out_shape=jax.ShapeDtypeStruct((rows, width), jnp.bfloat16),
        compiler_params=pltpu.CompilerParams(vmem_limit_bytes=48 * 1024 * 1024),
        name="attention",
    )(mask, queries, text_keys, text_values, image_keys, image_values)


def per_device(
    n_enc,
    n_req,
    n_seq,
    encoder_hidden,
    prompt_token_ids,
    context_weight,
    context_bias,
    modulation_shift,
    modulation_scale,
    key_value_weight,
    key_value_bias,
    request_prompt,
    adapter_of_request,
    adapter_down_maps,
    adapter_up_maps,
    image_stream_input,
    image_query_key,
    image_value_rows,
):
    f32, bf16 = jnp.float32, jnp.bfloat16
    e, r, s = lax.axis_index("enc"), lax.axis_index("req"), lax.axis_index("seq")
    req_bits = bits_of(n_req)
    model_width = context_weight.shape[1]
    features = context_bias.shape[0]
    tokens = encoder_hidden.shape[1]
    inner = key_value_weight.shape[1] // 2
    part = inner // n_seq

    def heads_of(array, share):
        return lax.dynamic_slice_in_dim(array, share * part, part, 1)

    qk = image_query_key[0, 0]
    sources = [qk[:, :inner], qk[:, inner:], image_value_rows[0, 0], image_stream_input[0, 0]]
    image_parts = [
        jnp.stack([heads_of(a, s ^ k) for a in sources]) for k in range(n_seq)
    ]
    image_parts = [image_parts[0]] + [
        swap(image_parts[k], "seq", n_seq, k) for k in range(1, n_seq)
    ]
    image_all = jnp.concatenate(image_parts, axis=1)
    queries, image_keys, base_values, stream = [image_all[i] for i in range(4)]

    partial_value = lax.dot_general(
        context_weight, encoder_hidden[0], (((0,), (1,)), ((), ())), preferred_element_type=f32
    )
    stat = jnp.sum(partial_value, axis=0) + jnp.sum(context_bias.astype(f32))
    acc = partial_value.reshape((n_enc,) + (2,) * len(req_bits) + (features, tokens))
    for i, bit in enumerate(req_bits):
        mine = (r // bit) % 2
        dim = len(req_bits) - i
        got = swap(with_stat_rows(pick(acc, 1 - mine, dim), stat), "req", n_req, bit).astype(f32)
        acc = pick(acc, mine, dim) + got[..., :features, :]
        got_stat = got.reshape((-1,) + got.shape[-2:])[0, features:]
        stat = stat + got_stat[0] + got_stat[1]
    arrived = [
        swap(with_stat_rows(pick(acc, e ^ k, 0), stat), "enc", n_enc, k).astype(f32)
        for k in range(1, n_enc)
    ]
    embedded = pick(acc, e, 0)
    for got in arrived:
        embedded = embedded + got[:features]
        stat = stat + got[features] + got[features + 1]
    embedded = embedded + context_bias.astype(f32)[:, None]
    centred = embedded - (stat / model_width)[None, :]
    squares = jnp.sum(centred * centred, axis=0)
    scaled = (1.0 + modulation_scale[0].astype(f32))[:, None] * centred

    own = with_stat_rows(scaled, squares)
    blocks = [own] + [swap(own, "seq", n_seq, k) for k in range(1, n_seq)]
    scaled_all = jnp.concatenate([b[:features] for b in blocks], axis=1)
    squares_all = jnp.concatenate(
        [b[features].astype(f32) + b[features + 1].astype(f32) for b in blocks]
    )
    weight_own = jnp.concatenate(
        [heads_of(key_value_weight[:, :inner], s), heads_of(key_value_weight[:, inner:], s)], axis=1
    )
    width = 2 * part
    projected = lax.dot_general(
        scaled_all, weight_own, (((0,), (0,)), ((), ())), preferred_element_type=f32
    )

    shift_part = jnp.dot(modulation_shift, key_value_weight, preferred_element_type=f32)
    for bit in req_bits:
        shift_part = shift_part + swap(shift_part, "req", n_req, bit)
    for bit in bits_of(n_enc):
        shift_part = shift_part + swap(shift_part, "enc", n_enc, bit)
    shift_part = shift_part + key_value_bias.astype(f32)[None]

    def columns_of(row, share):
        return jnp.concatenate(
            [heads_of(row[:, :inner], share), heads_of(row[:, inner:], share)], axis=1
        )

    shift_rows = jnp.concatenate(
        [columns_of(shift_part, s)]
        + [swap(columns_of(shift_part, s ^ k), "seq", n_seq, k) for k in range(1, n_seq)],
        axis=0,
    )

    halves = tokens // n_req // ROWS
    split = (n_seq,) + (2,) * len(req_bits) + (halves, ROWS)
    acc = projected.reshape(split + (width,))
    acc_stat = squares_all.reshape(split)

    def with_stat_columns(data, stat):
        high, low = split_two(stat)
        lane = lax.broadcasted_iota(jnp.int32, stat.shape + (HDIM,), stat.ndim)
        columns = jnp.where(
            lane == 0, high[..., None], jnp.where(lane == 1, low[..., None], jnp.zeros((), bf16))
        )
        return jnp.concatenate([data.astype(bf16), columns], axis=-1)

    for i, bit in enumerate(req_bits):
        mine = (r // bit) % 2
        dim = len(req_bits) - i
        got = swap(
            with_stat_columns(pick(acc, 1 - mine, dim), pick(acc_stat, 1 - mine, dim)),
            "req", n_req, bit,
        ).astype(f32)
        acc = pick(acc, mine, dim) + got[..., :width]
        acc_stat = pick(acc_stat, mine, dim) + got[..., width] + got[..., width + 1]
    acc = acc.reshape(n_enc, ROWS, width)
    acc_stat = acc_stat.reshape(n_enc, ROWS)
    arrived = [
        swap(with_stat_columns(pick(acc, e ^ k, 0), pick(acc_stat, e ^ k, 0)), "enc", n_enc, k)
        .astype(f32)
        for k in range(1, n_enc)
    ]
    rows = pick(acc, e, 0)
    row_squares = pick(acc_stat, e, 0)
    for got in arrived:
        rows = rows + got[:, :width]
        row_squares = row_squares + got[:, width] + got[:, width + 1]
    rows = rows * lax.rsqrt(row_squares / model_width + epsilon_norm)[:, None]
    rows = rows + pick(shift_rows, e // halves, 0)[None]
    keys = rows[:, :part].reshape(ROWS, part // HDIM, HDIM)
    keys = keys * lax.rsqrt(jnp.mean(keys * keys, axis=2, keepdims=True) + epsilon_norm)
    text = jnp.concatenate([keys.reshape(ROWS, part), rows[:, part:]], axis=1).astype(bf16)

    chosen = request_prompt[0, 0]
    relative = s ^ chosen
    by_enc = [text] + [swap(text, "enc", n_enc, k) for k in range(1, n_enc)]
    by_enc = jnp.stack(by_enc)
    by_enc = jnp.stack([pick(by_enc, k ^ e, 0) for k in range(n_enc)])
    held = by_enc.reshape(1, n_seq, halves, ROWS, width)
    first = req_bits[0]
    held = jnp.concatenate([held, swap(held, "req", n_req, first)], axis=0)
    groups = [pick(held, relative, 1)]
    for step in range(2, n_req, 2):
        wanted = swap(relative, "req", n_req, step)
        groups.append(swap(pick(held, wanted, 1), "req", n_req, step))
    text_rows = jnp.concatenate(groups, axis=0).reshape(-1, width)
    live = pick(prompt_token_ids, chosen, 0) != 0
    live = live.reshape(n_req, halves * ROWS)
    live = jnp.concatenate([pick(live, r ^ k, 0) for k in range(n_req)])

    down = lax.dynamic_slice_in_dim(adapter_down_maps[0], s * part, part, 0).T
    up = heads_of(adapter_up_maps[0], s)
    maps = jnp.concatenate([down, up], axis=0)[None]
    for bit in reversed(req_bits):
        maps = jnp.concatenate([maps, swap(maps, "req", n_req, bit)], axis=0)
    other = adapter_of_request[0, 0] ^ r
    index = 0
    for bit in req_bits:
        index = index * 2 + (other // bit) % 2
    chosen_maps = pick(maps, index, 0)
    rank = up.shape[0]
    lowrank = lax.dot_general(
        stream, chosen_maps[:rank], (((1,), (1,)), ((), ())), preferred_element_type=f32
    ).reshape(n_seq, -1, rank)
    for bit in bits_of(n_seq):
        got = swap(lowrank, "seq", n_seq, bit)
        lowrank = lowrank + jnp.stack([got[k ^ bit] for k in range(n_seq)])
    lowrank = lowrank.reshape(-1, rank).astype(bf16)
    image_values = (
        base_values.astype(f32) + jnp.dot(lowrank, chosen_maps[rank:], preferred_element_type=f32)
    ).astype(bf16)

    mixed = attention(
        queries, text_rows[:, :part], text_rows[:, part:], image_keys, image_values, live
    ).reshape(n_seq, -1, part)
    pieces = jnp.stack([mixed[0]] + [swap(mixed[k], "seq", n_seq, k) for k in range(1, n_seq)])
    result = jnp.concatenate([pick(pieces, s ^ k, 0) for k in range(n_seq)], axis=1)
    return result[None, None]


F32, BF16 = jnp.float32, jnp.bfloat16
ANY = pl.BlockSpec(memory_space=pl.ANY)
VMEM = pl.BlockSpec(memory_space=pltpu.VMEM)
SMEM = pl.BlockSpec(memory_space=pltpu.SMEM)
NT = (((1,), (1,)), ((), ()))
TN = (((0,), (0,)), ((), ()))


def partners(send, axis, size):
    return {k: swap(send(k), axis, size, k) for k in far_first(size)}


def far_first(size):
    return [k for k in range(2, size)] + [1]


def call(kernel, outs, ins, specs=None, scratch=(), name=None, out_specs=None, vmem=16):
    return pl.pallas_call(
        kernel,
        out_shape=outs,
        in_specs=specs if specs is not None else [VMEM] * len(ins),
        out_specs=out_specs if out_specs is not None else jax.tree.map(lambda _: VMEM, outs),
        scratch_shapes=list(scratch),
        compiler_params=pltpu.CompilerParams(vmem_limit_bytes=int(vmem * 1024 * 1024)),
        name=name,
    )(*ins)


def struct(shape, dtype=BF16):
    return jax.ShapeDtypeStruct(shape, dtype)


def at(index, size):
    return pl.ds(pl.multiple_of(index * size, size), size)


def stat_rows(stat):
    high = stat.astype(BF16).astype(F32)
    row = lax.broadcasted_iota(jnp.int32, (ROWS, stat.shape[1]), 0)
    return jnp.where(row == 0, high, jnp.where(row == 1, stat - high, 0.0)).astype(BF16)


def stat_of(rows):
    rows = rows.astype(F32)
    return rows[0:1] + rows[1:2]


def context_kernel(h_ref, w_ref, b_ref, send_ref, keep_ref, stat_ref):
    mine = lax.rem(lax.axis_index("req"), 2)
    features = b_ref.shape[0]
    pairs = w_ref.shape[1] // (2 * features)
    total = jnp.zeros((1, h_ref.shape[0]), F32)
    for p in range(pairs):
        product = jnp.dot(
            h_ref[...], w_ref[:, p * 2 * features : (p + 1) * 2 * features],
            preferred_element_type=F32,
        ).T
        total = total + jnp.sum(product, axis=0, keepdims=True)
        low, high = product[:features], product[features:]
        rows = slice(p * features, (p + 1) * features)
        keep_ref[rows] = jnp.where(mine == 0, low, high)
        send_ref[rows] = jnp.where(mine == 0, high, low).astype(BF16)
    stat = total + jnp.sum(b_ref[...].astype(F32))
    send_ref[pairs * features :] = stat_rows(stat)
    stat_ref[...] = jnp.broadcast_to(stat, stat_ref.shape)


def scatter_kernel(features, deps, got_ref, keep_ref, stat_ref, *refs):
    kept_ref, out_stat_ref, *send_refs = refs[deps:]
    e = lax.axis_index("enc")
    count = keep_ref.shape[0] // features
    stat = stat_ref[0:1] + stat_of(got_ref[count * features :])
    own = at(e, features)
    for k, send_ref in enumerate(send_refs):
        other = at(e ^ (k + 1), features)
        send_ref[:features] = (keep_ref[other] + got_ref[other].astype(F32)).astype(BF16)
        send_ref[features:] = stat_rows(stat)
    kept_ref[...] = keep_ref[own] + got_ref[own].astype(F32)
    out_stat_ref[...] = jnp.broadcast_to(stat, out_stat_ref.shape)


def lane_rows(rows, first, values, extra):
    tokens = extra.shape[1]
    for j in range(pl.cdiv(values.shape[1], tokens)):
        piece = values[:, j * tokens : min((j + 1) * tokens, values.shape[1])]
        gap = tokens - piece.shape[1]
        if gap:
            piece = jnp.concatenate([piece, jnp.zeros((1, gap), F32)], axis=1)
        extra = jnp.where(rows == first + j, piece, extra)
    return extra


def from_rows(extra, first, count):
    tokens = extra.shape[1]
    pieces = [extra[first + j : first + j + 1] for j in range(pl.cdiv(count, tokens))]
    return jnp.concatenate(pieces, axis=1)[:, :count]


def merge_kernel(deps, prompt_ref, keep_ref, stat_ref, bias_ref, scale_ref, shift_ref, *refs):
    got_refs, (send_ref, kept_ref, out_stat_ref) = refs[deps:-3], refs[-3:]
    features, tokens = bias_ref.shape
    mine = lax.rem(lax.axis_index("req") // 2, 2)
    total = keep_ref[...]
    stat = stat_ref[0:1]
    for got_ref in got_refs:
        total = total + got_ref[: 2 * features].astype(F32)
        stat = stat + stat_of(got_ref[2 * features :])
    kept_ref[...] = total
    own = at(mine, features)
    kept_ref[own] = kept_ref[own] + bias_ref[...]
    send_ref[: 2 * features] = kept_ref[...].astype(BF16)
    rows = lax.broadcasted_iota(jnp.int32, (ROWS, tokens), 0)
    extra = stat_rows(stat).astype(F32)
    extra = lane_rows(rows, 2, scale_ref[...].astype(F32), extra)
    extra = lane_rows(rows, 6, shift_ref[...].astype(F32), extra)
    extra = jnp.where(rows == ROWS - 1, prompt_ref[0, 0].astype(F32), extra)
    send_ref[2 * features :] = extra.astype(BF16)
    out_stat_ref[...] = jnp.broadcast_to(stat, out_stat_ref.shape)


def centre_kernel(
    width, prompt_ref, dep_ref, keep_ref, stat_ref, got_ref, scale_ref, shift_ref, out_ref
):
    features, tokens = scale_ref.shape
    mine = lax.rem(lax.axis_index("req") // 2, 2)
    extra = got_ref[2 * features :].astype(F32)
    stat = stat_ref[0:1] + extra[0:1] + extra[1:2]
    average = stat * (1.0 / width)
    scale = from_rows(extra, 2, features)
    columns = []
    for first in range(0, features, tokens):
        piece = scale[:, first : min(first + tokens, features)]
        piece = jnp.broadcast_to(piece, (tokens, piece.shape[1]))
        gap = tokens - piece.shape[1]
        if gap:
            piece = jnp.concatenate([piece, jnp.zeros((tokens, gap), F32)], axis=1)
        columns.append(piece.T[: min(tokens, features - first)])
    scales = (scale_ref[...], 1.0 + jnp.concatenate(columns, axis=0))
    squares = jnp.zeros((1, tokens), F32)
    for i in range(2):
        block = at(mine ^ i, features)
        centred = keep_ref[block] + got_ref[block].astype(F32) - average
        squares = squares + jnp.sum(centred * centred, axis=0, keepdims=True)
        out_ref[i * features : (i + 1) * features] = (scales[i] * centred).astype(BF16)
    shift = jnp.concatenate([shift_ref[...].astype(F32), from_rows(extra, 6, features)], axis=1)
    other_prompt = extra[ROWS - 1 : ROWS]
    rows = lax.broadcasted_iota(jnp.int32, (ROWS, tokens), 0)
    extra = stat_rows(squares).astype(F32)
    extra = lane_rows(rows, 2, shift, extra)
    extra = jnp.where(rows == ROWS - 1, prompt_ref[0, 0].astype(F32), extra)
    extra = jnp.where(rows == ROWS - 2, other_prompt, extra)
    out_ref[2 * features :] = extra.astype(BF16)


def pass_on_kernel(own_ref, core_ref, got_ref, dep_ref, mine_ref, next_ref):
    features = own_ref.shape[0]
    mine_ref[:features] = own_ref[...]
    mine_ref[features:] = got_ref[0]
    next_ref[:features] = core_ref[...]
    next_ref[features:] = got_ref[1]


def join_kernel(own_ref, got_ref, out_ref):
    size = own_ref.shape[0]
    out_ref[:size] = own_ref[...]
    out_ref[size:] = got_ref[...]


def project_kernel(n_seq, n_enc, *refs):
    payload_refs, weight_refs, refs = refs[:2], refs[2:4], refs[4:]
    prompts_ref, keep_ref, *send_refs = refs[:-1]
    rows_ref = refs[-1]
    features, width = weight_refs[0].shape
    tokens = payload_refs[0].shape[1]
    stride = features + ROWS
    total = None
    squares = [jnp.zeros((1, tokens), F32) for _ in range(n_seq)]
    for k, (payload, weight_ref) in enumerate(zip(payload_refs, weight_refs)):
        left = []
        shifts = []
        for p in range(n_seq):
            left.append(payload[p * stride : p * stride + features].T)
            extra = payload[p * stride + features : (p + 1) * stride].astype(F32)
            squares[p] = squares[p] + extra[0:1] + extra[1:2]
            shifts.append(from_rows(extra, 2, features))
            if p == 0:
                prompts_ref[k] = jnp.max(extra[ROWS - 1 : ROWS]).astype(jnp.int32)
                prompts_ref[2 + k] = jnp.max(extra[ROWS - 2 : ROWS - 1]).astype(jnp.int32)
        shifts.append(jnp.zeros((ROWS - n_seq, features), F32))
        left.append(jnp.concatenate(shifts, axis=0).astype(BF16))
        term = jnp.dot(
            jnp.concatenate(left, axis=0), weight_ref[...], preferred_element_type=F32
        )
        total = term if total is None else total + term
    size = n_seq * tokens // n_enc
    heads = width // HDIM
    step = heads * size + ROWS
    row = lax.broadcasted_iota(jnp.int32, (ROWS, HDIM), 0)
    for z in range(n_enc):
        p, first = divmod(z * size, tokens)
        shift = total[n_seq * tokens + p : n_seq * tokens + p + 1]
        square = squares[p][:, first : first + size]
        square = jnp.concatenate([square, jnp.zeros((1, HDIM - size), F32)], axis=1)
        high = square.astype(BF16).astype(F32)
        extra = jnp.where(
            row == 2 * heads, high, jnp.where(row == 2 * heads + 1, square - high, 0.0)
        )
        for h in range(heads):
            cols = slice(h * HDIM, (h + 1) * HDIM)
            rows_ref[z * step + h * size : z * step + (h + 1) * size] = total[
                z * size : (z + 1) * size, cols
            ]
            high = shift[:, cols].astype(BF16).astype(F32)
            extra = jnp.where(
                row == h, high, jnp.where(row == heads + h, shift[:, cols] - high, extra)
            )
        rows_ref[z * step + heads * size : (z + 1) * step] = extra
    e = lax.axis_index("enc")
    keep_ref[...] = rows_ref[at(e, step)]
    for k, send_ref in enumerate(send_refs):
        send_ref[...] = rows_ref[at(e ^ (k + 1), step)].astype(BF16)


def finish_kernel(n_req, model_width, keep_ref, bias_ref, *refs):
    got_refs, out_ref = refs[:-1], refs[-1]
    r, s = lax.axis_index("req"), lax.axis_index("seq")
    size, width = out_ref.shape
    heads = width // HDIM
    half = width // 2
    inner = bias_ref.shape[1] // 2
    total = keep_ref[...]
    for got_ref in got_refs:
        total = total + got_ref[...].astype(F32)
    extra = total[heads * size :]
    squares = extra[2 * heads : 2 * heads + 1] + extra[2 * heads + 1 : 2 * heads + 2]
    squares = jnp.broadcast_to(squares, (HDIM, HDIM)).T[:size]
    factor = lax.rsqrt(squares * (1.0 / model_width) + epsilon_norm)
    for h in range(heads):
        start = (h * HDIM // half) * inner + (s * n_req + r) * half + h * HDIM % half
        bias = bias_ref[:, pl.ds(pl.multiple_of(start, HDIM), HDIM)].astype(F32)
        shift = extra[h : h + 1] + extra[heads + h : heads + h + 1] + bias
        head = total[h * size : (h + 1) * size] * factor + shift
        if h * HDIM < half:
            head = head * lax.rsqrt(jnp.mean(head * head, axis=1, keepdims=True) + epsilon_norm)
        out_ref[:, h * HDIM : (h + 1) * HDIM] = head.astype(BF16)


def choose_kernel(n_seq, n_enc, chosen_ref, dep_ref, *refs):
    part_refs, out_refs = dict(zip([0] + far_first(n_enc), refs)), refs[n_enc:]
    e, r, s = lax.axis_index("enc"), lax.axis_index("req"), lax.axis_index("seq")
    halves = n_enc // n_seq
    size = part_refs[0].shape[0]
    for k, out_ref in enumerate(out_refs):
        prompt = s ^ chosen_ref[k]
        for h in range(halves):
            place = e ^ (prompt * halves + h)
            for j in range(n_enc):
                @pl.when(place == j)
                def _():
                    out_ref[h * size : (h + 1) * size] = part_refs[j][...]


def weight_kernel(n_req, part, inner, w_ref, dep_ref, own_ref, core_ref, pair_ref, sems):
    r, s = lax.axis_index("req"), lax.axis_index("seq")
    half = part // n_req
    copies = []
    for k, out_ref in enumerate((own_ref, core_ref, pair_ref.at[0], pair_ref.at[1])):
        for side in range(2):
            columns = pl.ds(
                pl.multiple_of(side * inner + (s * n_req + (r ^ k)) * half, HDIM), half
            )
            copies.append(
                pltpu.make_async_copy(
                    w_ref.at[:, columns],
                    out_ref.at[:, pl.ds(side * half, half)],
                    sems.at[2 * k + side],
                )
            )
    for copy in copies:
        copy.start()
    for copy in copies:
        copy.wait()


def image_kernel(part, inner, step, qk_ref, v_ref, x_ref, dep_ref, out_ref, sems):
    start = (lax.axis_index("seq") ^ step) * part
    copies = []
    for i, (ref, base) in enumerate(((qk_ref, 0), (qk_ref, inner), (v_ref, 0), (x_ref, 0))):
        columns = pl.ds(pl.multiple_of(base + start, HDIM), part)
        copies.append(pltpu.make_async_copy(ref.at[:, columns], out_ref.at[i], sems.at[i]))
    for copy in copies:
        copy.start()
    for copy in copies:
        copy.wait()


def maps_kernel(part, down_ref, up_ref, dep_ref, out_ref, sems):
    rank = down_ref.shape[0]
    columns = pl.ds(pl.multiple_of(lax.axis_index("seq") * part, HDIM), part)
    copies = [
        pltpu.make_async_copy(down_ref.at[:, columns], out_ref.at[pl.ds(0, rank)], sems.at[0]),
        pltpu.make_async_copy(up_ref.at[:, columns], out_ref.at[pl.ds(rank, rank)], sems.at[1]),
    ]
    for copy in copies:
        copy.start()
    for copy in copies:
        copy.wait()


def join_maps_kernel(own_ref, core_ref, dep_ref, out_ref):
    out_ref[0] = own_ref[...]
    out_ref[1] = core_ref[...]


def lowrank_kernel(part, adapter_ref, x_ref, got_ref, *refs):
    own_ref, pair_ref, out_ref, chosen_ref = refs
    map_refs = (own_ref.at[0], own_ref.at[1], pair_ref.at[0], pair_ref.at[1])
    place = adapter_ref[0, 0] ^ lax.axis_index("req")
    rank = out_ref.shape[-1]
    for k, ref in enumerate(map_refs):
        @pl.when(place == k)
        def _():
            chosen_ref[...] = ref[rank:]
            own = x_ref[:, pl.ds(pl.multiple_of(lax.axis_index("seq") * part, HDIM), part)]
            for i, rows in enumerate((own, got_ref[3])):
                out_ref[i] = lax.dot_general(
                    rows, ref[:rank], NT, preferred_element_type=F32
                )


def arrange_kernel(n_req, part, inner, low_ref, other_ref, maps_ref, qk_ref, v_ref, *refs):
    got_refs, (q_out, k_out, v_out) = refs[:-3], refs[-3:]
    r, s = lax.axis_index("req"), lax.axis_index("seq")
    half = part // n_req
    tokens = qk_ref.shape[0]
    low = [(low_ref[i] + other_ref[i ^ 1]).astype(BF16) for i in range(2)]
    for k in range(n_req):
        place = (r ^ k) * half
        up = maps_ref[:, pl.ds(pl.multiple_of(place, HDIM), half)]
        for i in range(len(got_refs) + 1):
            rows = slice(i * tokens, (i + 1) * tokens)
            if i == 0:
                own = s * part + place
                q = qk_ref[:, pl.ds(pl.multiple_of(own, HDIM), half)]
                key = qk_ref[:, pl.ds(pl.multiple_of(inner + own, HDIM), half)]
                base = v_ref[:, pl.ds(pl.multiple_of(own, HDIM), half)]
            else:
                columns = pl.ds(pl.multiple_of(place, HDIM), half)
                q = got_refs[i - 1][0, :, columns]
                key = got_refs[i - 1][1, :, columns]
                base = got_refs[i - 1][2, :, columns]
            q_out[k, rows] = q
            k_out[k, rows] = key
            v_out[k, rows] = (
                base.astype(F32) + jnp.dot(low[i], up, preferred_element_type=F32)
            ).astype(BF16)


def heads_kernel(place, first, scale, live_ref, text_ref, q_ref, k_ref, v_ref, *refs):
    out_refs = refs[2:]
    half = q_ref.shape[2]
    size = out_refs[0].shape[0]
    heads = [slice(h * HDIM, (h + 1) * HDIM) for h in range(half // HDIM)]
    live = live_ref[...]
    live = jnp.concatenate([live, jnp.ones((1, k_ref.shape[1]), live.dtype)], axis=1) != 0
    scores = []
    for cols in heads:
        q = q_ref[place, first * size : (first + len(out_refs)) * size, cols]
        keys = jnp.concatenate([text_ref[:, cols], k_ref[place, :, cols]], axis=0)
        score = lax.dot_general(q, keys, NT, preferred_element_type=F32) * scale
        scores.append(jnp.where(live, score, -jnp.inf))
    weights = [jnp.exp(x - jnp.max(x, axis=1, keepdims=True)) for x in scores]
    totals = [jnp.sum(w, axis=1, keepdims=True) for w in weights]
    mixed = []
    for cols, w in zip(heads, weights):
        vals = slice(half + cols.start, half + cols.stop)
        values = jnp.concatenate([text_ref[:, vals], v_ref[place, :, cols]], axis=0)
        mixed.append(jnp.dot(w.astype(BF16), values, preferred_element_type=F32))
    for cols, m, total in zip(heads, mixed, totals):
        rows = (m / total).astype(BF16)
        for i, out_ref in enumerate(out_refs):
            out_ref[:, cols] = rows[i * size : (i + 1) * size]


def assemble_kernel(n_req, n_seq, *refs):
    out_ref = refs[-1]
    r, s = lax.axis_index("req"), lax.axis_index("seq")
    half = refs[0].shape[1]
    for k in range(n_req):
        for i in range(n_seq):
            start = ((s ^ i) * n_req + (r ^ k)) * half
            out_ref[:, pl.ds(pl.multiple_of(start, HDIM), half)] = refs[k * n_seq + i][...]


def per_device_heads(
    n_enc,
    n_req,
    n_seq,
    encoder_hidden,
    prompt_token_ids,
    context_weight,
    context_bias,
    modulation_shift,
    modulation_scale,
    key_value_weight,
    key_value_bias,
    request_prompt,
    adapter_of_request,
    adapter_down_maps,
    adapter_up_maps,
    image_stream_input,
    image_query_key,
    image_value_rows,
):
    e, r, s = lax.axis_index("enc"), lax.axis_index("req"), lax.axis_index("seq")
    model_width = context_weight.shape[1]
    features = context_bias.shape[0]
    tokens = encoder_hidden.shape[1]
    inner = key_value_weight.shape[1] // 2
    part = inner // n_seq
    half = part // n_req
    image_rows = image_query_key.shape[2]
    rank = adapter_up_maps.shape[1]
    qk, base, stream = image_query_key[0, 0], image_value_rows[0, 0], image_stream_input[0, 0]
    dma = pltpu.SemaphoreType.DMA
    stat = struct((8, tokens), F32)

    send, keep, sums = call(
        context_kernel,
        (
            struct((model_width // 2 + ROWS, tokens)),
            struct((model_width // 2, tokens), F32),
            stat,
        ),
        (encoder_hidden[0], context_weight, context_bias),
        name="context",
    )
    got = swap(send, "req", n_req, 1)

    keep, sums, *sends = call(
        functools.partial(scatter_kernel, 2 * features, 0),
        (struct((2 * features, tokens), F32), stat)
        + tuple(struct((2 * features + ROWS, tokens)) for _ in range(1, n_enc)),
        (got, keep, sums),
        name="scatter",
    )
    arrived = partners(lambda k: sends[k - 1], "enc", n_enc).values()
    weight = struct((features, 2 * half))
    weight_own, weight_core, weight_pair = call(
        functools.partial(weight_kernel, n_req, part, inner),
        (weight, weight, struct((2, features, 2 * half))),
        (key_value_weight, keep),
        [ANY] * 2,
        [dma((2 * n_req,))],
        name="weight_pack",
        vmem=16,
    )

    weight_pair_got = swap(weight_pair, "req", n_req, 2)
    bias_columns = jnp.broadcast_to(context_bias.astype(F32)[:, None], (features, tokens))
    scale_columns = jnp.broadcast_to(
        1.0 + modulation_scale[0].astype(F32)[:, None], (features, tokens)
    )
    deps = ()
    send, keep, sums = call(
        functools.partial(merge_kernel, len(deps)),
        (
            struct((2 * features + ROWS, tokens)),
            struct((2 * features, tokens), F32),
            stat,
        ),
        (
            request_prompt,
            keep,
            sums,
            bias_columns,
            modulation_scale,
            modulation_shift,
            *deps,
            *arrived,
        ),
        [SMEM] + [VMEM] * 5 + [ANY] * len(deps) + [VMEM] * len(arrived),
        name="merge",
    )
    got = swap(send, "req", n_req, 2)
    weights = struct((2 * features, 2 * half))
    weight_mine, weight_next = call(
        pass_on_kernel,
        (weights, weights),
        (weight_own, weight_core, weight_pair_got, keep),
        [VMEM] * 3 + [ANY],
        name="pass_on",
    )
    weight_next = swap(weight_next, "req", n_req, 1)
    own = call(
        functools.partial(centre_kernel, model_width),
        struct((2 * features + ROWS, tokens)),
        (request_prompt, weight_mine, keep, sums, got, scale_columns, modulation_shift),
        [SMEM, ANY] + [VMEM] * 5,
        name="centre",
    )
    joined = call(
        join_kernel,
        struct((n_seq * (2 * features + ROWS), tokens)),
        (own, swap(own, "seq", n_seq, 1)),
        name="join",
    )
    packed = [
        call(
            functools.partial(image_kernel, part, inner, k),
            struct((4, image_rows, part)),
            (qk, base, stream, joined),
            [ANY] * 4,
            [dma((4,))],
            name="image_pack",
        )
        for k in range(1, n_seq)
    ]
    image_got = [swap(packed[k - 1], "seq", n_seq, k) for k in range(1, n_seq)]
    weight_pair = lax.optimization_barrier((weight_pair, keep))[0]
    joined_core = swap(joined, "req", n_req, 1)
    maps = call(
        functools.partial(maps_kernel, part),
        struct((2 * rank, part)),
        (adapter_down_maps[0].T, adapter_up_maps[0], joined),
        [ANY] * 3,
        [dma((2,))],
        name="maps_pack",
    )
    maps_core = swap(maps, "req", n_req, 1)
    maps = call(
        join_maps_kernel,
        struct((2, 2 * rank, part)),
        (maps, maps_core, joined),
        [VMEM, VMEM, ANY],
        name="maps_join",
    )

    size = n_seq * tokens // n_enc
    step = 2 * half // HDIM * size + ROWS
    ids, keep, *sends = call(
        functools.partial(project_kernel, n_seq, n_enc),
        (struct((n_req,), jnp.int32), struct((step, HDIM), F32))
        + tuple(struct((step, HDIM)) for _ in range(1, n_enc)),
        (joined, joined_core, weight_mine, weight_next),
        scratch=[pltpu.VMEM((n_enc * step, HDIM), F32)],
        out_specs=(SMEM,) + (VMEM,) * n_enc,
        name="project",
    )
    arrived = partners(lambda k: sends[k - 1], "enc", n_enc).values()

    maps = lax.optimization_barrier((maps, keep))[0]
    maps_pair = swap(maps, "req", n_req, 2)

    text = call(
        functools.partial(finish_kernel, n_req, model_width),
        struct((size, 2 * half)),
        (keep, key_value_bias[None], *arrived),
        [VMEM] * (2 + len(arrived)),
        name="finish",
    )
    low, chosen_maps = call(
        functools.partial(lowrank_kernel, part),
        (struct((n_seq, image_rows, rank), F32), struct((rank, part))),
        (
            adapter_of_request,
            stream,
            image_got[0],
            maps,
            maps_pair,
        ),
        [SMEM] + [VMEM] * 4,
        name="lowrank",
    )
    low_other = swap(low, "seq", n_seq, 1)
    arranged = struct((n_req, n_seq * image_rows, half))
    queries, image_keys, image_values = call(
        functools.partial(arrange_kernel, n_req, part, inner),
        (arranged, arranged, arranged),
        (low, low_other, chosen_maps, qk, base, *image_got),
        name="arrange",
    )
    parts = partners(lambda k: text, "enc", n_enc)
    rows = call(
        functools.partial(choose_kernel, n_seq, n_enc),
        [struct((tokens, 2 * half)) for _ in range(n_req)],
        (ids, low_other, text, *parts.values()),
        [SMEM, ANY] + [VMEM] * n_enc,
        name="choose",
    )
    rows = {0: rows[0], **partners(lambda k: rows[k], "req", n_req)}
    live = lax.dynamic_slice_in_dim(prompt_token_ids, request_prompt[0, 0], 1, 0)
    def heads(k, first, count, last):
        return call(
            functools.partial(heads_kernel, k, first, HDIM ** (-0.5)),
            [struct((image_rows, half))] * count,
            (live, rows[k], queries, image_keys, image_values, *last),
            [VMEM] * 5 + [ANY] * 2,
            name="heads",
        )

    pieces = [None] * n_req
    last = (live, live)
    for k in range(n_req):
        if k < n_req - 1:
            mixed = heads(k, 0, n_seq, last)
        else:
            (back,) = heads(k, 1, 1, last)
            (mine,) = heads(k, 0, 1, (back, last[1]))
            mixed = (mine, back)
        pieces[k] = [mixed[0], swap(mixed[1], "seq", n_seq, 1)]
        last = (mixed[0], pieces[k - 1][1] if k else live)
    result = call(
        functools.partial(assemble_kernel, n_req, n_seq),
        struct((image_rows, inner)),
        tuple(p for group in pieces for p in group),
        name="assemble",
    )
    return result[None, None]


def solution(mesh):
    sizes = mesh.shape
    n_enc, n_req, n_seq = sizes["enc"], sizes["req"], sizes["seq"]

    def run(*arrays):
        heads = arrays[6].shape[1] // (2 * HDIM)
        fits = n_seq == 2 and n_req == 4 and heads % (n_seq * n_req) == 0
        return (per_device_heads if fits else per_device)(n_enc, n_req, n_seq, *arrays)

    return jax.shard_map(
        run,
        mesh=mesh,
        in_specs=(
            P("seq", None, ("enc", "req")),
            P(),
            P(("enc", "req"), None),
            P(("enc", "req")),
            P("seq", ("enc", "req")),
            P("seq", ("enc", "req")),
            P(("enc", "req"), None),
            P(),
            P("enc", "req"),
            P("enc", "req"),
            P("req", None, None),
            P("req", None, None),
            P("enc", "req", "seq", None),
            P("enc", "req", "seq", None),
            P("enc", "req", "seq", None),
        ),
        out_specs=P("enc", "req", "seq", None),
        check_vma=False,
    )
```

```python
import functools

import jax
import jax.numpy as jnp
from jax import lax
from jax.experimental import pallas as pl
from jax.experimental.pallas import tpu as pltpu
from jax.sharding import PartitionSpec as P

HDIM = 128
ROWS = 16

epsilon_norm = 1e-06


def swap(block, axis, size, step):
    return lax.ppermute(block, axis, [(i, i ^ step) for i in range(size)])


def pick(array, index, dim):
    return lax.dynamic_index_in_dim(array, index, dim, keepdims=False)


def split_two(value):
    high = lax.reduce_precision(value, 8, 7)
    return high.astype(jnp.bfloat16), (value - high).astype(jnp.bfloat16)


def bits_of(size):
    return [1 << b for b in range(size.bit_length() - 1)]


def with_stat_rows(data, stat):
    high, low = split_two(stat)
    rows = jnp.concatenate(
        [high[None], low[None], jnp.zeros((ROWS - 2, stat.shape[0]), jnp.bfloat16)], axis=0
    )
    rows = jnp.broadcast_to(rows, data.shape[:-2] + rows.shape)
    return jnp.concatenate([data.astype(jnp.bfloat16), rows], axis=-2)


def attention_kernel(heads, inner, scale, mask_ref, q_ref, kt_ref, vt_ref, ki_ref, vi_ref, o_ref):
    live = mask_ref[...] != 0
    for h in range(heads):
        cols = slice(h * HDIM, (h + 1) * HDIM)
        q = q_ref[:, cols]
        dims = (((1,), (1,)), ((), ()))
        st = lax.dot_general(q, kt_ref[:, cols], dims, preferred_element_type=jnp.float32) * scale
        si = lax.dot_general(q, ki_ref[:, cols], dims, preferred_element_type=jnp.float32) * scale
        st = jnp.where(live, st, -jnp.inf)
        top = jnp.maximum(
            jnp.max(st, axis=1, keepdims=True), jnp.max(si, axis=1, keepdims=True)
        )
        wt = jnp.exp(st - top)
        wi = jnp.exp(si - top)
        total = jnp.sum(wt, axis=1, keepdims=True) + jnp.sum(wi, axis=1, keepdims=True)
        mixed = jnp.dot(
            wt.astype(jnp.bfloat16), vt_ref[:, cols], preferred_element_type=jnp.float32
        ) + jnp.dot(wi.astype(jnp.bfloat16), vi_ref[:, cols], preferred_element_type=jnp.float32)
        o_ref[:, cols] = (mixed / total).astype(o_ref.dtype)


def attention(queries, text_keys, text_values, image_keys, image_values, live):
    width = queries.shape[1]
    heads = width // HDIM
    rows = queries.shape[0]
    mask = jnp.broadcast_to(live.astype(jnp.int32)[None, :], (8, live.shape[0]))[:1]
    return pl.pallas_call(
        functools.partial(attention_kernel, heads, width, HDIM ** (-0.5)),
        out_shape=jax.ShapeDtypeStruct((rows, width), jnp.bfloat16),
        compiler_params=pltpu.CompilerParams(vmem_limit_bytes=48 * 1024 * 1024),
        name="attention",
    )(mask, queries, text_keys, text_values, image_keys, image_values)


def per_device(
    n_enc,
    n_req,
    n_seq,
    encoder_hidden,
    prompt_token_ids,
    context_weight,
    context_bias,
    modulation_shift,
    modulation_scale,
    key_value_weight,
    key_value_bias,
    request_prompt,
    adapter_of_request,
    adapter_down_maps,
    adapter_up_maps,
    image_stream_input,
    image_query_key,
    image_value_rows,
):
    f32, bf16 = jnp.float32, jnp.bfloat16
    e, r, s = lax.axis_index("enc"), lax.axis_index("req"), lax.axis_index("seq")
    req_bits = bits_of(n_req)
    model_width = context_weight.shape[1]
    features = context_bias.shape[0]
    tokens = encoder_hidden.shape[1]
    inner = key_value_weight.shape[1] // 2
    part = inner // n_seq

    def heads_of(array, share):
        return lax.dynamic_slice_in_dim(array, share * part, part, 1)

    qk = image_query_key[0, 0]
    sources = [qk[:, :inner], qk[:, inner:], image_value_rows[0, 0], image_stream_input[0, 0]]
    image_parts = [
        jnp.stack([heads_of(a, s ^ k) for a in sources]) for k in range(n_seq)
    ]
    image_parts = [image_parts[0]] + [
        swap(image_parts[k], "seq", n_seq, k) for k in range(1, n_seq)
    ]
    image_all = jnp.concatenate(image_parts, axis=1)
    queries, image_keys, base_values, stream = [image_all[i] for i in range(4)]

    partial_value = lax.dot_general(
        context_weight, encoder_hidden[0], (((0,), (1,)), ((), ())), preferred_element_type=f32
    )
    stat = jnp.sum(partial_value, axis=0) + jnp.sum(context_bias.astype(f32))
    acc = partial_value.reshape((n_enc,) + (2,) * len(req_bits) + (features, tokens))
    for i, bit in enumerate(req_bits):
        mine = (r // bit) % 2
        dim = len(req_bits) - i
        got = swap(with_stat_rows(pick(acc, 1 - mine, dim), stat), "req", n_req, bit).astype(f32)
        acc = pick(acc, mine, dim) + got[..., :features, :]
        got_stat = got.reshape((-1,) + got.shape[-2:])[0, features:]
        stat = stat + got_stat[0] + got_stat[1]
    arrived = [
        swap(with_stat_rows(pick(acc, e ^ k, 0), stat), "enc", n_enc, k).astype(f32)
        for k in range(1, n_enc)
    ]
    embedded = pick(acc, e, 0)
    for got in arrived:
        embedded = embedded + got[:features]
        stat = stat + got[features] + got[features + 1]
    embedded = embedded + context_bias.astype(f32)[:, None]
    centred = embedded - (stat / model_width)[None, :]
    squares = jnp.sum(centred * centred, axis=0)
    scaled = (1.0 + modulation_scale[0].astype(f32))[:, None] * centred

    own = with_stat_rows(scaled, squares)
    blocks = [own] + [swap(own, "seq", n_seq, k) for k in range(1, n_seq)]
    scaled_all = jnp.concatenate([b[:features] for b in blocks], axis=1)
    squares_all = jnp.concatenate(
        [b[features].astype(f32) + b[features + 1].astype(f32) for b in blocks]
    )
    weight_own = jnp.concatenate(
        [heads_of(key_value_weight[:, :inner], s), heads_of(key_value_weight[:, inner:], s)], axis=1
    )
    width = 2 * part
    projected = lax.dot_general(
        scaled_all, weight_own, (((0,), (0,)), ((), ())), preferred_element_type=f32
    )

    shift_part = jnp.dot(modulation_shift, key_value_weight, preferred_element_type=f32)
    for bit in req_bits:
        shift_part = shift_part + swap(shift_part, "req", n_req, bit)
    for bit in bits_of(n_enc):
        shift_part = shift_part + swap(shift_part, "enc", n_enc, bit)
    shift_part = shift_part + key_value_bias.astype(f32)[None]

    def columns_of(row, share):
        return jnp.concatenate(
            [heads_of(row[:, :inner], share), heads_of(row[:, inner:], share)], axis=1
        )

    shift_rows = jnp.concatenate(
        [columns_of(shift_part, s)]
        + [swap(columns_of(shift_part, s ^ k), "seq", n_seq, k) for k in range(1, n_seq)],
        axis=0,
    )

    halves = tokens // n_req // ROWS
    split = (n_seq,) + (2,) * len(req_bits) + (halves, ROWS)
    acc = projected.reshape(split + (width,))
    acc_stat = squares_all.reshape(split)

    def with_stat_columns(data, stat):
        high, low = split_two(stat)
        lane = lax.broadcasted_iota(jnp.int32, stat.shape + (HDIM,), stat.ndim)
        columns = jnp.where(
            lane == 0, high[..., None], jnp.where(lane == 1, low[..., None], jnp.zeros((), bf16))
        )
        return jnp.concatenate([data.astype(bf16), columns], axis=-1)

    for i, bit in enumerate(req_bits):
        mine = (r // bit) % 2
        dim = len(req_bits) - i
        got = swap(
            with_stat_columns(pick(acc, 1 - mine, dim), pick(acc_stat, 1 - mine, dim)),
            "req", n_req, bit,
        ).astype(f32)
        acc = pick(acc, mine, dim) + got[..., :width]
        acc_stat = pick(acc_stat, mine, dim) + got[..., width] + got[..., width + 1]
    acc = acc.reshape(n_enc, ROWS, width)
    acc_stat = acc_stat.reshape(n_enc, ROWS)
    arrived = [
        swap(with_stat_columns(pick(acc, e ^ k, 0), pick(acc_stat, e ^ k, 0)), "enc", n_enc, k)
        .astype(f32)
        for k in range(1, n_enc)
    ]
    rows = pick(acc, e, 0)
    row_squares = pick(acc_stat, e, 0)
    for got in arrived:
        rows = rows + got[:, :width]
        row_squares = row_squares + got[:, width] + got[:, width + 1]
    rows = rows * lax.rsqrt(row_squares / model_width + epsilon_norm)[:, None]
    rows = rows + pick(shift_rows, e // halves, 0)[None]
    keys = rows[:, :part].reshape(ROWS, part // HDIM, HDIM)
    keys = keys * lax.rsqrt(jnp.mean(keys * keys, axis=2, keepdims=True) + epsilon_norm)
    text = jnp.concatenate([keys.reshape(ROWS, part), rows[:, part:]], axis=1).astype(bf16)

    chosen = request_prompt[0, 0]
    relative = s ^ chosen
    by_enc = [text] + [swap(text, "enc", n_enc, k) for k in range(1, n_enc)]
    by_enc = jnp.stack(by_enc)
    by_enc = jnp.stack([pick(by_enc, k ^ e, 0) for k in range(n_enc)])
    held = by_enc.reshape(1, n_seq, halves, ROWS, width)
    first = req_bits[0]
    held = jnp.concatenate([held, swap(held, "req", n_req, first)], axis=0)
    groups = [pick(held, relative, 1)]
    for step in range(2, n_req, 2):
        wanted = swap(relative, "req", n_req, step)
        groups.append(swap(pick(held, wanted, 1), "req", n_req, step))
    text_rows = jnp.concatenate(groups, axis=0).reshape(-1, width)
    live = pick(prompt_token_ids, chosen, 0) != 0
    live = live.reshape(n_req, halves * ROWS)
    live = jnp.concatenate([pick(live, r ^ k, 0) for k in range(n_req)])

    down = lax.dynamic_slice_in_dim(adapter_down_maps[0], s * part, part, 0).T
    up = heads_of(adapter_up_maps[0], s)
    maps = jnp.concatenate([down, up], axis=0)[None]
    for bit in reversed(req_bits):
        maps = jnp.concatenate([maps, swap(maps, "req", n_req, bit)], axis=0)
    other = adapter_of_request[0, 0] ^ r
    index = 0
    for bit in req_bits:
        index = index * 2 + (other // bit) % 2
    chosen_maps = pick(maps, index, 0)
    rank = up.shape[0]
    lowrank = lax.dot_general(
        stream, chosen_maps[:rank], (((1,), (1,)), ((), ())), preferred_element_type=f32
    ).reshape(n_seq, -1, rank)
    for bit in bits_of(n_seq):
        got = swap(lowrank, "seq", n_seq, bit)
        lowrank = lowrank + jnp.stack([got[k ^ bit] for k in range(n_seq)])
    lowrank = lowrank.reshape(-1, rank).astype(bf16)
    image_values = (
        base_values.astype(f32) + jnp.dot(lowrank, chosen_maps[rank:], preferred_element_type=f32)
    ).astype(bf16)

    mixed = attention(
        queries, text_rows[:, :part], text_rows[:, part:], image_keys, image_values, live
    ).reshape(n_seq, -1, part)
    pieces = jnp.stack([mixed[0]] + [swap(mixed[k], "seq", n_seq, k) for k in range(1, n_seq)])
    result = jnp.concatenate([pick(pieces, s ^ k, 0) for k in range(n_seq)], axis=1)
    return result[None, None]


F32, BF16 = jnp.float32, jnp.bfloat16
ANY = pl.BlockSpec(memory_space=pl.ANY)
VMEM = pl.BlockSpec(memory_space=pltpu.VMEM)
SMEM = pl.BlockSpec(memory_space=pltpu.SMEM)
NT = (((1,), (1,)), ((), ()))
TN = (((0,), (0,)), ((), ()))


def partners(send, axis, size):
    return {k: swap(send(k), axis, size, k) for k in far_first(size)}


def far_first(size):
    return [k for k in range(2, size)] + [1]


def call(kernel, outs, ins, specs=None, scratch=(), name=None, out_specs=None, vmem=16):
    return pl.pallas_call(
        kernel,
        out_shape=outs,
        in_specs=specs if specs is not None else [VMEM] * len(ins),
        out_specs=out_specs if out_specs is not None else jax.tree.map(lambda _: VMEM, outs),
        scratch_shapes=list(scratch),
        compiler_params=pltpu.CompilerParams(vmem_limit_bytes=int(vmem * 1024 * 1024)),
        name=name,
    )(*ins)


def struct(shape, dtype=BF16):
    return jax.ShapeDtypeStruct(shape, dtype)


def at(index, size):
    return pl.ds(pl.multiple_of(index * size, size), size)


def stat_rows(stat):
    high = stat.astype(BF16).astype(F32)
    row = lax.broadcasted_iota(jnp.int32, (ROWS, stat.shape[1]), 0)
    return jnp.where(row == 0, high, jnp.where(row == 1, stat - high, 0.0)).astype(BF16)


def stat_of(rows):
    rows = rows.astype(F32)
    return rows[0:1] + rows[1:2]


def context_kernel(h_ref, w_ref, b_ref, send_ref, keep_ref, stat_ref):
    mine = lax.rem(lax.axis_index("req"), 2)
    features = b_ref.shape[0]
    pairs = w_ref.shape[1] // (2 * features)
    total = jnp.zeros((1, h_ref.shape[0]), F32)
    for p in range(pairs):
        product = jnp.dot(
            h_ref[...], w_ref[:, p * 2 * features : (p + 1) * 2 * features],
            preferred_element_type=F32,
        ).T
        total = total + jnp.sum(product, axis=0, keepdims=True)
        low, high = product[:features], product[features:]
        rows = slice(p * features, (p + 1) * features)
        keep_ref[rows] = jnp.where(mine == 0, low, high)
        send_ref[rows] = jnp.where(mine == 0, high, low).astype(BF16)
    stat = total + jnp.sum(b_ref[...].astype(F32))
    send_ref[pairs * features :] = stat_rows(stat)
    stat_ref[...] = jnp.broadcast_to(stat, stat_ref.shape)


def scatter_kernel(features, deps, got_ref, keep_ref, stat_ref, *refs):
    kept_ref, out_stat_ref, *send_refs = refs[deps:]
    e = lax.axis_index("enc")
    count = keep_ref.shape[0] // features
    stat = stat_ref[0:1] + stat_of(got_ref[count * features :])
    own = at(e, features)
    for k, send_ref in enumerate(send_refs):
        other = at(e ^ (k + 1), features)
        send_ref[:features] = (keep_ref[other] + got_ref[other].astype(F32)).astype(BF16)
        send_ref[features:] = stat_rows(stat)
    kept_ref[...] = keep_ref[own] + got_ref[own].astype(F32)
    out_stat_ref[...] = jnp.broadcast_to(stat, out_stat_ref.shape)


def lane_rows(rows, first, values, extra):
    tokens = extra.shape[1]
    for j in range(pl.cdiv(values.shape[1], tokens)):
        piece = values[:, j * tokens : min((j + 1) * tokens, values.shape[1])]
        gap = tokens - piece.shape[1]
        if gap:
            piece = jnp.concatenate([piece, jnp.zeros((1, gap), F32)], axis=1)
        extra = jnp.where(rows == first + j, piece, extra)
    return extra


def from_rows(extra, first, count):
    tokens = extra.shape[1]
    pieces = [extra[first + j : first + j + 1] for j in range(pl.cdiv(count, tokens))]
    return jnp.concatenate(pieces, axis=1)[:, :count]


def merge_kernel(deps, prompt_ref, keep_ref, stat_ref, bias_ref, scale_ref, shift_ref, *refs):
    got_refs, (send_ref, kept_ref, out_stat_ref) = refs[deps:-3], refs[-3:]
    features, tokens = bias_ref.shape
    mine = lax.rem(lax.axis_index("req") // 2, 2)
    total = keep_ref[...]
    stat = stat_ref[0:1]
    for got_ref in got_refs:
        total = total + got_ref[: 2 * features].astype(F32)
        stat = stat + stat_of(got_ref[2 * features :])
    kept_ref[...] = total
    own = at(mine, features)
    kept_ref[own] = kept_ref[own] + bias_ref[...]
    send_ref[: 2 * features] = kept_ref[...].astype(BF16)
    rows = lax.broadcasted_iota(jnp.int32, (ROWS, tokens), 0)
    extra = stat_rows(stat).astype(F32)
    extra = lane_rows(rows, 2, scale_ref[...].astype(F32), extra)
    extra = lane_rows(rows, 6, shift_ref[...].astype(F32), extra)
    extra = jnp.where(rows == ROWS - 1, prompt_ref[0, 0].astype(F32), extra)
    send_ref[2 * features :] = extra.astype(BF16)
    out_stat_ref[...] = jnp.broadcast_to(stat, out_stat_ref.shape)


def centre_kernel(
    width, prompt_ref, dep_ref, keep_ref, stat_ref, got_ref, scale_ref, shift_ref, out_ref
):
    features, tokens = scale_ref.shape
    mine = lax.rem(lax.axis_index("req") // 2, 2)
    extra = got_ref[2 * features :].astype(F32)
    stat = stat_ref[0:1] + extra[0:1] + extra[1:2]
    average = stat * (1.0 / width)
    scale = from_rows(extra, 2, features)
    columns = []
    for first in range(0, features, tokens):
        piece = scale[:, first : min(first + tokens, features)]
        piece = jnp.broadcast_to(piece, (tokens, piece.shape[1]))
        gap = tokens - piece.shape[1]
        if gap:
            piece = jnp.concatenate([piece, jnp.zeros((tokens, gap), F32)], axis=1)
        columns.append(piece.T[: min(tokens, features - first)])
    scales = (scale_ref[...], 1.0 + jnp.concatenate(columns, axis=0))
    squares = jnp.zeros((1, tokens), F32)
    for i in range(2):
        block = at(mine ^ i, features)
        centred = keep_ref[block] + got_ref[block].astype(F32) - average
        squares = squares + jnp.sum(centred * centred, axis=0, keepdims=True)
        out_ref[i * features : (i + 1) * features] = (scales[i] * centred).astype(BF16)
    shift = jnp.concatenate([shift_ref[...].astype(F32), from_rows(extra, 6, features)], axis=1)
    other_prompt = extra[ROWS - 1 : ROWS]
    rows = lax.broadcasted_iota(jnp.int32, (ROWS, tokens), 0)
    extra = stat_rows(squares).astype(F32)
    extra = lane_rows(rows, 2, shift, extra)
    extra = jnp.where(rows == ROWS - 1, prompt_ref[0, 0].astype(F32), extra)
    extra = jnp.where(rows == ROWS - 2, other_prompt, extra)
    out_ref[2 * features :] = extra.astype(BF16)


def pass_on_kernel(own_ref, core_ref, got_ref, dep_ref, mine_ref, next_ref):
    features = own_ref.shape[0]
    mine_ref[:features] = own_ref[...]
    mine_ref[features:] = got_ref[0]
    next_ref[:features] = core_ref[...]
    next_ref[features:] = got_ref[1]


def join_kernel(own_ref, got_ref, out_ref):
    size = own_ref.shape[0]
    out_ref[:size] = own_ref[...]
    out_ref[size:] = got_ref[...]


def project_kernel(n_seq, n_enc, *refs):
    payload_refs, weight_refs, refs = refs[:2], refs[2:4], refs[4:]
    prompts_ref, keep_ref, *send_refs = refs[:-1]
    rows_ref = refs[-1]
    features, width = weight_refs[0].shape
    tokens = payload_refs[0].shape[1]
    stride = features + ROWS
    total = None
    squares = [jnp.zeros((1, tokens), F32) for _ in range(n_seq)]
    for k, (payload, weight_ref) in enumerate(zip(payload_refs, weight_refs)):
        left = []
        shifts = []
        for p in range(n_seq):
            left.append(payload[p * stride : p * stride + features].T)
            extra = payload[p * stride + features : (p + 1) * stride].astype(F32)
            squares[p] = squares[p] + extra[0:1] + extra[1:2]
            shifts.append(from_rows(extra, 2, features))
            if p == 0:
                prompts_ref[k] = jnp.max(extra[ROWS - 1 : ROWS]).astype(jnp.int32)
                prompts_ref[2 + k] = jnp.max(extra[ROWS - 2 : ROWS - 1]).astype(jnp.int32)
        shifts.append(jnp.zeros((ROWS - n_seq, features), F32))
        left.append(jnp.concatenate(shifts, axis=0).astype(BF16))
        term = jnp.dot(
            jnp.concatenate(left, axis=0), weight_ref[...], preferred_element_type=F32
        )
        total = term if total is None else total + term
    size = n_seq * tokens // n_enc
    heads = width // HDIM
    step = heads * size + ROWS
    row = lax.broadcasted_iota(jnp.int32, (ROWS, HDIM), 0)
    for z in range(n_enc):
        p, first = divmod(z * size, tokens)
        shift = total[n_seq * tokens + p : n_seq * tokens + p + 1]
        square = squares[p][:, first : first + size]
        square = jnp.concatenate([square, jnp.zeros((1, HDIM - size), F32)], axis=1)
        high = square.astype(BF16).astype(F32)
        extra = jnp.where(
            row == 2 * heads, high, jnp.where(row == 2 * heads + 1, square - high, 0.0)
        )
        for h in range(heads):
            cols = slice(h * HDIM, (h + 1) * HDIM)
            rows_ref[z * step + h * size : z * step + (h + 1) * size] = total[
                z * size : (z + 1) * size, cols
            ]
            high = shift[:, cols].astype(BF16).astype(F32)
            extra = jnp.where(
                row == h, high, jnp.where(row == heads + h, shift[:, cols] - high, extra)
            )
        rows_ref[z * step + heads * size : (z + 1) * step] = extra
    e = lax.axis_index("enc")
    keep_ref[...] = rows_ref[at(e, step)]
    for k, send_ref in enumerate(send_refs):
        send_ref[...] = rows_ref[at(e ^ (k + 1), step)].astype(BF16)


def finish_kernel(n_req, model_width, keep_ref, bias_ref, *refs):
    got_refs, out_ref = refs[:-1], refs[-1]
    r, s = lax.axis_index("req"), lax.axis_index("seq")
    size, width = out_ref.shape
    heads = width // HDIM
    half = width // 2
    inner = bias_ref.shape[1] // 2
    total = keep_ref[...]
    for got_ref in got_refs:
        total = total + got_ref[...].astype(F32)
    extra = total[heads * size :]
    squares = extra[2 * heads : 2 * heads + 1] + extra[2 * heads + 1 : 2 * heads + 2]
    squares = jnp.broadcast_to(squares, (HDIM, HDIM)).T[:size]
    factor = lax.rsqrt(squares * (1.0 / model_width) + epsilon_norm)
    for h in range(heads):
        start = (h * HDIM // half) * inner + (s * n_req + r) * half + h * HDIM % half
        bias = bias_ref[:, pl.ds(pl.multiple_of(start, HDIM), HDIM)].astype(F32)
        shift = extra[h : h + 1] + extra[heads + h : heads + h + 1] + bias
        head = total[h * size : (h + 1) * size] * factor + shift
        if h * HDIM < half:
            head = head * lax.rsqrt(jnp.mean(head * head, axis=1, keepdims=True) + epsilon_norm)
        out_ref[:, h * HDIM : (h + 1) * HDIM] = head.astype(BF16)


def choose_kernel(n_seq, n_enc, chosen_ref, dep_ref, *refs):
    part_refs, out_refs = dict(zip([0] + far_first(n_enc), refs)), refs[n_enc:]
    e, r, s = lax.axis_index("enc"), lax.axis_index("req"), lax.axis_index("seq")
    halves = n_enc // n_seq
    size = part_refs[0].shape[0]
    for k, out_ref in enumerate(out_refs):
        prompt = s ^ chosen_ref[k]
        for h in range(halves):
            place = e ^ (prompt * halves + h)
            for j in range(n_enc):
                @pl.when(place == j)
                def _():
                    out_ref[h * size : (h + 1) * size] = part_refs[j][...]


def weight_kernel(n_req, part, inner, w_ref, dep_ref, own_ref, core_ref, pair_ref, sems):
    r, s = lax.axis_index("req"), lax.axis_index("seq")
    half = part // n_req
    copies = []
    for k, out_ref in enumerate((own_ref, core_ref, pair_ref.at[0], pair_ref.at[1])):
        for side in range(2):
            columns = pl.ds(
                pl.multiple_of(side * inner + (s * n_req + (r ^ k)) * half, HDIM), half
            )
            copies.append(
                pltpu.make_async_copy(
                    w_ref.at[:, columns],
                    out_ref.at[:, pl.ds(side * half, half)],
                    sems.at[2 * k + side],
                )
            )
    for copy in copies:
        copy.start()
    for copy in copies:
        copy.wait()


def image_kernel(part, inner, step, qk_ref, v_ref, x_ref, dep_ref, out_ref, sems):
    start = (lax.axis_index("seq") ^ step) * part
    copies = []
    for i, (ref, base) in enumerate(((qk_ref, 0), (qk_ref, inner), (v_ref, 0), (x_ref, 0))):
        columns = pl.ds(pl.multiple_of(base + start, HDIM), part)
        copies.append(pltpu.make_async_copy(ref.at[:, columns], out_ref.at[i], sems.at[i]))
    for copy in copies:
        copy.start()
    for copy in copies:
        copy.wait()


def maps_kernel(part, down_ref, up_ref, dep_ref, out_ref, sems):
    rank = down_ref.shape[0]
    columns = pl.ds(pl.multiple_of(lax.axis_index("seq") * part, HDIM), part)
    copies = [
        pltpu.make_async_copy(down_ref.at[:, columns], out_ref.at[pl.ds(0, rank)], sems.at[0]),
        pltpu.make_async_copy(up_ref.at[:, columns], out_ref.at[pl.ds(rank, rank)], sems.at[1]),
    ]
    for copy in copies:
        copy.start()
    for copy in copies:
        copy.wait()


def join_maps_kernel(own_ref, core_ref, dep_ref, out_ref):
    out_ref[0] = own_ref[...]
    out_ref[1] = core_ref[...]


def lowrank_kernel(part, adapter_ref, x_ref, got_ref, *refs):
    own_ref, pair_ref, out_ref, chosen_ref = refs
    map_refs = (own_ref.at[0], own_ref.at[1], pair_ref.at[0], pair_ref.at[1])
    place = adapter_ref[0, 0] ^ lax.axis_index("req")
    rank = out_ref.shape[-1]
    for k, ref in enumerate(map_refs):
        @pl.when(place == k)
        def _():
            chosen_ref[...] = ref[rank:]
            own = x_ref[:, pl.ds(pl.multiple_of(lax.axis_index("seq") * part, HDIM), part)]
            for i, rows in enumerate((own, got_ref[3])):
                out_ref[i] = lax.dot_general(
                    rows, ref[:rank], NT, preferred_element_type=F32
                )


def arrange_kernel(n_req, part, inner, low_ref, other_ref, maps_ref, qk_ref, v_ref, *refs):
    got_refs, (q_out, k_out, v_out) = refs[:-3], refs[-3:]
    r, s = lax.axis_index("req"), lax.axis_index("seq")
    half = part // n_req
    tokens = qk_ref.shape[0]
    low = [(low_ref[i] + other_ref[i ^ 1]).astype(BF16) for i in range(2)]
    for k in range(n_req):
        place = (r ^ k) * half
        up = maps_ref[:, pl.ds(pl.multiple_of(place, HDIM), half)]
        for i in range(len(got_refs) + 1):
            rows = slice(i * tokens, (i + 1) * tokens)
            if i == 0:
                own = s * part + place
                q = qk_ref[:, pl.ds(pl.multiple_of(own, HDIM), half)]
                key = qk_ref[:, pl.ds(pl.multiple_of(inner + own, HDIM), half)]
                base = v_ref[:, pl.ds(pl.multiple_of(own, HDIM), half)]
            else:
                columns = pl.ds(pl.multiple_of(place, HDIM), half)
                q = got_refs[i - 1][0, :, columns]
                key = got_refs[i - 1][1, :, columns]
                base = got_refs[i - 1][2, :, columns]
            q_out[k, rows] = q
            k_out[k, rows] = key
            v_out[k, rows] = (
                base.astype(F32) + jnp.dot(low[i], up, preferred_element_type=F32)
            ).astype(BF16)


def heads_kernel(place, first, scale, live_ref, text_ref, q_ref, k_ref, v_ref, *refs):
    out_refs = refs[2:]
    half = q_ref.shape[2]
    size = out_refs[0].shape[0]
    heads = [slice(h * HDIM, (h + 1) * HDIM) for h in range(half // HDIM)]
    live = live_ref[...]
    live = jnp.concatenate([live, jnp.ones((1, k_ref.shape[1]), live.dtype)], axis=1) != 0
    scores = []
    for cols in heads:
        q = q_ref[place, first * size : (first + len(out_refs)) * size, cols]
        keys = jnp.concatenate([text_ref[:, cols], k_ref[place, :, cols]], axis=0)
        score = lax.dot_general(q, keys, NT, preferred_element_type=F32) * scale
        scores.append(jnp.where(live, score, -jnp.inf))
    weights = [jnp.exp(x - jnp.max(x, axis=1, keepdims=True)) for x in scores]
    totals = [jnp.sum(w, axis=1, keepdims=True) for w in weights]
    mixed = []
    for cols, w in zip(heads, weights):
        vals = slice(half + cols.start, half + cols.stop)
        values = jnp.concatenate([text_ref[:, vals], v_ref[place, :, cols]], axis=0)
        mixed.append(jnp.dot(w.astype(BF16), values, preferred_element_type=F32))
    for cols, m, total in zip(heads, mixed, totals):
        rows = (m / total).astype(BF16)
        for i, out_ref in enumerate(out_refs):
            out_ref[:, cols] = rows[i * size : (i + 1) * size]


def assemble_kernel(n_req, n_seq, *refs):
    out_ref = refs[-1]
    r, s = lax.axis_index("req"), lax.axis_index("seq")
    half = refs[0].shape[1]
    for k in range(n_req):
        for i in range(n_seq):
            start = ((s ^ i) * n_req + (r ^ k)) * half
            out_ref[:, pl.ds(pl.multiple_of(start, HDIM), half)] = refs[k * n_seq + i][...]


def per_device_heads(
    n_enc,
    n_req,
    n_seq,
    encoder_hidden,
    prompt_token_ids,
    context_weight,
    context_bias,
    modulation_shift,
    modulation_scale,
    key_value_weight,
    key_value_bias,
    request_prompt,
    adapter_of_request,
    adapter_down_maps,
    adapter_up_maps,
    image_stream_input,
    image_query_key,
    image_value_rows,
):
    e, r, s = lax.axis_index("enc"), lax.axis_index("req"), lax.axis_index("seq")
    model_width = context_weight.shape[1]
    features = context_bias.shape[0]
    tokens = encoder_hidden.shape[1]
    inner = key_value_weight.shape[1] // 2
    part = inner // n_seq
    half = part // n_req
    image_rows = image_query_key.shape[2]
    rank = adapter_up_maps.shape[1]
    qk, base, stream = image_query_key[0, 0], image_value_rows[0, 0], image_stream_input[0, 0]
    dma = pltpu.SemaphoreType.DMA
    stat = struct((8, tokens), F32)

    send, keep, sums = call(
        context_kernel,
        (
            struct((model_width // 2 + ROWS, tokens)),
            struct((model_width // 2, tokens), F32),
            stat,
        ),
        (encoder_hidden[0], context_weight, context_bias),
        name="context",
    )
    got = swap(send, "req", n_req, 1)

    keep, sums, *sends = call(
        functools.partial(scatter_kernel, 2 * features, 0),
        (struct((2 * features, tokens), F32), stat)
        + tuple(struct((2 * features + ROWS, tokens)) for _ in range(1, n_enc)),
        (got, keep, sums),
        name="scatter",
    )
    arrived = partners(lambda k: sends[k - 1], "enc", n_enc).values()
    weight = struct((features, 2 * half))
    weight_own, weight_core, weight_pair = call(
        functools.partial(weight_kernel, n_req, part, inner),
        (weight, weight, struct((2, features, 2 * half))),
        (key_value_weight, keep),
        [ANY] * 2,
        [dma((2 * n_req,))],
        name="weight_pack",
        vmem=16,
    )

    weight_pair_got = swap(weight_pair, "req", n_req, 2)
    bias_columns = jnp.broadcast_to(context_bias.astype(F32)[:, None], (features, tokens))
    scale_columns = jnp.broadcast_to(
        1.0 + modulation_scale[0].astype(F32)[:, None], (features, tokens)
    )
    deps = ()
    send, keep, sums = call(
        functools.partial(merge_kernel, len(deps)),
        (
            struct((2 * features + ROWS, tokens)),
            struct((2 * features, tokens), F32),
            stat,
        ),
        (
            request_prompt,
            keep,
            sums,
            bias_columns,
            modulation_scale,
            modulation_shift,
            *deps,
            *arrived,
        ),
        [SMEM] + [VMEM] * 5 + [ANY] * len(deps) + [VMEM] * len(arrived),
        name="merge",
    )
    got = swap(send, "req", n_req, 2)
    weights = struct((2 * features, 2 * half))
    weight_mine, weight_next = call(
        pass_on_kernel,
        (weights, weights),
        (weight_own, weight_core, weight_pair_got, keep),
        [VMEM] * 3 + [ANY],
        name="pass_on",
    )
    weight_next = swap(weight_next, "req", n_req, 1)
    own = call(
        functools.partial(centre_kernel, model_width),
        struct((2 * features + ROWS, tokens)),
        (request_prompt, weight_mine, keep, sums, got, scale_columns, modulation_shift),
        [SMEM, ANY] + [VMEM] * 5,
        name="centre",
    )
    joined = call(
        join_kernel,
        struct((n_seq * (2 * features + ROWS), tokens)),
        (own, swap(own, "seq", n_seq, 1)),
        name="join",
    )
    packed = [
        call(
            functools.partial(image_kernel, part, inner, k),
            struct((4, image_rows, part)),
            (qk, base, stream, joined),
            [ANY] * 4,
            [dma((4,))],
            name="image_pack",
        )
        for k in range(1, n_seq)
    ]
    image_got = [swap(packed[k - 1], "seq", n_seq, k) for k in range(1, n_seq)]
    weight_pair = lax.optimization_barrier((weight_pair, keep))[0]
    joined_core = swap(joined, "req", n_req, 1)
    maps = call(
        functools.partial(maps_kernel, part),
        struct((2 * rank, part)),
        (adapter_down_maps[0].T, adapter_up_maps[0], joined),
        [ANY] * 3,
        [dma((2,))],
        name="maps_pack",
    )
    maps_core = swap(maps, "req", n_req, 1)
    maps = call(
        join_maps_kernel,
        struct((2, 2 * rank, part)),
        (maps, maps_core, joined),
        [VMEM, VMEM, ANY],
        name="maps_join",
    )

    size = n_seq * tokens // n_enc
    step = 2 * half // HDIM * size + ROWS
    ids, keep, *sends = call(
        functools.partial(project_kernel, n_seq, n_enc),
        (struct((n_req,), jnp.int32), struct((step, HDIM), F32))
        + tuple(struct((step, HDIM)) for _ in range(1, n_enc)),
        (joined, joined_core, weight_mine, weight_next),
        scratch=[pltpu.VMEM((n_enc * step, HDIM), F32)],
        out_specs=(SMEM,) + (VMEM,) * n_enc,
        name="project",
    )
    arrived = partners(lambda k: sends[k - 1], "enc", n_enc).values()

    maps = lax.optimization_barrier((maps, keep))[0]
    maps_pair = swap(maps, "req", n_req, 2)

    text = call(
        functools.partial(finish_kernel, n_req, model_width),
        struct((size, 2 * half)),
        (keep, key_value_bias[None], *arrived),
        [VMEM] * (2 + len(arrived)),
        name="finish",
    )
    low, chosen_maps = call(
        functools.partial(lowrank_kernel, part),
        (struct((n_seq, image_rows, rank), F32), struct((rank, part))),
        (
            adapter_of_request,
            stream,
            image_got[0],
            maps,
            maps_pair,
        ),
        [SMEM] + [VMEM] * 4,
        name="lowrank",
    )
    low_other = swap(low, "seq", n_seq, 1)
    arranged = struct((n_req, n_seq * image_rows, half))
    queries, image_keys, image_values = call(
        functools.partial(arrange_kernel, n_req, part, inner),
        (arranged, arranged, arranged),
        (low, low_other, chosen_maps, qk, base, *image_got),
        name="arrange",
    )
    parts = partners(lambda k: text, "enc", n_enc)
    rows = call(
        functools.partial(choose_kernel, n_seq, n_enc),
        [struct((tokens, 2 * half)) for _ in range(n_req)],
        (ids, image_values, text, *parts.values()),
        [SMEM, ANY] + [VMEM] * n_enc,
        name="choose",
    )
    rows = {0: rows[0], **partners(lambda k: rows[k], "req", n_req)}
    live = lax.dynamic_slice_in_dim(prompt_token_ids, request_prompt[0, 0], 1, 0)
    def heads(k, first, count, last):
        return call(
            functools.partial(heads_kernel, k, first, HDIM ** (-0.5)),
            [struct((image_rows, half))] * count,
            (live, rows[k], queries, image_keys, image_values, *last),
            [VMEM] * 5 + [ANY] * 2,
            name="heads",
        )

    pieces = [None] * n_req
    last = (live, live)
    for k in range(n_req):
        if k < n_req - 1:
            mixed = heads(k, 0, n_seq, last)
        else:
            (back,) = heads(k, 1, 1, last)
            (mine,) = heads(k, 0, 1, (back, last[1]))
            mixed = (mine, back)
        pieces[k] = [mixed[0], swap(mixed[1], "seq", n_seq, 1)]
        last = (mixed[0], pieces[k - 1][1] if k else live)
    result = call(
        functools.partial(assemble_kernel, n_req, n_seq),
        struct((image_rows, inner)),
        tuple(p for group in pieces for p in group),
        name="assemble",
    )
    return result[None, None]


def solution(mesh):
    sizes = mesh.shape
    n_enc, n_req, n_seq = sizes["enc"], sizes["req"], sizes["seq"]

    def run(*arrays):
        heads = arrays[6].shape[1] // (2 * HDIM)
        fits = n_seq == 2 and n_req == 4 and heads % (n_seq * n_req) == 0
        return (per_device_heads if fits else per_device)(n_enc, n_req, n_seq, *arrays)

    return jax.shard_map(
        run,
        mesh=mesh,
        in_specs=(
            P("seq", None, ("enc", "req")),
            P(),
            P(("enc", "req"), None),
            P(("enc", "req")),
            P("seq", ("enc", "req")),
            P("seq", ("enc", "req")),
            P(("enc", "req"), None),
            P(),
            P("enc", "req"),
            P("enc", "req"),
            P("req", None, None),
            P("req", None, None),
            P("enc", "req", "seq", None),
            P("enc", "req", "seq", None),
            P("enc", "req", "seq", None),
        ),
        out_specs=P("enc", "req", "seq", None),
        check_vma=False,
    )
```

```python
import functools

import jax
import jax.numpy as jnp
from jax import lax
from jax.experimental import pallas as pl
from jax.experimental.pallas import tpu as pltpu
from jax.sharding import PartitionSpec as P

HDIM = 128
ROWS = 16

epsilon_norm = 1e-06


def swap(block, axis, size, step):
    return lax.ppermute(block, axis, [(i, i ^ step) for i in range(size)])


def pick(array, index, dim):
    return lax.dynamic_index_in_dim(array, index, dim, keepdims=False)


def split_two(value):
    high = lax.reduce_precision(value, 8, 7)
    return high.astype(jnp.bfloat16), (value - high).astype(jnp.bfloat16)


def bits_of(size):
    return [1 << b for b in range(size.bit_length() - 1)]


def with_stat_rows(data, stat):
    high, low = split_two(stat)
    rows = jnp.concatenate(
        [high[None], low[None], jnp.zeros((ROWS - 2, stat.shape[0]), jnp.bfloat16)], axis=0
    )
    rows = jnp.broadcast_to(rows, data.shape[:-2] + rows.shape)
    return jnp.concatenate([data.astype(jnp.bfloat16), rows], axis=-2)


def attention_kernel(heads, inner, scale, mask_ref, q_ref, kt_ref, vt_ref, ki_ref, vi_ref, o_ref):
    live = mask_ref[...] != 0
    for h in range(heads):
        cols = slice(h * HDIM, (h + 1) * HDIM)
        q = q_ref[:, cols]
        dims = (((1,), (1,)), ((), ()))
        st = lax.dot_general(q, kt_ref[:, cols], dims, preferred_element_type=jnp.float32) * scale
        si = lax.dot_general(q, ki_ref[:, cols], dims, preferred_element_type=jnp.float32) * scale
        st = jnp.where(live, st, -jnp.inf)
        top = jnp.maximum(
            jnp.max(st, axis=1, keepdims=True), jnp.max(si, axis=1, keepdims=True)
        )
        wt = jnp.exp(st - top)
        wi = jnp.exp(si - top)
        total = jnp.sum(wt, axis=1, keepdims=True) + jnp.sum(wi, axis=1, keepdims=True)
        mixed = jnp.dot(
            wt.astype(jnp.bfloat16), vt_ref[:, cols], preferred_element_type=jnp.float32
        ) + jnp.dot(wi.astype(jnp.bfloat16), vi_ref[:, cols], preferred_element_type=jnp.float32)
        o_ref[:, cols] = (mixed / total).astype(o_ref.dtype)


def attention(queries, text_keys, text_values, image_keys, image_values, live):
    width = queries.shape[1]
    heads = width // HDIM
    rows = queries.shape[0]
    mask = jnp.broadcast_to(live.astype(jnp.int32)[None, :], (8, live.shape[0]))[:1]
    return pl.pallas_call(
        functools.partial(attention_kernel, heads, width, HDIM ** (-0.5)),
        out_shape=jax.ShapeDtypeStruct((rows, width), jnp.bfloat16),
        compiler_params=pltpu.CompilerParams(vmem_limit_bytes=48 * 1024 * 1024),
        name="attention",
    )(mask, queries, text_keys, text_values, image_keys, image_values)


def per_device(
    n_enc,
    n_req,
    n_seq,
    encoder_hidden,
    prompt_token_ids,
    context_weight,
    context_bias,
    modulation_shift,
    modulation_scale,
    key_value_weight,
    key_value_bias,
    request_prompt,
    adapter_of_request,
    adapter_down_maps,
    adapter_up_maps,
    image_stream_input,
    image_query_key,
    image_value_rows,
):
    f32, bf16 = jnp.float32, jnp.bfloat16
    e, r, s = lax.axis_index("enc"), lax.axis_index("req"), lax.axis_index("seq")
    req_bits = bits_of(n_req)
    model_width = context_weight.shape[1]
    features = context_bias.shape[0]
    tokens = encoder_hidden.shape[1]
    inner = key_value_weight.shape[1] // 2
    part = inner // n_seq

    def heads_of(array, share):
        return lax.dynamic_slice_in_dim(array, share * part, part, 1)

    qk = image_query_key[0, 0]
    sources = [qk[:, :inner], qk[:, inner:], image_value_rows[0, 0], image_stream_input[0, 0]]
    image_parts = [
        jnp.stack([heads_of(a, s ^ k) for a in sources]) for k in range(n_seq)
    ]
    image_parts = [image_parts[0]] + [
        swap(image_parts[k], "seq", n_seq, k) for k in range(1, n_seq)
    ]
    image_all = jnp.concatenate(image_parts, axis=1)
    queries, image_keys, base_values, stream = [image_all[i] for i in range(4)]

    partial_value = lax.dot_general(
        context_weight, encoder_hidden[0], (((0,), (1,)), ((), ())), preferred_element_type=f32
    )
    stat = jnp.sum(partial_value, axis=0) + jnp.sum(context_bias.astype(f32))
    acc = partial_value.reshape((n_enc,) + (2,) * len(req_bits) + (features, tokens))
    for i, bit in enumerate(req_bits):
        mine = (r // bit) % 2
        dim = len(req_bits) - i
        got = swap(with_stat_rows(pick(acc, 1 - mine, dim), stat), "req", n_req, bit).astype(f32)
        acc = pick(acc, mine, dim) + got[..., :features, :]
        got_stat = got.reshape((-1,) + got.shape[-2:])[0, features:]
        stat = stat + got_stat[0] + got_stat[1]
    arrived = [
        swap(with_stat_rows(pick(acc, e ^ k, 0), stat), "enc", n_enc, k).astype(f32)
        for k in range(1, n_enc)
    ]
    embedded = pick(acc, e, 0)
    for got in arrived:
        embedded = embedded + got[:features]
        stat = stat + got[features] + got[features + 1]
    embedded = embedded + context_bias.astype(f32)[:, None]
    centred = embedded - (stat / model_width)[None, :]
    squares = jnp.sum(centred * centred, axis=0)
    scaled = (1.0 + modulation_scale[0].astype(f32))[:, None] * centred

    own = with_stat_rows(scaled, squares)
    blocks = [own] + [swap(own, "seq", n_seq, k) for k in range(1, n_seq)]
    scaled_all = jnp.concatenate([b[:features] for b in blocks], axis=1)
    squares_all = jnp.concatenate(
        [b[features].astype(f32) + b[features + 1].astype(f32) for b in blocks]
    )
    weight_own = jnp.concatenate(
        [heads_of(key_value_weight[:, :inner], s), heads_of(key_value_weight[:, inner:], s)], axis=1
    )
    width = 2 * part
    projected = lax.dot_general(
        scaled_all, weight_own, (((0,), (0,)), ((), ())), preferred_element_type=f32
    )

    shift_part = jnp.dot(modulation_shift, key_value_weight, preferred_element_type=f32)
    for bit in req_bits:
        shift_part = shift_part + swap(shift_part, "req", n_req, bit)
    for bit in bits_of(n_enc):
        shift_part = shift_part + swap(shift_part, "enc", n_enc, bit)
    shift_part = shift_part + key_value_bias.astype(f32)[None]

    def columns_of(row, share):
        return jnp.concatenate(
            [heads_of(row[:, :inner], share), heads_of(row[:, inner:], share)], axis=1
        )

    shift_rows = jnp.concatenate(
        [columns_of(shift_part, s)]
        + [swap(columns_of(shift_part, s ^ k), "seq", n_seq, k) for k in range(1, n_seq)],
        axis=0,
    )

    halves = tokens // n_req // ROWS
    split = (n_seq,) + (2,) * len(req_bits) + (halves, ROWS)
    acc = projected.reshape(split + (width,))
    acc_stat = squares_all.reshape(split)

    def with_stat_columns(data, stat):
        high, low = split_two(stat)
        lane = lax.broadcasted_iota(jnp.int32, stat.shape + (HDIM,), stat.ndim)
        columns = jnp.where(
            lane == 0, high[..., None], jnp.where(lane == 1, low[..., None], jnp.zeros((), bf16))
        )
        return jnp.concatenate([data.astype(bf16), columns], axis=-1)

    for i, bit in enumerate(req_bits):
        mine = (r // bit) % 2
        dim = len(req_bits) - i
        got = swap(
            with_stat_columns(pick(acc, 1 - mine, dim), pick(acc_stat, 1 - mine, dim)),
            "req", n_req, bit,
        ).astype(f32)
        acc = pick(acc, mine, dim) + got[..., :width]
        acc_stat = pick(acc_stat, mine, dim) + got[..., width] + got[..., width + 1]
    acc = acc.reshape(n_enc, ROWS, width)
    acc_stat = acc_stat.reshape(n_enc, ROWS)
    arrived = [
        swap(with_stat_columns(pick(acc, e ^ k, 0), pick(acc_stat, e ^ k, 0)), "enc", n_enc, k)
        .astype(f32)
        for k in range(1, n_enc)
    ]
    rows = pick(acc, e, 0)
    row_squares = pick(acc_stat, e, 0)
    for got in arrived:
        rows = rows + got[:, :width]
        row_squares = row_squares + got[:, width] + got[:, width + 1]
    rows = rows * lax.rsqrt(row_squares / model_width + epsilon_norm)[:, None]
    rows = rows + pick(shift_rows, e // halves, 0)[None]
    keys = rows[:, :part].reshape(ROWS, part // HDIM, HDIM)
    keys = keys * lax.rsqrt(jnp.mean(keys * keys, axis=2, keepdims=True) + epsilon_norm)
    text = jnp.concatenate([keys.reshape(ROWS, part), rows[:, part:]], axis=1).astype(bf16)

    chosen = request_prompt[0, 0]
    relative = s ^ chosen
    by_enc = [text] + [swap(text, "enc", n_enc, k) for k in range(1, n_enc)]
    by_enc = jnp.stack(by_enc)
    by_enc = jnp.stack([pick(by_enc, k ^ e, 0) for k in range(n_enc)])
    held = by_enc.reshape(1, n_seq, halves, ROWS, width)
    first = req_bits[0]
    held = jnp.concatenate([held, swap(held, "req", n_req, first)], axis=0)
    groups = [pick(held, relative, 1)]
    for step in range(2, n_req, 2):
        wanted = swap(relative, "req", n_req, step)
        groups.append(swap(pick(held, wanted, 1), "req", n_req, step))
    text_rows = jnp.concatenate(groups, axis=0).reshape(-1, width)
    live = pick(prompt_token_ids, chosen, 0) != 0
    live = live.reshape(n_req, halves * ROWS)
    live = jnp.concatenate([pick(live, r ^ k, 0) for k in range(n_req)])

    down = lax.dynamic_slice_in_dim(adapter_down_maps[0], s * part, part, 0).T
    up = heads_of(adapter_up_maps[0], s)
    maps = jnp.concatenate([down, up], axis=0)[None]
    for bit in reversed(req_bits):
        maps = jnp.concatenate([maps, swap(maps, "req", n_req, bit)], axis=0)
    other = adapter_of_request[0, 0] ^ r
    index = 0
    for bit in req_bits:
        index = index * 2 + (other // bit) % 2
    chosen_maps = pick(maps, index, 0)
    rank = up.shape[0]
    lowrank = lax.dot_general(
        stream, chosen_maps[:rank], (((1,), (1,)), ((), ())), preferred_element_type=f32
    ).reshape(n_seq, -1, rank)
    for bit in bits_of(n_seq):
        got = swap(lowrank, "seq", n_seq, bit)
        lowrank = lowrank + jnp.stack([got[k ^ bit] for k in range(n_seq)])
    lowrank = lowrank.reshape(-1, rank).astype(bf16)
    image_values = (
        base_values.astype(f32) + jnp.dot(lowrank, chosen_maps[rank:], preferred_element_type=f32)
    ).astype(bf16)

    mixed = attention(
        queries, text_rows[:, :part], text_rows[:, part:], image_keys, image_values, live
    ).reshape(n_seq, -1, part)
    pieces = jnp.stack([mixed[0]] + [swap(mixed[k], "seq", n_seq, k) for k in range(1, n_seq)])
    result = jnp.concatenate([pick(pieces, s ^ k, 0) for k in range(n_seq)], axis=1)
    return result[None, None]


F32, BF16 = jnp.float32, jnp.bfloat16
ANY = pl.BlockSpec(memory_space=pl.ANY)
VMEM = pl.BlockSpec(memory_space=pltpu.VMEM)
SMEM = pl.BlockSpec(memory_space=pltpu.SMEM)
NT = (((1,), (1,)), ((), ()))
TN = (((0,), (0,)), ((), ()))


def partners(send, axis, size):
    return {k: swap(send(k), axis, size, k) for k in far_first(size)}


def far_first(size):
    return list(range(size - 1, 0, -1))


def call(kernel, outs, ins, specs=None, scratch=(), name=None, out_specs=None, vmem=16):
    return pl.pallas_call(
        kernel,
        out_shape=outs,
        in_specs=specs if specs is not None else [VMEM] * len(ins),
        out_specs=out_specs if out_specs is not None else jax.tree.map(lambda _: VMEM, outs),
        scratch_shapes=list(scratch),
        compiler_params=pltpu.CompilerParams(vmem_limit_bytes=int(vmem * 1024 * 1024)),
        name=name,
    )(*ins)


def struct(shape, dtype=BF16):
    return jax.ShapeDtypeStruct(shape, dtype)


def at(index, size):
    return pl.ds(pl.multiple_of(index * size, size), size)


def stat_rows(stat):
    high = stat.astype(BF16).astype(F32)
    row = lax.broadcasted_iota(jnp.int32, (ROWS, stat.shape[1]), 0)
    return jnp.where(row == 0, high, jnp.where(row == 1, stat - high, 0.0)).astype(BF16)


def stat_of(rows):
    rows = rows.astype(F32)
    return rows[0:1] + rows[1:2]


def context_kernel(h_ref, w_ref, b_ref, send_ref, keep_ref, stat_ref):
    mine = lax.rem(lax.axis_index("req"), 2)
    features = b_ref.shape[0]
    pairs = w_ref.shape[1] // (2 * features)
    total = jnp.zeros((1, h_ref.shape[0]), F32)
    for p in range(pairs):
        product = jnp.dot(
            h_ref[...], w_ref[:, p * 2 * features : (p + 1) * 2 * features],
            preferred_element_type=F32,
        ).T
        total = total + jnp.sum(product, axis=0, keepdims=True)
        low, high = product[:features], product[features:]
        rows = slice(p * features, (p + 1) * features)
        keep_ref[rows] = jnp.where(mine == 0, low, high)
        send_ref[rows] = jnp.where(mine == 0, high, low).astype(BF16)
    stat = total + jnp.sum(b_ref[...].astype(F32))
    send_ref[pairs * features :] = stat_rows(stat)
    stat_ref[...] = jnp.broadcast_to(stat, stat_ref.shape)


def scatter_kernel(features, deps, got_ref, keep_ref, stat_ref, *refs):
    kept_ref, out_stat_ref, *send_refs = refs[deps:]
    e = lax.axis_index("enc")
    count = keep_ref.shape[0] // features
    stat = stat_ref[0:1] + stat_of(got_ref[count * features :])
    own = at(e, features)
    for k, send_ref in enumerate(send_refs):
        other = at(e ^ (k + 1), features)
        send_ref[:features] = (keep_ref[other] + got_ref[other].astype(F32)).astype(BF16)
        send_ref[features:] = stat_rows(stat)
    kept_ref[...] = keep_ref[own] + got_ref[own].astype(F32)
    out_stat_ref[...] = jnp.broadcast_to(stat, out_stat_ref.shape)


def lane_rows(rows, first, values, extra):
    tokens = extra.shape[1]
    for j in range(pl.cdiv(values.shape[1], tokens)):
        piece = values[:, j * tokens : min((j + 1) * tokens, values.shape[1])]
        gap = tokens - piece.shape[1]
        if gap:
            piece = jnp.concatenate([piece, jnp.zeros((1, gap), F32)], axis=1)
        extra = jnp.where(rows == first + j, piece, extra)
    return extra


def from_rows(extra, first, count):
    tokens = extra.shape[1]
    pieces = [extra[first + j : first + j + 1] for j in range(pl.cdiv(count, tokens))]
    return jnp.concatenate(pieces, axis=1)[:, :count]


def merge_kernel(deps, prompt_ref, keep_ref, stat_ref, bias_ref, scale_ref, shift_ref, *refs):
    got_refs, (send_ref, kept_ref, out_stat_ref) = refs[deps:-3], refs[-3:]
    features, tokens = bias_ref.shape
    mine = lax.rem(lax.axis_index("req") // 2, 2)
    total = keep_ref[...]
    stat = stat_ref[0:1]
    for got_ref in got_refs:
        total = total + got_ref[: 2 * features].astype(F32)
        stat = stat + stat_of(got_ref[2 * features :])
    kept_ref[...] = total
    own = at(mine, features)
    kept_ref[own] = kept_ref[own] + bias_ref[...]
    send_ref[: 2 * features] = kept_ref[...].astype(BF16)
    rows = lax.broadcasted_iota(jnp.int32, (ROWS, tokens), 0)
    extra = stat_rows(stat).astype(F32)
    extra = lane_rows(rows, 2, scale_ref[...].astype(F32), extra)
    extra = lane_rows(rows, 6, shift_ref[...].astype(F32), extra)
    extra = jnp.where(rows == ROWS - 1, prompt_ref[0, 0].astype(F32), extra)
    send_ref[2 * features :] = extra.astype(BF16)
    out_stat_ref[...] = jnp.broadcast_to(stat, out_stat_ref.shape)


def centre_kernel(
    width, prompt_ref, dep_ref, keep_ref, stat_ref, got_ref, scale_ref, shift_ref, out_ref
):
    features, tokens = scale_ref.shape
    mine = lax.rem(lax.axis_index("req") // 2, 2)
    extra = got_ref[2 * features :].astype(F32)
    stat = stat_ref[0:1] + extra[0:1] + extra[1:2]
    average = stat * (1.0 / width)
    scale = from_rows(extra, 2, features)
    columns = []
    for first in range(0, features, tokens):
        piece = scale[:, first : min(first + tokens, features)]
        piece = jnp.broadcast_to(piece, (tokens, piece.shape[1]))
        gap = tokens - piece.shape[1]
        if gap:
            piece = jnp.concatenate([piece, jnp.zeros((tokens, gap), F32)], axis=1)
        columns.append(piece.T[: min(tokens, features - first)])
    scales = (scale_ref[...], 1.0 + jnp.concatenate(columns, axis=0))
    squares = jnp.zeros((1, tokens), F32)
    for i in range(2):
        block = at(mine ^ i, features)
        centred = keep_ref[block] + got_ref[block].astype(F32) - average
        squares = squares + jnp.sum(centred * centred, axis=0, keepdims=True)
        out_ref[i * features : (i + 1) * features] = (scales[i] * centred).astype(BF16)
    shift = jnp.concatenate([shift_ref[...].astype(F32), from_rows(extra, 6, features)], axis=1)
    other_prompt = extra[ROWS - 1 : ROWS]
    rows = lax.broadcasted_iota(jnp.int32, (ROWS, tokens), 0)
    extra = stat_rows(squares).astype(F32)
    extra = lane_rows(rows, 2, shift, extra)
    extra = jnp.where(rows == ROWS - 1, prompt_ref[0, 0].astype(F32), extra)
    extra = jnp.where(rows == ROWS - 2, other_prompt, extra)
    out_ref[2 * features :] = extra.astype(BF16)


def pass_on_kernel(own_ref, core_ref, got_ref, dep_ref, mine_ref, next_ref):
    features = own_ref.shape[0]
    mine_ref[:features] = own_ref[...]
    mine_ref[features:] = got_ref[0]
    next_ref[:features] = core_ref[...]
    next_ref[features:] = got_ref[1]


def join_kernel(own_ref, got_ref, out_ref):
    size = own_ref.shape[0]
    out_ref[:size] = own_ref[...]
    out_ref[size:] = got_ref[...]


def project_kernel(n_seq, n_enc, *refs):
    payload_refs, weight_refs, refs = refs[:2], refs[2:4], refs[4:]
    prompts_ref, keep_ref, *send_refs = refs[:-1]
    rows_ref = refs[-1]
    features, width = weight_refs[0].shape
    tokens = payload_refs[0].shape[1]
    stride = features + ROWS
    total = None
    squares = [jnp.zeros((1, tokens), F32) for _ in range(n_seq)]
    for k, (payload, weight_ref) in enumerate(zip(payload_refs, weight_refs)):
        left = []
        shifts = []
        for p in range(n_seq):
            left.append(payload[p * stride : p * stride + features].T)
            extra = payload[p * stride + features : (p + 1) * stride].astype(F32)
            squares[p] = squares[p] + extra[0:1] + extra[1:2]
            shifts.append(from_rows(extra, 2, features))
            if p == 0:
                prompts_ref[k] = jnp.max(extra[ROWS - 1 : ROWS]).astype(jnp.int32)
                prompts_ref[2 + k] = jnp.max(extra[ROWS - 2 : ROWS - 1]).astype(jnp.int32)
        shifts.append(jnp.zeros((ROWS - n_seq, features), F32))
        left.append(jnp.concatenate(shifts, axis=0).astype(BF16))
        term = jnp.dot(
            jnp.concatenate(left, axis=0), weight_ref[...], preferred_element_type=F32
        )
        total = term if total is None else total + term
    size = n_seq * tokens // n_enc
    heads = width // HDIM
    step = heads * size + ROWS
    row = lax.broadcasted_iota(jnp.int32, (ROWS, HDIM), 0)
    for z in range(n_enc):
        p, first = divmod(z * size, tokens)
        shift = total[n_seq * tokens + p : n_seq * tokens + p + 1]
        square = squares[p][:, first : first + size]
        square = jnp.concatenate([square, jnp.zeros((1, HDIM - size), F32)], axis=1)
        high = square.astype(BF16).astype(F32)
        extra = jnp.where(
            row == 2 * heads, high, jnp.where(row == 2 * heads + 1, square - high, 0.0)
        )
        for h in range(heads):
            cols = slice(h * HDIM, (h + 1) * HDIM)
            rows_ref[z * step + h * size : z * step + (h + 1) * size] = total[
                z * size : (z + 1) * size, cols
            ]
            high = shift[:, cols].astype(BF16).astype(F32)
            extra = jnp.where(
                row == h, high, jnp.where(row == heads + h, shift[:, cols] - high, extra)
            )
        rows_ref[z * step + heads * size : (z + 1) * step] = extra
    e = lax.axis_index("enc")
    keep_ref[...] = rows_ref[at(e, step)]
    for k, send_ref in enumerate(send_refs):
        send_ref[...] = rows_ref[at(e ^ (k + 1), step)].astype(BF16)


def finish_kernel(n_req, model_width, keep_ref, bias_ref, *refs):
    got_refs, out_ref = refs[:-1], refs[-1]
    r, s = lax.axis_index("req"), lax.axis_index("seq")
    size, width = out_ref.shape
    heads = width // HDIM
    half = width // 2
    inner = bias_ref.shape[1] // 2
    total = keep_ref[...]
    for got_ref in got_refs:
        total = total + got_ref[...].astype(F32)
    extra = total[heads * size :]
    squares = extra[2 * heads : 2 * heads + 1] + extra[2 * heads + 1 : 2 * heads + 2]
    squares = jnp.broadcast_to(squares, (HDIM, HDIM)).T[:size]
    factor = lax.rsqrt(squares * (1.0 / model_width) + epsilon_norm)
    for h in range(heads):
        start = (h * HDIM // half) * inner + (s * n_req + r) * half + h * HDIM % half
        bias = bias_ref[:, pl.ds(pl.multiple_of(start, HDIM), HDIM)].astype(F32)
        shift = extra[h : h + 1] + extra[heads + h : heads + h + 1] + bias
        head = total[h * size : (h + 1) * size] * factor + shift
        if h * HDIM < half:
            head = head * lax.rsqrt(jnp.mean(head * head, axis=1, keepdims=True) + epsilon_norm)
        out_ref[:, h * HDIM : (h + 1) * HDIM] = head.astype(BF16)


def choose_kernel(n_seq, n_enc, chosen_ref, dep_ref, *refs):
    part_refs, out_refs = dict(zip([0] + far_first(n_enc), refs)), refs[n_enc:]
    e, r, s = lax.axis_index("enc"), lax.axis_index("req"), lax.axis_index("seq")
    halves = n_enc // n_seq
    size = part_refs[0].shape[0]
    for k, out_ref in enumerate(out_refs):
        prompt = s ^ chosen_ref[k]
        for h in range(halves):
            place = e ^ (prompt * halves + h)
            for j in range(n_enc):
                @pl.when(place == j)
                def _():
                    out_ref[h * size : (h + 1) * size] = part_refs[j][...]


def weight_kernel(n_req, part, inner, w_ref, dep_ref, own_ref, core_ref, pair_ref, sems):
    r, s = lax.axis_index("req"), lax.axis_index("seq")
    half = part // n_req
    copies = []
    for k, out_ref in enumerate((own_ref, core_ref, pair_ref.at[0], pair_ref.at[1])):
        for side in range(2):
            columns = pl.ds(
                pl.multiple_of(side * inner + (s * n_req + (r ^ k)) * half, HDIM), half
            )
            copies.append(
                pltpu.make_async_copy(
                    w_ref.at[:, columns],
                    out_ref.at[:, pl.ds(side * half, half)],
                    sems.at[2 * k + side],
                )
            )
    for copy in copies:
        copy.start()
    for copy in copies:
        copy.wait()


def image_kernel(part, inner, step, qk_ref, v_ref, x_ref, dep_ref, out_ref, sems):
    start = (lax.axis_index("seq") ^ step) * part
    copies = []
    for i, (ref, base) in enumerate(((qk_ref, 0), (qk_ref, inner), (v_ref, 0), (x_ref, 0))):
        columns = pl.ds(pl.multiple_of(base + start, HDIM), part)
        copies.append(pltpu.make_async_copy(ref.at[:, columns], out_ref.at[i], sems.at[i]))
    for copy in copies:
        copy.start()
    for copy in copies:
        copy.wait()


def maps_kernel(part, down_ref, up_ref, dep_ref, out_ref, sems):
    rank = down_ref.shape[0]
    columns = pl.ds(pl.multiple_of(lax.axis_index("seq") * part, HDIM), part)
    copies = [
        pltpu.make_async_copy(down_ref.at[:, columns], out_ref.at[pl.ds(0, rank)], sems.at[0]),
        pltpu.make_async_copy(up_ref.at[:, columns], out_ref.at[pl.ds(rank, rank)], sems.at[1]),
    ]
    for copy in copies:
        copy.start()
    for copy in copies:
        copy.wait()


def join_maps_kernel(own_ref, core_ref, dep_ref, out_ref):
    out_ref[0] = own_ref[...]
    out_ref[1] = core_ref[...]


def lowrank_kernel(part, adapter_ref, x_ref, got_ref, *refs):
    own_ref, pair_ref, out_ref, chosen_ref = refs
    map_refs = (own_ref.at[0], own_ref.at[1], pair_ref.at[0], pair_ref.at[1])
    place = adapter_ref[0, 0] ^ lax.axis_index("req")
    rank = out_ref.shape[-1]
    for k, ref in enumerate(map_refs):
        @pl.when(place == k)
        def _():
            chosen_ref[...] = ref[rank:]
            own = x_ref[:, pl.ds(pl.multiple_of(lax.axis_index("seq") * part, HDIM), part)]
            for i, rows in enumerate((own, got_ref[3])):
                out_ref[i] = lax.dot_general(
                    rows, ref[:rank], NT, preferred_element_type=F32
                )


def arrange_kernel(n_req, part, inner, low_ref, other_ref, maps_ref, qk_ref, v_ref, *refs):
    got_refs, (q_out, k_out, v_out) = refs[:-3], refs[-3:]
    r, s = lax.axis_index("req"), lax.axis_index("seq")
    half = part // n_req
    tokens = qk_ref.shape[0]
    low = [(low_ref[i] + other_ref[i ^ 1]).astype(BF16) for i in range(2)]
    for k in range(n_req):
        place = (r ^ k) * half
        up = maps_ref[:, pl.ds(pl.multiple_of(place, HDIM), half)]
        for i in range(len(got_refs) + 1):
            rows = slice(i * tokens, (i + 1) * tokens)
            if i == 0:
                own = s * part + place
                q = qk_ref[:, pl.ds(pl.multiple_of(own, HDIM), half)]
                key = qk_ref[:, pl.ds(pl.multiple_of(inner + own, HDIM), half)]
                base = v_ref[:, pl.ds(pl.multiple_of(own, HDIM), half)]
            else:
                columns = pl.ds(pl.multiple_of(place, HDIM), half)
                q = got_refs[i - 1][0, :, columns]
                key = got_refs[i - 1][1, :, columns]
                base = got_refs[i - 1][2, :, columns]
            q_out[k, rows] = q
            k_out[k, rows] = key
            v_out[k, rows] = (
                base.astype(F32) + jnp.dot(low[i], up, preferred_element_type=F32)
            ).astype(BF16)


def heads_kernel(place, first, scale, live_ref, text_ref, q_ref, k_ref, v_ref, *refs):
    out_refs = refs[2:]
    half = q_ref.shape[2]
    size = out_refs[0].shape[0]
    heads = [slice(h * HDIM, (h + 1) * HDIM) for h in range(half // HDIM)]
    live = live_ref[...]
    live = jnp.concatenate([live, jnp.ones((1, k_ref.shape[1]), live.dtype)], axis=1) != 0
    scores = []
    for cols in heads:
        q = q_ref[place, first * size : (first + len(out_refs)) * size, cols]
        keys = jnp.concatenate([text_ref[:, cols], k_ref[place, :, cols]], axis=0)
        score = lax.dot_general(q, keys, NT, preferred_element_type=F32) * scale
        scores.append(jnp.where(live, score, -jnp.inf))
    weights = [jnp.exp(x - jnp.max(x, axis=1, keepdims=True)) for x in scores]
    totals = [jnp.sum(w, axis=1, keepdims=True) for w in weights]
    mixed = []
    for cols, w in zip(heads, weights):
        vals = slice(half + cols.start, half + cols.stop)
        values = jnp.concatenate([text_ref[:, vals], v_ref[place, :, cols]], axis=0)
        mixed.append(jnp.dot(w.astype(BF16), values, preferred_element_type=F32))
    for cols, m, total in zip(heads, mixed, totals):
        rows = (m / total).astype(BF16)
        for i, out_ref in enumerate(out_refs):
            out_ref[:, cols] = rows[i * size : (i + 1) * size]


def assemble_kernel(n_req, n_seq, *refs):
    out_ref = refs[-1]
    r, s = lax.axis_index("req"), lax.axis_index("seq")
    half = refs[0].shape[1]
    for k in range(n_req):
        for i in range(n_seq):
            start = ((s ^ i) * n_req + (r ^ k)) * half
            out_ref[:, pl.ds(pl.multiple_of(start, HDIM), half)] = refs[k * n_seq + i][...]


def per_device_heads(
    n_enc,
    n_req,
    n_seq,
    encoder_hidden,
    prompt_token_ids,
    context_weight,
    context_bias,
    modulation_shift,
    modulation_scale,
    key_value_weight,
    key_value_bias,
    request_prompt,
    adapter_of_request,
    adapter_down_maps,
    adapter_up_maps,
    image_stream_input,
    image_query_key,
    image_value_rows,
):
    e, r, s = lax.axis_index("enc"), lax.axis_index("req"), lax.axis_index("seq")
    model_width = context_weight.shape[1]
    features = context_bias.shape[0]
    tokens = encoder_hidden.shape[1]
    inner = key_value_weight.shape[1] // 2
    part = inner // n_seq
    half = part // n_req
    image_rows = image_query_key.shape[2]
    rank = adapter_up_maps.shape[1]
    qk, base, stream = image_query_key[0, 0], image_value_rows[0, 0], image_stream_input[0, 0]
    dma = pltpu.SemaphoreType.DMA
    stat = struct((8, tokens), F32)

    send, keep, sums = call(
        context_kernel,
        (
            struct((model_width // 2 + ROWS, tokens)),
            struct((model_width // 2, tokens), F32),
            stat,
        ),
        (encoder_hidden[0], context_weight, context_bias),
        name="context",
    )
    got = swap(send, "req", n_req, 1)

    keep, sums, *sends = call(
        functools.partial(scatter_kernel, 2 * features, 0),
        (struct((2 * features, tokens), F32), stat)
        + tuple(struct((2 * features + ROWS, tokens)) for _ in range(1, n_enc)),
        (got, keep, sums),
        name="scatter",
    )
    arrived = partners(lambda k: sends[k - 1], "enc", n_enc).values()
    weight = struct((features, 2 * half))
    weight_own, weight_core, weight_pair = call(
        functools.partial(weight_kernel, n_req, part, inner),
        (weight, weight, struct((2, features, 2 * half))),
        (key_value_weight, keep),
        [ANY] * 2,
        [dma((2 * n_req,))],
        name="weight_pack",
        vmem=16,
    )

    weight_pair_got = swap(weight_pair, "req", n_req, 2)
    bias_columns = jnp.broadcast_to(context_bias.astype(F32)[:, None], (features, tokens))
    scale_columns = jnp.broadcast_to(
        1.0 + modulation_scale[0].astype(F32)[:, None], (features, tokens)
    )
    deps = ()
    send, keep, sums = call(
        functools.partial(merge_kernel, len(deps)),
        (
            struct((2 * features + ROWS, tokens)),
            struct((2 * features, tokens), F32),
            stat,
        ),
        (
            request_prompt,
            keep,
            sums,
            bias_columns,
            modulation_scale,
            modulation_shift,
            *deps,
            *arrived,
        ),
        [SMEM] + [VMEM] * 5 + [ANY] * len(deps) + [VMEM] * len(arrived),
        name="merge",
    )
    got = swap(send, "req", n_req, 2)
    weights = struct((2 * features, 2 * half))
    weight_mine, weight_next = call(
        pass_on_kernel,
        (weights, weights),
        (weight_own, weight_core, weight_pair_got, keep),
        [VMEM] * 3 + [ANY],
        name="pass_on",
    )
    weight_next = swap(weight_next, "req", n_req, 1)
    own = call(
        functools.partial(centre_kernel, model_width),
        struct((2 * features + ROWS, tokens)),
        (request_prompt, weight_mine, keep, sums, got, scale_columns, modulation_shift),
        [SMEM, ANY] + [VMEM] * 5,
        name="centre",
    )
    joined = call(
        join_kernel,
        struct((n_seq * (2 * features + ROWS), tokens)),
        (own, swap(own, "seq", n_seq, 1)),
        name="join",
    )
    packed = [
        call(
            functools.partial(image_kernel, part, inner, k),
            struct((4, image_rows, part)),
            (qk, base, stream, joined),
            [ANY] * 4,
            [dma((4,))],
            name="image_pack",
        )
        for k in range(1, n_seq)
    ]
    image_got = [swap(packed[k - 1], "seq", n_seq, k) for k in range(1, n_seq)]
    weight_pair = lax.optimization_barrier((weight_pair, keep))[0]
    joined_core = swap(joined, "req", n_req, 1)
    maps = call(
        functools.partial(maps_kernel, part),
        struct((2 * rank, part)),
        (adapter_down_maps[0].T, adapter_up_maps[0], joined),
        [ANY] * 3,
        [dma((2,))],
        name="maps_pack",
    )
    maps_core = swap(maps, "req", n_req, 1)
    maps = call(
        join_maps_kernel,
        struct((2, 2 * rank, part)),
        (maps, maps_core, joined),
        [VMEM, VMEM, ANY],
        name="maps_join",
    )

    size = n_seq * tokens // n_enc
    step = 2 * half // HDIM * size + ROWS
    ids, keep, *sends = call(
        functools.partial(project_kernel, n_seq, n_enc),
        (struct((n_req,), jnp.int32), struct((step, HDIM), F32))
        + tuple(struct((step, HDIM)) for _ in range(1, n_enc)),
        (joined, joined_core, weight_mine, weight_next),
        scratch=[pltpu.VMEM((n_enc * step, HDIM), F32)],
        out_specs=(SMEM,) + (VMEM,) * n_enc,
        name="project",
    )
    arrived = partners(lambda k: sends[k - 1], "enc", n_enc).values()

    maps = lax.optimization_barrier((maps, keep))[0]
    maps_pair = swap(maps, "req", n_req, 2)

    text = call(
        functools.partial(finish_kernel, n_req, model_width),
        struct((size, 2 * half)),
        (keep, key_value_bias[None], *arrived),
        [VMEM] * (2 + len(arrived)),
        name="finish",
    )
    low, chosen_maps = call(
        functools.partial(lowrank_kernel, part),
        (struct((n_seq, image_rows, rank), F32), struct((rank, part))),
        (
            adapter_of_request,
            stream,
            image_got[0],
            maps,
            maps_pair,
        ),
        [SMEM] + [VMEM] * 4,
        name="lowrank",
    )
    low_other = swap(low, "seq", n_seq, 1)
    arranged = struct((n_req, n_seq * image_rows, half))
    queries, image_keys, image_values = call(
        functools.partial(arrange_kernel, n_req, part, inner),
        (arranged, arranged, arranged),
        (low, low_other, chosen_maps, qk, base, *image_got),
        name="arrange",
    )
    parts = partners(lambda k: text, "enc", n_enc)
    rows = call(
        functools.partial(choose_kernel, n_seq, n_enc),
        [struct((tokens, 2 * half)) for _ in range(n_req)],
        (ids, image_values, text, *parts.values()),
        [SMEM, ANY] + [VMEM] * n_enc,
        name="choose",
    )
    rows = {0: rows[0], **partners(lambda k: rows[k], "req", n_req)}
    live = lax.dynamic_slice_in_dim(prompt_token_ids, request_prompt[0, 0], 1, 0)
    def heads(k, first, count, last):
        return call(
            functools.partial(heads_kernel, k, first, HDIM ** (-0.5)),
            [struct((image_rows, half))] * count,
            (live, rows[k], queries, image_keys, image_values, *last),
            [VMEM] * 5 + [ANY] * 2,
            name="heads",
        )

    pieces = [None] * n_req
    last = (live, live)
    for k in range(n_req):
        if k < n_req - 1:
            mixed = heads(k, 0, n_seq, last)
        else:
            (back,) = heads(k, 1, 1, last)
            (mine,) = heads(k, 0, 1, (back, last[1]))
            mixed = (mine, back)
        pieces[k] = [mixed[0], swap(mixed[1], "seq", n_seq, 1)]
        last = (mixed[0], pieces[k - 1][1] if k else live)
    result = call(
        functools.partial(assemble_kernel, n_req, n_seq),
        struct((image_rows, inner)),
        tuple(p for group in pieces for p in group),
        name="assemble",
    )
    return result[None, None]


def solution(mesh):
    sizes = mesh.shape
    n_enc, n_req, n_seq = sizes["enc"], sizes["req"], sizes["seq"]

    def run(*arrays):
        heads = arrays[6].shape[1] // (2 * HDIM)
        fits = n_seq == 2 and n_req == 4 and heads % (n_seq * n_req) == 0
        return (per_device_heads if fits else per_device)(n_enc, n_req, n_seq, *arrays)

    return jax.shard_map(
        run,
        mesh=mesh,
        in_specs=(
            P("seq", None, ("enc", "req")),
            P(),
            P(("enc", "req"), None),
            P(("enc", "req")),
            P("seq", ("enc", "req")),
            P("seq", ("enc", "req")),
            P(("enc", "req"), None),
            P(),
            P("enc", "req"),
            P("enc", "req"),
            P("req", None, None),
            P("req", None, None),
            P("enc", "req", "seq", None),
            P("enc", "req", "seq", None),
            P("enc", "req", "seq", None),
        ),
        out_specs=P("enc", "req", "seq", None),
        check_vma=False,
    )
```
